32 devices in a mesh: stream: 4 (over z), girth: 8 (over y, x, core).
Axes of the slice: x: 2, y: 2, z: 4, core: 2. Of those that a mesh axis runs over, the one named last changes fastest.
Arguments:
- velocity: float32 [3, 16, 64, 256], P(None, 'stream', 'girth'), may hold values from -6 to 6
- pressure: float32 [16, 64, 256], P('stream', 'girth'), may hold values from -6 to 6
- kinetic_energy: float32 [16, 64, 256], P('stream', 'girth'), may hold values from 0.01 to 1
- dissipation_rate: float32 [16, 64, 256], P('stream', 'girth'), may hold values from 0.5 to 20
- corner_ids: int32 [128, 1024], replicated, may hold values from 0 to 30462, as said below
- fractions: float32 [3, 128, 1024], replicated, may hold values from 0 to 1
- sector_owner: int32 [64, 1], replicated, may hold values from 0 to 7; in each aligned block of 64 rows (0 to 63, 64 to 127, ...) at most 24 rows name the same one
Outputs:
- new_velocity: float32 [3, 16, 64, 256], P(None, 'stream', 'girth')
- new_energy: float32 [16, 64, 256], P('stream', 'girth')
- new_rate: float32 [16, 64, 256], P('stream', 'girth')
- harmonics: float32 [128, 768], P(('stream', 'girth'))
The draws below stay inside these ranges and needn't reach their ends.
Inputs may be any that keep to these rules, and one draw needn't show every extreme that they name: `corner_ids`: each entry is s * 8 * 256 + g * 256 + q with s from 0 to 14, g from 0 to 6 and q from 0 to 254. `sector_owner`: sector s covers azimuths s * 16 to (s + 1) * 16 - 1. Every girth index owns at least one sector and at most 24, and some girth index owns exactly 24.
All inputs are finite; a program needn't handle non-finite values.
Results may differ from the reference program's by a relative error of at most 0.000076.
Values sent between devices are 32-bit elements; how exact they have to be, the bound alone decides.
No kernel may reach another device: no remote copies, remote signals or barrier semaphores. Data moves between devices by JAX's collectives and lax.ppermute only.
A program may use at most 192 MiB of HBM per device.

```python
import math
import jax
import jax.numpy as jnp
import numpy as np
from jax import lax

CG = 8
NR = 256
NRAD = 128
NAZ = 1024
NH = 128
NSEC = 64
NS = 16
NG = 64
SW = 16
MAXSEC = 24
N_GIRTH = 8


def draw_corner_ids(key, part):
    key = jax.random.fold_in(key, 7)
    stream_key, girth_key, radial_key = jax.random.split(key, 3)
    stream_cell = jax.random.randint(stream_key, (NRAD, NAZ), 0, NS - 1)
    girth_cell = jax.random.randint(girth_key, (NRAD, NAZ), 0, CG - 1)
    radial_cell = jax.random.randint(radial_key, (NRAD, NAZ), 0, NR - 1)
    cell_ids = stream_cell * (CG * NR) + girth_cell * NR + radial_cell
    flat_index = lax.broadcasted_iota(jnp.int32, (NRAD, NAZ), 0) * NAZ + lax.broadcasted_iota(jnp.int32, (NRAD, NAZ), 1)
    cell_ids = jnp.where(flat_index == 0, 0, cell_ids)
    cell_ids = jnp.where(flat_index == NRAD * NAZ - 1, (NS - 2) * CG * NR + (CG - 2) * NR + NR - 2, cell_ids)
    return cell_ids.astype(jnp.int32)


def shard_levels(own_key, shape, cuts, smallest, largest):
    def one(dim, blocks):
        draws = jax.random.uniform(jax.random.fold_in(jax.random.fold_in(own_key, 6), dim), (blocks,), jnp.float32, smallest / len(cuts), largest / len(cuts))
        return jnp.repeat(jnp.exp(draws), shape[dim] // blocks).reshape((-1,) + (1,) * (len(shape) - dim - 1))

    loudness = one(*cuts[0])
    for cut in cuts[1:]:
        loudness = loudness * one(*cut)
    return loudness


def assign_block(key, own, number, rows, count, top, bound, slope):
    sequence = jax.random.permutation(key, count)
    crowded, ordinary = load_shares(count, rows * top, bound, slope, True), load_shares(count, rows * top, bound, slope, False)
    places = jnp.arange(count)

    def named(sizes, turn):
        used = int((sizes > 0).sum())
        fixed = max(1, used // 4)
        moved = fixed + (places - fixed + turn * (used - fixed)) % max(1, count - fixed)
        return jnp.zeros((count,), jnp.int32).at[sequence[jnp.where(places < fixed, places, moved)]].set(jnp.asarray(sizes, jnp.int32))

    sizes = jnp.where(number % 4 == 0, named(crowded, number // 4), named(ordinary, number - number // 4 - 1))
    mixed = jax.random.permutation(jax.random.fold_in(own, 3), count)
    source_of, taker = mixed[0:count // 2 * 2:2], mixed[1:count // 2 * 2:2]
    slack = jnp.minimum(sizes[source_of] - 1, bound - sizes[taker]) // 2
    slack = jnp.where((source_of == sequence[0]) | (taker == sequence[0]) | (sizes[taker] == 0), 0, jnp.maximum(slack, 0))
    moved = jax.random.randint(jax.random.fold_in(own, 4), (count // 2,), 0, 1 << 20) % (slack + 1)
    sizes = sizes.at[source_of].add(-moved).at[taker].add(moved)
    labels = jnp.searchsorted(jnp.cumsum(sizes), jnp.arange(rows * top), side="right").astype(jnp.int32)
    table = labels.reshape(top, rows).T
    table = table[jax.random.permutation(jax.random.fold_in(own, 1), rows)]
    turn = jax.random.randint(jax.random.fold_in(own, 2), (rows, 1), 0, top)
    return jnp.take_along_axis(table, (jnp.arange(top)[None, :] + turn) % top, axis=1)


def load_shares(count, total, bound, slope, full):
    loads = [(1 << 20) // math.isqrt(grade ** slope) + 1 for grade in range(1, count + 1)]
    largest = bound if full else min(bound, max(-(-total // count), total * loads[0] // sum(loads)))
    least = 1 if total - largest >= count - 1 else 0
    counts, spare = [largest] + [least] * (count - 1), total - largest - least * (count - 1)
    while spare > 0:
        free = [i for i in range(1, count) if counts[i] < largest] or [i for i in range(1, count) if counts[i] < bound]
        whole, budget = sum([loads[i] for i in free]), spare
        for i in free:
            extra = min(bound - counts[i], max(1, budget * loads[i] // whole), spare)
            counts[i] = counts[i] + extra
            spare = spare - extra
    return np.array(counts)


def bell_draw(own_key, dims, deviation, reach, cuts=(), dtype=jnp.bfloat16):
    drawn = jax.random.normal(own_key, dims, jnp.float32) * deviation
    if len(cuts) > 0:
        drawn = shard_levels(own_key, dims, cuts, -0.22, 0.18) * drawn
    return jnp.clip(drawn, min=-reach, max=reach).astype(dtype)


def setup_inputs(seed: int = 0) -> dict:
    keys = jax.random.split(jax.random.key(seed), 8)
    velocity = bell_draw(keys[0], (3, NS, NG, NR), 1.0, 6.0, ((1, 4), (2, 8)), jnp.float32)
    pressure = bell_draw(keys[1], (NS, NG, NR), 1.0, 6.0, ((0, 4), (1, 8)), jnp.float32)
    kinetic_energy = jnp.clip(jnp.exp(math.log(1.0) - 4.6051702 * jax.random.uniform(keys[2], (NS, NG, NR), jnp.float32) ** shard_levels(keys[2], (NS, NG, NR), ((0, 4), (1, 8)), -0.2, 0.2)), 0.01, 1.0)
    dissipation_rate = jnp.clip(jnp.exp(math.log(20.0) - 3.6888795 * jax.random.uniform(keys[3], (NS, NG, NR), jnp.float32) ** shard_levels(keys[3], (NS, NG, NR), ((0, 4), (1, 8)), -0.2, 0.2)), 0.5, 20.0)
    corner_ids = draw_corner_ids(jax.random.fold_in(keys[7], 71), 0)
    fractions = jnp.clip(jax.random.uniform(keys[5], (3, NRAD, NAZ), jnp.float32, 0.0, 1.0), 0.0, 1.0)
    sector_owner_keys = jax.random.split(jax.random.fold_in(keys[6], 1), NSEC // NSEC)
    sector_owner_turns = jax.random.permutation(jax.random.fold_in(keys[6], 3), NSEC // NSEC)
    sector_owner = jax.vmap(lambda own, number: assign_block(jax.random.fold_in(keys[6], 2), own, number, NSEC, N_GIRTH, 1, MAXSEC, 2))(sector_owner_keys, sector_owner_turns).reshape((NSEC, 1))
    return dict(velocity=velocity, pressure=pressure, kinetic_energy=kinetic_energy, dissipation_rate=dissipation_rate, corner_ids=corner_ids, fractions=fractions, sector_owner=sector_owner)


base_viscosity = 0.05
time_step = 0.2
beta_star = 0.09
beta_rate = 0.075
alpha_rate = 0.52
wall_rate = 1.0


def shifted(values, offsets):
    extent = values.shape
    return values[2 + offsets[0]:extent[0] - 2 + offsets[0], 2 + offsets[1]:extent[1] - 2 + offsets[1], 2 + offsets[2]:extent[2] - 2 + offsets[2]]


def offset_of(direction, amount):
    offsets = [0, 0, 0]
    offsets[direction] = amount
    return tuple(offsets)


def derivative(values, direction):
    near_pair = shifted(values, offset_of(direction, 1)) - shifted(values, offset_of(direction, -1))
    far_pair = shifted(values, offset_of(direction, 2)) - shifted(values, offset_of(direction, -2))
    return (8.0 * near_pair - far_pair) / 12.0


def diffusion(values, viscosity, direction):
    center = shifted(values, (0, 0, 0))
    middle = shifted(viscosity, (0, 0, 0))
    upper_face = 0.5 * (middle + shifted(viscosity, offset_of(direction, 1)))
    lower_face = 0.5 * (middle + shifted(viscosity, offset_of(direction, -1)))
    return upper_face * (shifted(values, offset_of(direction, 1)) - center) - lower_face * (center - shifted(values, offset_of(direction, -1)))


def advance(padded):
    viscosity = base_viscosity + padded[4] / (padded[5] + wall_rate)
    centers = [shifted(padded[component], (0, 0, 0)) for component in range(6)]
    strain = jnp.zeros_like(centers[0])
    updated = []
    for component in range(3):
        change = -derivative(padded[3], component)
        for direction in range(3):
            gradient = derivative(padded[component], direction)
            strain = strain + gradient * gradient
            change = change - centers[direction] * gradient + diffusion(padded[component], viscosity, direction)
        updated.append(centers[component] + time_step * change)
    eddy_viscosity = centers[4] / (centers[5] + wall_rate)
    energy_change = eddy_viscosity * strain - beta_star * centers[4] * centers[5]
    rate_change = alpha_rate * strain - beta_rate * centers[5] * centers[5]
    for direction in range(3):
        energy_change = energy_change - centers[direction] * derivative(padded[4], direction) + diffusion(padded[4], viscosity, direction)
        rate_change = rate_change - centers[direction] * derivative(padded[5], direction) + diffusion(padded[5], viscosity, direction)
    return jnp.stack(updated), centers[4] + time_step * energy_change, centers[5] + time_step * rate_change


def side_weight(fraction, upper_side):
    if upper_side:
        return fraction
    return 1.0 - fraction


def reference(velocity, pressure, kinetic_energy, dissipation_rate, corner_ids, fractions, sector_owner):
    stacked = jnp.concatenate([velocity, pressure[None], kinetic_energy[None], dissipation_rate[None]], axis=0)
    padded = jnp.pad(stacked, ((0, 0), (2, 2), (2, 2), (2, 2)))
    new_velocity, new_energy, new_rate = advance(padded)
    flat_field = new_velocity.reshape(3, -1)
    plane_cells = CG * NR
    stream_cell = corner_ids // plane_cells
    remainder = corner_ids - stream_cell * plane_cells
    girth_cell = remainder // NR
    radial_cell = remainder - girth_cell * NR
    owners = jnp.repeat(sector_owner[:, 0], SW)
    girth_global = owners[None, :] * CG + girth_cell
    sampled = jnp.zeros((3, NRAD, NAZ), jnp.float32)
    for along_s in (0, 1):
        for along_g in (0, 1):
            for along_r in (0, 1):
                weight = side_weight(fractions[0], along_s) * side_weight(fractions[1], along_g) * side_weight(fractions[2], along_r)
                position = ((stream_cell + along_s) * NG + girth_global + along_g) * NR + radial_cell + along_r
                picked = jnp.take(flat_field, position.reshape(-1).astype(jnp.int32), axis=1).reshape(3, NRAD, NAZ)
                sampled = sampled + weight * picked
    spectrum = jnp.fft.rfft(sampled, axis=2, norm="ortho")[:, :, :NH]
    pieces = jnp.stack([jnp.real(spectrum), jnp.imag(spectrum)], axis=1).astype(jnp.float32)
    harmonics = jnp.transpose(pieces, (2, 0, 1, 3)).reshape(NRAD, 6 * NH)
    return new_velocity, new_energy, new_rate, harmonics
```

```python
import functools
import math

import jax
import jax.numpy as jnp
import numpy as np
from jax import lax
from jax.experimental import pallas as pl
from jax.experimental.pallas import tpu as pltpu
from jax.sharding import PartitionSpec as P

NH = 128

base_viscosity = 0.05
time_step = 0.2
beta_star = 0.09
beta_rate = 0.075
alpha_rate = 0.52
wall_rate = 1.0

LANES = 128
ROWS = 8
VMEM_LIMIT = 48 * 1024 * 1024


def prepare_kernel(cells_s, cells_g, cells_r, ids_ref, frac_ref, q_ref, fr_ref, xg_ref, hs_ref):
    stream_first = lax.axis_index("stream") * cells_s
    plane_cells = cells_g * cells_r
    azimuths = ids_ref.shape[1]
    for block in range(azimuths // LANES):
        cols = pl.ds(block * LANES, LANES)
        ids = ids_ref[:, cols].T
        fs = frac_ref[0, :, cols].T
        fg = frac_ref[1, :, cols].T
        fr = frac_ref[2, :, cols].T
        stream_cell = ids // plane_cells
        remainder = ids - stream_cell * plane_cells
        girth_cell = remainder // cells_r
        q_ref[cols, :] = remainder - girth_cell * cells_r
        fr_ref[cols, :] = fr
        xg_ref[cols, :] = girth_cell.astype(jnp.float32) + fg
        local = stream_cell - stream_first
        for layer in range(cells_s):
            hs_ref[layer, cols, :] = jnp.where(
                local == layer, 1.0 - fs, jnp.where(local == layer - 1, fs, 0.0)
            )


def prepare(corner_ids, fractions, cells_s, cells_g, cells_r):
    radii, azimuths = corner_ids.shape
    shape = jax.ShapeDtypeStruct
    return pl.pallas_call(
        functools.partial(prepare_kernel, cells_s, cells_g, cells_r),
        out_shape=(
            shape((azimuths, radii), jnp.int32),
            shape((azimuths, radii), jnp.float32),
            shape((azimuths, radii), jnp.float32),
            shape((cells_s, azimuths, radii), jnp.float32),
        ),
        compiler_params=pltpu.CompilerParams(vmem_limit_bytes=VMEM_LIMIT),
        cost_estimate=pl.CostEstimate(
            flops=20 * radii * azimuths, bytes_accessed=44 * radii * azimuths, transcendentals=0
        ),
        name="prepare_points",
    )(corner_ids, fractions)


def radial(values, amount, fill):
    extent = values.shape[-1]
    rolled = pltpu.roll(values, (-amount) % extent, values.ndim - 1)
    position = lax.broadcasted_iota(jnp.int32, values.shape, values.ndim - 1) + amount
    return jnp.where((position >= 0) & (position < extent), rolled, fill)


def advance(own, before, after, left, right, ext_ref, visc_ref):
    cells_s, cells_g, _ = own[0].shape
    mid = ROWS

    def along_s(stack, amount):
        return stack[2 + amount : 2 + amount + cells_s]

    def along_g(ref, amount):
        return ref[:, mid + amount : mid + amount + cells_g, :]

    def viscosity(energy, rate):
        return base_viscosity + energy / (rate + wall_rate)

    stacks = [jnp.concatenate([before[f], own[f], after[f]], axis=0) for f in range(6)]
    for f in range(6):
        ext_ref[f, :, mid - 2 : mid, :] = left[f]
        ext_ref[f, :, mid : mid + cells_g, :] = own[f]
        ext_ref[f, :, mid + cells_g : mid + cells_g + 2, :] = right[f]
    middle = viscosity(own[4], own[5])
    visc_stack = viscosity(stacks[4], stacks[5])
    visc_ref[:, mid - 2 : mid, :] = viscosity(left[4], left[5])
    visc_ref[:, mid : mid + cells_g, :] = middle
    visc_ref[:, mid + cells_g : mid + cells_g + 2, :] = viscosity(right[4], right[5])
    faces = [
        (
            0.5 * (middle + along_s(visc_stack, 1)),
            0.5 * (middle + along_s(visc_stack, -1)),
        ),
        (
            0.5 * (middle + along_g(visc_ref, 1)),
            0.5 * (middle + along_g(visc_ref, -1)),
        ),
        (
            0.5 * (middle + radial(middle, 1, base_viscosity)),
            0.5 * (middle + radial(middle, -1, base_viscosity)),
        ),
    ]

    def neighbour(f, direction, amount):
        if direction == 0:
            return along_s(stacks[f], amount)
        if direction == 1:
            return along_g(ext_ref.at[f], amount)
        return radial(own[f], amount, 0.0)

    def terms(f, direction):
        up, down = neighbour(f, direction, 1), neighbour(f, direction, -1)
        far = neighbour(f, direction, 2) - neighbour(f, direction, -2)
        gradient = (8.0 * (up - down) - far) * (1.0 / 12.0)
        above, below = faces[direction]
        return gradient, above * (up - own[f]) - below * (own[f] - down)

    strain = None
    updated = []
    for f in range(3):
        change = -terms(3, f)[0]
        for direction in range(3):
            gradient, spread = terms(f, direction)
            strain = gradient * gradient if strain is None else strain + gradient * gradient
            change = change - own[direction] * gradient + spread
        updated.append(own[f] + time_step * change)
    energy = own[4] / (own[5] + wall_rate) * strain - beta_star * own[4] * own[5]
    rate = alpha_rate * strain - beta_rate * own[5] * own[5]
    for direction in range(3):
        gradient, spread = terms(4, direction)
        energy = energy - own[direction] * gradient + spread
        gradient, spread = terms(5, direction)
        rate = rate - own[direction] * gradient + spread
    return updated, own[4] + time_step * energy, own[5] + time_step * rate


def section_kernel(
    owner_ref,
    vel_ref,
    p_ref,
    k_ref,
    w_ref,
    before_ref,
    after_ref,
    left_ref,
    right_ref,
    q_ref,
    fr_ref,
    xg_ref,
    hs_ref,
    table_ref,
    new_vel_ref,
    new_k_ref,
    new_w_ref,
    harm_ref,
    ext_ref,
    visc_ref,
    field_ref,
    slope_ref,
    disk_ref,
    chosen_ref,
):
    cells_s, cells_g, cells_r = p_ref.shape
    halves = cells_r // LANES
    sectors = owner_ref.shape[0]
    width = q_ref.shape[0] // sectors
    me = lax.axis_index("girth")

    own = [vel_ref[0], vel_ref[1], vel_ref[2], p_ref[...], k_ref[...], w_ref[...]]
    six = range(6)
    updated, energy, rate = advance(
        own,
        [before_ref[f] for f in six],
        [after_ref[f] for f in six],
        [left_ref[f] for f in six],
        [right_ref[f] for f in six],
        ext_ref,
        visc_ref,
    )
    new_k_ref[...] = energy
    new_w_ref[...] = rate
    for c in range(3):
        new_vel_ref[c] = updated[c]
        slope = radial(updated[c], 1, 0.0) - updated[c]
        for h in range(halves):
            lanes = slice(h * LANES, (h + 1) * LANES)
            field_ref[c, :, h] = updated[c][:, :, lanes]
            slope_ref[c, :, h] = slope[:, :, lanes]

    disk_ref[...] = jnp.zeros_like(disk_ref)
    chosen_ref[...] = jnp.zeros_like(chosen_ref)
    girth_row = lax.broadcasted_iota(jnp.int32, (cells_g, LANES), 0).astype(jnp.float32)

    def pick(ref, c, s, index, half_of):
        out = None
        for h in range(halves):
            got = jnp.take_along_axis(ref[c, s, h], index, axis=1, mode="promise_in_bounds")
            out = got if out is None else jnp.where(half_of[h], got, out)
        return out

    def spread(row):
        return jnp.broadcast_to(row, (cells_g, LANES))

    def eight(source, target):
        rows = pl.ds(pl.multiple_of(source, ROWS), ROWS)
        q8, fr8, xg8 = q_ref[rows, :], fr_ref[rows, :], xg_ref[rows, :]
        hs8 = [hs_ref[s, rows, :] for s in range(cells_s)]
        for j in range(ROWS):
            q = spread(q8[j : j + 1])
            fr = spread(fr8[j : j + 1])
            hg = jnp.maximum(1.0 - jnp.abs(spread(xg8[j : j + 1]) - girth_row), 0.0)
            hs = [spread(hs8[s][j : j + 1]) for s in range(cells_s)]
            index = q % LANES
            half_of = [q >= h * LANES for h in range(halves)]
            for c in range(3):
                total = None
                for s in range(cells_s):
                    value = pick(field_ref, c, s, index, half_of)
                    value = value + fr * pick(slope_ref, c, s, index, half_of)
                    total = hs[s] * value if total is None else total + hs[s] * value
                disk_ref[c, pl.ds(target + j, 1), :] = jnp.sum(hg * total, axis=0, keepdims=True)

    def sector(number, count):
        mine = owner_ref[number] == me

        @pl.when(mine)
        def _():
            source = pl.multiple_of(number * width, width)
            target = pl.multiple_of(count * width, width)
            chosen_ref[pl.ds(target, width), :] = table_ref[pl.ds(source, width), :]
            for part in range(width // ROWS):
                eight(source + part * ROWS, target + part * ROWS)

        return count + mine.astype(jnp.int32)

    lax.fori_loop(0, sectors, sector, jnp.int32(0))

    for c in range(3):
        harm_ref[:, c * 2 * NH : (c + 1) * 2 * NH] = lax.dot_general(
            disk_ref[c],
            chosen_ref[...],
            (((0,), (0,)), ((), ())),
            precision=lax.Precision.HIGHEST,
            preferred_element_type=jnp.float32,
        )


def section(
    owners, velocity, pressure, energy, rate, before, after, left, right, points, table, girth_count
):
    _, cells_s, cells_g, cells_r = velocity.shape
    azimuths, radii = points[0].shape
    sectors = owners.shape[0]
    columns = 3 * sectors // girth_count * (azimuths // sectors)
    shape = functools.partial(jax.ShapeDtypeStruct, dtype=jnp.float32)
    scratch = lambda *dims: pltpu.VMEM(dims, jnp.float32)
    vmem = pl.BlockSpec(memory_space=pltpu.VMEM)
    smem = pl.BlockSpec(memory_space=pltpu.SMEM)
    return pl.pallas_call(
        section_kernel,
        out_shape=(
            shape(velocity.shape),
            shape(energy.shape),
            shape(rate.shape),
            shape((radii, 6 * NH)),
        ),
        in_specs=[smem] + [vmem] * 13,
        scratch_shapes=[
            scratch(6, cells_s, 3 * ROWS, cells_r),
            scratch(cells_s, 3 * ROWS, cells_r),
            scratch(3, cells_s, cells_r // LANES, cells_g, LANES),
            scratch(3, cells_s, cells_r // LANES, cells_g, LANES),
            scratch(3, columns, radii),
            scratch(columns, 2 * NH),
        ],
        compiler_params=pltpu.CompilerParams(vmem_limit_bytes=VMEM_LIMIT),
        name="section_and_disk",
    )(owners, velocity, pressure, energy, rate, before, after, left, right, *points, table)


def fourier_table(azimuths, modes):
    phase = np.arange(azimuths)[:, None] * np.arange(modes)[None, :] % azimuths
    angles = phase * (2.0 * math.pi / azimuths)
    table = np.concatenate([np.cos(angles), -np.sin(angles)], axis=1) / math.sqrt(azimuths)
    return jnp.asarray(table.astype(np.float32))


def body(velocity, pressure, kinetic_energy, dissipation_rate, corner_ids, fractions, sector_owner):
    _, cells_s, cells_g, cells_r = velocity.shape
    radii, azimuths = corner_ids.shape
    stream_count, girth_count = lax.axis_size("stream"), lax.axis_size("girth")
    devices = stream_count * girth_count

    def slab(dim, start):
        def cut(values, at):
            return lax.slice_in_dim(values, start, start + 2, axis=at)

        scalars = [cut(x, dim)[None] for x in (pressure, kinetic_energy, dissipation_rate)]
        return jnp.concatenate([cut(velocity, dim + 1)] + scalars, axis=0)

    def send(values, axis, count, step):
        pairs = [(i, i + step) for i in range(count) if 0 <= i + step < count]
        return lax.ppermute(values, axis, pairs)

    before = send(slab(0, cells_s - 2), "stream", stream_count, 1)
    after = send(slab(0, 0), "stream", stream_count, -1)
    left = send(slab(1, cells_g - 2), "girth", girth_count, 1)
    right = send(slab(1, 0), "girth", girth_count, -1)
    points = prepare(corner_ids, fractions, cells_s, cells_g, cells_r)
    new_velocity, new_energy, new_rate, partial = section(
        sector_owner[:, 0],
        velocity,
        pressure,
        kinetic_energy,
        dissipation_rate,
        before,
        after,
        left,
        right,
        points,
        fourier_table(azimuths, NH),
        girth_count,
    )
    shares = lax.all_to_all(
        partial.reshape(devices, radii // devices, 6 * NH),
        ("stream", "girth"),
        split_axis=0,
        concat_axis=0,
        tiled=True,
    )
    return new_velocity, new_energy, new_rate, jnp.sum(shares, axis=0)


def solution(mesh):
    return jax.shard_map(
        body,
        mesh=mesh,
        in_specs=(
            P(None, "stream", "girth", None),
            P("stream", "girth", None),
            P("stream", "girth", None),
            P("stream", "girth", None),
            P(),
            P(),
            P(),
        ),
        out_specs=(
            P(None, "stream", "girth", None),
            P("stream", "girth", None),
            P("stream", "girth", None),
            P(("stream", "girth"), None),
        ),
        check_vma=False,
    )
```

```python
import functools
import math

import jax
import jax.numpy as jnp
import numpy as np
from jax import lax
from jax.experimental import pallas as pl
from jax.experimental.pallas import tpu as pltpu
from jax.sharding import PartitionSpec as P

NH = 128

base_viscosity = 0.05
time_step = 0.2
beta_star = 0.09
beta_rate = 0.075
alpha_rate = 0.52
wall_rate = 1.0

LANES = 128
ROWS = 8
SHIFT = 10
CHUNK = 64
VMEM_LIMIT = 48 * 1024 * 1024


def pack_kernel(vel_ref, p_ref, k_ref, w_ref, last_ref, first_ref, right_ref, left_ref):
    cells_s, cells_g, _ = p_ref.shape
    for f in range(6):
        own = vel_ref.at[f] if f < 3 else (p_ref, k_ref, w_ref)[f - 3]
        last_ref[f] = own[cells_s - 2 : cells_s]
        first_ref[f] = own[0:2]
        right_ref[f] = own[:, cells_g - 2 : cells_g, :]
        left_ref[f] = own[:, 0:2, :]


def pack(velocity, pressure, energy, rate):
    _, cells_s, cells_g, cells_r = velocity.shape
    stream = jax.ShapeDtypeStruct((6, 2, cells_g, cells_r), jnp.float32)
    girth = jax.ShapeDtypeStruct((6, cells_s, 2, cells_r), jnp.float32)
    return pl.pallas_call(
        pack_kernel, out_shape=(stream, stream, girth, girth), name="pack_halos"
    )(velocity, pressure, energy, rate)


def prepare_kernel(
    cells_s,
    cells_g,
    cells_r,
    owner_ref,
    ids_ref,
    frac_ref,
    table_ref,
    key_ref,
    fr_ref,
    xs_ref,
    xg_ref,
    moves_ref,
    chosen_ref,
    count_ref,
    all_key,
    all_fr,
    all_xs,
    all_xg,
    keys,
    frs,
    xss,
    xgs,
):
    stream_first = lax.axis_index("stream") * cells_s
    me = lax.axis_index("girth")
    plane_cells = cells_g * cells_r
    sectors = owner_ref.shape[0]
    azimuths = ids_ref.shape[1]
    width = azimuths // sectors
    halves, rows, _ = fr_ref.shape
    pad = moves_ref.shape[1] - rows
    steps = (rows - 1).bit_length()
    for block in range(azimuths // LANES):
        cols = pl.ds(block * LANES, LANES)
        ids = ids_ref[:, cols].T
        stream_cell = ids // plane_cells
        remainder = ids - stream_cell * plane_cells
        girth_cell = remainder // cells_r
        all_key[cols, :] = (remainder - girth_cell * cells_r) << SHIFT
        all_fr[cols, :] = frac_ref[2, :, cols].T
        all_xg[cols, :] = girth_cell.astype(jnp.float32) + frac_ref[1, :, cols].T
        local = stream_cell - stream_first
        all_xs[cols, :] = local.astype(jnp.float32) + frac_ref[0, :, cols].T

    chosen_ref[...] = jnp.zeros_like(chosen_ref)
    keys[...] = jnp.zeros_like(keys)
    frs[0] = jnp.zeros_like(frs[0])
    xgs[0] = jnp.zeros_like(xgs[0])
    xss[0] = jnp.full_like(xss[0], -2.0)

    def sector(number, count):
        mine = owner_ref[number] == me

        @pl.when(mine)
        def _():
            source = pl.ds(pl.multiple_of(number * width, width), width)
            target = pl.ds(pl.multiple_of(count * width, width), width)
            chosen_ref[target, :] = table_ref[source, :]
            keys[0, target, :] = all_key[source, :]
            frs[0, target, :] = all_fr[source, :]
            xss[0, target, :] = all_xs[source, :]
            xgs[0, target, :] = all_xg[source, :]

        return count + mine.astype(jnp.int32)

    lax.fori_loop(0, sectors, sector, jnp.int32(0))

    held = pl.ds(0, rows)
    earlier = lax.broadcasted_iota(jnp.int32, (rows, rows), 0) > lax.broadcasted_iota(
        jnp.int32, (rows, rows), 1
    )
    earlier = earlier.astype(jnp.float32).astype(jnp.bfloat16)
    xs = xss[0, held, :]
    touched = (xs > -1.0) & (xs < float(cells_s))
    fresh = keys[0, held, :]
    for half in range(halves):
        first = half * LANES << SHIFT
        kept = touched & (fresh >= first) & (fresh < first + (LANES << SHIFT))
        skipped = jnp.where(kept, 0.0, 1.0)
        before = jnp.dot(
            earlier, skipped.astype(jnp.bfloat16), preferred_element_type=jnp.float32
        ).astype(jnp.int32)
        counts = rows - jnp.sum(skipped, axis=0, keepdims=True).astype(jnp.int32)
        count_ref[half] = jnp.max(counts)
        moves_ref[half, 0:pad, :] = jnp.zeros((pad, LANES), jnp.int32)
        moves_ref[half, pad : pad + rows, :] = jnp.where(kept, 1 << steps, 0)
        keys[1, held, :] = fresh + jnp.where(kept, before, 0)
        for step in range(steps):
            bit = 1 << step
            a, b = (1, 2) if step % 2 == 0 else (2, 1)
            data = 0 if step == 0 else a
            last = step == steps - 1
            for at in range(0, rows, CHUNK):
                here, there = pl.ds(at, CHUNK), pl.ds(at + bit, CHUNK)
                key, arriving = keys[a, here, :], keys[a, there, :]
                moved = (arriving & bit) != 0
                target = pl.ds(pad + at, CHUNK)
                moves_ref[half, target, :] = moves_ref[half, target, :] | jnp.where(moved, bit, 0)
                stays = jnp.where((key & bit) != 0, key & -(1 << SHIFT), key)
                key = jnp.where(moved, arriving, stays)
                out = [jnp.where(moved, r[data, there, :], r[data, here, :]) for r in (frs, xss, xgs)]
                if last:
                    key_ref[half, here, :] = key >> SHIFT
                    fr_ref[half, here, :] = out[0]
                    xs_ref[half, here, :] = out[1]
                    xg_ref[half, here, :] = out[2]
                else:
                    keys[b, here, :] = key
                    frs[b, here, :] = out[0]
                    xss[b, here, :] = out[1]
                    xgs[b, here, :] = out[2]


def prepare(owners, corner_ids, fractions, table, cells, girth_count):
    cells_s, cells_g, cells_r = cells
    radii, azimuths = corner_ids.shape
    sectors = owners.shape[0]
    rows = 3 * sectors // girth_count * (azimuths // sectors)
    halves = cells_r // LANES
    pad = 1 << ((rows - 1).bit_length() - 1)
    shape = jax.ShapeDtypeStruct
    lists = (halves, rows, radii)
    vmem = pl.BlockSpec(memory_space=pltpu.VMEM)
    smem = pl.BlockSpec(memory_space=pltpu.SMEM)
    return pl.pallas_call(
        functools.partial(prepare_kernel, cells_s, cells_g, cells_r),
        out_shape=(
            shape(lists, jnp.int32),
            shape(lists, jnp.float32),
            shape(lists, jnp.float32),
            shape(lists, jnp.float32),
            shape((halves, pad + rows, radii), jnp.int32),
            shape((rows, 2 * NH), jnp.float32),
            shape((halves,), jnp.int32),
        ),
        in_specs=[smem, vmem, vmem, vmem],
        out_specs=[vmem] * 6 + [smem],
        scratch_shapes=[pltpu.VMEM((azimuths, radii), jnp.int32)]
        + [pltpu.VMEM((azimuths, radii), jnp.float32)] * 3
        + [pltpu.VMEM((3, rows + pad, radii), jnp.int32)]
        + [pltpu.VMEM((3, rows + pad, radii), jnp.float32)] * 3,
        compiler_params=pltpu.CompilerParams(vmem_limit_bytes=VMEM_LIMIT),
        cost_estimate=pl.CostEstimate(
            flops=20 * radii * azimuths, bytes_accessed=44 * radii * azimuths, transcendentals=0
        ),
        name="prepare_points",
    )(owners, corner_ids, fractions, table)


def radial(values, amount, fill):
    extent = values.shape[-1]
    rolled = pltpu.roll(values, (-amount) % extent, values.ndim - 1)
    position = lax.broadcasted_iota(jnp.int32, values.shape, values.ndim - 1) + amount
    return jnp.where((position >= 0) & (position < extent), rolled, fill)


def advance(own, before, after, left, right, ext_ref, visc_ref):
    cells_s, cells_g, _ = own[0].shape
    mid = ROWS

    def along_s(stack, amount):
        return stack[2 + amount : 2 + amount + cells_s]

    def along_g(ref, amount):
        return ref[:, mid + amount : mid + amount + cells_g, :]

    def viscosity(energy, rate):
        return base_viscosity + energy / (rate + wall_rate)

    stacks = [jnp.concatenate([before[f], own[f], after[f]], axis=0) for f in range(6)]
    for f in range(6):
        ext_ref[f, :, mid - 2 : mid, :] = left[f]
        ext_ref[f, :, mid : mid + cells_g, :] = own[f]
        ext_ref[f, :, mid + cells_g : mid + cells_g + 2, :] = right[f]
    middle = viscosity(own[4], own[5])
    visc_stack = viscosity(stacks[4], stacks[5])
    visc_ref[:, mid - 2 : mid, :] = viscosity(left[4], left[5])
    visc_ref[:, mid : mid + cells_g, :] = middle
    visc_ref[:, mid + cells_g : mid + cells_g + 2, :] = viscosity(right[4], right[5])
    faces = [
        (
            0.5 * (middle + along_s(visc_stack, 1)),
            0.5 * (middle + along_s(visc_stack, -1)),
        ),
        (
            0.5 * (middle + along_g(visc_ref, 1)),
            0.5 * (middle + along_g(visc_ref, -1)),
        ),
        (
            0.5 * (middle + radial(middle, 1, base_viscosity)),
            0.5 * (middle + radial(middle, -1, base_viscosity)),
        ),
    ]

    def neighbour(f, direction, amount):
        if direction == 0:
            return along_s(stacks[f], amount)
        if direction == 1:
            return along_g(ext_ref.at[f], amount)
        return radial(own[f], amount, 0.0)

    def terms(f, direction):
        up, down = neighbour(f, direction, 1), neighbour(f, direction, -1)
        far = neighbour(f, direction, 2) - neighbour(f, direction, -2)
        gradient = (8.0 * (up - down) - far) * (1.0 / 12.0)
        above, below = faces[direction]
        return gradient, above * (up - own[f]) - below * (own[f] - down)

    strain = None
    updated = []
    for f in range(3):
        change = -terms(3, f)[0]
        for direction in range(3):
            gradient, spread = terms(f, direction)
            strain = gradient * gradient if strain is None else strain + gradient * gradient
            change = change - own[direction] * gradient + spread
        updated.append(own[f] + time_step * change)
    energy = own[4] / (own[5] + wall_rate) * strain - beta_star * own[4] * own[5]
    rate = alpha_rate * strain - beta_rate * own[5] * own[5]
    for direction in range(3):
        gradient, spread = terms(4, direction)
        energy = energy - own[direction] * gradient + spread
        gradient, spread = terms(5, direction)
        rate = rate - own[direction] * gradient + spread
    return updated, own[4] + time_step * energy, own[5] + time_step * rate


def girth_sums(parts):
    row = lax.broadcasted_iota(jnp.int32, parts[0].shape, 0)

    def swapped(values, distance):
        up = pltpu.roll(values, distance, 0)
        if 2 * distance == ROWS:
            return up
        return jnp.where((row & distance) != 0, up, pltpu.roll(values, ROWS - distance, 0))

    distance = ROWS // 2
    while distance > 0:
        low = (row & distance) == 0
        parts = [
            jnp.where(low, x, y) + swapped(jnp.where(low, y, x), distance)
            for x, y in zip(parts[:distance], parts[distance:])
        ]
        distance //= 2
    return parts[0]


def section_kernel(
    count_ref,
    vel_ref,
    p_ref,
    k_ref,
    w_ref,
    before_ref,
    after_ref,
    left_ref,
    right_ref,
    key_ref,
    fr_ref,
    xs_ref,
    xg_ref,
    moves_ref,
    chosen_ref,
    new_vel_ref,
    new_k_ref,
    new_w_ref,
    harm_ref,
    ext_ref,
    visc_ref,
    field_ref,
    slope_ref,
    value_ref,
    disk_ref,
):
    cells_s, cells_g, _ = p_ref.shape
    halves, rows, _ = fr_ref.shape
    pad = moves_ref.shape[1] - rows
    steps = (rows - 1).bit_length()

    own = [vel_ref[0], vel_ref[1], vel_ref[2], p_ref[...], k_ref[...], w_ref[...]]
    six = range(6)
    updated, energy, rate = advance(
        own,
        [before_ref[f] for f in six],
        [after_ref[f] for f in six],
        [left_ref[f] for f in six],
        [right_ref[f] for f in six],
        ext_ref,
        visc_ref,
    )
    new_k_ref[...] = energy
    new_w_ref[...] = rate
    for c in range(3):
        new_vel_ref[c] = updated[c]
        slope = radial(updated[c], 1, 0.0) - updated[c]
        for h in range(halves):
            lanes = slice(h * LANES, (h + 1) * LANES)
            field_ref[h, c] = updated[c][:, :, lanes]
            slope_ref[h, c] = slope[:, :, lanes]

    girth_row = lax.broadcasted_iota(jnp.int32, (cells_g, LANES), 0).astype(jnp.float32)

    def pick(table, index):
        return jnp.take_along_axis(table, index, axis=1, mode="promise_in_bounds")

    def spread(row):
        return jnp.broadcast_to(row, (cells_g, LANES))

    for half in range(halves):

        def eight(group, carry):
            at = pl.multiple_of(group * ROWS, ROWS)
            here = pl.ds(at, ROWS)
            q8, fr8, xg8, xs8 = (r[half, here, :] for r in (key_ref, fr_ref, xg_ref, xs_ref))
            index8 = q8 % LANES
            hs8 = [jnp.maximum(1.0 - jnp.abs(xs8 - float(s)), 0.0) for s in range(cells_s)]
            sums = [[], [], []]
            for j in range(ROWS):
                one = slice(j, j + 1)
                fr, index = spread(fr8[one]), spread(index8[one])
                hg = jnp.maximum(1.0 - jnp.abs(spread(xg8[one]) - girth_row), 0.0)
                hs = [spread(hs8[s][one]) for s in range(cells_s)]
                for c in range(3):
                    total = None
                    for s in range(cells_s):
                        value = pick(field_ref[half, c, s], index)
                        value = hs[s] * (value + fr * pick(slope_ref[half, c, s], index))
                        total = value if total is None else total + value
                    sums[c].append(hg * total)
            for c in range(3):
                value_ref[0, c, pl.ds(pad + at, ROWS), :] = girth_sums(sums[c])
            return carry

        lax.fori_loop(0, (count_ref[half] + ROWS - 1) // ROWS, eight, jnp.int32(0))

        for step in reversed(range(steps)):
            bit = 1 << step
            a, b = (0, 1) if (steps - 1 - step) % 2 == 0 else (1, 0)
            for at in range(0, rows, CHUNK):
                here, there = pl.ds(pad + at, CHUNK), pl.ds(pad + at - bit, CHUNK)
                moved = (moves_ref[half, there, :] & bit) != 0
                if step == 0:
                    kept = moves_ref[half, here, :] >= 1 << steps
                for c in range(3):
                    value = jnp.where(moved, value_ref[a, c, there, :], value_ref[a, c, here, :])
                    if step > 0:
                        value_ref[b, c, here, :] = value
                    elif half == 0:
                        disk_ref[c, pl.ds(at, CHUNK), :] = jnp.where(kept, value, 0.0)
                    else:
                        other = disk_ref[c, pl.ds(at, CHUNK), :]
                        disk_ref[c, pl.ds(at, CHUNK), :] = jnp.where(kept, value, other)

    for c in range(3):
        harm_ref[:, c * 2 * NH : (c + 1) * 2 * NH] = lax.dot_general(
            disk_ref[c],
            chosen_ref[...],
            (((0,), (0,)), ((), ())),
            precision=lax.Precision.HIGHEST,
            preferred_element_type=jnp.float32,
        )


def section(velocity, pressure, energy, rate, before, after, left, right, points):
    _, cells_s, cells_g, cells_r = velocity.shape
    *lists, moves, chosen, counts = points
    halves, rows, radii = lists[0].shape
    shape = functools.partial(jax.ShapeDtypeStruct, dtype=jnp.float32)
    scratch = lambda *dims: pltpu.VMEM(dims, jnp.float32)
    vmem = pl.BlockSpec(memory_space=pltpu.VMEM)
    smem = pl.BlockSpec(memory_space=pltpu.SMEM)
    return pl.pallas_call(
        section_kernel,
        out_shape=(
            shape(velocity.shape),
            shape(energy.shape),
            shape(rate.shape),
            shape((radii, 6 * NH)),
        ),
        in_specs=[smem] + [vmem] * 14,
        scratch_shapes=[
            scratch(6, cells_s, 3 * ROWS, cells_r),
            scratch(cells_s, 3 * ROWS, cells_r),
            scratch(halves, 3, cells_s, cells_g, LANES),
            scratch(halves, 3, cells_s, cells_g, LANES),
            scratch(2, 3, moves.shape[1], radii),
            scratch(3, rows, radii),
        ],
        compiler_params=pltpu.CompilerParams(vmem_limit_bytes=VMEM_LIMIT),
        name="section_and_disk",
    )(counts, velocity, pressure, energy, rate, before, after, left, right, *lists, moves, chosen)


def fourier_table(azimuths, modes):
    phase = np.arange(azimuths)[:, None] * np.arange(modes)[None, :] % azimuths
    angles = phase * (2.0 * math.pi / azimuths)
    table = np.concatenate([np.cos(angles), -np.sin(angles)], axis=1) / math.sqrt(azimuths)
    return jnp.asarray(table.astype(np.float32))


def body(velocity, pressure, kinetic_energy, dissipation_rate, corner_ids, fractions, sector_owner):
    _, cells_s, cells_g, cells_r = velocity.shape
    radii, azimuths = corner_ids.shape
    stream_count, girth_count = lax.axis_size("stream"), lax.axis_size("girth")
    devices = stream_count * girth_count

    def send(values, axis, count, step):
        pairs = [(i, i + step) for i in range(count) if 0 <= i + step < count]
        return lax.ppermute(values, axis, pairs)

    last, first, rightmost, leftmost = pack(velocity, pressure, kinetic_energy, dissipation_rate)
    before = send(last, "stream", stream_count, 1)
    after = send(first, "stream", stream_count, -1)
    left = send(rightmost, "girth", girth_count, 1)
    right = send(leftmost, "girth", girth_count, -1)
    points = prepare(
        sector_owner[:, 0],
        corner_ids,
        fractions,
        fourier_table(azimuths, NH),
        (cells_s, cells_g, cells_r),
        girth_count,
    )
    new_velocity, new_energy, new_rate, partial = section(
        velocity, pressure, kinetic_energy, dissipation_rate, before, after, left, right, points
    )
    shares = lax.all_to_all(
        partial.reshape(devices, radii // devices, 6 * NH),
        ("stream", "girth"),
        split_axis=0,
        concat_axis=0,
        tiled=True,
    )
    return new_velocity, new_energy, new_rate, jnp.sum(shares, axis=0)


def solution(mesh):
    return jax.shard_map(
        body,
        mesh=mesh,
        in_specs=(
            P(None, "stream", "girth", None),
            P("stream", "girth", None),
            P("stream", "girth", None),
            P("stream", "girth", None),
            P(),
            P(),
            P(),
        ),
        out_specs=(
            P(None, "stream", "girth", None),
            P("stream", "girth", None),
            P("stream", "girth", None),
            P(("stream", "girth"), None),
        ),
        check_vma=False,
    )
```

```python
import functools
import math

import jax
import jax.numpy as jnp
import numpy as np
from jax import lax
from jax.experimental import pallas as pl
from jax.experimental.pallas import tpu as pltpu
from jax.sharding import PartitionSpec as P

NH = 128

base_viscosity = 0.05
time_step = 0.2
beta_star = 0.09
beta_rate = 0.075
alpha_rate = 0.52
wall_rate = 1.0

LANES = 128
ROWS = 8
SHIFT = 10
CHUNK = 64
VMEM_LIMIT = 48 * 1024 * 1024


def pack_kernel(vel_ref, p_ref, k_ref, w_ref, *slabs):
    cells_s, cells_g, _ = p_ref.shape
    stream_odd = lax.axis_index("stream") % 2 == 1
    girth_odd = lax.axis_index("girth") % 2 == 1
    for f in range(6):
        own = vel_ref.at[f] if f < 3 else (p_ref, k_ref, w_ref)[f - 3]
        first, last = own[0:2], own[cells_s - 2 : cells_s]
        slabs[0][f] = jnp.where(stream_odd, first, last)
        slabs[1][f] = jnp.where(stream_odd, last, first)
        first, last = own[:, 0:2, :], own[:, cells_g - 2 : cells_g, :]
        slabs[2][f] = jnp.where(girth_odd, first, last)
        slabs[3][f] = jnp.where(girth_odd, last, first)


def pack(velocity, pressure, energy, rate):
    _, cells_s, cells_g, cells_r = velocity.shape
    stream = jax.ShapeDtypeStruct((6, 2, cells_g, cells_r), jnp.float32)
    girth = jax.ShapeDtypeStruct((6, cells_s, 2, cells_r), jnp.float32)
    return pl.pallas_call(
        pack_kernel, out_shape=(stream, stream, girth, girth), name="pack_halos"
    )(velocity, pressure, energy, rate)


def prepare_kernel(
    cells_s,
    cells_g,
    cells_r,
    owner_ref,
    ids_hbm,
    frac_hbm,
    table_hbm,
    q_ref,
    fr_ref,
    xs_ref,
    xg_ref,
    moves_ref,
    chosen_ref,
    count_ref,
    ids_ref,
    frac_ref,
    table_ref,
    all_q,
    all_fr,
    all_xs,
    all_xg,
    keys,
    frs,
    xss,
    xgs,
    arrived,
):
    copies = [pltpu.make_async_copy(ids_hbm, ids_ref, arrived.at[0])]
    for d in range(3):
        copies.append(pltpu.make_async_copy(frac_hbm.at[d], frac_ref.at[d], arrived.at[1 + d]))
    copies.append(pltpu.make_async_copy(table_hbm, table_ref, arrived.at[4]))
    for copy in copies:
        copy.start()
    stream_first = lax.axis_index("stream") * cells_s
    me = lax.axis_index("girth")
    plane_cells = cells_g * cells_r
    sectors = owner_ref.shape[0]
    azimuths = ids_ref.shape[1]
    width = azimuths // sectors
    rows = fr_ref.shape[0]
    pad = moves_ref.shape[0] - rows
    steps = (rows - 1).bit_length()

    keys[...] = jnp.zeros_like(keys)
    frs[0] = jnp.zeros_like(frs[0])
    xgs[0] = jnp.zeros_like(xgs[0])
    xss[0] = jnp.full_like(xss[0], -2.0)
    chosen_ref[...] = jnp.zeros_like(chosen_ref)
    moves_ref[0:pad, :] = jnp.zeros((pad, LANES), jnp.int32)

    blocks = [pl.ds(at, LANES) for at in range(0, azimuths, LANES)]
    copies[0].wait()
    for cols in blocks:
        ids = ids_ref[:, cols].T
        stream_cell = ids // plane_cells
        remainder = ids - stream_cell * plane_cells
        girth_cell = remainder // cells_r
        all_q[cols, :] = (remainder - girth_cell * cells_r) << SHIFT
        all_xg[cols, :] = girth_cell.astype(jnp.float32)
        all_xs[cols, :] = (stream_cell - stream_first).astype(jnp.float32)
    copies[1].wait()
    for cols in blocks:
        all_xs[cols, :] += frac_ref[0, :, cols].T
    copies[2].wait()
    for cols in blocks:
        all_xg[cols, :] += frac_ref[1, :, cols].T
    copies[3].wait()
    for cols in blocks:
        all_fr[cols, :] = frac_ref[2, :, cols].T
    copies[4].wait()

    def sector(number, count):
        mine = owner_ref[number] == me

        @pl.when(mine)
        def _():
            source = pl.ds(pl.multiple_of(number * width, width), width)
            target = pl.ds(pl.multiple_of(count * width, width), width)
            chosen_ref[target, :] = table_ref[source, :]
            keys[0, target, :] = all_q[source, :]
            frs[0, target, :] = all_fr[source, :]
            xss[0, target, :] = all_xs[source, :]
            xgs[0, target, :] = all_xg[source, :]

        return count + mine.astype(jnp.int32)

    lax.fori_loop(0, sectors, sector, jnp.int32(0))

    held = pl.ds(0, rows)
    earlier = lax.broadcasted_iota(jnp.int32, (rows, rows), 0) > lax.broadcasted_iota(
        jnp.int32, (rows, rows), 1
    )
    earlier = earlier.astype(jnp.float32).astype(jnp.bfloat16)
    xs = xss[0, held, :]
    kept = (xs > -1.0) & (xs < float(cells_s))
    skipped = jnp.where(kept, 0.0, 1.0)
    before = jnp.dot(
        earlier, skipped.astype(jnp.bfloat16), preferred_element_type=jnp.float32
    ).astype(jnp.int32)
    counts = rows - jnp.sum(skipped, axis=0, keepdims=True).astype(jnp.int32)
    count_ref[0] = jnp.max(counts)
    moves_ref[pad : pad + rows, :] = jnp.where(kept, 1 << steps, 0)
    keys[0, held, :] = keys[0, held, :] + jnp.where(kept, before, 0)
    for step in range(steps):
        bit = 1 << step
        a, b = step % 2, 1 - step % 2
        last = step == steps - 1
        for at in range(0, rows, CHUNK):
            here, there = pl.ds(at, CHUNK), pl.ds(at + bit, CHUNK)
            key, arriving = keys[a, here, :], keys[a, there, :]
            moved = (arriving & bit) != 0
            target = pl.ds(pad + at, CHUNK)
            moves_ref[target, :] = moves_ref[target, :] | jnp.where(moved, bit, 0)
            stays = jnp.where((key & bit) != 0, key & -(1 << SHIFT), key)
            key = jnp.where(moved, arriving, stays)
            out = [jnp.where(moved, r[a, there, :], r[a, here, :]) for r in (frs, xss, xgs)]
            if last:
                q_ref[here, :] = key >> SHIFT
                fr_ref[here, :] = out[0]
                xs_ref[here, :] = out[1]
                xg_ref[here, :] = out[2]
            else:
                keys[b, here, :] = key
                frs[b, here, :] = out[0]
                xss[b, here, :] = out[1]
                xgs[b, here, :] = out[2]


def prepare(owners, corner_ids, fractions, table, cells, girth_count):
    cells_s, cells_g, cells_r = cells
    radii, azimuths = corner_ids.shape
    sectors = owners.shape[0]
    rows = 3 * sectors // girth_count * (azimuths // sectors)
    pad = 1 << ((rows - 1).bit_length() - 1)
    shape = jax.ShapeDtypeStruct
    lists = (rows, radii)
    vmem = pl.BlockSpec(memory_space=pltpu.VMEM)
    smem = pl.BlockSpec(memory_space=pltpu.SMEM)
    hbm = pl.BlockSpec(memory_space=pl.ANY)
    return pl.pallas_call(
        functools.partial(prepare_kernel, cells_s, cells_g, cells_r),
        out_shape=(
            shape(lists, jnp.int32),
            shape(lists, jnp.float32),
            shape(lists, jnp.float32),
            shape(lists, jnp.float32),
            shape((pad + rows, radii), jnp.int32),
            shape((rows, 2 * NH), jnp.float32),
            shape((1,), jnp.int32),
        ),
        in_specs=[smem, hbm, hbm, hbm],
        out_specs=[vmem] * 6 + [smem],
        scratch_shapes=[
            pltpu.VMEM(corner_ids.shape, jnp.int32),
            pltpu.VMEM(fractions.shape, jnp.float32),
            pltpu.VMEM(table.shape, jnp.float32),
            pltpu.VMEM((azimuths, radii), jnp.int32),
        ]
        + [pltpu.VMEM((azimuths, radii), jnp.float32)] * 3
        + [pltpu.VMEM((2, rows + pad, radii), jnp.int32)]
        + [pltpu.VMEM((2, rows + pad, radii), jnp.float32)] * 3
        + [pltpu.SemaphoreType.DMA((5,))],
        compiler_params=pltpu.CompilerParams(vmem_limit_bytes=VMEM_LIMIT),
        cost_estimate=pl.CostEstimate(
            flops=20 * radii * azimuths, bytes_accessed=44 * radii * azimuths, transcendentals=0
        ),
        name="prepare_points",
    )(owners, corner_ids, fractions, table)


def radial(values, amount, fill):
    extent = values.shape[-1]
    rolled = pltpu.roll(values, (-amount) % extent, values.ndim - 1)
    position = lax.broadcasted_iota(jnp.int32, values.shape, values.ndim - 1) + amount
    return jnp.where((position >= 0) & (position < extent), rolled, fill)


def advance(own, before, after, left, right, ext_ref, visc_ref):
    cells_s, cells_g, _ = own[0].shape
    mid = ROWS

    def along_s(stack, amount):
        return stack[2 + amount : 2 + amount + cells_s]

    def along_g(ref, amount):
        return ref[:, mid + amount : mid + amount + cells_g, :]

    def viscosity(energy, rate):
        return base_viscosity + energy / (rate + wall_rate)

    stacks = [jnp.concatenate([before[f], own[f], after[f]], axis=0) for f in range(6)]
    for f in range(6):
        ext_ref[f, :, mid - 2 : mid, :] = left[f]
        ext_ref[f, :, mid : mid + cells_g, :] = own[f]
        ext_ref[f, :, mid + cells_g : mid + cells_g + 2, :] = right[f]
    middle = viscosity(own[4], own[5])
    visc_stack = viscosity(stacks[4], stacks[5])
    visc_ref[:, mid - 2 : mid, :] = viscosity(left[4], left[5])
    visc_ref[:, mid : mid + cells_g, :] = middle
    visc_ref[:, mid + cells_g : mid + cells_g + 2, :] = viscosity(right[4], right[5])
    faces = [
        (
            0.5 * (middle + along_s(visc_stack, 1)),
            0.5 * (middle + along_s(visc_stack, -1)),
        ),
        (
            0.5 * (middle + along_g(visc_ref, 1)),
            0.5 * (middle + along_g(visc_ref, -1)),
        ),
        (
            0.5 * (middle + radial(middle, 1, base_viscosity)),
            0.5 * (middle + radial(middle, -1, base_viscosity)),
        ),
    ]

    def neighbour(f, direction, amount):
        if direction == 0:
            return along_s(stacks[f], amount)
        if direction == 1:
            return along_g(ext_ref.at[f], amount)
        return radial(own[f], amount, 0.0)

    def terms(f, direction):
        up, down = neighbour(f, direction, 1), neighbour(f, direction, -1)
        far = neighbour(f, direction, 2) - neighbour(f, direction, -2)
        gradient = (8.0 * (up - down) - far) * (1.0 / 12.0)
        above, below = faces[direction]
        return gradient, above * (up - own[f]) - below * (own[f] - down)

    strain = None
    updated = []
    for f in range(3):
        change = -terms(3, f)[0]
        for direction in range(3):
            gradient, spread = terms(f, direction)
            strain = gradient * gradient if strain is None else strain + gradient * gradient
            change = change - own[direction] * gradient + spread
        updated.append(own[f] + time_step * change)
    energy = own[4] / (own[5] + wall_rate) * strain - beta_star * own[4] * own[5]
    rate = alpha_rate * strain - beta_rate * own[5] * own[5]
    for direction in range(3):
        gradient, spread = terms(4, direction)
        energy = energy - own[direction] * gradient + spread
        gradient, spread = terms(5, direction)
        rate = rate - own[direction] * gradient + spread
    return updated, own[4] + time_step * energy, own[5] + time_step * rate


def girth_sums(parts):
    row = lax.broadcasted_iota(jnp.int32, parts[0].shape, 0)

    def swapped(values, distance):
        up = pltpu.roll(values, distance, 0)
        if 2 * distance == ROWS:
            return up
        return jnp.where((row & distance) != 0, up, pltpu.roll(values, ROWS - distance, 0))

    distance = ROWS // 2
    while distance > 0:
        low = (row & distance) == 0
        parts = [
            jnp.where(low, x, y) + swapped(jnp.where(low, y, x), distance)
            for x, y in zip(parts[:distance], parts[distance:])
        ]
        distance //= 2
    return parts[0]


def section_kernel(
    count_ref,
    vel_ref,
    p_ref,
    k_ref,
    w_ref,
    stream_a,
    stream_b,
    girth_a,
    girth_b,
    q_ref,
    fr_ref,
    xs_ref,
    xg_ref,
    moves_ref,
    chosen_ref,
    new_vel_ref,
    new_k_ref,
    new_w_ref,
    harm_ref,
    ext_ref,
    visc_ref,
    field_ref,
    value_ref,
    disk_ref,
):
    cells_s, cells_g, cells_r = p_ref.shape
    rows = fr_ref.shape[0]
    pad = moves_ref.shape[0] - rows
    steps = (rows - 1).bit_length()
    stream_odd = lax.axis_index("stream") % 2 == 1
    girth_odd = lax.axis_index("girth") % 2 == 1

    own = [vel_ref[0], vel_ref[1], vel_ref[2], p_ref[...], k_ref[...], w_ref[...]]
    six = range(6)
    updated, energy, rate = advance(
        own,
        [jnp.where(stream_odd, stream_a[f], stream_b[f]) for f in six],
        [jnp.where(stream_odd, stream_b[f], stream_a[f]) for f in six],
        [jnp.where(girth_odd, girth_a[f], girth_b[f]) for f in six],
        [jnp.where(girth_odd, girth_b[f], girth_a[f]) for f in six],
        ext_ref,
        visc_ref,
    )
    new_k_ref[...] = energy
    new_w_ref[...] = rate

    def rounded(values):
        return values.astype(jnp.bfloat16).astype(jnp.float32)

    for c in range(3):
        new_vel_ref[c] = updated[c]
        slope = radial(updated[c], 1, 0.0) - updated[c]
        for kind, values in enumerate((updated[c], slope)):
            high = rounded(values)
            field_ref[c, :, 2 * kind] = high
            field_ref[c, :, 2 * kind + 1] = rounded(values - high)

    kinds = 4
    table = field_ref[...].reshape(3 * cells_s * kinds * cells_g, cells_r).astype(jnp.bfloat16)
    pair = 2 * LANES
    girth_row = lax.broadcasted_iota(jnp.int32, (cells_g, pair), 0).astype(jnp.float32)
    radial_row = lax.broadcasted_iota(jnp.int32, (cells_r, pair), 0)

    def two(values, j):
        return jnp.concatenate([values[j : j + 1], values[j + 1 : j + 2]], axis=1)

    def eight(group, carry):
        at = pl.multiple_of(group * ROWS, ROWS)
        here = pl.ds(at, ROWS)
        q8, fr8, xg8, xs8 = (r[here, :] for r in (q_ref, fr_ref, xg_ref, xs_ref))
        hs8 = [jnp.maximum(1.0 - jnp.abs(xs8 - float(s)), 0.0) for s in range(cells_s)]
        sums = [[], [], []]
        for j in range(0, ROWS, 2):
            hot = jnp.where(radial_row == two(q8, j), 1.0, 0.0).astype(jnp.bfloat16)
            got = jnp.dot(table, hot, preferred_element_type=jnp.float32)
            got = got.reshape(3, cells_s, kinds, cells_g, pair)
            fr = two(fr8, j)
            hg = jnp.maximum(1.0 - jnp.abs(two(xg8, j) - girth_row), 0.0)
            hs = [two(hs8[s], j) for s in range(cells_s)]
            for c in range(3):
                total = None
                for s in range(cells_s):
                    value = got[c, s, 0] + got[c, s, 1] + fr * (got[c, s, 2] + got[c, s, 3])
                    value = hs[s] * value
                    total = value if total is None else total + value
                total = hg * total
                sums[c] += [total[:, :LANES], total[:, LANES:]]
        for c in range(3):
            value_ref[0, c, pl.ds(pad + at, ROWS), :] = girth_sums(sums[c])
        return carry

    lax.fori_loop(0, (count_ref[0] + ROWS - 1) // ROWS, eight, jnp.int32(0))

    for step in reversed(range(steps)):
        bit = 1 << step
        a, b = (0, 1) if (steps - 1 - step) % 2 == 0 else (1, 0)
        for at in range(0, rows, CHUNK):
            here, there = pl.ds(pad + at, CHUNK), pl.ds(pad + at - bit, CHUNK)
            moved = (moves_ref[there, :] & bit) != 0
            if step == 0:
                kept = moves_ref[here, :] >= 1 << steps
            for c in range(3):
                value = jnp.where(moved, value_ref[a, c, there, :], value_ref[a, c, here, :])
                if step > 0:
                    value_ref[b, c, here, :] = value
                else:
                    disk_ref[c, pl.ds(at, CHUNK), :] = jnp.where(kept, value, 0.0)

    for c in range(3):
        harm_ref[:, c * 2 * NH : (c + 1) * 2 * NH] = lax.dot_general(
            disk_ref[c],
            chosen_ref[...],
            (((0,), (0,)), ((), ())),
            precision=lax.Precision.HIGHEST,
            preferred_element_type=jnp.float32,
        )


def section(velocity, pressure, energy, rate, halos, points):
    _, cells_s, cells_g, cells_r = velocity.shape
    *lists, moves, chosen, counts = points
    rows, radii = lists[0].shape
    shape = functools.partial(jax.ShapeDtypeStruct, dtype=jnp.float32)
    scratch = lambda *dims: pltpu.VMEM(dims, jnp.float32)
    vmem = pl.BlockSpec(memory_space=pltpu.VMEM)
    smem = pl.BlockSpec(memory_space=pltpu.SMEM)
    return pl.pallas_call(
        section_kernel,
        out_shape=(
            shape(velocity.shape),
            shape(energy.shape),
            shape(rate.shape),
            shape((radii, 6 * NH)),
        ),
        in_specs=[smem] + [vmem] * 14,
        scratch_shapes=[
            scratch(6, cells_s, 3 * ROWS, cells_r),
            scratch(cells_s, 3 * ROWS, cells_r),
            scratch(3, cells_s, 4, cells_g, cells_r),
            scratch(2, 3, moves.shape[0], radii),
            scratch(3, rows, radii),
        ],
        compiler_params=pltpu.CompilerParams(vmem_limit_bytes=VMEM_LIMIT),
        name="section_and_disk",
    )(counts, velocity, pressure, energy, rate, *halos, *lists, moves, chosen)


def fourier_table(azimuths, modes):
    phase = np.arange(azimuths)[:, None] * np.arange(modes)[None, :] % azimuths
    angles = phase * (2.0 * math.pi / azimuths)
    table = np.concatenate([np.cos(angles), -np.sin(angles)], axis=1) / math.sqrt(azimuths)
    return jnp.asarray(table.astype(np.float32))


def body(velocity, pressure, kinetic_energy, dissipation_rate, corner_ids, fractions, sector_owner):
    _, cells_s, cells_g, cells_r = velocity.shape
    radii, azimuths = corner_ids.shape
    stream_count, girth_count = lax.axis_size("stream"), lax.axis_size("girth")
    devices = stream_count * girth_count

    def swap(values, axis, count, start):
        pairs = []
        for i in range(start, count - 1, 2):
            pairs += [(i, i + 1), (i + 1, i)]
        return lax.ppermute(values, axis, pairs)

    slabs = pack(velocity, pressure, kinetic_energy, dissipation_rate)
    halos = (
        swap(slabs[0], "stream", stream_count, 0),
        swap(slabs[1], "stream", stream_count, 1),
        swap(slabs[2], "girth", girth_count, 0),
        swap(slabs[3], "girth", girth_count, 1),
    )
    points = prepare(
        sector_owner[:, 0],
        corner_ids,
        fractions,
        fourier_table(azimuths, NH),
        (cells_s, cells_g, cells_r),
        girth_count,
    )
    new_velocity, new_energy, new_rate, partial = section(
        velocity, pressure, kinetic_energy, dissipation_rate, halos, points
    )
    shares = lax.all_to_all(
        partial.reshape(devices, radii // devices, 6 * NH),
        ("stream", "girth"),
        split_axis=0,
        concat_axis=0,
        tiled=True,
    )
    return new_velocity, new_energy, new_rate, jnp.sum(shares, axis=0)


def solution(mesh):
    return jax.shard_map(
        body,
        mesh=mesh,
        in_specs=(
            P(None, "stream", "girth", None),
            P("stream", "girth", None),
            P("stream", "girth", None),
            P("stream", "girth", None),
            P(),
            P(),
            P(),
        ),
        out_specs=(
            P(None, "stream", "girth", None),
            P("stream", "girth", None),
            P("stream", "girth", None),
            P(("stream", "girth"), None),
        ),
        check_vma=False,
    )
```

```python
import functools
import math

import jax
import jax.numpy as jnp
import numpy as np
from jax import lax
from jax.experimental import pallas as pl
from jax.experimental.pallas import tpu as pltpu
from jax.sharding import PartitionSpec as P

NH = 128

base_viscosity = 0.05
time_step = 0.2
beta_star = 0.09
beta_rate = 0.075
alpha_rate = 0.52
wall_rate = 1.0

LANES = 128
ROWS = 8
SHIFT = 10
CHUNK = 64
PRODUCTS = 2
VMEM_LIMIT = 48 * 1024 * 1024


def in_hbm(values):
    return pltpu.with_memory_space_constraint(values, pltpu.HBM)


def pack_kernel(vel_ref, p_ref, k_ref, w_ref, *slabs):
    cells_s, cells_g, _ = p_ref.shape
    stream_odd = lax.axis_index("stream") % 2 == 1
    girth_odd = lax.axis_index("girth") % 2 == 1
    for f in range(6):
        own = vel_ref.at[f] if f < 3 else (p_ref, k_ref, w_ref)[f - 3]
        first, last = own[0:2], own[cells_s - 2 : cells_s]
        slabs[0][f] = jnp.where(stream_odd, first, last)
        slabs[1][f] = jnp.where(stream_odd, last, first)
        first, last = own[:, 0:2, :], own[:, cells_g - 2 : cells_g, :]
        slabs[2][f] = jnp.where(girth_odd, first, last)
        slabs[3][f] = jnp.where(girth_odd, last, first)


def pack(velocity, pressure, energy, rate):
    _, cells_s, cells_g, cells_r = velocity.shape
    stream = pltpu.VMEM((6, 2, cells_g, cells_r), jnp.float32)
    girth = pltpu.VMEM((6, cells_s, 2, cells_r), jnp.float32)
    return pl.pallas_call(
        pack_kernel, out_shape=(stream, stream, girth, girth), name="pack_halos"
    )(velocity, pressure, energy, rate)


def prepare_kernel(
    cells_s,
    cells_g,
    cells_r,
    owner_ref,
    ids_hbm,
    frac_hbm,
    table_hbm,
    q_ref,
    fr_ref,
    xs_ref,
    xg_ref,
    moves_ref,
    chosen_ref,
    count_ref,
    ids_ref,
    frac_ref,
    table_ref,
    all_q,
    all_fr,
    all_xs,
    all_xg,
    keys,
    frs,
    xss,
    xgs,
    arrived,
):
    copies = [pltpu.make_async_copy(ids_hbm, ids_ref, arrived.at[0])]
    for d in range(3):
        copies.append(pltpu.make_async_copy(frac_hbm.at[d], frac_ref.at[d], arrived.at[1 + d]))
    copies.append(pltpu.make_async_copy(table_hbm, table_ref, arrived.at[4]))
    for copy in copies:
        copy.start()
    stream_first = lax.axis_index("stream") * cells_s
    me = lax.axis_index("girth")
    plane_cells = cells_g * cells_r
    sectors = owner_ref.shape[0]
    azimuths = ids_ref.shape[1]
    width = azimuths // sectors
    rows = fr_ref.shape[0]
    pad = moves_ref.shape[0] - rows
    steps = (rows - 1).bit_length()

    keys[...] = jnp.zeros_like(keys)
    frs[0] = jnp.zeros_like(frs[0])
    xgs[0] = jnp.zeros_like(xgs[0])
    xss[0] = jnp.full_like(xss[0], -2.0)
    chosen_ref[...] = jnp.zeros_like(chosen_ref)
    moves_ref[0:pad, :] = jnp.zeros((pad, LANES), jnp.int32)

    blocks = [pl.ds(at, LANES) for at in range(0, azimuths, LANES)]
    copies[0].wait()
    for cols in blocks:
        ids = ids_ref[:, cols].T
        stream_cell = ids // plane_cells
        remainder = ids - stream_cell * plane_cells
        girth_cell = remainder // cells_r
        all_q[cols, :] = (remainder - girth_cell * cells_r) << SHIFT
        all_xg[cols, :] = girth_cell.astype(jnp.float32)
        all_xs[cols, :] = (stream_cell - stream_first).astype(jnp.float32)
    copies[1].wait()
    for cols in blocks:
        all_xs[cols, :] += frac_ref[0, :, cols].T
    copies[2].wait()
    for cols in blocks:
        all_xg[cols, :] += frac_ref[1, :, cols].T
    copies[3].wait()
    for cols in blocks:
        all_fr[cols, :] = frac_ref[2, :, cols].T
    copies[4].wait()

    def sector(number, count):
        mine = owner_ref[number] == me

        @pl.when(mine)
        def _():
            source = pl.ds(pl.multiple_of(number * width, width), width)
            target = pl.ds(pl.multiple_of(count * width, width), width)
            chosen_ref[target, :] = table_ref[source, :]
            keys[0, target, :] = all_q[source, :]
            frs[0, target, :] = all_fr[source, :]
            xss[0, target, :] = all_xs[source, :]
            xgs[0, target, :] = all_xg[source, :]

        return count + mine.astype(jnp.int32)

    lax.fori_loop(0, sectors, sector, jnp.int32(0))

    held = pl.ds(0, rows)
    earlier = lax.broadcasted_iota(jnp.int32, (rows, rows), 0) > lax.broadcasted_iota(
        jnp.int32, (rows, rows), 1
    )
    earlier = earlier.astype(jnp.float32).astype(jnp.bfloat16)
    xs = xss[0, held, :]
    kept = (xs > -1.0) & (xs < float(cells_s))
    skipped = jnp.where(kept, 0.0, 1.0)
    before = jnp.dot(
        earlier, skipped.astype(jnp.bfloat16), preferred_element_type=jnp.float32
    ).astype(jnp.int32)
    counts = rows - jnp.sum(skipped, axis=0, keepdims=True).astype(jnp.int32)
    count_ref[0] = jnp.max(counts)
    moves_ref[pad : pad + rows, :] = jnp.where(kept, 1 << steps, 0)
    keys[0, held, :] = keys[0, held, :] + jnp.where(kept, before, 0)
    for step in range(steps):
        bit = 1 << step
        a, b = step % 2, 1 - step % 2
        last = step == steps - 1
        for at in range(0, rows, CHUNK):
            here, there = pl.ds(at, CHUNK), pl.ds(at + bit, CHUNK)
            key, arriving = keys[a, here, :], keys[a, there, :]
            moved = (arriving & bit) != 0
            target = pl.ds(pad + at, CHUNK)
            moves_ref[target, :] = moves_ref[target, :] | jnp.where(moved, bit, 0)
            stays = jnp.where((key & bit) != 0, key & -(1 << SHIFT), key)
            key = jnp.where(moved, arriving, stays)
            out = [jnp.where(moved, r[a, there, :], r[a, here, :]) for r in (frs, xss, xgs)]
            if last:
                q_ref[here, :] = key >> SHIFT
                fr_ref[here, :] = out[0]
                xs_ref[here, :] = out[1]
                xg_ref[here, :] = out[2]
            else:
                keys[b, here, :] = key
                frs[b, here, :] = out[0]
                xss[b, here, :] = out[1]
                xgs[b, here, :] = out[2]


def prepare(owners, corner_ids, fractions, table, cells, girth_count):
    cells_s, cells_g, cells_r = cells
    radii, azimuths = corner_ids.shape
    sectors = owners.shape[0]
    rows = 3 * sectors // girth_count * (azimuths // sectors)
    pad = 1 << ((rows - 1).bit_length() - 1)
    shape = jax.ShapeDtypeStruct
    lists = (rows, radii)
    vmem = pl.BlockSpec(memory_space=pltpu.VMEM)
    smem = pl.BlockSpec(memory_space=pltpu.SMEM)
    hbm = pl.BlockSpec(memory_space=pltpu.HBM)
    return pl.pallas_call(
        functools.partial(prepare_kernel, cells_s, cells_g, cells_r),
        out_shape=(
            shape(lists, jnp.int32),
            shape(lists, jnp.float32),
            shape(lists, jnp.float32),
            shape(lists, jnp.float32),
            shape((pad + rows, radii), jnp.int32),
            shape((rows, 2 * NH), jnp.float32),
            shape((1,), jnp.int32),
        ),
        in_specs=[smem, hbm, hbm, hbm],
        out_specs=[vmem] * 6 + [smem],
        scratch_shapes=[
            pltpu.VMEM(corner_ids.shape, jnp.int32),
            pltpu.VMEM(fractions.shape, jnp.float32),
            pltpu.VMEM(table.shape, jnp.float32),
            pltpu.VMEM((azimuths, radii), jnp.int32),
        ]
        + [pltpu.VMEM((azimuths, radii), jnp.float32)] * 3
        + [pltpu.VMEM((2, rows + pad, radii), jnp.int32)]
        + [pltpu.VMEM((2, rows + pad, radii), jnp.float32)] * 3
        + [pltpu.SemaphoreType.DMA((5,))],
        compiler_params=pltpu.CompilerParams(vmem_limit_bytes=VMEM_LIMIT),
        cost_estimate=pl.CostEstimate(
            flops=20 * radii * azimuths, bytes_accessed=44 * radii * azimuths, transcendentals=0
        ),
        name="prepare_points",
    )(*(in_hbm(x) for x in (owners, corner_ids, fractions, table)))


def radial(values, amount, fill):
    extent = values.shape[-1]
    rolled = pltpu.roll(values, (-amount) % extent, values.ndim - 1)
    position = lax.broadcasted_iota(jnp.int32, values.shape, values.ndim - 1) + amount
    return jnp.where((position >= 0) & (position < extent), rolled, fill)


def advance(own, before, after, left, right, ext_ref, visc_ref):
    cells_s, cells_g, _ = own[0].shape
    mid = ROWS

    def along_s(stack, amount):
        return stack[2 + amount : 2 + amount + cells_s]

    def along_g(ref, amount):
        return ref[:, mid + amount : mid + amount + cells_g, :]

    def viscosity(energy, rate):
        return base_viscosity + energy / (rate + wall_rate)

    stacks = [jnp.concatenate([before[f], own[f], after[f]], axis=0) for f in range(6)]
    for f in range(6):
        ext_ref[f, :, mid - 2 : mid, :] = left[f]
        ext_ref[f, :, mid : mid + cells_g, :] = own[f]
        ext_ref[f, :, mid + cells_g : mid + cells_g + 2, :] = right[f]
    middle = viscosity(own[4], own[5])
    visc_stack = viscosity(stacks[4], stacks[5])
    visc_ref[:, mid - 2 : mid, :] = viscosity(left[4], left[5])
    visc_ref[:, mid : mid + cells_g, :] = middle
    visc_ref[:, mid + cells_g : mid + cells_g + 2, :] = viscosity(right[4], right[5])
    faces = [
        (
            0.5 * (middle + along_s(visc_stack, 1)),
            0.5 * (middle + along_s(visc_stack, -1)),
        ),
        (
            0.5 * (middle + along_g(visc_ref, 1)),
            0.5 * (middle + along_g(visc_ref, -1)),
        ),
        (
            0.5 * (middle + radial(middle, 1, base_viscosity)),
            0.5 * (middle + radial(middle, -1, base_viscosity)),
        ),
    ]

    def neighbour(f, direction, amount):
        if direction == 0:
            return along_s(stacks[f], amount)
        if direction == 1:
            return along_g(ext_ref.at[f], amount)
        return radial(own[f], amount, 0.0)

    def terms(f, direction):
        up, down = neighbour(f, direction, 1), neighbour(f, direction, -1)
        far = neighbour(f, direction, 2) - neighbour(f, direction, -2)
        gradient = (8.0 * (up - down) - far) * (1.0 / 12.0)
        above, below = faces[direction]
        return gradient, above * (up - own[f]) - below * (own[f] - down)

    strain = None
    updated = []
    for f in range(3):
        change = -terms(3, f)[0]
        for direction in range(3):
            gradient, spread = terms(f, direction)
            strain = gradient * gradient if strain is None else strain + gradient * gradient
            change = change - own[direction] * gradient + spread
        updated.append(own[f] + time_step * change)
    energy = own[4] / (own[5] + wall_rate) * strain - beta_star * own[4] * own[5]
    rate = alpha_rate * strain - beta_rate * own[5] * own[5]
    for direction in range(3):
        gradient, spread = terms(4, direction)
        energy = energy - own[direction] * gradient + spread
        gradient, spread = terms(5, direction)
        rate = rate - own[direction] * gradient + spread
    return updated, own[4] + time_step * energy, own[5] + time_step * rate


def girth_sums(parts):
    row = lax.broadcasted_iota(jnp.int32, parts[0].shape, 0)

    def swapped(values, distance):
        up = pltpu.roll(values, distance, 0)
        if 2 * distance == ROWS:
            return up
        return jnp.where((row & distance) != 0, up, pltpu.roll(values, ROWS - distance, 0))

    distance = ROWS // 2
    while distance > 0:
        low = (row & distance) == 0
        parts = [
            jnp.where(low, x, y) + swapped(jnp.where(low, y, x), distance)
            for x, y in zip(parts[:distance], parts[distance:])
        ]
        distance //= 2
    return parts[0]


def section_kernel(
    count_ref,
    vel_ref,
    p_ref,
    k_ref,
    w_ref,
    stream_a,
    stream_b,
    girth_a,
    girth_b,
    q_ref,
    fr_ref,
    xs_ref,
    xg_ref,
    moves_ref,
    chosen_ref,
    new_vel_ref,
    new_k_ref,
    new_w_ref,
    harm_ref,
    ext_ref,
    visc_ref,
    field_ref,
    gather_ref,
    value_ref,
    disk_ref,
):
    cells_s, cells_g, cells_r = p_ref.shape
    rows = fr_ref.shape[0]
    pad = moves_ref.shape[0] - rows
    steps = (rows - 1).bit_length()
    stream_odd = lax.axis_index("stream") % 2 == 1
    girth_odd = lax.axis_index("girth") % 2 == 1

    own = [vel_ref[0], vel_ref[1], vel_ref[2], p_ref[...], k_ref[...], w_ref[...]]
    six = range(6)
    updated, energy, rate = advance(
        own,
        [jnp.where(stream_odd, stream_a[f], stream_b[f]) for f in six],
        [jnp.where(stream_odd, stream_b[f], stream_a[f]) for f in six],
        [jnp.where(girth_odd, girth_a[f], girth_b[f]) for f in six],
        [jnp.where(girth_odd, girth_b[f], girth_a[f]) for f in six],
        ext_ref,
        visc_ref,
    )
    new_k_ref[...] = energy
    new_w_ref[...] = rate

    def halved(values):
        high = values.astype(jnp.bfloat16)
        return high, (values - high.astype(jnp.float32)).astype(jnp.bfloat16)

    def rounded(values):
        return values.astype(jnp.bfloat16).astype(jnp.float32)

    halves = cells_r // LANES
    for c in range(3):
        new_vel_ref[c] = updated[c]
        slope = radial(updated[c], 1, 0.0) - updated[c]
        for kind, values in enumerate((updated[c], slope)):
            if c < PRODUCTS:
                high = rounded(values)
                field_ref[c, :, 2 * kind] = high
                field_ref[c, :, 2 * kind + 1] = rounded(values - high)
            else:
                for h in range(halves):
                    lanes = slice(h * LANES, (h + 1) * LANES)
                    gather_ref[c - PRODUCTS, :, kind, h] = values[:, :, lanes]

    kinds = 4
    table = field_ref[...].reshape(PRODUCTS * cells_s * kinds * cells_g, cells_r)
    table = table.astype(jnp.bfloat16)
    pair = 2 * LANES
    girth_row = lax.broadcasted_iota(jnp.int32, (cells_g, pair), 0).astype(jnp.float32)
    radial_row = lax.broadcasted_iota(jnp.int32, (cells_r, pair), 0)

    def two(values, j):
        return jnp.concatenate([values[j : j + 1], values[j + 1 : j + 2]], axis=1)

    def spread(values, j):
        return jnp.broadcast_to(values[j : j + 1], (cells_g, LANES))

    def pick(c, s, kind, index, half_of):
        out = None
        for h in range(halves):
            got = jnp.take_along_axis(
                gather_ref[c - PRODUCTS, s, kind, h], index, axis=1, mode="promise_in_bounds"
            )
            out = got if out is None else jnp.where(half_of[h], got, out)
        return out

    def eight(group, carry):
        at = pl.multiple_of(group * ROWS, ROWS)
        here = pl.ds(at, ROWS)
        q8, fr8, xg8, xs8 = (r[here, :] for r in (q_ref, fr_ref, xg_ref, xs_ref))
        hs8 = [jnp.maximum(1.0 - jnp.abs(xs8 - float(s)), 0.0) for s in range(cells_s)]
        index8 = q8 % LANES
        sums = [[], [], []]
        for j in range(0, ROWS, 2):
            hot = jnp.where(radial_row == two(q8, j), 1.0, 0.0).astype(jnp.bfloat16)
            got = jnp.dot(table, hot, preferred_element_type=jnp.float32)
            got = got.reshape(PRODUCTS, cells_s, kinds, cells_g, pair)
            fr = two(fr8, j)
            hg = jnp.maximum(1.0 - jnp.abs(two(xg8, j) - girth_row), 0.0)
            hs = [two(hs8[s], j) for s in range(cells_s)]
            for c in range(PRODUCTS):
                total = None
                for s in range(cells_s):
                    value = got[c, s, 0] + got[c, s, 1] + fr * (got[c, s, 2] + got[c, s, 3])
                    value = hs[s] * value
                    total = value if total is None else total + value
                total = hg * total
                sums[c] += [total[:, :LANES], total[:, LANES:]]
            for i in (j, j + 1):
                index, q = spread(index8, i), spread(q8, i)
                half_of = [q >= h * LANES for h in range(halves)]
                own_hg = hg[:, (i - j) * LANES : (i - j + 1) * LANES]
                for c in range(PRODUCTS, 3):
                    total = None
                    for s in range(cells_s):
                        value = pick(c, s, 0, index, half_of)
                        value = value + fr8[i : i + 1] * pick(c, s, 1, index, half_of)
                        value = hs8[s][i : i + 1] * value
                        total = value if total is None else total + value
                    sums[c].append(own_hg * total)
        for c in range(3):
            value_ref[0, c, pl.ds(pad + at, ROWS), :] = girth_sums(sums[c])
        return carry

    lax.fori_loop(0, (count_ref[0] + ROWS - 1) // ROWS, eight, jnp.int32(0))

    for step in reversed(range(steps)):
        bit = 1 << step
        a, b = (0, 1) if (steps - 1 - step) % 2 == 0 else (1, 0)
        for at in range(0, rows, CHUNK):
            here, there = pl.ds(pad + at, CHUNK), pl.ds(pad + at - bit, CHUNK)
            moved = (moves_ref[there, :] & bit) != 0
            if step == 0:
                kept = moves_ref[here, :] >= 1 << steps
            for c in range(3):
                value = jnp.where(moved, value_ref[a, c, there, :], value_ref[a, c, here, :])
                if step > 0:
                    value_ref[b, c, here, :] = value
                else:
                    disk_ref[c, pl.ds(at, CHUNK), :] = jnp.where(kept, value, 0.0)

    turned = jnp.concatenate([disk_ref[c].T for c in range(3)], axis=0)
    high, low = halved(turned)
    wave_high, wave_low = halved(chosen_ref[...])
    waves = jnp.dot(high, wave_high, preferred_element_type=jnp.float32)
    waves += jnp.dot(high, wave_low, preferred_element_type=jnp.float32)
    waves += jnp.dot(low, wave_high, preferred_element_type=jnp.float32)
    radii = harm_ref.shape[0]
    for c in range(3):
        harm_ref[:, c * 2 * NH : (c + 1) * 2 * NH] = waves[c * radii : (c + 1) * radii]


def section(velocity, pressure, energy, rate, halos, points):
    _, cells_s, cells_g, cells_r = velocity.shape
    *lists, moves, chosen, counts = points
    rows, radii = lists[0].shape
    shape = functools.partial(jax.ShapeDtypeStruct, dtype=jnp.float32)
    scratch = lambda *dims: pltpu.VMEM(dims, jnp.float32)
    vmem = pl.BlockSpec(memory_space=pltpu.VMEM)
    smem = pl.BlockSpec(memory_space=pltpu.SMEM)
    return pl.pallas_call(
        section_kernel,
        out_shape=(
            shape(velocity.shape),
            shape(energy.shape),
            shape(rate.shape),
            shape((radii, 6 * NH)),
        ),
        in_specs=[smem] + [vmem] * 14,
        scratch_shapes=[
            scratch(6, cells_s, 3 * ROWS, cells_r),
            scratch(cells_s, 3 * ROWS, cells_r),
            scratch(PRODUCTS, cells_s, 4, cells_g, cells_r),
            scratch(3 - PRODUCTS, cells_s, 2, cells_r // LANES, cells_g, LANES),
            scratch(2, 3, moves.shape[0], radii),
            scratch(3, rows, radii),
        ],
        compiler_params=pltpu.CompilerParams(vmem_limit_bytes=VMEM_LIMIT),
        name="section_and_disk",
    )(counts, velocity, pressure, energy, rate, *halos, *lists, moves, chosen)


def fourier_table(azimuths, modes):
    phase = np.arange(azimuths)[:, None] * np.arange(modes)[None, :] % azimuths
    angles = phase * (2.0 * math.pi / azimuths)
    table = np.concatenate([np.cos(angles), -np.sin(angles)], axis=1) / math.sqrt(azimuths)
    return jnp.asarray(table.astype(np.float32))


def body(velocity, pressure, kinetic_energy, dissipation_rate, corner_ids, fractions, sector_owner):
    _, cells_s, cells_g, cells_r = velocity.shape
    radii, azimuths = corner_ids.shape
    stream_count, girth_count = lax.axis_size("stream"), lax.axis_size("girth")
    devices = stream_count * girth_count

    def swap(values, axis, count, start):
        pairs = []
        for i in range(start, count - 1, 2):
            pairs += [(i, i + 1), (i + 1, i)]
        return lax.ppermute(values, axis, pairs)

    slabs = pack(velocity, pressure, kinetic_energy, dissipation_rate)
    halos = (
        swap(slabs[0], "stream", stream_count, 0),
        swap(slabs[1], "stream", stream_count, 1),
        swap(slabs[2], "girth", girth_count, 0),
        swap(slabs[3], "girth", girth_count, 1),
    )
    points = prepare(
        sector_owner[:, 0],
        corner_ids,
        fractions,
        fourier_table(azimuths, NH),
        (cells_s, cells_g, cells_r),
        girth_count,
    )
    new_velocity, new_energy, new_rate, partial = section(
        velocity, pressure, kinetic_energy, dissipation_rate, halos, points
    )
    shares = lax.all_to_all(
        partial.reshape(devices, radii // devices, 6 * NH),
        ("stream", "girth"),
        split_axis=0,
        concat_axis=0,
        tiled=True,
    )
    return new_velocity, new_energy, new_rate, jnp.sum(shares, axis=0)


def solution(mesh):
    return jax.shard_map(
        body,
        mesh=mesh,
        in_specs=(
            P(None, "stream", "girth", None),
            P("stream", "girth", None),
            P("stream", "girth", None),
            P("stream", "girth", None),
            P(),
            P(),
            P(),
        ),
        out_specs=(
            P(None, "stream", "girth", None),
            P("stream", "girth", None),
            P("stream", "girth", None),
            P(("stream", "girth"), None),
        ),
        check_vma=False,
    )
```

```python
import functools
import math

import jax
import jax.numpy as jnp
import numpy as np
from jax import lax
from jax.experimental import pallas as pl
from jax.experimental.pallas import tpu as pltpu
from jax.sharding import PartitionSpec as P

NH = 128

base_viscosity = 0.05
time_step = 0.2
beta_star = 0.09
beta_rate = 0.075
alpha_rate = 0.52
wall_rate = 1.0

LANES = 128
ROWS = 8
SHIFT = 10
CHUNK = 32
PRODUCTS = 2
VMEM_LIMIT = 48 * 1024 * 1024


def in_hbm(values):
    return pltpu.with_memory_space_constraint(values, pltpu.HBM)


def pack_kernel(vel_ref, p_ref, k_ref, w_ref, ids_hbm, frac_hbm, *rest):
    *slabs, ids_ref, frac_ref, arrived = rest
    copies = [
        pltpu.make_async_copy(ids_hbm, ids_ref, arrived.at[0]),
        pltpu.make_async_copy(frac_hbm, frac_ref, arrived.at[1]),
    ]
    for copy in copies:
        copy.start()
    cells_s, cells_g, _ = p_ref.shape
    stream_odd = lax.axis_index("stream") % 2 == 1
    girth_odd = lax.axis_index("girth") % 2 == 1
    for f in range(6):
        own = vel_ref.at[f] if f < 3 else (p_ref, k_ref, w_ref)[f - 3]
        first, last = own[0:2], own[cells_s - 2 : cells_s]
        slabs[0][f] = jnp.where(stream_odd, first, last)
        slabs[1][f] = jnp.where(stream_odd, last, first)
        first, last = own[:, 0:2, :], own[:, cells_g - 2 : cells_g, :]
        slabs[2][f] = jnp.where(girth_odd, first, last)
        slabs[3][f] = jnp.where(girth_odd, last, first)
    for copy in copies:
        copy.wait()


def pack(velocity, pressure, energy, rate, corner_ids, fractions):
    _, cells_s, cells_g, cells_r = velocity.shape
    stream = pltpu.VMEM((6, 2, cells_g, cells_r), jnp.float32)
    girth = pltpu.VMEM((6, cells_s, 2, cells_r), jnp.float32)
    vmem = pl.BlockSpec(memory_space=pltpu.VMEM)
    hbm = pl.BlockSpec(memory_space=pltpu.HBM)
    return pl.pallas_call(
        pack_kernel,
        out_shape=(stream, stream, girth, girth)
        + (pltpu.VMEM(corner_ids.shape, jnp.int32), pltpu.VMEM(fractions.shape, jnp.float32)),
        in_specs=[vmem] * 4 + [hbm] * 2,
        out_specs=[vmem] * 6,
        scratch_shapes=[pltpu.SemaphoreType.DMA((2,))],
        compiler_params=pltpu.CompilerParams(vmem_limit_bytes=VMEM_LIMIT),
        name="pack_halos",
    )(velocity, pressure, energy, rate, in_hbm(corner_ids), in_hbm(fractions))


def network(rows):
    steps = (rows - 1).bit_length()
    return [(low, 1 << min(2, steps - low)) for low in range(0, steps, 2)]


def reach(rows):
    return max((digits - 1) << low for low, digits in network(rows))


def split(values, size):
    if size & (size - 1) == 0:
        return values >> (size.bit_length() - 1), values & (size - 1)
    return values // size, values % size


def prepare_kernel(
    cells_s,
    cells_g,
    cells_r,
    owner_ref,
    ids_ref,
    frac_ref,
    table_hbm,
    q_ref,
    fr_ref,
    xs_ref,
    xg_ref,
    moves_ref,
    chosen_ref,
    count_ref,
    table_ref,
    turned,
    picked,
    keys,
    frs,
    xss,
    xgs,
    order,
    arrived,
):
    copy = pltpu.make_async_copy(table_hbm, table_ref, arrived.at[0])
    copy.start()
    stream_first = lax.axis_index("stream") * cells_s
    me = lax.axis_index("girth")
    sectors = owner_ref.shape[0]
    azimuths = ids_ref.shape[1]
    width = azimuths // sectors
    rows = fr_ref.shape[0]
    pad = moves_ref.shape[0] - rows
    passes = network(rows)
    valid = 1 << SHIFT - 1

    def listed(number, count):
        order[jnp.minimum(count, rows // width)] = number
        return count + (owner_ref[number] == me).astype(jnp.int32)

    owned = lax.fori_loop(0, sectors, listed, jnp.int32(0), unroll=8)

    for at in range(0, azimuths, LANES):
        cols = pl.ds(at, LANES)
        turned[0, cols, :] = ids_ref[:, cols].astype(jnp.float32).T
        for d in range(3):
            turned[1 + d, cols, :] = frac_ref[d, :, cols].T
    for d in range(4):
        picked[d] = jnp.full(picked.shape[1:], -1.0 if d == 0 else 0.0, jnp.float32)
    chosen_ref[...] = jnp.zeros_like(chosen_ref)
    beyond = pl.ds(rows, pad)
    for slot in range(2):
        keys[slot, beyond, :] = jnp.zeros((pad, LANES), jnp.int32)
    moves_ref[0:pad, :] = jnp.zeros((pad, LANES), jnp.int32)
    copy.wait()

    def sector(place, carry):
        source = pl.ds(pl.multiple_of(order[place] * width, width), width)
        target = pl.ds(pl.multiple_of(place * width, width), width)
        chosen_ref[target, :] = table_ref[source, :]
        for d in range(4):
            picked[d, target, :] = turned[d, source, :]
        return carry

    lax.fori_loop(0, owned, sector, jnp.int32(0))

    held = pl.ds(0, rows)
    ids = picked[0].astype(jnp.int32)
    stream_cell, rest = split(jnp.maximum(ids, 0), cells_g * cells_r)
    girth_cell, radial_cell = split(rest, cells_r)
    xs = (stream_cell - stream_first).astype(jnp.float32) + picked[1]
    kept = (ids >= 0) & (xs > -1.0) & (xs < float(cells_s))
    xss[0, held, :] = xs
    xgs[0, held, :] = girth_cell.astype(jnp.float32) + picked[2]
    frs[0, held, :] = picked[3]
    earlier = lax.broadcasted_iota(jnp.int32, (rows, rows), 0) > lax.broadcasted_iota(
        jnp.int32, (rows, rows), 1
    )
    earlier = earlier.astype(jnp.float32).astype(jnp.bfloat16)
    skipped = jnp.where(kept, 0.0, 1.0)
    before = jnp.dot(
        earlier, skipped.astype(jnp.bfloat16), preferred_element_type=jnp.float32
    ).astype(jnp.int32)
    counts = rows - jnp.sum(skipped, axis=0, keepdims=True).astype(jnp.int32)
    count_ref[0] = jnp.max(counts)
    moves_ref[pad : pad + rows, :] = jnp.where(kept, valid, 0)
    keys[0, held, :] = (radial_cell << SHIFT) + jnp.where(kept, before, 0)
    for number, (low, digits) in enumerate(passes):
        a, b = number % 2, 1 - number % 2
        mask = digits - 1 << low
        last = number == len(passes) - 1
        for at in range(0, rows, CHUNK):
            here, target = pl.ds(at, CHUNK), pl.ds(pad + at, CHUNK)
            there = [pl.ds(at + (k << low), CHUNK) for k in range(1, digits)]
            key = keys[a, here, :]
            arriving = [keys[a, t, :] for t in there]
            moved = [(arriving[k] & mask) == (k + 1 << low) for k in range(digits - 1)]
            key = jnp.where((key & mask) != 0, key & -(1 << SHIFT), key)
            came = moves_ref[target, :]
            out = [r[a, here, :] for r in (frs, xss, xgs)]
            for k in range(digits - 1):
                key = jnp.where(moved[k], arriving[k], key)
                came = came | jnp.where(moved[k], k + 1 << low, 0)
                out = [
                    jnp.where(moved[k], r[a, there[k], :], o) for r, o in zip((frs, xss, xgs), out)
                ]
            moves_ref[target, :] = came
            if last:
                q_ref[here, :] = key >> SHIFT
                fr_ref[here, :] = out[0]
                xs_ref[here, :] = out[1]
                xg_ref[here, :] = out[2]
            else:
                keys[b, here, :] = key
                frs[b, here, :] = out[0]
                xss[b, here, :] = out[1]
                xgs[b, here, :] = out[2]


def prepare(owners, corner_ids, fractions, table, cells, girth_count):
    cells_s, cells_g, cells_r = cells
    radii, azimuths = corner_ids.shape
    sectors = owners.shape[0]
    rows = 3 * sectors // girth_count * (azimuths // sectors)
    pad = reach(rows)
    shape = jax.ShapeDtypeStruct
    lists = (rows, radii)
    vmem = pl.BlockSpec(memory_space=pltpu.VMEM)
    smem = pl.BlockSpec(memory_space=pltpu.SMEM)
    hbm = pl.BlockSpec(memory_space=pltpu.HBM)
    return pl.pallas_call(
        functools.partial(prepare_kernel, cells_s, cells_g, cells_r),
        out_shape=(
            shape(lists, jnp.int32),
            shape(lists, jnp.float32),
            shape(lists, jnp.float32),
            shape(lists, jnp.float32),
            shape((pad + rows, radii), jnp.int32),
            shape((rows, 2 * NH), jnp.float32),
            shape((1,), jnp.int32),
        ),
        in_specs=[smem, vmem, vmem, hbm],
        out_specs=[vmem] * 6 + [smem],
        scratch_shapes=[
            pltpu.VMEM(table.shape, jnp.float32),
            pltpu.VMEM((4, azimuths, radii), jnp.float32),
            pltpu.VMEM((4, rows, radii), jnp.float32),
            pltpu.VMEM((2, rows + pad, radii), jnp.int32),
        ]
        + [pltpu.VMEM((2, rows + pad, radii), jnp.float32)] * 3
        + [pltpu.SMEM((rows // (azimuths // sectors) + 1,), jnp.int32)]
        + [pltpu.SemaphoreType.DMA((1,))],
        compiler_params=pltpu.CompilerParams(vmem_limit_bytes=VMEM_LIMIT),
        cost_estimate=pl.CostEstimate(
            flops=20 * radii * azimuths, bytes_accessed=44 * radii * azimuths, transcendentals=0
        ),
        name="prepare_points",
    )(in_hbm(owners), corner_ids, fractions, in_hbm(table))


def radial(values, amount, fill):
    extent = values.shape[-1]
    rolled = pltpu.roll(values, (-amount) % extent, values.ndim - 1)
    position = lax.broadcasted_iota(jnp.int32, values.shape, values.ndim - 1) + amount
    return jnp.where((position >= 0) & (position < extent), rolled, fill)


def advance(own, before, after, left, right, ext_ref, visc_ref):
    cells_s, cells_g, _ = own[0].shape
    mid = ROWS

    def along_s(stack, amount):
        return stack[2 + amount : 2 + amount + cells_s]

    def along_g(ref, amount):
        return ref[:, mid + amount : mid + amount + cells_g, :]

    def viscosity(energy, rate):
        return base_viscosity + energy / (rate + wall_rate)

    stacks = [jnp.concatenate([before[f], own[f], after[f]], axis=0) for f in range(6)]
    for f in range(6):
        ext_ref[f, :, mid - 2 : mid, :] = left[f]
        ext_ref[f, :, mid : mid + cells_g, :] = own[f]
        ext_ref[f, :, mid + cells_g : mid + cells_g + 2, :] = right[f]
    middle = viscosity(own[4], own[5])
    visc_stack = viscosity(stacks[4], stacks[5])
    visc_ref[:, mid - 2 : mid, :] = viscosity(left[4], left[5])
    visc_ref[:, mid : mid + cells_g, :] = middle
    visc_ref[:, mid + cells_g : mid + cells_g + 2, :] = viscosity(right[4], right[5])
    faces = [
        (
            0.5 * (middle + along_s(visc_stack, 1)),
            0.5 * (middle + along_s(visc_stack, -1)),
        ),
        (
            0.5 * (middle + along_g(visc_ref, 1)),
            0.5 * (middle + along_g(visc_ref, -1)),
        ),
        (
            0.5 * (middle + radial(middle, 1, base_viscosity)),
            0.5 * (middle + radial(middle, -1, base_viscosity)),
        ),
    ]

    def neighbour(f, direction, amount):
        if direction == 0:
            return along_s(stacks[f], amount)
        if direction == 1:
            return along_g(ext_ref.at[f], amount)
        return radial(own[f], amount, 0.0)

    def terms(f, direction):
        up, down = neighbour(f, direction, 1), neighbour(f, direction, -1)
        far = neighbour(f, direction, 2) - neighbour(f, direction, -2)
        gradient = (8.0 * (up - down) - far) * (1.0 / 12.0)
        above, below = faces[direction]
        return gradient, above * (up - own[f]) - below * (own[f] - down)

    strain = None
    updated = []
    for f in range(3):
        change = -terms(3, f)[0]
        for direction in range(3):
            gradient, spread = terms(f, direction)
            strain = gradient * gradient if strain is None else strain + gradient * gradient
            change = change - own[direction] * gradient + spread
        updated.append(own[f] + time_step * change)
    energy = own[4] / (own[5] + wall_rate) * strain - beta_star * own[4] * own[5]
    rate = alpha_rate * strain - beta_rate * own[5] * own[5]
    for direction in range(3):
        gradient, spread = terms(4, direction)
        energy = energy - own[direction] * gradient + spread
        gradient, spread = terms(5, direction)
        rate = rate - own[direction] * gradient + spread
    return updated, own[4] + time_step * energy, own[5] + time_step * rate


def girth_sums(parts):
    row = lax.broadcasted_iota(jnp.int32, parts[0].shape, 0)

    def swapped(values, distance):
        up = pltpu.roll(values, distance, 0)
        if 2 * distance == ROWS:
            return up
        return jnp.where((row & distance) != 0, up, pltpu.roll(values, ROWS - distance, 0))

    distance = ROWS // 2
    while distance > 0:
        low = (row & distance) == 0
        parts = [
            jnp.where(low, x, y) + swapped(jnp.where(low, y, x), distance)
            for x, y in zip(parts[:distance], parts[distance:])
        ]
        distance //= 2
    return parts[0]


def section_kernel(
    count_ref,
    vel_ref,
    p_ref,
    k_ref,
    w_ref,
    stream_a,
    stream_b,
    girth_a,
    girth_b,
    q_ref,
    fr_ref,
    xs_ref,
    xg_ref,
    moves_ref,
    chosen_ref,
    new_vel_hbm,
    new_k_hbm,
    new_w_hbm,
    harm_ref,
    new_vel_ref,
    new_k_ref,
    new_w_ref,
    ext_ref,
    visc_ref,
    field_ref,
    gather_ref,
    value_ref,
    disk_ref,
    stored,
):
    cells_s, cells_g, cells_r = p_ref.shape
    rows = fr_ref.shape[0]
    pad = moves_ref.shape[0] - rows
    passes = network(rows)
    valid = 1 << SHIFT - 1
    stream_odd = lax.axis_index("stream") % 2 == 1
    girth_odd = lax.axis_index("girth") % 2 == 1

    own = [vel_ref[0], vel_ref[1], vel_ref[2], p_ref[...], k_ref[...], w_ref[...]]
    six = range(6)
    updated, energy, rate = advance(
        own,
        [jnp.where(stream_odd, stream_a[f], stream_b[f]) for f in six],
        [jnp.where(stream_odd, stream_b[f], stream_a[f]) for f in six],
        [jnp.where(girth_odd, girth_a[f], girth_b[f]) for f in six],
        [jnp.where(girth_odd, girth_b[f], girth_a[f]) for f in six],
        ext_ref,
        visc_ref,
    )
    new_k_ref[...] = energy
    new_w_ref[...] = rate

    def halved(values):
        high = values.astype(jnp.bfloat16)
        return high, (values - high.astype(jnp.float32)).astype(jnp.bfloat16)

    def rounded(values):
        return values.astype(jnp.bfloat16).astype(jnp.float32)

    halves = cells_r // LANES
    for c in range(3):
        new_vel_ref[c] = updated[c]
        slope = radial(updated[c], 1, 0.0) - updated[c]
        for kind, values in enumerate((updated[c], slope)):
            if c < PRODUCTS:
                high = rounded(values)
                field_ref[c, :, 2 * kind] = high
                field_ref[c, :, 2 * kind + 1] = rounded(values - high)
            else:
                for h in range(halves):
                    lanes = slice(h * LANES, (h + 1) * LANES)
                    gather_ref[c - PRODUCTS, :, kind, h] = values[:, :, lanes]
    results = ((new_vel_ref, new_vel_hbm), (new_k_ref, new_k_hbm), (new_w_ref, new_w_hbm))
    copies = [
        pltpu.make_async_copy(source, target, stored.at[i])
        for i, (source, target) in enumerate(results)
    ]
    for copy in copies:
        copy.start()

    kinds = 4
    table = field_ref[...].reshape(PRODUCTS * cells_s * kinds * cells_g, cells_r)
    table = table.astype(jnp.bfloat16)
    pair = 2 * LANES
    girth_row = lax.broadcasted_iota(jnp.int32, (cells_g, pair), 0).astype(jnp.float32)
    radial_row = lax.broadcasted_iota(jnp.int32, (cells_r, pair), 0)

    def two(values, j):
        return jnp.concatenate([values[j : j + 1], values[j + 1 : j + 2]], axis=1)

    def spread(values, j):
        return jnp.broadcast_to(values[j : j + 1], (cells_g, LANES))

    def pick(c, s, kind, index, half_of):
        out = None
        for h in range(halves):
            got = jnp.take_along_axis(
                gather_ref[c - PRODUCTS, s, kind, h], index, axis=1, mode="promise_in_bounds"
            )
            out = got if out is None else jnp.where(half_of[h], got, out)
        return out

    def eight(group, carry):
        at = pl.multiple_of(group * ROWS, ROWS)
        here = pl.ds(at, ROWS)
        q8, fr8, xg8, xs8 = (r[here, :] for r in (q_ref, fr_ref, xg_ref, xs_ref))
        hs8 = [jnp.maximum(1.0 - jnp.abs(xs8 - float(s)), 0.0) for s in range(cells_s)]
        index8 = q8 & (LANES - 1)
        sums = [[], [], []]
        for j in range(0, ROWS, 2):
            hot = jnp.where(radial_row == two(q8, j), 1.0, 0.0).astype(jnp.bfloat16)
            got = jnp.dot(table, hot, preferred_element_type=jnp.float32)
            got = got.reshape(PRODUCTS, cells_s, kinds, cells_g, pair)
            fr = two(fr8, j)
            hg = jnp.maximum(1.0 - jnp.abs(two(xg8, j) - girth_row), 0.0)
            hs = [two(hs8[s], j) for s in range(cells_s)]
            for c in range(PRODUCTS):
                total = None
                for s in range(cells_s):
                    value = got[c, s, 0] + got[c, s, 1] + fr * (got[c, s, 2] + got[c, s, 3])
                    value = hs[s] * value
                    total = value if total is None else total + value
                total = hg * total
                sums[c] += [total[:, :LANES], total[:, LANES:]]
            for i in (j, j + 1):
                index, q = spread(index8, i), spread(q8, i)
                half_of = [q >= h * LANES for h in range(halves)]
                own_hg = hg[:, (i - j) * LANES : (i - j + 1) * LANES]
                for c in range(PRODUCTS, 3):
                    total = None
                    for s in range(cells_s):
                        value = pick(c, s, 0, index, half_of)
                        value = value + fr8[i : i + 1] * pick(c, s, 1, index, half_of)
                        value = hs8[s][i : i + 1] * value
                        total = value if total is None else total + value
                    sums[c].append(own_hg * total)
        for c in range(3):
            value_ref[0, c, pl.ds(pad + at, ROWS), :] = girth_sums(sums[c])
        return carry

    lax.fori_loop(0, (count_ref[0] + ROWS - 1) // ROWS, eight, jnp.int32(0))

    for number, (low, digits) in enumerate(reversed(passes)):
        a, b = number % 2, 1 - number % 2
        mask = digits - 1 << low
        last = number == len(passes) - 1
        for at in range(0, rows, CHUNK):
            here = pl.ds(pad + at, CHUNK)
            there = [pl.ds(pad + at - (k << low), CHUNK) for k in range(1, digits)]
            moved = [(moves_ref[there[k], :] & mask) == (k + 1 << low) for k in range(digits - 1)]
            if last:
                kept = (moves_ref[here, :] & valid) != 0
            for c in range(3):
                value = value_ref[a, c, here, :]
                for k in range(digits - 1):
                    value = jnp.where(moved[k], value_ref[a, c, there[k], :], value)
                if last:
                    disk_ref[c, pl.ds(at, CHUNK), :] = jnp.where(kept, value, 0.0)
                else:
                    value_ref[b, c, here, :] = value

    turned = jnp.concatenate([disk_ref[c].T for c in range(3)], axis=0)
    high, low = halved(turned)
    wave_high, wave_low = halved(chosen_ref[...])
    waves = jnp.dot(high, wave_high, preferred_element_type=jnp.float32)
    waves += jnp.dot(high, wave_low, preferred_element_type=jnp.float32)
    waves += jnp.dot(low, wave_high, preferred_element_type=jnp.float32)
    radii = harm_ref.shape[0]
    for c in range(3):
        harm_ref[:, c * 2 * NH : (c + 1) * 2 * NH] = waves[c * radii : (c + 1) * radii]
    for copy in copies:
        copy.wait()


def section(velocity, pressure, energy, rate, halos, points):
    _, cells_s, cells_g, cells_r = velocity.shape
    *lists, moves, chosen, counts = points
    rows, radii = lists[0].shape
    shape = functools.partial(jax.ShapeDtypeStruct, dtype=jnp.float32)
    scratch = lambda *dims: pltpu.VMEM(dims, jnp.float32)
    vmem = pl.BlockSpec(memory_space=pltpu.VMEM)
    smem = pl.BlockSpec(memory_space=pltpu.SMEM)
    return pl.pallas_call(
        section_kernel,
        out_shape=(
            shape(velocity.shape),
            shape(energy.shape),
            shape(rate.shape),
            shape((radii, 6 * NH)),
        ),
        in_specs=[smem] + [vmem] * 14,
        out_specs=[pl.BlockSpec(memory_space=pl.ANY)] * 3 + [vmem],
        scratch_shapes=[
            scratch(*velocity.shape),
            scratch(*energy.shape),
            scratch(*rate.shape),
            scratch(6, cells_s, 3 * ROWS, cells_r),
            scratch(cells_s, 3 * ROWS, cells_r),
            scratch(PRODUCTS, cells_s, 4, cells_g, cells_r),
            scratch(3 - PRODUCTS, cells_s, 2, cells_r // LANES, cells_g, LANES),
            scratch(2, 3, moves.shape[0], radii),
            scratch(3, rows, radii),
            pltpu.SemaphoreType.DMA((3,)),
        ],
        compiler_params=pltpu.CompilerParams(vmem_limit_bytes=VMEM_LIMIT),
        name="section_and_disk",
    )(counts, velocity, pressure, energy, rate, *halos, *lists, moves, chosen)


def fourier_table(azimuths, modes):
    phase = np.arange(azimuths)[:, None] * np.arange(modes)[None, :] % azimuths
    angles = phase * (2.0 * math.pi / azimuths)
    table = np.concatenate([np.cos(angles), -np.sin(angles)], axis=1) / math.sqrt(azimuths)
    return jnp.asarray(table.astype(np.float32))


def body(velocity, pressure, kinetic_energy, dissipation_rate, corner_ids, fractions, sector_owner):
    _, cells_s, cells_g, cells_r = velocity.shape
    radii, azimuths = corner_ids.shape
    stream_count, girth_count = lax.axis_size("stream"), lax.axis_size("girth")
    devices = stream_count * girth_count

    def swap(values, axis, count, start):
        pairs = []
        for i in range(start, count - 1, 2):
            pairs += [(i, i + 1), (i + 1, i)]
        return lax.ppermute(values, axis, pairs)

    *slabs, ids, fracs = pack(
        velocity, pressure, kinetic_energy, dissipation_rate, corner_ids, fractions
    )
    girth_halos = (
        swap(slabs[2], "girth", girth_count, 0),
        swap(slabs[3], "girth", girth_count, 1),
    )
    stream_halos = (
        swap(slabs[0], "stream", stream_count, 0),
        swap(slabs[1], "stream", stream_count, 1),
    )
    halos = stream_halos + girth_halos
    points = prepare(
        sector_owner[:, 0],
        ids,
        fracs,
        fourier_table(azimuths, NH),
        (cells_s, cells_g, cells_r),
        girth_count,
    )
    new_velocity, new_energy, new_rate, partial = section(
        velocity, pressure, kinetic_energy, dissipation_rate, halos, points
    )
    shares = lax.all_to_all(
        partial.reshape(devices, radii // devices, 6 * NH),
        ("stream", "girth"),
        split_axis=0,
        concat_axis=0,
        tiled=True,
    )
    return new_velocity, new_energy, new_rate, jnp.sum(shares, axis=0)


def solution(mesh):
    return jax.shard_map(
        body,
        mesh=mesh,
        in_specs=(
            P(None, "stream", "girth", None),
            P("stream", "girth", None),
            P("stream", "girth", None),
            P("stream", "girth", None),
            P(),
            P(),
            P(),
        ),
        out_specs=(
            P(None, "stream", "girth", None),
            P("stream", "girth", None),
            P("stream", "girth", None),
            P(("stream", "girth"), None),
        ),
        check_vma=False,
    )
```

```python
import functools
import math

import jax
import jax.numpy as jnp
import numpy as np
from jax import lax
from jax.experimental import pallas as pl
from jax.experimental.pallas import tpu as pltpu
from jax.sharding import PartitionSpec as P

NH = 128

base_viscosity = 0.05
time_step = 0.2
beta_star = 0.09
beta_rate = 0.075
alpha_rate = 0.52
wall_rate = 1.0

LANES = 128
ROWS = 8
SHIFT = 10
CHUNK = 32
PRODUCTS = 2
VMEM_LIMIT = 48 * 1024 * 1024


def in_hbm(values):
    return pltpu.with_memory_space_constraint(values, pltpu.HBM)


def pack_kernel(vel_ref, p_ref, k_ref, w_ref, ids_hbm, frac_hbm, *rest):
    *slabs, ids_ref, frac_ref, arrived = rest
    copies = [
        pltpu.make_async_copy(ids_hbm, ids_ref, arrived.at[0]),
        pltpu.make_async_copy(frac_hbm, frac_ref, arrived.at[1]),
    ]
    for copy in copies:
        copy.start()
    cells_s, cells_g, _ = p_ref.shape
    stream_odd = lax.axis_index("stream") % 2 == 1
    girth_odd = lax.axis_index("girth") % 2 == 1
    for f in range(6):
        own = vel_ref.at[f] if f < 3 else (p_ref, k_ref, w_ref)[f - 3]
        first, last = own[0:2], own[cells_s - 2 : cells_s]
        slabs[0][f] = jnp.where(stream_odd, first, last)
        slabs[1][f] = jnp.where(stream_odd, last, first)
        first, last = own[:, 0:2, :], own[:, cells_g - 2 : cells_g, :]
        slabs[2][f] = jnp.where(girth_odd, first, last)
        slabs[3][f] = jnp.where(girth_odd, last, first)
    for copy in copies:
        copy.wait()


def pack(velocity, pressure, energy, rate, corner_ids, fractions):
    _, cells_s, cells_g, cells_r = velocity.shape
    stream = pltpu.VMEM((6, 2, cells_g, cells_r), jnp.float32)
    girth = pltpu.VMEM((6, cells_s, 2, cells_r), jnp.float32)
    vmem = pl.BlockSpec(memory_space=pltpu.VMEM)
    hbm = pl.BlockSpec(memory_space=pltpu.HBM)
    return pl.pallas_call(
        pack_kernel,
        out_shape=(stream, stream, girth, girth)
        + (pltpu.VMEM(corner_ids.shape, jnp.int32), pltpu.VMEM(fractions.shape, jnp.float32)),
        in_specs=[vmem] * 4 + [hbm] * 2,
        out_specs=[vmem] * 6,
        scratch_shapes=[pltpu.SemaphoreType.DMA((2,))],
        compiler_params=pltpu.CompilerParams(vmem_limit_bytes=VMEM_LIMIT),
        name="pack_halos",
    )(*(in_hbm(x) for x in (velocity, pressure, energy, rate, corner_ids, fractions)))


def network(rows):
    steps = (rows - 1).bit_length()
    return [(low, 1 << min(2, steps - low)) for low in range(0, steps, 2)]


def reach(rows):
    return max((digits - 1) << low for low, digits in network(rows))


def split(values, size):
    if size & (size - 1) == 0:
        return values >> (size.bit_length() - 1), values & (size - 1)
    return values // size, values % size


def prepare_kernel(
    cells_s,
    cells_g,
    cells_r,
    owner_ref,
    ids_ref,
    frac_ref,
    table_hbm,
    q_ref,
    fr_ref,
    xs_ref,
    xg_ref,
    moves_ref,
    chosen_ref,
    count_ref,
    table_ref,
    turned,
    picked,
    keys,
    frs,
    xss,
    xgs,
    order,
    arrived,
):
    copy = pltpu.make_async_copy(table_hbm, table_ref, arrived.at[0])
    copy.start()
    stream_first = lax.axis_index("stream") * cells_s
    me = lax.axis_index("girth")
    sectors = owner_ref.shape[0]
    azimuths = ids_ref.shape[1]
    width = azimuths // sectors
    rows = fr_ref.shape[0]
    pad = moves_ref.shape[0] - rows
    passes = network(rows)
    valid = 1 << SHIFT - 1

    def listed(number, count):
        order[jnp.minimum(count, rows // width)] = number
        return count + (owner_ref[number] == me).astype(jnp.int32)

    owned = lax.fori_loop(0, sectors, listed, jnp.int32(0), unroll=8)

    for at in range(0, azimuths, LANES):
        cols = pl.ds(at, LANES)
        turned[0, cols, :] = ids_ref[:, cols].astype(jnp.float32).T
        for d in range(3):
            turned[1 + d, cols, :] = frac_ref[d, :, cols].T
    for d in range(4):
        picked[d] = jnp.full(picked.shape[1:], -1.0 if d == 0 else 0.0, jnp.float32)
    chosen_ref[...] = jnp.zeros_like(chosen_ref)
    beyond = pl.ds(rows, pad)
    for slot in range(2):
        keys[slot, beyond, :] = jnp.zeros((pad, LANES), jnp.int32)
    moves_ref[0:pad, :] = jnp.zeros((pad, LANES), jnp.int32)
    copy.wait()

    def sector(place, carry):
        source = pl.ds(pl.multiple_of(order[place] * width, width), width)
        target = pl.ds(pl.multiple_of(place * width, width), width)
        chosen_ref[target, :] = table_ref[source, :]
        for d in range(4):
            picked[d, target, :] = turned[d, source, :]
        return carry

    lax.fori_loop(0, owned, sector, jnp.int32(0))

    held = pl.ds(0, rows)
    ids = picked[0].astype(jnp.int32)
    stream_cell, rest = split(jnp.maximum(ids, 0), cells_g * cells_r)
    girth_cell, radial_cell = split(rest, cells_r)
    xs = (stream_cell - stream_first).astype(jnp.float32) + picked[1]
    kept = (ids >= 0) & (xs > -1.0) & (xs < float(cells_s))
    xss[0, held, :] = xs
    xgs[0, held, :] = girth_cell.astype(jnp.float32) + picked[2]
    frs[0, held, :] = picked[3]
    earlier = lax.broadcasted_iota(jnp.int32, (rows, rows), 0) > lax.broadcasted_iota(
        jnp.int32, (rows, rows), 1
    )
    earlier = earlier.astype(jnp.float32).astype(jnp.bfloat16)
    skipped = jnp.where(kept, 0.0, 1.0)
    before = jnp.dot(
        earlier, skipped.astype(jnp.bfloat16), preferred_element_type=jnp.float32
    ).astype(jnp.int32)
    counts = rows - jnp.sum(skipped, axis=0, keepdims=True).astype(jnp.int32)
    count_ref[0] = jnp.max(counts)
    moves_ref[pad : pad + rows, :] = jnp.where(kept, valid, 0)
    keys[0, held, :] = (radial_cell << SHIFT) + jnp.where(kept, before, 0)
    for number, (low, digits) in enumerate(passes):
        a, b = number % 2, 1 - number % 2
        mask = digits - 1 << low
        last = number == len(passes) - 1
        for at in range(0, rows, CHUNK):
            here, target = pl.ds(at, CHUNK), pl.ds(pad + at, CHUNK)
            there = [pl.ds(at + (k << low), CHUNK) for k in range(1, digits)]
            key = keys[a, here, :]
            arriving = [keys[a, t, :] for t in there]
            moved = [(arriving[k] & mask) == (k + 1 << low) for k in range(digits - 1)]
            key = jnp.where((key & mask) != 0, key & -(1 << SHIFT), key)
            came = moves_ref[target, :]
            out = [r[a, here, :] for r in (frs, xss, xgs)]
            for k in range(digits - 1):
                key = jnp.where(moved[k], arriving[k], key)
                came = came | jnp.where(moved[k], k + 1 << low, 0)
                out = [
                    jnp.where(moved[k], r[a, there[k], :], o) for r, o in zip((frs, xss, xgs), out)
                ]
            moves_ref[target, :] = came
            if last:
                q_ref[here, :] = key >> SHIFT
                fr_ref[here, :] = out[0]
                xs_ref[here, :] = out[1]
                xg_ref[here, :] = out[2]
            else:
                keys[b, here, :] = key
                frs[b, here, :] = out[0]
                xss[b, here, :] = out[1]
                xgs[b, here, :] = out[2]


def prepare(owners, corner_ids, fractions, table, cells, girth_count):
    cells_s, cells_g, cells_r = cells
    radii, azimuths = corner_ids.shape
    sectors = owners.shape[0]
    rows = 3 * sectors // girth_count * (azimuths // sectors)
    pad = reach(rows)
    shape = jax.ShapeDtypeStruct
    lists = (rows, radii)
    vmem = pl.BlockSpec(memory_space=pltpu.VMEM)
    smem = pl.BlockSpec(memory_space=pltpu.SMEM)
    hbm = pl.BlockSpec(memory_space=pltpu.HBM)
    return pl.pallas_call(
        functools.partial(prepare_kernel, cells_s, cells_g, cells_r),
        out_shape=(
            shape(lists, jnp.int32),
            shape(lists, jnp.float32),
            shape(lists, jnp.float32),
            shape(lists, jnp.float32),
            shape((pad + rows, radii), jnp.int32),
            shape((rows, 2 * NH), jnp.float32),
            shape((1,), jnp.int32),
        ),
        in_specs=[smem, vmem, vmem, hbm],
        out_specs=[vmem] * 6 + [smem],
        scratch_shapes=[
            pltpu.VMEM(table.shape, jnp.float32),
            pltpu.VMEM((4, azimuths, radii), jnp.float32),
            pltpu.VMEM((4, rows, radii), jnp.float32),
            pltpu.VMEM((2, rows + pad, radii), jnp.int32),
        ]
        + [pltpu.VMEM((2, rows + pad, radii), jnp.float32)] * 3
        + [pltpu.SMEM((rows // (azimuths // sectors) + 1,), jnp.int32)]
        + [pltpu.SemaphoreType.DMA((1,))],
        compiler_params=pltpu.CompilerParams(vmem_limit_bytes=VMEM_LIMIT),
        cost_estimate=pl.CostEstimate(
            flops=20 * radii * azimuths, bytes_accessed=44 * radii * azimuths, transcendentals=0
        ),
        name="prepare_points",
    )(in_hbm(owners), corner_ids, fractions, in_hbm(table))


def radial(values, amount, fill):
    extent = values.shape[-1]
    rolled = pltpu.roll(values, (-amount) % extent, values.ndim - 1)
    position = lax.broadcasted_iota(jnp.int32, values.shape, values.ndim - 1) + amount
    return jnp.where((position >= 0) & (position < extent), rolled, fill)


def advance(own, before, after, left, right, ext_ref, visc_ref):
    cells_s, cells_g, _ = own[0].shape
    mid = ROWS

    def along_s(stack, amount):
        return stack[2 + amount : 2 + amount + cells_s]

    def along_g(ref, amount):
        return ref[:, mid + amount : mid + amount + cells_g, :]

    def viscosity(energy, rate):
        return base_viscosity + energy / (rate + wall_rate)

    stacks = [jnp.concatenate([before[f], own[f], after[f]], axis=0) for f in range(6)]
    for f in range(6):
        ext_ref[f, :, mid - 2 : mid, :] = left[f]
        ext_ref[f, :, mid : mid + cells_g, :] = own[f]
        ext_ref[f, :, mid + cells_g : mid + cells_g + 2, :] = right[f]
    middle = viscosity(own[4], own[5])
    visc_stack = viscosity(stacks[4], stacks[5])
    visc_ref[:, mid - 2 : mid, :] = viscosity(left[4], left[5])
    visc_ref[:, mid : mid + cells_g, :] = middle
    visc_ref[:, mid + cells_g : mid + cells_g + 2, :] = viscosity(right[4], right[5])
    faces = [
        (
            0.5 * (middle + along_s(visc_stack, 1)),
            0.5 * (middle + along_s(visc_stack, -1)),
        ),
        (
            0.5 * (middle + along_g(visc_ref, 1)),
            0.5 * (middle + along_g(visc_ref, -1)),
        ),
        (
            0.5 * (middle + radial(middle, 1, base_viscosity)),
            0.5 * (middle + radial(middle, -1, base_viscosity)),
        ),
    ]

    def neighbour(f, direction, amount):
        if direction == 0:
            return along_s(stacks[f], amount)
        if direction == 1:
            return along_g(ext_ref.at[f], amount)
        return radial(own[f], amount, 0.0)

    def terms(f, direction):
        up, down = neighbour(f, direction, 1), neighbour(f, direction, -1)
        far = neighbour(f, direction, 2) - neighbour(f, direction, -2)
        gradient = (8.0 * (up - down) - far) * (1.0 / 12.0)
        above, below = faces[direction]
        return gradient, above * (up - own[f]) - below * (own[f] - down)

    strain = None
    updated = []
    for f in range(3):
        change = -terms(3, f)[0]
        for direction in range(3):
            gradient, spread = terms(f, direction)
            strain = gradient * gradient if strain is None else strain + gradient * gradient
            change = change - own[direction] * gradient + spread
        updated.append(own[f] + time_step * change)
    energy = own[4] / (own[5] + wall_rate) * strain - beta_star * own[4] * own[5]
    rate = alpha_rate * strain - beta_rate * own[5] * own[5]
    for direction in range(3):
        gradient, spread = terms(4, direction)
        energy = energy - own[direction] * gradient + spread
        gradient, spread = terms(5, direction)
        rate = rate - own[direction] * gradient + spread
    return updated, own[4] + time_step * energy, own[5] + time_step * rate


def girth_sums(parts):
    row = lax.broadcasted_iota(jnp.int32, parts[0].shape, 0)

    def swapped(values, distance):
        up = pltpu.roll(values, distance, 0)
        if 2 * distance == ROWS:
            return up
        return jnp.where((row & distance) != 0, up, pltpu.roll(values, ROWS - distance, 0))

    distance = ROWS // 2
    while distance > 0:
        low = (row & distance) == 0
        parts = [
            jnp.where(low, x, y) + swapped(jnp.where(low, y, x), distance)
            for x, y in zip(parts[:distance], parts[distance:])
        ]
        distance //= 2
    return parts[0]


def section_kernel(
    count_ref,
    vel_ref,
    p_ref,
    k_ref,
    w_ref,
    stream_a,
    stream_b,
    girth_a,
    girth_b,
    q_ref,
    fr_ref,
    xs_ref,
    xg_ref,
    moves_ref,
    chosen_ref,
    new_vel_hbm,
    new_k_hbm,
    new_w_hbm,
    harm_ref,
    new_vel_ref,
    new_k_ref,
    new_w_ref,
    ext_ref,
    visc_ref,
    field_ref,
    gather_ref,
    value_ref,
    disk_ref,
    stored,
):
    cells_s, cells_g, cells_r = p_ref.shape
    rows = fr_ref.shape[0]
    pad = moves_ref.shape[0] - rows
    passes = network(rows)
    valid = 1 << SHIFT - 1
    stream_odd = lax.axis_index("stream") % 2 == 1
    girth_odd = lax.axis_index("girth") % 2 == 1

    own = [vel_ref[0], vel_ref[1], vel_ref[2], p_ref[...], k_ref[...], w_ref[...]]
    six = range(6)
    updated, energy, rate = advance(
        own,
        [jnp.where(stream_odd, stream_a[f], stream_b[f]) for f in six],
        [jnp.where(stream_odd, stream_b[f], stream_a[f]) for f in six],
        [jnp.where(girth_odd, girth_a[f], girth_b[f]) for f in six],
        [jnp.where(girth_odd, girth_b[f], girth_a[f]) for f in six],
        ext_ref,
        visc_ref,
    )
    new_k_ref[...] = energy
    new_w_ref[...] = rate

    def halved(values):
        high = values.astype(jnp.bfloat16)
        return high, (values - high.astype(jnp.float32)).astype(jnp.bfloat16)

    def rounded(values):
        return values.astype(jnp.bfloat16).astype(jnp.float32)

    halves = cells_r // LANES
    for c in range(3):
        new_vel_ref[c] = updated[c]
        slope = radial(updated[c], 1, 0.0) - updated[c]
        for kind, values in enumerate((updated[c], slope)):
            if c < PRODUCTS:
                high = rounded(values)
                field_ref[c, :, 2 * kind] = high
                field_ref[c, :, 2 * kind + 1] = rounded(values - high)
            else:
                for h in range(halves):
                    lanes = slice(h * LANES, (h + 1) * LANES)
                    gather_ref[c - PRODUCTS, :, kind, h] = values[:, :, lanes]
    results = ((new_vel_ref, new_vel_hbm), (new_k_ref, new_k_hbm), (new_w_ref, new_w_hbm))
    copies = [
        pltpu.make_async_copy(source, target, stored.at[i])
        for i, (source, target) in enumerate(results)
    ]
    for copy in copies:
        copy.start()

    kinds = 4
    table = field_ref[...].reshape(PRODUCTS * cells_s * kinds * cells_g, cells_r)
    table = table.astype(jnp.bfloat16)
    pair = 2 * LANES
    girth_row = lax.broadcasted_iota(jnp.int32, (cells_g, pair), 0).astype(jnp.float32)
    radial_row = lax.broadcasted_iota(jnp.int32, (cells_r, pair), 0)

    def two(values, j):
        return jnp.concatenate([values[j : j + 1], values[j + 1 : j + 2]], axis=1)

    def spread(values, j):
        return jnp.broadcast_to(values[j : j + 1], (cells_g, LANES))

    def pick(c, s, kind, index, half_of):
        out = None
        for h in range(halves):
            got = jnp.take_along_axis(
                gather_ref[c - PRODUCTS, s, kind, h], index, axis=1, mode="promise_in_bounds"
            )
            out = got if out is None else jnp.where(half_of[h], got, out)
        return out

    def eight(group, carry):
        at = pl.multiple_of(group * ROWS, ROWS)
        here = pl.ds(at, ROWS)
        q8, fr8, xg8, xs8 = (r[here, :] for r in (q_ref, fr_ref, xg_ref, xs_ref))
        hs8 = [jnp.maximum(1.0 - jnp.abs(xs8 - float(s)), 0.0) for s in range(cells_s)]
        index8 = q8 & (LANES - 1)
        sums = [[], [], []]
        for j in range(0, ROWS, 2):
            hot = jnp.where(radial_row == two(q8, j), 1.0, 0.0).astype(jnp.bfloat16)
            got = jnp.dot(table, hot, preferred_element_type=jnp.float32)
            got = got.reshape(PRODUCTS, cells_s, kinds, cells_g, pair)
            fr = two(fr8, j)
            hg = jnp.maximum(1.0 - jnp.abs(two(xg8, j) - girth_row), 0.0)
            hs = [two(hs8[s], j) for s in range(cells_s)]
            for c in range(PRODUCTS):
                total = None
                for s in range(cells_s):
                    value = got[c, s, 0] + got[c, s, 1] + fr * (got[c, s, 2] + got[c, s, 3])
                    value = hs[s] * value
                    total = value if total is None else total + value
                total = hg * total
                sums[c] += [total[:, :LANES], total[:, LANES:]]
            for i in (j, j + 1):
                index, q = spread(index8, i), spread(q8, i)
                half_of = [q >= h * LANES for h in range(halves)]
                own_hg = hg[:, (i - j) * LANES : (i - j + 1) * LANES]
                for c in range(PRODUCTS, 3):
                    total = None
                    for s in range(cells_s):
                        value = pick(c, s, 0, index, half_of)
                        value = value + fr8[i : i + 1] * pick(c, s, 1, index, half_of)
                        value = hs8[s][i : i + 1] * value
                        total = value if total is None else total + value
                    sums[c].append(own_hg * total)
        for c in range(3):
            value_ref[0, c, pl.ds(pad + at, ROWS), :] = girth_sums(sums[c])
        return carry

    lax.fori_loop(0, (count_ref[0] + ROWS - 1) // ROWS, eight, jnp.int32(0))

    for number, (low, digits) in enumerate(reversed(passes)):
        a, b = number % 2, 1 - number % 2
        mask = digits - 1 << low
        last = number == len(passes) - 1
        for at in range(0, rows, CHUNK):
            here = pl.ds(pad + at, CHUNK)
            there = [pl.ds(pad + at - (k << low), CHUNK) for k in range(1, digits)]
            moved = [(moves_ref[there[k], :] & mask) == (k + 1 << low) for k in range(digits - 1)]
            if last:
                kept = (moves_ref[here, :] & valid) != 0
            for c in range(3):
                value = value_ref[a, c, here, :]
                for k in range(digits - 1):
                    value = jnp.where(moved[k], value_ref[a, c, there[k], :], value)
                if last:
                    disk_ref[c, pl.ds(at, CHUNK), :] = jnp.where(kept, value, 0.0)
                else:
                    value_ref[b, c, here, :] = value

    turned = jnp.concatenate([disk_ref[c].T for c in range(3)], axis=0)
    high, low = halved(turned)
    wave_high, wave_low = halved(chosen_ref[...])
    waves = jnp.dot(high, wave_high, preferred_element_type=jnp.float32)
    waves += jnp.dot(high, wave_low, preferred_element_type=jnp.float32)
    waves += jnp.dot(low, wave_high, preferred_element_type=jnp.float32)
    radii = harm_ref.shape[0]
    for c in range(3):
        harm_ref[:, c * 2 * NH : (c + 1) * 2 * NH] = waves[c * radii : (c + 1) * radii]
    for copy in copies:
        copy.wait()


def section(velocity, pressure, energy, rate, halos, points):
    _, cells_s, cells_g, cells_r = velocity.shape
    *lists, moves, chosen, counts = points
    rows, radii = lists[0].shape
    shape = functools.partial(jax.ShapeDtypeStruct, dtype=jnp.float32)
    scratch = lambda *dims: pltpu.VMEM(dims, jnp.float32)
    vmem = pl.BlockSpec(memory_space=pltpu.VMEM)
    smem = pl.BlockSpec(memory_space=pltpu.SMEM)
    return pl.pallas_call(
        section_kernel,
        out_shape=(
            shape(velocity.shape),
            shape(energy.shape),
            shape(rate.shape),
            shape((radii, 6 * NH)),
        ),
        in_specs=[smem] + [vmem] * 14,
        out_specs=[pl.BlockSpec(memory_space=pl.ANY)] * 3 + [vmem],
        scratch_shapes=[
            scratch(*velocity.shape),
            scratch(*energy.shape),
            scratch(*rate.shape),
            scratch(6, cells_s, 3 * ROWS, cells_r),
            scratch(cells_s, 3 * ROWS, cells_r),
            scratch(PRODUCTS, cells_s, 4, cells_g, cells_r),
            scratch(3 - PRODUCTS, cells_s, 2, cells_r // LANES, cells_g, LANES),
            scratch(2, 3, moves.shape[0], radii),
            scratch(3, rows, radii),
            pltpu.SemaphoreType.DMA((3,)),
        ],
        compiler_params=pltpu.CompilerParams(vmem_limit_bytes=VMEM_LIMIT),
        name="section_and_disk",
    )(counts, velocity, pressure, energy, rate, *halos, *lists, moves, chosen)


def fourier_table(azimuths, modes):
    phase = np.arange(azimuths)[:, None] * np.arange(modes)[None, :] % azimuths
    angles = phase * (2.0 * math.pi / azimuths)
    table = np.concatenate([np.cos(angles), -np.sin(angles)], axis=1) / math.sqrt(azimuths)
    return jnp.asarray(table.astype(np.float32))


def body(velocity, pressure, kinetic_energy, dissipation_rate, corner_ids, fractions, sector_owner):
    _, cells_s, cells_g, cells_r = velocity.shape
    radii, azimuths = corner_ids.shape
    stream_count, girth_count = lax.axis_size("stream"), lax.axis_size("girth")
    devices = stream_count * girth_count

    def swap(values, axis, count, start):
        pairs = []
        for i in range(start, count - 1, 2):
            pairs += [(i, i + 1), (i + 1, i)]
        return lax.ppermute(values, axis, pairs)

    *slabs, ids, fracs = pack(
        velocity, pressure, kinetic_energy, dissipation_rate, corner_ids, fractions
    )
    girth_halos = (
        swap(slabs[2], "girth", girth_count, 0),
        swap(slabs[3], "girth", girth_count, 1),
    )
    stream_halos = (
        swap(slabs[0], "stream", stream_count, 0),
        swap(slabs[1], "stream", stream_count, 1),
    )
    halos = stream_halos + girth_halos
    points = prepare(
        sector_owner[:, 0],
        ids,
        fracs,
        fourier_table(azimuths, NH),
        (cells_s, cells_g, cells_r),
        girth_count,
    )
    new_velocity, new_energy, new_rate, partial = section(
        velocity, pressure, kinetic_energy, dissipation_rate, halos, points
    )
    shares = lax.all_to_all(
        partial.reshape(devices, radii // devices, 6 * NH),
        ("stream", "girth"),
        split_axis=0,
        concat_axis=0,
        tiled=True,
    )
    return new_velocity, new_energy, new_rate, jnp.sum(shares, axis=0)


def solution(mesh):
    return jax.shard_map(
        body,
        mesh=mesh,
        in_specs=(
            P(None, "stream", "girth", None),
            P("stream", "girth", None),
            P("stream", "girth", None),
            P("stream", "girth", None),
            P(),
            P(),
            P(),
        ),
        out_specs=(
            P(None, "stream", "girth", None),
            P("stream", "girth", None),
            P("stream", "girth", None),
            P(("stream", "girth"), None),
        ),
        check_vma=False,
    )
```

```python
import functools
import math

import jax
import jax.numpy as jnp
import numpy as np
from jax import lax
from jax.experimental import pallas as pl
from jax.experimental.pallas import tpu as pltpu
from jax.sharding import PartitionSpec as P

NH = 128

base_viscosity = 0.05
time_step = 0.2
beta_star = 0.09
beta_rate = 0.075
alpha_rate = 0.52
wall_rate = 1.0

LANES = 128
ROWS = 8
SHIFT = 10
CHUNK = 32
PRODUCTS = 2
VMEM_LIMIT = 48 * 1024 * 1024


def in_hbm(values):
    return pltpu.with_memory_space_constraint(values, pltpu.HBM)


def pack_kernel(vel_ref, p_ref, k_ref, w_ref, *slabs):
    cells_s, cells_g, _ = p_ref.shape
    stream_odd = lax.axis_index("stream") % 2 == 1
    girth_odd = lax.axis_index("girth") % 2 == 1
    for f in range(6):
        own = vel_ref.at[f] if f < 3 else (p_ref, k_ref, w_ref)[f - 3]
        first, last = own[0:2], own[cells_s - 2 : cells_s]
        slabs[0][f] = jnp.where(stream_odd, first, last)
        slabs[1][f] = jnp.where(stream_odd, last, first)
        first, last = own[:, 0:2, :], own[:, cells_g - 2 : cells_g, :]
        slabs[2][f] = jnp.where(girth_odd, first, last)
        slabs[3][f] = jnp.where(girth_odd, last, first)


def pack(velocity, pressure, energy, rate):
    _, cells_s, cells_g, cells_r = velocity.shape
    stream = pltpu.VMEM((6, 2, cells_g, cells_r), jnp.float32)
    girth = pltpu.VMEM((6, cells_s, 2, cells_r), jnp.float32)
    vmem = pl.BlockSpec(memory_space=pltpu.VMEM)
    return pl.pallas_call(
        pack_kernel,
        out_shape=(stream, stream, girth, girth),
        in_specs=[vmem] * 4,
        out_specs=[vmem] * 4,
        name="pack_halos",
    )(*(in_hbm(x) for x in (velocity, pressure, energy, rate)))


def network(rows):
    steps = (rows - 1).bit_length()
    return [(low, 1 << min(2, steps - low)) for low in range(0, steps, 2)]


def reach(rows):
    return max((digits - 1) << low for low, digits in network(rows))


def split(values, size):
    if size & (size - 1) == 0:
        return values >> (size.bit_length() - 1), values & (size - 1)
    return values // size, values % size


def prepare_kernel(
    cells_s,
    cells_g,
    cells_r,
    owner_ref,
    ids_hbm,
    frac_hbm,
    table_hbm,
    q_ref,
    fr_ref,
    xs_ref,
    xg_ref,
    moves_ref,
    chosen_ref,
    count_ref,
    ids_ref,
    frac_ref,
    table_ref,
    turned,
    picked,
    keys,
    frs,
    xss,
    xgs,
    order,
    arrived,
):
    copies = [pltpu.make_async_copy(ids_hbm, ids_ref, arrived.at[0])]
    for d in range(3):
        copies.append(pltpu.make_async_copy(frac_hbm.at[d], frac_ref.at[d], arrived.at[1 + d]))
    copies.append(pltpu.make_async_copy(table_hbm, table_ref, arrived.at[4]))
    for copy in copies:
        copy.start()
    stream_first = lax.axis_index("stream") * cells_s
    me = lax.axis_index("girth")
    sectors = owner_ref.shape[0]
    azimuths = ids_ref.shape[1]
    width = azimuths // sectors
    rows = fr_ref.shape[0]
    pad = moves_ref.shape[0] - rows
    passes = network(rows)
    valid = 1 << SHIFT - 1

    def listed(number, count):
        order[jnp.minimum(count, rows // width)] = number
        return count + (owner_ref[number] == me).astype(jnp.int32)

    owned = lax.fori_loop(0, sectors, listed, jnp.int32(0), unroll=8)

    for d in range(4):
        picked[d] = jnp.full(picked.shape[1:], -1.0 if d == 0 else 0.0, jnp.float32)
    chosen_ref[...] = jnp.zeros_like(chosen_ref)
    beyond = pl.ds(rows, pad)
    for slot in range(2):
        keys[slot, beyond, :] = jnp.zeros((pad, LANES), jnp.int32)
    moves_ref[0:pad, :] = jnp.zeros((pad, LANES), jnp.int32)
    for d in range(4):
        copies[d].wait()
        for at in range(0, azimuths, LANES):
            cols = pl.ds(at, LANES)
            plane = ids_ref[:, cols].astype(jnp.float32) if d == 0 else frac_ref[d - 1, :, cols]
            turned[d, cols, :] = plane.T
    copies[4].wait()

    def sector(place, carry):
        source = pl.ds(pl.multiple_of(order[place] * width, width), width)
        target = pl.ds(pl.multiple_of(place * width, width), width)
        chosen_ref[target, :] = table_ref[source, :]
        for d in range(4):
            picked[d, target, :] = turned[d, source, :]
        return carry

    lax.fori_loop(0, owned, sector, jnp.int32(0))

    held = pl.ds(0, rows)
    ids = picked[0].astype(jnp.int32)
    stream_cell, rest = split(jnp.maximum(ids, 0), cells_g * cells_r)
    girth_cell, radial_cell = split(rest, cells_r)
    xs = (stream_cell - stream_first).astype(jnp.float32) + picked[1]
    kept = (ids >= 0) & (xs > -1.0) & (xs < float(cells_s))
    xss[0, held, :] = xs
    xgs[0, held, :] = girth_cell.astype(jnp.float32) + picked[2]
    frs[0, held, :] = picked[3]
    earlier = lax.broadcasted_iota(jnp.int32, (rows, rows), 0) > lax.broadcasted_iota(
        jnp.int32, (rows, rows), 1
    )
    earlier = earlier.astype(jnp.float32).astype(jnp.bfloat16)
    skipped = jnp.where(kept, 0.0, 1.0)
    before = jnp.dot(
        earlier, skipped.astype(jnp.bfloat16), preferred_element_type=jnp.float32
    ).astype(jnp.int32)
    counts = rows - jnp.sum(skipped, axis=0, keepdims=True).astype(jnp.int32)
    count_ref[0] = jnp.max(counts)
    moves_ref[pad : pad + rows, :] = jnp.where(kept, valid, 0)
    keys[0, held, :] = (radial_cell << SHIFT) + jnp.where(kept, before, 0)
    for number, (low, digits) in enumerate(passes):
        a, b = number % 2, 1 - number % 2
        mask = digits - 1 << low
        last = number == len(passes) - 1
        for at in range(0, rows, CHUNK):
            here, target = pl.ds(at, CHUNK), pl.ds(pad + at, CHUNK)
            there = [pl.ds(at + (k << low), CHUNK) for k in range(1, digits)]
            key = keys[a, here, :]
            arriving = [keys[a, t, :] for t in there]
            moved = [(arriving[k] & mask) == (k + 1 << low) for k in range(digits - 1)]
            key = jnp.where((key & mask) != 0, key & -(1 << SHIFT), key)
            came = moves_ref[target, :]
            out = [r[a, here, :] for r in (frs, xss, xgs)]
            for k in range(digits - 1):
                key = jnp.where(moved[k], arriving[k], key)
                came = came | jnp.where(moved[k], k + 1 << low, 0)
                out = [
                    jnp.where(moved[k], r[a, there[k], :], o) for r, o in zip((frs, xss, xgs), out)
                ]
            moves_ref[target, :] = came
            if last:
                q_ref[here, :] = key >> SHIFT
                fr_ref[here, :] = out[0]
                xs_ref[here, :] = out[1]
                xg_ref[here, :] = out[2]
            else:
                keys[b, here, :] = key
                frs[b, here, :] = out[0]
                xss[b, here, :] = out[1]
                xgs[b, here, :] = out[2]


def prepare(owners, corner_ids, fractions, table, cells, girth_count):
    cells_s, cells_g, cells_r = cells
    radii, azimuths = corner_ids.shape
    sectors = owners.shape[0]
    rows = 3 * sectors // girth_count * (azimuths // sectors)
    pad = reach(rows)
    shape = jax.ShapeDtypeStruct
    lists = (rows, radii)
    vmem = pl.BlockSpec(memory_space=pltpu.VMEM)
    smem = pl.BlockSpec(memory_space=pltpu.SMEM)
    hbm = pl.BlockSpec(memory_space=pltpu.HBM)
    return pl.pallas_call(
        functools.partial(prepare_kernel, cells_s, cells_g, cells_r),
        out_shape=(
            shape(lists, jnp.int32),
            shape(lists, jnp.float32),
            shape(lists, jnp.float32),
            shape(lists, jnp.float32),
            shape((pad + rows, radii), jnp.int32),
            shape((rows, 2 * NH), jnp.float32),
            shape((1,), jnp.int32),
        ),
        in_specs=[smem, hbm, hbm, hbm],
        out_specs=[vmem] * 6 + [smem],
        scratch_shapes=[
            pltpu.VMEM(corner_ids.shape, jnp.int32),
            pltpu.VMEM(fractions.shape, jnp.float32),
            pltpu.VMEM(table.shape, jnp.float32),
            pltpu.VMEM((4, azimuths, radii), jnp.float32),
            pltpu.VMEM((4, rows, radii), jnp.float32),
            pltpu.VMEM((2, rows + pad, radii), jnp.int32),
        ]
        + [pltpu.VMEM((2, rows + pad, radii), jnp.float32)] * 3
        + [pltpu.SMEM((rows // (azimuths // sectors) + 1,), jnp.int32)]
        + [pltpu.SemaphoreType.DMA((5,))],
        compiler_params=pltpu.CompilerParams(vmem_limit_bytes=VMEM_LIMIT),
        cost_estimate=pl.CostEstimate(
            flops=20 * radii * azimuths, bytes_accessed=44 * radii * azimuths, transcendentals=0
        ),
        name="prepare_points",
    )(*(in_hbm(x) for x in (owners, corner_ids, fractions, table)))


def radial(values, amount, fill):
    extent = values.shape[-1]
    rolled = pltpu.roll(values, (-amount) % extent, values.ndim - 1)
    position = lax.broadcasted_iota(jnp.int32, values.shape, values.ndim - 1) + amount
    return jnp.where((position >= 0) & (position < extent), rolled, fill)


def advance(own, before, after, left, right, ext_ref, visc_ref):
    cells_s, cells_g, _ = own[0].shape
    mid = ROWS

    def along_s(stack, amount):
        return stack[2 + amount : 2 + amount + cells_s]

    def along_g(ref, amount):
        return ref[:, mid + amount : mid + amount + cells_g, :]

    def viscosity(energy, rate):
        return base_viscosity + energy / (rate + wall_rate)

    stacks = [jnp.concatenate([before[f], own[f], after[f]], axis=0) for f in range(6)]
    for f in range(6):
        ext_ref[f, :, mid - 2 : mid, :] = left[f]
        ext_ref[f, :, mid : mid + cells_g, :] = own[f]
        ext_ref[f, :, mid + cells_g : mid + cells_g + 2, :] = right[f]
    middle = viscosity(own[4], own[5])
    visc_stack = viscosity(stacks[4], stacks[5])
    visc_ref[:, mid - 2 : mid, :] = viscosity(left[4], left[5])
    visc_ref[:, mid : mid + cells_g, :] = middle
    visc_ref[:, mid + cells_g : mid + cells_g + 2, :] = viscosity(right[4], right[5])
    faces = [
        (
            0.5 * (middle + along_s(visc_stack, 1)),
            0.5 * (middle + along_s(visc_stack, -1)),
        ),
        (
            0.5 * (middle + along_g(visc_ref, 1)),
            0.5 * (middle + along_g(visc_ref, -1)),
        ),
        (
            0.5 * (middle + radial(middle, 1, base_viscosity)),
            0.5 * (middle + radial(middle, -1, base_viscosity)),
        ),
    ]

    def neighbour(f, direction, amount):
        if direction == 0:
            return along_s(stacks[f], amount)
        if direction == 1:
            return along_g(ext_ref.at[f], amount)
        return radial(own[f], amount, 0.0)

    def terms(f, direction):
        up, down = neighbour(f, direction, 1), neighbour(f, direction, -1)
        far = neighbour(f, direction, 2) - neighbour(f, direction, -2)
        gradient = (8.0 * (up - down) - far) * (1.0 / 12.0)
        above, below = faces[direction]
        return gradient, above * (up - own[f]) - below * (own[f] - down)

    strain = None
    updated = []
    for f in range(3):
        change = -terms(3, f)[0]
        for direction in range(3):
            gradient, spread = terms(f, direction)
            strain = gradient * gradient if strain is None else strain + gradient * gradient
            change = change - own[direction] * gradient + spread
        updated.append(own[f] + time_step * change)
    energy = own[4] / (own[5] + wall_rate) * strain - beta_star * own[4] * own[5]
    rate = alpha_rate * strain - beta_rate * own[5] * own[5]
    for direction in range(3):
        gradient, spread = terms(4, direction)
        energy = energy - own[direction] * gradient + spread
        gradient, spread = terms(5, direction)
        rate = rate - own[direction] * gradient + spread
    return updated, own[4] + time_step * energy, own[5] + time_step * rate


def girth_sums(parts):
    row = lax.broadcasted_iota(jnp.int32, parts[0].shape, 0)

    def swapped(values, distance):
        up = pltpu.roll(values, distance, 0)
        if 2 * distance == ROWS:
            return up
        return jnp.where((row & distance) != 0, up, pltpu.roll(values, ROWS - distance, 0))

    distance = ROWS // 2
    while distance > 0:
        low = (row & distance) == 0
        parts = [
            jnp.where(low, x, y) + swapped(jnp.where(low, y, x), distance)
            for x, y in zip(parts[:distance], parts[distance:])
        ]
        distance //= 2
    return parts[0]


def section_kernel(
    count_ref,
    vel_ref,
    p_ref,
    k_ref,
    w_ref,
    stream_a,
    stream_b,
    girth_a,
    girth_b,
    q_ref,
    fr_ref,
    xs_ref,
    xg_ref,
    moves_ref,
    chosen_ref,
    new_vel_hbm,
    new_k_hbm,
    new_w_hbm,
    harm_ref,
    new_vel_ref,
    new_k_ref,
    new_w_ref,
    ext_ref,
    visc_ref,
    field_ref,
    gather_ref,
    value_ref,
    disk_ref,
    stored,
):
    cells_s, cells_g, cells_r = p_ref.shape
    rows = fr_ref.shape[0]
    pad = moves_ref.shape[0] - rows
    passes = network(rows)
    valid = 1 << SHIFT - 1
    stream_odd = lax.axis_index("stream") % 2 == 1
    girth_odd = lax.axis_index("girth") % 2 == 1

    own = [vel_ref[0], vel_ref[1], vel_ref[2], p_ref[...], k_ref[...], w_ref[...]]
    six = range(6)
    updated, energy, rate = advance(
        own,
        [jnp.where(stream_odd, stream_a[f], stream_b[f]) for f in six],
        [jnp.where(stream_odd, stream_b[f], stream_a[f]) for f in six],
        [jnp.where(girth_odd, girth_a[f], girth_b[f]) for f in six],
        [jnp.where(girth_odd, girth_b[f], girth_a[f]) for f in six],
        ext_ref,
        visc_ref,
    )
    new_k_ref[...] = energy
    new_w_ref[...] = rate

    def halved(values):
        high = values.astype(jnp.bfloat16)
        return high, (values - high.astype(jnp.float32)).astype(jnp.bfloat16)

    def rounded(values):
        return values.astype(jnp.bfloat16).astype(jnp.float32)

    halves = cells_r // LANES
    for c in range(3):
        new_vel_ref[c] = updated[c]
        slope = radial(updated[c], 1, 0.0) - updated[c]
        for kind, values in enumerate((updated[c], slope)):
            if c < PRODUCTS:
                high = rounded(values)
                field_ref[c, :, 2 * kind] = high
                field_ref[c, :, 2 * kind + 1] = rounded(values - high)
            else:
                for h in range(halves):
                    lanes = slice(h * LANES, (h + 1) * LANES)
                    gather_ref[c - PRODUCTS, :, kind, h] = values[:, :, lanes]
    results = ((new_vel_ref, new_vel_hbm), (new_k_ref, new_k_hbm), (new_w_ref, new_w_hbm))
    copies = [
        pltpu.make_async_copy(source, target, stored.at[i])
        for i, (source, target) in enumerate(results)
    ]
    for copy in copies:
        copy.start()

    kinds = 4
    table = field_ref[...].reshape(PRODUCTS * cells_s * kinds * cells_g, cells_r)
    table = table.astype(jnp.bfloat16)
    pair = 2 * LANES
    girth_row = lax.broadcasted_iota(jnp.int32, (cells_g, pair), 0).astype(jnp.float32)
    radial_row = lax.broadcasted_iota(jnp.int32, (cells_r, pair), 0)

    def two(values, j):
        return jnp.concatenate([values[j : j + 1], values[j + 1 : j + 2]], axis=1)

    def spread(values, j):
        return jnp.broadcast_to(values[j : j + 1], (cells_g, LANES))

    def pick(c, s, kind, index, half_of):
        out = None
        for h in range(halves):
            got = jnp.take_along_axis(
                gather_ref[c - PRODUCTS, s, kind, h], index, axis=1, mode="promise_in_bounds"
            )
            out = got if out is None else jnp.where(half_of[h], got, out)
        return out

    def eight(group, carry):
        at = pl.multiple_of(group * ROWS, ROWS)
        here = pl.ds(at, ROWS)
        q8, fr8, xg8, xs8 = (r[here, :] for r in (q_ref, fr_ref, xg_ref, xs_ref))
        hs8 = [jnp.maximum(1.0 - jnp.abs(xs8 - float(s)), 0.0) for s in range(cells_s)]
        index8 = q8 & (LANES - 1)
        sums = [[], [], []]
        for j in range(0, ROWS, 2):
            hot = jnp.where(radial_row == two(q8, j), 1.0, 0.0).astype(jnp.bfloat16)
            got = jnp.dot(table, hot, preferred_element_type=jnp.float32)
            got = got.reshape(PRODUCTS, cells_s, kinds, cells_g, pair)
            fr = two(fr8, j)
            hg = jnp.maximum(1.0 - jnp.abs(two(xg8, j) - girth_row), 0.0)
            hs = [two(hs8[s], j) for s in range(cells_s)]
            for c in range(PRODUCTS):
                total = None
                for s in range(cells_s):
                    value = got[c, s, 0] + got[c, s, 1] + fr * (got[c, s, 2] + got[c, s, 3])
                    value = hs[s] * value
                    total = value if total is None else total + value
                total = hg * total
                sums[c] += [total[:, :LANES], total[:, LANES:]]
            for i in (j, j + 1):
                index, q = spread(index8, i), spread(q8, i)
                half_of = [q >= h * LANES for h in range(halves)]
                own_hg = hg[:, (i - j) * LANES : (i - j + 1) * LANES]
                for c in range(PRODUCTS, 3):
                    total = None
                    for s in range(cells_s):
                        value = pick(c, s, 0, index, half_of)
                        value = value + fr8[i : i + 1] * pick(c, s, 1, index, half_of)
                        value = hs8[s][i : i + 1] * value
                        total = value if total is None else total + value
                    sums[c].append(own_hg * total)
        for c in range(3):
            value_ref[0, c, pl.ds(pad + at, ROWS), :] = girth_sums(sums[c])
        return carry

    lax.fori_loop(0, (count_ref[0] + ROWS - 1) // ROWS, eight, jnp.int32(0))

    for number, (low, digits) in enumerate(reversed(passes)):
        a, b = number % 2, 1 - number % 2
        mask = digits - 1 << low
        last = number == len(passes) - 1
        for at in range(0, rows, CHUNK):
            here = pl.ds(pad + at, CHUNK)
            there = [pl.ds(pad + at - (k << low), CHUNK) for k in range(1, digits)]
            moved = [(moves_ref[there[k], :] & mask) == (k + 1 << low) for k in range(digits - 1)]
            if last:
                kept = (moves_ref[here, :] & valid) != 0
            for c in range(3):
                value = value_ref[a, c, here, :]
                for k in range(digits - 1):
                    value = jnp.where(moved[k], value_ref[a, c, there[k], :], value)
                if last:
                    disk_ref[c, pl.ds(at, CHUNK), :] = jnp.where(kept, value, 0.0)
                else:
                    value_ref[b, c, here, :] = value

    turned = jnp.concatenate([disk_ref[c].T for c in range(3)], axis=0)
    high, low = halved(turned)
    wave_high, wave_low = halved(chosen_ref[...])
    waves = jnp.dot(high, wave_high, preferred_element_type=jnp.float32)
    waves += jnp.dot(high, wave_low, preferred_element_type=jnp.float32)
    waves += jnp.dot(low, wave_high, preferred_element_type=jnp.float32)
    radii = harm_ref.shape[0]
    for c in range(3):
        harm_ref[:, c * 2 * NH : (c + 1) * 2 * NH] = waves[c * radii : (c + 1) * radii]
    for copy in copies:
        copy.wait()


def section(velocity, pressure, energy, rate, halos, points):
    _, cells_s, cells_g, cells_r = velocity.shape
    *lists, moves, chosen, counts = points
    rows, radii = lists[0].shape
    shape = functools.partial(jax.ShapeDtypeStruct, dtype=jnp.float32)
    scratch = lambda *dims: pltpu.VMEM(dims, jnp.float32)
    vmem = pl.BlockSpec(memory_space=pltpu.VMEM)
    smem = pl.BlockSpec(memory_space=pltpu.SMEM)
    return pl.pallas_call(
        section_kernel,
        out_shape=(
            shape(velocity.shape),
            shape(energy.shape),
            shape(rate.shape),
            shape((radii, 6 * NH)),
        ),
        in_specs=[smem] + [vmem] * 14,
        out_specs=[pl.BlockSpec(memory_space=pl.ANY)] * 3 + [vmem],
        scratch_shapes=[
            scratch(*velocity.shape),
            scratch(*energy.shape),
            scratch(*rate.shape),
            scratch(6, cells_s, 3 * ROWS, cells_r),
            scratch(cells_s, 3 * ROWS, cells_r),
            scratch(PRODUCTS, cells_s, 4, cells_g, cells_r),
            scratch(3 - PRODUCTS, cells_s, 2, cells_r // LANES, cells_g, LANES),
            scratch(2, 3, moves.shape[0], radii),
            scratch(3, rows, radii),
            pltpu.SemaphoreType.DMA((3,)),
        ],
        compiler_params=pltpu.CompilerParams(vmem_limit_bytes=VMEM_LIMIT),
        name="section_and_disk",
    )(counts, velocity, pressure, energy, rate, *halos, *lists, moves, chosen)


def fourier_table(azimuths, modes):
    phase = np.arange(azimuths)[:, None] * np.arange(modes)[None, :] % azimuths
    angles = phase * (2.0 * math.pi / azimuths)
    table = np.concatenate([np.cos(angles), -np.sin(angles)], axis=1) / math.sqrt(azimuths)
    return jnp.asarray(table.astype(np.float32))


def body(velocity, pressure, kinetic_energy, dissipation_rate, corner_ids, fractions, sector_owner):
    _, cells_s, cells_g, cells_r = velocity.shape
    radii, azimuths = corner_ids.shape
    stream_count, girth_count = lax.axis_size("stream"), lax.axis_size("girth")
    devices = stream_count * girth_count

    def swap(values, axis, count, start):
        pairs = []
        for i in range(start, count - 1, 2):
            pairs += [(i, i + 1), (i + 1, i)]
        return lax.ppermute(values, axis, pairs)

    slabs = pack(velocity, pressure, kinetic_energy, dissipation_rate)
    girth_halos = (
        swap(slabs[2], "girth", girth_count, 0),
        swap(slabs[3], "girth", girth_count, 1),
    )
    stream_halos = (
        swap(slabs[0], "stream", stream_count, 0),
        swap(slabs[1], "stream", stream_count, 1),
    )
    halos = stream_halos + girth_halos
    points = prepare(
        sector_owner[:, 0],
        corner_ids,
        fractions,
        fourier_table(azimuths, NH),
        (cells_s, cells_g, cells_r),
        girth_count,
    )
    new_velocity, new_energy, new_rate, partial = section(
        velocity, pressure, kinetic_energy, dissipation_rate, halos, points
    )
    shares = lax.all_to_all(
        partial.reshape(devices, radii // devices, 6 * NH),
        ("stream", "girth"),
        split_axis=0,
        concat_axis=0,
        tiled=True,
    )
    return new_velocity, new_energy, new_rate, jnp.sum(shares, axis=0)


def solution(mesh):
    return jax.shard_map(
        body,
        mesh=mesh,
        in_specs=(
            P(None, "stream", "girth", None),
            P("stream", "girth", None),
            P("stream", "girth", None),
            P("stream", "girth", None),
            P(),
            P(),
            P(),
        ),
        out_specs=(
            P(None, "stream", "girth", None),
            P("stream", "girth", None),
            P("stream", "girth", None),
            P(("stream", "girth"), None),
        ),
        check_vma=False,
    )
```

```python
import functools
import math

import jax
import jax.numpy as jnp
import numpy as np
from jax import lax
from jax.experimental import pallas as pl
from jax.experimental.pallas import tpu as pltpu
from jax.sharding import PartitionSpec as P

NH = 128

base_viscosity = 0.05
time_step = 0.2
beta_star = 0.09
beta_rate = 0.075
alpha_rate = 0.52
wall_rate = 1.0

LANES = 128
ROWS = 8
SHIFT = 10
CHUNK = 32
PRODUCTS = 2
VMEM_LIMIT = 48 * 1024 * 1024


def in_hbm(values):
    return pltpu.with_memory_space_constraint(values, pltpu.HBM)


def pack_kernel(vel_ref, p_ref, k_ref, w_ref, *slabs):
    cells_s, cells_g, _ = p_ref.shape
    stream_odd = lax.axis_index("stream") % 2 == 1
    girth_odd = lax.axis_index("girth") % 2 == 1
    for f in range(6):
        own = vel_ref.at[f] if f < 3 else (p_ref, k_ref, w_ref)[f - 3]
        first, last = own[0:2], own[cells_s - 2 : cells_s]
        slabs[0][f] = jnp.where(stream_odd, first, last)
        slabs[1][f] = jnp.where(stream_odd, last, first)
        first, last = own[:, 0:2, :], own[:, cells_g - 2 : cells_g, :]
        slabs[2][f] = jnp.where(girth_odd, first, last)
        slabs[3][f] = jnp.where(girth_odd, last, first)


def pack(velocity, pressure, energy, rate):
    _, cells_s, cells_g, cells_r = velocity.shape
    stream = pltpu.VMEM((6, 2, cells_g, cells_r), jnp.float32)
    girth = pltpu.VMEM((6, cells_s, 2, cells_r), jnp.float32)
    vmem = pl.BlockSpec(memory_space=pltpu.VMEM)
    return pl.pallas_call(
        pack_kernel,
        out_shape=(stream, stream, girth, girth),
        in_specs=[vmem] * 4,
        out_specs=[vmem] * 4,
        name="pack_halos",
    )(*(in_hbm(x) for x in (velocity, pressure, energy, rate)))


def network(rows):
    steps = (rows - 1).bit_length()
    return [(low, 1 << min(2, steps - low)) for low in range(0, steps, 2)]


def reach(rows):
    return max((digits - 1) << low for low, digits in network(rows))


def split(values, size):
    if size & (size - 1) == 0:
        return values >> (size.bit_length() - 1), values & (size - 1)
    return values // size, values % size


def prepare_kernel(
    cells_s,
    cells_g,
    cells_r,
    owner_ref,
    ids_hbm,
    frac_hbm,
    table_hbm,
    q_ref,
    fr_ref,
    xs_ref,
    xg_ref,
    moves_ref,
    chosen_ref,
    count_ref,
    ids_ref,
    frac_ref,
    table_ref,
    turned,
    picked,
    keys,
    frs,
    xss,
    xgs,
    order,
    arrived,
):
    copies = [pltpu.make_async_copy(ids_hbm, ids_ref, arrived.at[0])]
    for d in range(3):
        copies.append(pltpu.make_async_copy(frac_hbm.at[d], frac_ref.at[d], arrived.at[1 + d]))
    copies.append(pltpu.make_async_copy(table_hbm, table_ref, arrived.at[4]))
    for copy in copies:
        copy.start()
    stream_first = lax.axis_index("stream") * cells_s
    me = lax.axis_index("girth")
    sectors = owner_ref.shape[0]
    azimuths = ids_ref.shape[1]
    width = azimuths // sectors
    rows = fr_ref.shape[0]
    pad = moves_ref.shape[0] - rows
    passes = network(rows)
    valid = 1 << SHIFT - 1

    def listed(number, count):
        order[jnp.minimum(count, rows // width)] = number
        return count + (owner_ref[number] == me).astype(jnp.int32)

    owned = lax.fori_loop(0, sectors, listed, jnp.int32(0), unroll=8)

    for d in range(4):
        picked[d] = jnp.full(picked.shape[1:], -1.0 if d == 0 else 0.0, jnp.float32)
    chosen_ref[...] = jnp.zeros_like(chosen_ref)
    beyond = pl.ds(rows, pad)
    for slot in range(2):
        keys[slot, beyond, :] = jnp.zeros((pad, LANES), jnp.int32)
    moves_ref[0:pad, :] = jnp.zeros((pad, LANES), jnp.int32)
    for d in range(4):
        copies[d].wait()
        for at in range(0, azimuths, LANES):
            cols = pl.ds(at, LANES)
            plane = ids_ref[:, cols].astype(jnp.float32) if d == 0 else frac_ref[d - 1, :, cols]
            turned[d, cols, :] = plane.T
    copies[4].wait()

    def sector(place, carry):
        source = pl.ds(pl.multiple_of(order[place] * width, width), width)
        target = pl.ds(pl.multiple_of(place * width, width), width)
        chosen_ref[target, :] = table_ref[source, :]
        for d in range(4):
            picked[d, target, :] = turned[d, source, :]
        return carry

    lax.fori_loop(0, owned, sector, jnp.int32(0))

    held = pl.ds(0, rows)
    ids = picked[0].astype(jnp.int32)
    stream_cell, rest = split(jnp.maximum(ids, 0), cells_g * cells_r)
    girth_cell, radial_cell = split(rest, cells_r)
    xs = (stream_cell - stream_first).astype(jnp.float32) + picked[1]
    kept = (ids >= 0) & (xs > -1.0) & (xs < float(cells_s))
    xss[0, held, :] = xs
    xgs[0, held, :] = girth_cell.astype(jnp.float32) + picked[2]
    frs[0, held, :] = picked[3]
    earlier = lax.broadcasted_iota(jnp.int32, (rows, rows), 0) > lax.broadcasted_iota(
        jnp.int32, (rows, rows), 1
    )
    earlier = earlier.astype(jnp.float32).astype(jnp.bfloat16)
    skipped = jnp.where(kept, 0.0, 1.0)
    before = jnp.dot(
        earlier, skipped.astype(jnp.bfloat16), preferred_element_type=jnp.float32
    ).astype(jnp.int32)
    counts = rows - jnp.sum(skipped, axis=0, keepdims=True).astype(jnp.int32)
    count_ref[0] = jnp.max(counts)
    moves_ref[pad : pad + rows, :] = jnp.where(kept, valid, 0)
    keys[0, held, :] = (radial_cell << SHIFT) + jnp.where(kept, before, 0)
    for number, (low, digits) in enumerate(passes):
        a, b = number % 2, 1 - number % 2
        mask = digits - 1 << low
        last = number == len(passes) - 1
        for at in range(0, rows, CHUNK):
            here, target = pl.ds(at, CHUNK), pl.ds(pad + at, CHUNK)
            there = [pl.ds(at + (k << low), CHUNK) for k in range(1, digits)]
            key = keys[a, here, :]
            arriving = [keys[a, t, :] for t in there]
            moved = [(arriving[k] & mask) == (k + 1 << low) for k in range(digits - 1)]
            key = jnp.where((key & mask) != 0, key & -(1 << SHIFT), key)
            came = moves_ref[target, :]
            out = [r[a, here, :] for r in (frs, xss, xgs)]
            for k in range(digits - 1):
                key = jnp.where(moved[k], arriving[k], key)
                came = came | jnp.where(moved[k], k + 1 << low, 0)
                out = [
                    jnp.where(moved[k], r[a, there[k], :], o) for r, o in zip((frs, xss, xgs), out)
                ]
            moves_ref[target, :] = came
            if last:
                q_ref[here, :] = key >> SHIFT
                fr_ref[here, :] = out[0]
                xs_ref[here, :] = out[1]
                xg_ref[here, :] = out[2]
            else:
                keys[b, here, :] = key
                frs[b, here, :] = out[0]
                xss[b, here, :] = out[1]
                xgs[b, here, :] = out[2]


def prepare(owners, corner_ids, fractions, table, cells, girth_count):
    cells_s, cells_g, cells_r = cells
    radii, azimuths = corner_ids.shape
    sectors = owners.shape[0]
    rows = 3 * sectors // girth_count * (azimuths // sectors)
    pad = reach(rows)
    shape = jax.ShapeDtypeStruct
    lists = (rows, radii)
    vmem = pl.BlockSpec(memory_space=pltpu.VMEM)
    smem = pl.BlockSpec(memory_space=pltpu.SMEM)
    hbm = pl.BlockSpec(memory_space=pltpu.HBM)
    return pl.pallas_call(
        functools.partial(prepare_kernel, cells_s, cells_g, cells_r),
        out_shape=(
            shape(lists, jnp.int32),
            shape(lists, jnp.float32),
            shape(lists, jnp.float32),
            shape(lists, jnp.float32),
            shape((pad + rows, radii), jnp.int32),
            shape((rows, 2 * NH), jnp.float32),
            shape((1,), jnp.int32),
        ),
        in_specs=[smem, hbm, hbm, hbm],
        out_specs=[vmem] * 6 + [smem],
        scratch_shapes=[
            pltpu.VMEM(corner_ids.shape, jnp.int32),
            pltpu.VMEM(fractions.shape, jnp.float32),
            pltpu.VMEM(table.shape, jnp.float32),
            pltpu.VMEM((4, azimuths, radii), jnp.float32),
            pltpu.VMEM((4, rows, radii), jnp.float32),
            pltpu.VMEM((2, rows + pad, radii), jnp.int32),
        ]
        + [pltpu.VMEM((2, rows + pad, radii), jnp.float32)] * 3
        + [pltpu.SMEM((rows // (azimuths // sectors) + 1,), jnp.int32)]
        + [pltpu.SemaphoreType.DMA((5,))],
        compiler_params=pltpu.CompilerParams(vmem_limit_bytes=VMEM_LIMIT),
        cost_estimate=pl.CostEstimate(
            flops=20 * radii * azimuths, bytes_accessed=44 * radii * azimuths, transcendentals=0
        ),
        name="prepare_points",
    )(*(in_hbm(x) for x in (owners, corner_ids, fractions, table)))


def radial(values, amount, fill):
    extent = values.shape[-1]
    rolled = pltpu.roll(values, (-amount) % extent, values.ndim - 1)
    position = lax.broadcasted_iota(jnp.int32, values.shape, values.ndim - 1) + amount
    return jnp.where((position >= 0) & (position < extent), rolled, fill)


def advance(own, before, after, left, right, ext_ref, visc_ref):
    cells_s, cells_g, _ = own[0].shape
    mid = ROWS

    def along_s(stack, amount):
        return stack[2 + amount : 2 + amount + cells_s]

    def along_g(ref, amount):
        return ref[:, mid + amount : mid + amount + cells_g, :]

    def viscosity(energy, rate):
        return base_viscosity + energy / (rate + wall_rate)

    stacks = [jnp.concatenate([before[f], own[f], after[f]], axis=0) for f in range(6)]
    for f in range(6):
        ext_ref[f, :, mid - 2 : mid, :] = left[f]
        ext_ref[f, :, mid : mid + cells_g, :] = own[f]
        ext_ref[f, :, mid + cells_g : mid + cells_g + 2, :] = right[f]
    middle = viscosity(own[4], own[5])
    visc_stack = viscosity(stacks[4], stacks[5])
    visc_ref[:, mid - 2 : mid, :] = viscosity(left[4], left[5])
    visc_ref[:, mid : mid + cells_g, :] = middle
    visc_ref[:, mid + cells_g : mid + cells_g + 2, :] = viscosity(right[4], right[5])
    faces = [
        (
            0.5 * (middle + along_s(visc_stack, 1)),
            0.5 * (middle + along_s(visc_stack, -1)),
        ),
        (
            0.5 * (middle + along_g(visc_ref, 1)),
            0.5 * (middle + along_g(visc_ref, -1)),
        ),
        (
            0.5 * (middle + radial(middle, 1, base_viscosity)),
            0.5 * (middle + radial(middle, -1, base_viscosity)),
        ),
    ]

    def neighbour(f, direction, amount):
        if direction == 0:
            return along_s(stacks[f], amount)
        if direction == 1:
            return along_g(ext_ref.at[f], amount)
        return radial(own[f], amount, 0.0)

    def terms(f, direction):
        up, down = neighbour(f, direction, 1), neighbour(f, direction, -1)
        far = neighbour(f, direction, 2) - neighbour(f, direction, -2)
        gradient = (8.0 * (up - down) - far) * (1.0 / 12.0)
        above, below = faces[direction]
        return gradient, above * (up - own[f]) - below * (own[f] - down)

    strain = None
    updated = []
    for f in range(3):
        change = -terms(3, f)[0]
        for direction in range(3):
            gradient, spread = terms(f, direction)
            strain = gradient * gradient if strain is None else strain + gradient * gradient
            change = change - own[direction] * gradient + spread
        updated.append(own[f] + time_step * change)
    energy = own[4] / (own[5] + wall_rate) * strain - beta_star * own[4] * own[5]
    rate = alpha_rate * strain - beta_rate * own[5] * own[5]
    for direction in range(3):
        gradient, spread = terms(4, direction)
        energy = energy - own[direction] * gradient + spread
        gradient, spread = terms(5, direction)
        rate = rate - own[direction] * gradient + spread
    return updated, own[4] + time_step * energy, own[5] + time_step * rate


def girth_sums(parts):
    row = lax.broadcasted_iota(jnp.int32, parts[0].shape, 0)

    def swapped(values, distance):
        up = pltpu.roll(values, distance, 0)
        if 2 * distance == ROWS:
            return up
        return jnp.where((row & distance) != 0, up, pltpu.roll(values, ROWS - distance, 0))

    distance = ROWS // 2
    while distance > 0:
        low = (row & distance) == 0
        parts = [
            jnp.where(low, x, y) + swapped(jnp.where(low, y, x), distance)
            for x, y in zip(parts[:distance], parts[distance:])
        ]
        distance //= 2
    return parts[0]


def section_kernel(
    devices,
    count_ref,
    vel_ref,
    p_ref,
    k_ref,
    w_ref,
    stream_a,
    stream_b,
    girth_a,
    girth_b,
    q_ref,
    fr_ref,
    xs_ref,
    xg_ref,
    moves_ref,
    chosen_ref,
    new_vel_hbm,
    new_k_hbm,
    new_w_hbm,
    keep_ref,
    give_ref,
    new_vel_ref,
    new_k_ref,
    new_w_ref,
    ext_ref,
    visc_ref,
    field_ref,
    gather_ref,
    value_ref,
    disk_ref,
    harm_ref,
    stored,
):
    cells_s, cells_g, cells_r = p_ref.shape
    rows = fr_ref.shape[0]
    pad = moves_ref.shape[0] - rows
    passes = network(rows)
    valid = 1 << SHIFT - 1
    stream_odd = lax.axis_index("stream") % 2 == 1
    girth_odd = lax.axis_index("girth") % 2 == 1

    own = [vel_ref[0], vel_ref[1], vel_ref[2], p_ref[...], k_ref[...], w_ref[...]]
    six = range(6)
    updated, energy, rate = advance(
        own,
        [jnp.where(stream_odd, stream_a[f], stream_b[f]) for f in six],
        [jnp.where(stream_odd, stream_b[f], stream_a[f]) for f in six],
        [jnp.where(girth_odd, girth_a[f], girth_b[f]) for f in six],
        [jnp.where(girth_odd, girth_b[f], girth_a[f]) for f in six],
        ext_ref,
        visc_ref,
    )
    new_k_ref[...] = energy
    new_w_ref[...] = rate

    def halved(values):
        high = values.astype(jnp.bfloat16)
        return high, (values - high.astype(jnp.float32)).astype(jnp.bfloat16)

    def rounded(values):
        return values.astype(jnp.bfloat16).astype(jnp.float32)

    halves = cells_r // LANES
    for c in range(3):
        new_vel_ref[c] = updated[c]
        slope = radial(updated[c], 1, 0.0) - updated[c]
        for kind, values in enumerate((updated[c], slope)):
            if c < PRODUCTS:
                high = rounded(values)
                field_ref[c, :, 2 * kind] = high
                field_ref[c, :, 2 * kind + 1] = rounded(values - high)
            else:
                for h in range(halves):
                    lanes = slice(h * LANES, (h + 1) * LANES)
                    gather_ref[c - PRODUCTS, :, kind, h] = values[:, :, lanes]
    results = ((new_vel_ref, new_vel_hbm), (new_k_ref, new_k_hbm), (new_w_ref, new_w_hbm))
    copies = [
        pltpu.make_async_copy(source, target, stored.at[i])
        for i, (source, target) in enumerate(results)
    ]
    for copy in copies:
        copy.start()

    kinds = 4
    table = field_ref[...].reshape(PRODUCTS * cells_s * kinds * cells_g, cells_r)
    table = table.astype(jnp.bfloat16)
    pair = 2 * LANES
    girth_row = lax.broadcasted_iota(jnp.int32, (cells_g, pair), 0).astype(jnp.float32)
    radial_row = lax.broadcasted_iota(jnp.int32, (cells_r, pair), 0)

    def two(values, j):
        return jnp.concatenate([values[j : j + 1], values[j + 1 : j + 2]], axis=1)

    def spread(values, j):
        return jnp.broadcast_to(values[j : j + 1], (cells_g, LANES))

    def pick(c, s, kind, index, half_of):
        out = None
        for h in range(halves):
            got = jnp.take_along_axis(
                gather_ref[c - PRODUCTS, s, kind, h], index, axis=1, mode="promise_in_bounds"
            )
            out = got if out is None else jnp.where(half_of[h], got, out)
        return out

    def eight(group, carry):
        at = pl.multiple_of(group * ROWS, ROWS)
        here = pl.ds(at, ROWS)
        q8, fr8, xg8, xs8 = (r[here, :] for r in (q_ref, fr_ref, xg_ref, xs_ref))
        hs8 = [jnp.maximum(1.0 - jnp.abs(xs8 - float(s)), 0.0) for s in range(cells_s)]
        index8 = q8 & (LANES - 1)
        sums = [[], [], []]
        for j in range(0, ROWS, 2):
            hot = jnp.where(radial_row == two(q8, j), 1.0, 0.0).astype(jnp.bfloat16)
            got = jnp.dot(table, hot, preferred_element_type=jnp.float32)
            got = got.reshape(PRODUCTS, cells_s, kinds, cells_g, pair)
            fr = two(fr8, j)
            hg = jnp.maximum(1.0 - jnp.abs(two(xg8, j) - girth_row), 0.0)
            hs = [two(hs8[s], j) for s in range(cells_s)]
            for c in range(PRODUCTS):
                total = None
                for s in range(cells_s):
                    value = got[c, s, 0] + got[c, s, 1] + fr * (got[c, s, 2] + got[c, s, 3])
                    value = hs[s] * value
                    total = value if total is None else total + value
                total = hg * total
                sums[c] += [total[:, :LANES], total[:, LANES:]]
            for i in (j, j + 1):
                index, q = spread(index8, i), spread(q8, i)
                half_of = [q >= h * LANES for h in range(halves)]
                own_hg = hg[:, (i - j) * LANES : (i - j + 1) * LANES]
                for c in range(PRODUCTS, 3):
                    total = None
                    for s in range(cells_s):
                        value = pick(c, s, 0, index, half_of)
                        value = value + fr8[i : i + 1] * pick(c, s, 1, index, half_of)
                        value = hs8[s][i : i + 1] * value
                        total = value if total is None else total + value
                    sums[c].append(own_hg * total)
        for c in range(3):
            value_ref[0, c, pl.ds(pad + at, ROWS), :] = girth_sums(sums[c])
        return carry

    lax.fori_loop(0, (count_ref[0] + ROWS - 1) // ROWS, eight, jnp.int32(0))

    for number, (low, digits) in enumerate(reversed(passes)):
        a, b = number % 2, 1 - number % 2
        mask = digits - 1 << low
        last = number == len(passes) - 1
        for at in range(0, rows, CHUNK):
            here = pl.ds(pad + at, CHUNK)
            there = [pl.ds(pad + at - (k << low), CHUNK) for k in range(1, digits)]
            moved = [(moves_ref[there[k], :] & mask) == (k + 1 << low) for k in range(digits - 1)]
            if last:
                kept = (moves_ref[here, :] & valid) != 0
            for c in range(3):
                value = value_ref[a, c, here, :]
                for k in range(digits - 1):
                    value = jnp.where(moved[k], value_ref[a, c, there[k], :], value)
                if last:
                    disk_ref[c, pl.ds(at, CHUNK), :] = jnp.where(kept, value, 0.0)
                else:
                    value_ref[b, c, here, :] = value

    turned = jnp.concatenate([disk_ref[c].T for c in range(3)], axis=0)
    high, low = halved(turned)
    wave_high, wave_low = halved(chosen_ref[...])
    waves = jnp.dot(high, wave_high, preferred_element_type=jnp.float32)
    waves += jnp.dot(high, wave_low, preferred_element_type=jnp.float32)
    waves += jnp.dot(low, wave_high, preferred_element_type=jnp.float32)
    radii = harm_ref.shape[0]
    for c in range(3):
        harm_ref[:, c * 2 * NH : (c + 1) * 2 * NH] = waves[c * radii : (c + 1) * radii]
    block = radii // devices
    for place in range(devices // 2):
        even = harm_ref[2 * place * block : (2 * place + 1) * block, :]
        odd = harm_ref[(2 * place + 1) * block : (2 * place + 2) * block, :]
        keep_ref[place * block : (place + 1) * block, :] = jnp.where(girth_odd, odd, even)
        give_ref[place * block : (place + 1) * block, :] = jnp.where(girth_odd, even, odd)
    for copy in copies:
        copy.wait()


def section(velocity, pressure, energy, rate, halos, points, devices):
    _, cells_s, cells_g, cells_r = velocity.shape
    *lists, moves, chosen, counts = points
    rows, radii = lists[0].shape
    shape = functools.partial(jax.ShapeDtypeStruct, dtype=jnp.float32)
    scratch = lambda *dims: pltpu.VMEM(dims, jnp.float32)
    vmem = pl.BlockSpec(memory_space=pltpu.VMEM)
    smem = pl.BlockSpec(memory_space=pltpu.SMEM)
    return pl.pallas_call(
        functools.partial(section_kernel, devices),
        out_shape=(
            shape(velocity.shape),
            shape(energy.shape),
            shape(rate.shape),
            shape((radii // 2, 6 * NH)),
            shape((radii // 2, 6 * NH)),
        ),
        in_specs=[smem] + [vmem] * 14,
        out_specs=[pl.BlockSpec(memory_space=pl.ANY)] * 3 + [vmem] * 2,
        scratch_shapes=[
            scratch(*velocity.shape),
            scratch(*energy.shape),
            scratch(*rate.shape),
            scratch(6, cells_s, 3 * ROWS, cells_r),
            scratch(cells_s, 3 * ROWS, cells_r),
            scratch(PRODUCTS, cells_s, 4, cells_g, cells_r),
            scratch(3 - PRODUCTS, cells_s, 2, cells_r // LANES, cells_g, LANES),
            scratch(2, 3, moves.shape[0], radii),
            scratch(3, rows, radii),
            scratch(radii, 6 * NH),
            pltpu.SemaphoreType.DMA((3,)),
        ],
        compiler_params=pltpu.CompilerParams(vmem_limit_bytes=VMEM_LIMIT),
        name="section_and_disk",
    )(counts, velocity, pressure, energy, rate, *halos, *lists, moves, chosen)


def fourier_table(azimuths, modes):
    phase = np.arange(azimuths)[:, None] * np.arange(modes)[None, :] % azimuths
    angles = phase * (2.0 * math.pi / azimuths)
    table = np.concatenate([np.cos(angles), -np.sin(angles)], axis=1) / math.sqrt(azimuths)
    return jnp.asarray(table.astype(np.float32))


def body(velocity, pressure, kinetic_energy, dissipation_rate, corner_ids, fractions, sector_owner):
    _, cells_s, cells_g, cells_r = velocity.shape
    radii, azimuths = corner_ids.shape
    stream_count, girth_count = lax.axis_size("stream"), lax.axis_size("girth")
    devices = stream_count * girth_count

    def swap(values, axis, count, start):
        pairs = []
        for i in range(start, count - 1, 2):
            pairs += [(i, i + 1), (i + 1, i)]
        return lax.ppermute(values, axis, pairs)

    slabs = pack(velocity, pressure, kinetic_energy, dissipation_rate)
    girth_halos = (
        swap(slabs[2], "girth", girth_count, 0),
        swap(slabs[3], "girth", girth_count, 1),
    )
    stream_halos = (
        swap(slabs[0], "stream", stream_count, 0),
        swap(slabs[1], "stream", stream_count, 1),
    )
    halos = stream_halos + girth_halos
    points = prepare(
        sector_owner[:, 0],
        corner_ids,
        fractions,
        fourier_table(azimuths, NH),
        (cells_s, cells_g, cells_r),
        girth_count,
    )
    new_velocity, new_energy, new_rate, keep, give = section(
        velocity, pressure, kinetic_energy, dissipation_rate, halos, points, devices
    )
    total = keep + swap(give, "girth", girth_count, 0)
    shares = lax.all_to_all(
        total.reshape(devices // 2, radii // devices, 6 * NH),
        ("stream", "girth"),
        split_axis=0,
        concat_axis=0,
        tiled=True,
        axis_index_groups=[list(range(parity, devices, 2)) for parity in (0, 1)],
    )
    return new_velocity, new_energy, new_rate, jnp.sum(shares, axis=0)


def solution(mesh):
    return jax.shard_map(
        body,
        mesh=mesh,
        in_specs=(
            P(None, "stream", "girth", None),
            P("stream", "girth", None),
            P("stream", "girth", None),
            P("stream", "girth", None),
            P(),
            P(),
            P(),
        ),
        out_specs=(
            P(None, "stream", "girth", None),
            P("stream", "girth", None),
            P("stream", "girth", None),
            P(("stream", "girth"), None),
        ),
        check_vma=False,
    )
```

```python
import functools
import math

import jax
import jax.numpy as jnp
import numpy as np
from jax import lax
from jax.experimental import pallas as pl
from jax.experimental.pallas import tpu as pltpu
from jax.sharding import PartitionSpec as P

NH = 128

base_viscosity = 0.05
time_step = 0.2
beta_star = 0.09
beta_rate = 0.075
alpha_rate = 0.52
wall_rate = 1.0

LANES = 128
ROWS = 8
SHIFT = 10
CHUNK = 32
PRODUCTS = 2
VMEM_LIMIT = 48 * 1024 * 1024


def in_hbm(values):
    return pltpu.with_memory_space_constraint(values, pltpu.HBM)


def pack_kernel(vel_ref, p_ref, k_ref, w_ref, *slabs):
    cells_s, cells_g, _ = p_ref.shape
    stream_odd = lax.axis_index("stream") % 2 == 1
    girth_odd = lax.axis_index("girth") % 2 == 1
    for f in range(6):
        own = vel_ref.at[f] if f < 3 else (p_ref, k_ref, w_ref)[f - 3]
        first, last = own[0:2], own[cells_s - 2 : cells_s]
        slabs[0][f] = jnp.where(stream_odd, first, last)
        slabs[1][f] = jnp.where(stream_odd, last, first)
        first, last = own[:, 0:2, :], own[:, cells_g - 2 : cells_g, :]
        slabs[2][f] = jnp.where(girth_odd, first, last)
        slabs[3][f] = jnp.where(girth_odd, last, first)


def pack(velocity, pressure, energy, rate):
    _, cells_s, cells_g, cells_r = velocity.shape
    stream = pltpu.VMEM((6, 2, cells_g, cells_r), jnp.float32)
    girth = pltpu.VMEM((6, cells_s, 2, cells_r), jnp.float32)
    vmem = pl.BlockSpec(memory_space=pltpu.VMEM)
    return pl.pallas_call(
        pack_kernel,
        out_shape=(stream, stream, girth, girth),
        in_specs=[vmem] * 4,
        out_specs=[vmem] * 4,
        name="pack_halos",
    )(*(in_hbm(x) for x in (velocity, pressure, energy, rate)))


def network(rows):
    steps = (rows - 1).bit_length()
    return [(low, 1 << min(2, steps - low)) for low in range(0, steps, 2)]


def reach(rows):
    return max((digits - 1) << low for low, digits in network(rows))


def split(values, size):
    if size & (size - 1) == 0:
        return values >> (size.bit_length() - 1), values & (size - 1)
    return values // size, values % size


def prepare_kernel(
    cells_s,
    cells_g,
    cells_r,
    owner_ref,
    ids_hbm,
    frac_hbm,
    table_hbm,
    q_ref,
    fr_ref,
    xs_ref,
    xg_ref,
    moves_ref,
    chosen_ref,
    count_ref,
    ids_ref,
    frac_ref,
    table_ref,
    turned,
    picked,
    keys,
    frs,
    xss,
    xgs,
    order,
    arrived,
):
    copies = [pltpu.make_async_copy(ids_hbm, ids_ref, arrived.at[0])]
    for d in range(3):
        copies.append(pltpu.make_async_copy(frac_hbm.at[d], frac_ref.at[d], arrived.at[1 + d]))
    copies.append(pltpu.make_async_copy(table_hbm, table_ref, arrived.at[4]))
    for copy in copies:
        copy.start()
    stream_first = lax.axis_index("stream") * cells_s
    me = lax.axis_index("girth")
    sectors = owner_ref.shape[0]
    azimuths = ids_ref.shape[1]
    width = azimuths // sectors
    rows = fr_ref.shape[0]
    pad = moves_ref.shape[0] - rows
    passes = network(rows)
    valid = 1 << SHIFT - 1

    def listed(number, count):
        order[jnp.minimum(count, rows // width)] = number
        return count + (owner_ref[number] == me).astype(jnp.int32)

    owned = lax.fori_loop(0, sectors, listed, jnp.int32(0), unroll=8)

    for d in range(4):
        picked[d] = jnp.full(picked.shape[1:], -1.0 if d == 0 else 0.0, jnp.float32)
    chosen_ref[...] = jnp.zeros_like(chosen_ref)
    beyond = pl.ds(rows, pad)
    for slot in range(2):
        keys[slot, beyond, :] = jnp.zeros((pad, LANES), jnp.int32)
    moves_ref[0:pad, :] = jnp.zeros((pad, LANES), jnp.int32)
    for d in range(4):
        copies[d].wait()
        for at in range(0, azimuths, LANES):
            cols = pl.ds(at, LANES)
            plane = ids_ref[:, cols].astype(jnp.float32) if d == 0 else frac_ref[d - 1, :, cols]
            turned[d, cols, :] = plane.T
    copies[4].wait()

    def sector(place, carry):
        source = pl.ds(pl.multiple_of(order[place] * width, width), width)
        target = pl.ds(pl.multiple_of(place * width, width), width)
        chosen_ref[target, :] = table_ref[source, :]
        for d in range(4):
            picked[d, target, :] = turned[d, source, :]
        return carry

    lax.fori_loop(0, owned, sector, jnp.int32(0))

    held = pl.ds(0, rows)
    ids = picked[0].astype(jnp.int32)
    stream_cell, rest = split(jnp.maximum(ids, 0), cells_g * cells_r)
    girth_cell, radial_cell = split(rest, cells_r)
    xs = (stream_cell - stream_first).astype(jnp.float32) + picked[1]
    kept = (ids >= 0) & (xs > -1.0) & (xs < float(cells_s))
    xss[0, held, :] = xs
    xgs[0, held, :] = girth_cell.astype(jnp.float32) + picked[2]
    frs[0, held, :] = picked[3]
    earlier = lax.broadcasted_iota(jnp.int32, (rows, rows), 0) > lax.broadcasted_iota(
        jnp.int32, (rows, rows), 1
    )
    earlier = earlier.astype(jnp.float32).astype(jnp.bfloat16)
    skipped = jnp.where(kept, 0.0, 1.0)
    before = jnp.dot(
        earlier, skipped.astype(jnp.bfloat16), preferred_element_type=jnp.float32
    ).astype(jnp.int32)
    counts = rows - jnp.sum(skipped, axis=0, keepdims=True).astype(jnp.int32)
    count_ref[0] = jnp.max(counts)
    moves_ref[pad : pad + rows, :] = jnp.where(kept, valid, 0)
    keys[0, held, :] = (radial_cell << SHIFT) + jnp.where(kept, before, 0)
    for number, (low, digits) in enumerate(passes):
        a, b = number % 2, 1 - number % 2
        mask = digits - 1 << low
        last = number == len(passes) - 1
        for at in range(0, rows, CHUNK):
            here, target = pl.ds(at, CHUNK), pl.ds(pad + at, CHUNK)
            there = [pl.ds(at + (k << low), CHUNK) for k in range(1, digits)]
            key = keys[a, here, :]
            arriving = [keys[a, t, :] for t in there]
            moved = [(arriving[k] & mask) == (k + 1 << low) for k in range(digits - 1)]
            key = jnp.where((key & mask) != 0, key & -(1 << SHIFT), key)
            came = moves_ref[target, :]
            out = [r[a, here, :] for r in (frs, xss, xgs)]
            for k in range(digits - 1):
                key = jnp.where(moved[k], arriving[k], key)
                came = came | jnp.where(moved[k], k + 1 << low, 0)
                out = [
                    jnp.where(moved[k], r[a, there[k], :], o) for r, o in zip((frs, xss, xgs), out)
                ]
            moves_ref[target, :] = came
            if last:
                q_ref[here, :] = key >> SHIFT
                fr_ref[here, :] = out[0]
                xs_ref[here, :] = out[1]
                xg_ref[here, :] = out[2]
            else:
                keys[b, here, :] = key
                frs[b, here, :] = out[0]
                xss[b, here, :] = out[1]
                xgs[b, here, :] = out[2]


def prepare(owners, corner_ids, fractions, table, cells, girth_count):
    cells_s, cells_g, cells_r = cells
    radii, azimuths = corner_ids.shape
    sectors = owners.shape[0]
    rows = 3 * sectors // girth_count * (azimuths // sectors)
    pad = reach(rows)
    shape = jax.ShapeDtypeStruct
    lists = (rows, radii)
    vmem = pl.BlockSpec(memory_space=pltpu.VMEM)
    smem = pl.BlockSpec(memory_space=pltpu.SMEM)
    hbm = pl.BlockSpec(memory_space=pltpu.HBM)
    return pl.pallas_call(
        functools.partial(prepare_kernel, cells_s, cells_g, cells_r),
        out_shape=(
            shape(lists, jnp.int32),
            shape(lists, jnp.float32),
            shape(lists, jnp.float32),
            shape(lists, jnp.float32),
            shape((pad + rows, radii), jnp.int32),
            shape((rows, 2 * NH), jnp.float32),
            shape((1,), jnp.int32),
        ),
        in_specs=[smem, hbm, hbm, hbm],
        out_specs=[vmem] * 6 + [smem],
        scratch_shapes=[
            pltpu.VMEM(corner_ids.shape, jnp.int32),
            pltpu.VMEM(fractions.shape, jnp.float32),
            pltpu.VMEM(table.shape, jnp.float32),
            pltpu.VMEM((4, azimuths, radii), jnp.float32),
            pltpu.VMEM((4, rows, radii), jnp.float32),
            pltpu.VMEM((2, rows + pad, radii), jnp.int32),
        ]
        + [pltpu.VMEM((2, rows + pad, radii), jnp.float32)] * 3
        + [pltpu.SMEM((rows // (azimuths // sectors) + 1,), jnp.int32)]
        + [pltpu.SemaphoreType.DMA((5,))],
        compiler_params=pltpu.CompilerParams(vmem_limit_bytes=VMEM_LIMIT),
        cost_estimate=pl.CostEstimate(
            flops=20 * radii * azimuths, bytes_accessed=44 * radii * azimuths, transcendentals=0
        ),
        name="prepare_points",
    )(*(in_hbm(x) for x in (owners, corner_ids, fractions, table)))


def radial(values, amount, fill):
    extent = values.shape[-1]
    rolled = pltpu.roll(values, (-amount) % extent, values.ndim - 1)
    position = lax.broadcasted_iota(jnp.int32, values.shape, values.ndim - 1) + amount
    return jnp.where((position >= 0) & (position < extent), rolled, fill)


def advance(own, before, after, left, right, ext_ref, visc_ref):
    cells_s, cells_g, _ = own[0].shape
    mid = ROWS

    def along_s(stack, amount):
        return stack[2 + amount : 2 + amount + cells_s]

    def along_g(ref, amount):
        return ref[:, mid + amount : mid + amount + cells_g, :]

    def viscosity(energy, rate):
        return base_viscosity + energy / (rate + wall_rate)

    stacks = [jnp.concatenate([before[f], own[f], after[f]], axis=0) for f in range(6)]
    for f in range(6):
        ext_ref[f, :, mid - 2 : mid, :] = left[f]
        ext_ref[f, :, mid : mid + cells_g, :] = own[f]
        ext_ref[f, :, mid + cells_g : mid + cells_g + 2, :] = right[f]
    middle = viscosity(own[4], own[5])
    visc_stack = viscosity(stacks[4], stacks[5])
    visc_ref[:, mid - 2 : mid, :] = viscosity(left[4], left[5])
    visc_ref[:, mid : mid + cells_g, :] = middle
    visc_ref[:, mid + cells_g : mid + cells_g + 2, :] = viscosity(right[4], right[5])
    faces = [
        (
            0.5 * (middle + along_s(visc_stack, 1)),
            0.5 * (middle + along_s(visc_stack, -1)),
        ),
        (
            0.5 * (middle + along_g(visc_ref, 1)),
            0.5 * (middle + along_g(visc_ref, -1)),
        ),
        (
            0.5 * (middle + radial(middle, 1, base_viscosity)),
            0.5 * (middle + radial(middle, -1, base_viscosity)),
        ),
    ]

    def neighbour(f, direction, amount):
        if direction == 0:
            return along_s(stacks[f], amount)
        if direction == 1:
            return along_g(ext_ref.at[f], amount)
        return radial(own[f], amount, 0.0)

    def terms(f, direction):
        up, down = neighbour(f, direction, 1), neighbour(f, direction, -1)
        far = neighbour(f, direction, 2) - neighbour(f, direction, -2)
        gradient = (8.0 * (up - down) - far) * (1.0 / 12.0)
        above, below = faces[direction]
        return gradient, above * (up - own[f]) - below * (own[f] - down)

    strain = None
    updated = []
    for f in range(3):
        change = -terms(3, f)[0]
        for direction in range(3):
            gradient, spread = terms(f, direction)
            strain = gradient * gradient if strain is None else strain + gradient * gradient
            change = change - own[direction] * gradient + spread
        updated.append(own[f] + time_step * change)
    energy = own[4] / (own[5] + wall_rate) * strain - beta_star * own[4] * own[5]
    rate = alpha_rate * strain - beta_rate * own[5] * own[5]
    for direction in range(3):
        gradient, spread = terms(4, direction)
        energy = energy - own[direction] * gradient + spread
        gradient, spread = terms(5, direction)
        rate = rate - own[direction] * gradient + spread
    return updated, own[4] + time_step * energy, own[5] + time_step * rate


def girth_sums(parts):
    row = lax.broadcasted_iota(jnp.int32, parts[0].shape, 0)

    def swapped(values, distance):
        up = pltpu.roll(values, distance, 0)
        if 2 * distance == ROWS:
            return up
        return jnp.where((row & distance) != 0, up, pltpu.roll(values, ROWS - distance, 0))

    distance = ROWS // 2
    while distance > 0:
        low = (row & distance) == 0
        parts = [
            jnp.where(low, x, y) + swapped(jnp.where(low, y, x), distance)
            for x, y in zip(parts[:distance], parts[distance:])
        ]
        distance //= 2
    return parts[0]


def section_kernel(
    devices,
    count_ref,
    vel_ref,
    p_ref,
    k_ref,
    w_ref,
    stream_a,
    stream_b,
    girth_a,
    girth_b,
    q_ref,
    fr_ref,
    xs_ref,
    xg_ref,
    moves_ref,
    chosen_ref,
    new_vel_hbm,
    new_k_hbm,
    new_w_hbm,
    keep_ref,
    give_ref,
    new_vel_ref,
    new_k_ref,
    new_w_ref,
    ext_ref,
    visc_ref,
    field_ref,
    gather_ref,
    value_ref,
    disk_ref,
    harm_ref,
    stored,
):
    cells_s, cells_g, cells_r = p_ref.shape
    rows = fr_ref.shape[0]
    pad = moves_ref.shape[0] - rows
    passes = network(rows)
    valid = 1 << SHIFT - 1
    stream_odd = lax.axis_index("stream") % 2 == 1
    girth_odd = lax.axis_index("girth") % 2 == 1

    own = [vel_ref[0], vel_ref[1], vel_ref[2], p_ref[...], k_ref[...], w_ref[...]]
    six = range(6)
    updated, energy, rate = advance(
        own,
        [jnp.where(stream_odd, stream_a[f], stream_b[f]) for f in six],
        [jnp.where(stream_odd, stream_b[f], stream_a[f]) for f in six],
        [jnp.where(girth_odd, girth_a[f], girth_b[f]) for f in six],
        [jnp.where(girth_odd, girth_b[f], girth_a[f]) for f in six],
        ext_ref,
        visc_ref,
    )
    new_k_ref[...] = energy
    new_w_ref[...] = rate

    def halved(values):
        high = values.astype(jnp.bfloat16)
        return high, (values - high.astype(jnp.float32)).astype(jnp.bfloat16)

    def rounded(values):
        return values.astype(jnp.bfloat16).astype(jnp.float32)

    halves = cells_r // LANES
    for c in range(3):
        new_vel_ref[c] = updated[c]
        slope = radial(updated[c], 1, 0.0) - updated[c]
        for kind, values in enumerate((updated[c], slope)):
            if c < PRODUCTS:
                high = rounded(values)
                field_ref[c, :, 2 * kind] = high
                field_ref[c, :, 2 * kind + 1] = rounded(values - high)
            else:
                for h in range(halves):
                    lanes = slice(h * LANES, (h + 1) * LANES)
                    gather_ref[c - PRODUCTS, :, kind, h] = values[:, :, lanes]
    results = ((new_vel_ref, new_vel_hbm), (new_k_ref, new_k_hbm), (new_w_ref, new_w_hbm))
    copies = [
        pltpu.make_async_copy(source, target, stored.at[i])
        for i, (source, target) in enumerate(results)
    ]
    for copy in copies:
        copy.start()

    kinds = 4
    table = field_ref[...].reshape(PRODUCTS * cells_s * kinds * cells_g, cells_r)
    table = table.astype(jnp.bfloat16)
    pair = 2 * LANES
    girth_row = lax.broadcasted_iota(jnp.int32, (cells_g, pair), 0).astype(jnp.float32)
    index_type = jnp.bfloat16 if cells_r <= 256 else jnp.float32
    radial_row = lax.broadcasted_iota(jnp.int32, (cells_r, pair), 0).astype(jnp.float32)
    radial_row = radial_row.astype(index_type)
    one, none = jnp.ones((), jnp.bfloat16), jnp.zeros((), jnp.bfloat16)

    def two(values, j):
        return jnp.concatenate([values[j : j + 1], values[j + 1 : j + 2]], axis=1)

    def spread(values, j):
        return jnp.broadcast_to(values[j : j + 1], (cells_g, LANES))

    def pick(c, s, kind, index, half_of):
        out = None
        for h in range(halves):
            got = jnp.take_along_axis(
                gather_ref[c - PRODUCTS, s, kind, h], index, axis=1, mode="promise_in_bounds"
            )
            out = got if out is None else jnp.where(half_of[h], got, out)
        return out

    def eight(at):
        here = pl.ds(at, ROWS)
        q8, fr8, xg8, xs8 = (r[here, :] for r in (q_ref, fr_ref, xg_ref, xs_ref))
        hs8 = [jnp.maximum(1.0 - jnp.abs(xs8 - float(s)), 0.0) for s in range(cells_s)]
        index8 = q8 & (LANES - 1)
        qf8 = q8.astype(jnp.float32)
        sums = [[], [], []]
        for j in range(0, ROWS, 2):
            chosen_q = jnp.broadcast_to(two(qf8, j), (cells_r, pair)).astype(index_type)
            hot = jnp.where(radial_row == chosen_q, one, none)
            got = jnp.dot(table, hot, preferred_element_type=jnp.float32)
            got = got.reshape(PRODUCTS, cells_s, kinds, cells_g, pair)
            fr = two(fr8, j)
            hg = jnp.maximum(1.0 - jnp.abs(two(xg8, j) - girth_row), 0.0)
            hs = [two(hs8[s], j) for s in range(cells_s)]
            for c in range(PRODUCTS):
                total = None
                for s in range(cells_s):
                    value = got[c, s, 0] + got[c, s, 1] + fr * (got[c, s, 2] + got[c, s, 3])
                    value = hs[s] * value
                    total = value if total is None else total + value
                total = hg * total
                sums[c] += [total[:, :LANES], total[:, LANES:]]
            for i in (j, j + 1):
                index, q = spread(index8, i), spread(q8, i)
                half_of = [q >= h * LANES for h in range(halves)]
                own_hg = hg[:, (i - j) * LANES : (i - j + 1) * LANES]
                for c in range(PRODUCTS, 3):
                    total = None
                    for s in range(cells_s):
                        value = pick(c, s, 0, index, half_of)
                        value = value + fr8[i : i + 1] * pick(c, s, 1, index, half_of)
                        value = hs8[s][i : i + 1] * value
                        total = value if total is None else total + value
                    sums[c].append(own_hg * total)
        for c in range(3):
            value_ref[0, c, pl.ds(pad + at, ROWS), :] = girth_sums(sums[c])

    def step(group, carry):
        for part in range(2):
            eight(pl.multiple_of((2 * group + part) * ROWS, ROWS))
        return carry

    lax.fori_loop(0, (count_ref[0] + 2 * ROWS - 1) // (2 * ROWS), step, jnp.int32(0))

    for number, (low, digits) in enumerate(reversed(passes)):
        a, b = number % 2, 1 - number % 2
        mask = digits - 1 << low
        last = number == len(passes) - 1
        for at in range(0, rows, CHUNK):
            here = pl.ds(pad + at, CHUNK)
            there = [pl.ds(pad + at - (k << low), CHUNK) for k in range(1, digits)]
            moved = [(moves_ref[there[k], :] & mask) == (k + 1 << low) for k in range(digits - 1)]
            if last:
                kept = (moves_ref[here, :] & valid) != 0
            for c in range(3):
                value = value_ref[a, c, here, :]
                for k in range(digits - 1):
                    value = jnp.where(moved[k], value_ref[a, c, there[k], :], value)
                if last:
                    disk_ref[c, pl.ds(at, CHUNK), :] = jnp.where(kept, value, 0.0)
                else:
                    value_ref[b, c, here, :] = value

    turned = jnp.concatenate([disk_ref[c].T for c in range(3)], axis=0)
    high, low = halved(turned)
    wave_high, wave_low = halved(chosen_ref[...])
    waves = jnp.dot(high, wave_high, preferred_element_type=jnp.float32)
    waves += jnp.dot(high, wave_low, preferred_element_type=jnp.float32)
    waves += jnp.dot(low, wave_high, preferred_element_type=jnp.float32)
    radii = harm_ref.shape[0]
    for c in range(3):
        harm_ref[:, c * 2 * NH : (c + 1) * 2 * NH] = waves[c * radii : (c + 1) * radii]
    block = radii // devices
    for place in range(devices // 2):
        even = harm_ref[2 * place * block : (2 * place + 1) * block, :]
        odd = harm_ref[(2 * place + 1) * block : (2 * place + 2) * block, :]
        keep_ref[place * block : (place + 1) * block, :] = jnp.where(girth_odd, odd, even)
        give_ref[place * block : (place + 1) * block, :] = jnp.where(girth_odd, even, odd)
    for copy in copies:
        copy.wait()


def section(velocity, pressure, energy, rate, halos, points, devices):
    _, cells_s, cells_g, cells_r = velocity.shape
    *lists, moves, chosen, counts = points
    rows, radii = lists[0].shape
    shape = functools.partial(jax.ShapeDtypeStruct, dtype=jnp.float32)
    scratch = lambda *dims: pltpu.VMEM(dims, jnp.float32)
    vmem = pl.BlockSpec(memory_space=pltpu.VMEM)
    smem = pl.BlockSpec(memory_space=pltpu.SMEM)
    return pl.pallas_call(
        functools.partial(section_kernel, devices),
        out_shape=(
            shape(velocity.shape),
            shape(energy.shape),
            shape(rate.shape),
            shape((radii // 2, 6 * NH)),
            shape((radii // 2, 6 * NH)),
        ),
        in_specs=[smem] + [vmem] * 14,
        out_specs=[pl.BlockSpec(memory_space=pl.ANY)] * 3 + [vmem] * 2,
        scratch_shapes=[
            scratch(*velocity.shape),
            scratch(*energy.shape),
            scratch(*rate.shape),
            scratch(6, cells_s, 3 * ROWS, cells_r),
            scratch(cells_s, 3 * ROWS, cells_r),
            scratch(PRODUCTS, cells_s, 4, cells_g, cells_r),
            scratch(3 - PRODUCTS, cells_s, 2, cells_r // LANES, cells_g, LANES),
            scratch(2, 3, moves.shape[0], radii),
            scratch(3, rows, radii),
            scratch(radii, 6 * NH),
            pltpu.SemaphoreType.DMA((3,)),
        ],
        compiler_params=pltpu.CompilerParams(vmem_limit_bytes=VMEM_LIMIT),
        name="section_and_disk",
    )(counts, velocity, pressure, energy, rate, *halos, *lists, moves, chosen)


def fourier_table(azimuths, modes):
    phase = np.arange(azimuths)[:, None] * np.arange(modes)[None, :] % azimuths
    angles = phase * (2.0 * math.pi / azimuths)
    table = np.concatenate([np.cos(angles), -np.sin(angles)], axis=1) / math.sqrt(azimuths)
    return jnp.asarray(table.astype(np.float32))


def body(velocity, pressure, kinetic_energy, dissipation_rate, corner_ids, fractions, sector_owner):
    _, cells_s, cells_g, cells_r = velocity.shape
    radii, azimuths = corner_ids.shape
    stream_count, girth_count = lax.axis_size("stream"), lax.axis_size("girth")
    devices = stream_count * girth_count

    def swap(values, axis, count, start):
        pairs = []
        for i in range(start, count - 1, 2):
            pairs += [(i, i + 1), (i + 1, i)]
        return lax.ppermute(values, axis, pairs)

    slabs = pack(velocity, pressure, kinetic_energy, dissipation_rate)
    girth_halos = (
        swap(slabs[2], "girth", girth_count, 0),
        swap(slabs[3], "girth", girth_count, 1),
    )
    stream_halos = (
        swap(slabs[0], "stream", stream_count, 0),
        swap(slabs[1], "stream", stream_count, 1),
    )
    halos = stream_halos + girth_halos
    points = prepare(
        sector_owner[:, 0],
        corner_ids,
        fractions,
        fourier_table(azimuths, NH),
        (cells_s, cells_g, cells_r),
        girth_count,
    )
    new_velocity, new_energy, new_rate, keep, give = section(
        velocity, pressure, kinetic_energy, dissipation_rate, halos, points, devices
    )
    total = keep + swap(give, "girth", girth_count, 0)
    shares = lax.all_to_all(
        total.reshape(devices // 2, radii // devices, 6 * NH),
        ("stream", "girth"),
        split_axis=0,
        concat_axis=0,
        tiled=True,
        axis_index_groups=[list(range(parity, devices, 2)) for parity in (0, 1)],
    )
    return new_velocity, new_energy, new_rate, jnp.sum(shares, axis=0)


def solution(mesh):
    return jax.shard_map(
        body,
        mesh=mesh,
        in_specs=(
            P(None, "stream", "girth", None),
            P("stream", "girth", None),
            P("stream", "girth", None),
            P("stream", "girth", None),
            P(),
            P(),
            P(),
        ),
        out_specs=(
            P(None, "stream", "girth", None),
            P("stream", "girth", None),
            P("stream", "girth", None),
            P(("stream", "girth"), None),
        ),
        check_vma=False,
    )
```

```python
import functools
import math

import jax
import jax.numpy as jnp
import numpy as np
from jax import lax
from jax.experimental import pallas as pl
from jax.experimental.pallas import tpu as pltpu
from jax.sharding import PartitionSpec as P

NH = 128

base_viscosity = 0.05
time_step = 0.2
beta_star = 0.09
beta_rate = 0.075
alpha_rate = 0.52
wall_rate = 1.0

LANES = 128
ROWS = 8
SHIFT = 10
CHUNK = 32
PRODUCTS = 2
VMEM_LIMIT = 48 * 1024 * 1024


def in_hbm(values):
    return pltpu.with_memory_space_constraint(values, pltpu.HBM)


def pack_kernel(vel_ref, p_ref, k_ref, w_ref, *slabs):
    cells_s, cells_g, _ = p_ref.shape
    stream_odd = lax.axis_index("stream") % 2 == 1
    girth_odd = lax.axis_index("girth") % 2 == 1
    for f in range(6):
        own = vel_ref.at[f] if f < 3 else (p_ref, k_ref, w_ref)[f - 3]
        first, last = own[0:2], own[cells_s - 2 : cells_s]
        slabs[0][f] = jnp.where(stream_odd, first, last)
        slabs[1][f] = jnp.where(stream_odd, last, first)
        first, last = own[:, 0:2, :], own[:, cells_g - 2 : cells_g, :]
        slabs[2][f] = jnp.where(girth_odd, first, last)
        slabs[3][f] = jnp.where(girth_odd, last, first)


def pack(velocity, pressure, energy, rate):
    _, cells_s, cells_g, cells_r = velocity.shape
    stream = pltpu.VMEM((6, 2, cells_g, cells_r), jnp.float32)
    girth = pltpu.VMEM((6, cells_s, 2, cells_r), jnp.float32)
    vmem = pl.BlockSpec(memory_space=pltpu.VMEM)
    return pl.pallas_call(
        pack_kernel,
        out_shape=(stream, stream, girth, girth),
        in_specs=[vmem] * 4,
        out_specs=[vmem] * 4,
        name="pack_halos",
    )(*(in_hbm(x) for x in (velocity, pressure, energy, rate)))


def network(rows):
    steps = (rows - 1).bit_length()
    return [(low, 1 << min(2, steps - low)) for low in range(0, steps, 2)]


def reach(rows):
    return max((digits - 1) << low for low, digits in network(rows))


def split(values, size):
    if size & (size - 1) == 0:
        return values >> (size.bit_length() - 1), values & (size - 1)
    return values // size, values % size


def choose_kernel(
    owner_ref,
    ids_hbm,
    frac_hbm,
    table_hbm,
    slab_a,
    slab_b,
    picked,
    chosen_ref,
    out_a,
    out_b,
    ids_ref,
    frac_ref,
    table_ref,
    turned,
    order,
    arrived,
):
    copies = [pltpu.make_async_copy(ids_hbm, ids_ref, arrived.at[0])]
    for d in range(3):
        copies.append(pltpu.make_async_copy(frac_hbm.at[d], frac_ref.at[d], arrived.at[1 + d]))
    copies.append(pltpu.make_async_copy(table_hbm, table_ref, arrived.at[4]))
    for copy in copies:
        copy.start()
    out_a[...] = slab_a[...]
    out_b[...] = slab_b[...]
    me = lax.axis_index("girth")
    sectors = owner_ref.shape[0]
    azimuths = ids_ref.shape[1]
    width = azimuths // sectors
    rows = picked.shape[1]

    def listed(number, count):
        order[jnp.minimum(count, rows // width)] = number
        return count + (owner_ref[number] == me).astype(jnp.int32)

    owned = lax.fori_loop(0, sectors, listed, jnp.int32(0), unroll=8)

    for d in range(4):
        picked[d] = jnp.full(picked.shape[1:], -1.0 if d == 0 else 0.0, jnp.float32)
    chosen_ref[...] = jnp.zeros_like(chosen_ref)
    for d in range(4):
        copies[d].wait()
        for at in range(0, azimuths, LANES):
            cols = pl.ds(at, LANES)
            plane = ids_ref[:, cols].astype(jnp.float32) if d == 0 else frac_ref[d - 1, :, cols]
            turned[d, cols, :] = plane.T
    copies[4].wait()

    def sector(place, carry):
        source = pl.ds(pl.multiple_of(order[place] * width, width), width)
        target = pl.ds(pl.multiple_of(place * width, width), width)
        chosen_ref[target, :] = table_ref[source, :]
        for d in range(4):
            picked[d, target, :] = turned[d, source, :]
        return carry

    lax.fori_loop(0, owned, sector, jnp.int32(0))


def choose(owners, corner_ids, fractions, table, slabs, girth_count):
    radii, azimuths = corner_ids.shape
    sectors = owners.shape[0]
    rows = 3 * sectors // girth_count * (azimuths // sectors)
    vmem = pl.BlockSpec(memory_space=pltpu.VMEM)
    smem = pl.BlockSpec(memory_space=pltpu.SMEM)
    hbm = pl.BlockSpec(memory_space=pltpu.HBM)
    return pl.pallas_call(
        choose_kernel,
        out_shape=[
            jax.ShapeDtypeStruct((4, rows, radii), jnp.float32),
            jax.ShapeDtypeStruct((rows, 2 * NH), jnp.float32),
        ]
        + [pltpu.VMEM(slab.shape, jnp.float32) for slab in slabs],
        in_specs=[smem, hbm, hbm, hbm, vmem, vmem],
        out_specs=[vmem] * 4,
        scratch_shapes=[
            pltpu.VMEM(corner_ids.shape, jnp.int32),
            pltpu.VMEM(fractions.shape, jnp.float32),
            pltpu.VMEM(table.shape, jnp.float32),
            pltpu.VMEM((4, azimuths, radii), jnp.float32),
            pltpu.SMEM((rows // (azimuths // sectors) + 1,), jnp.int32),
            pltpu.SemaphoreType.DMA((5,)),
        ],
        compiler_params=pltpu.CompilerParams(vmem_limit_bytes=VMEM_LIMIT),
        cost_estimate=pl.CostEstimate(
            flops=8 * radii * azimuths, bytes_accessed=32 * radii * azimuths, transcendentals=0
        ),
        name="choose_points",
    )(*(in_hbm(x) for x in (owners, corner_ids, fractions, table)), *slabs)


def prepare_kernel(
    cells_s,
    cells_g,
    cells_r,
    picked,
    q_ref,
    fr_ref,
    xs_ref,
    xg_ref,
    moves_ref,
    count_ref,
    keys,
    frs,
    xss,
    xgs,
):
    stream_first = lax.axis_index("stream") * cells_s
    rows = fr_ref.shape[0]
    pad = moves_ref.shape[0] - rows
    passes = network(rows)
    valid = 1 << SHIFT - 1
    beyond = pl.ds(rows, pad)
    for slot in range(2):
        keys[slot, beyond, :] = jnp.zeros((pad, LANES), jnp.int32)
    moves_ref[0:pad, :] = jnp.zeros((pad, LANES), jnp.int32)
    held = pl.ds(0, rows)
    ids = picked[0].astype(jnp.int32)
    stream_cell, rest = split(jnp.maximum(ids, 0), cells_g * cells_r)
    girth_cell, radial_cell = split(rest, cells_r)
    xs = (stream_cell - stream_first).astype(jnp.float32) + picked[1]
    kept = (ids >= 0) & (xs > -1.0) & (xs < float(cells_s))
    xss[0, held, :] = xs
    xgs[0, held, :] = girth_cell.astype(jnp.float32) + picked[2]
    frs[0, held, :] = picked[3]
    earlier = lax.broadcasted_iota(jnp.int32, (rows, rows), 0) > lax.broadcasted_iota(
        jnp.int32, (rows, rows), 1
    )
    earlier = earlier.astype(jnp.float32).astype(jnp.bfloat16)
    skipped = jnp.where(kept, 0.0, 1.0)
    before = jnp.dot(
        earlier, skipped.astype(jnp.bfloat16), preferred_element_type=jnp.float32
    ).astype(jnp.int32)
    counts = rows - jnp.sum(skipped, axis=0, keepdims=True).astype(jnp.int32)
    count_ref[0] = jnp.max(counts)
    moves_ref[pad : pad + rows, :] = jnp.where(kept, valid, 0)
    keys[0, held, :] = (radial_cell << SHIFT) + jnp.where(kept, before, 0)
    for number, (low, digits) in enumerate(passes):
        a, b = number % 2, 1 - number % 2
        mask = digits - 1 << low
        last = number == len(passes) - 1
        for at in range(0, rows, CHUNK):
            here, target = pl.ds(at, CHUNK), pl.ds(pad + at, CHUNK)
            there = [pl.ds(at + (k << low), CHUNK) for k in range(1, digits)]
            key = keys[a, here, :]
            arriving = [keys[a, t, :] for t in there]
            moved = [(arriving[k] & mask) == (k + 1 << low) for k in range(digits - 1)]
            key = jnp.where((key & mask) != 0, key & -(1 << SHIFT), key)
            came = moves_ref[target, :]
            out = [r[a, here, :] for r in (frs, xss, xgs)]
            for k in range(digits - 1):
                key = jnp.where(moved[k], arriving[k], key)
                came = came | jnp.where(moved[k], k + 1 << low, 0)
                out = [
                    jnp.where(moved[k], r[a, there[k], :], o) for r, o in zip((frs, xss, xgs), out)
                ]
            moves_ref[target, :] = came
            if last:
                q_ref[here, :] = key >> SHIFT
                fr_ref[here, :] = out[0]
                xs_ref[here, :] = out[1]
                xg_ref[here, :] = out[2]
            else:
                keys[b, here, :] = key
                frs[b, here, :] = out[0]
                xss[b, here, :] = out[1]
                xgs[b, here, :] = out[2]


def prepare(picked, cells):
    _, rows, radii = picked.shape
    pad = reach(rows)
    shape = jax.ShapeDtypeStruct
    lists = (rows, radii)
    vmem = pl.BlockSpec(memory_space=pltpu.VMEM)
    smem = pl.BlockSpec(memory_space=pltpu.SMEM)
    return pl.pallas_call(
        functools.partial(prepare_kernel, *cells),
        out_shape=(
            shape(lists, jnp.int32),
            shape(lists, jnp.float32),
            shape(lists, jnp.float32),
            shape(lists, jnp.float32),
            shape((pad + rows, radii), jnp.int32),
            shape((1,), jnp.int32),
        ),
        in_specs=[vmem],
        out_specs=[vmem] * 5 + [smem],
        scratch_shapes=[pltpu.VMEM((2, rows + pad, radii), jnp.int32)]
        + [pltpu.VMEM((2, rows + pad, radii), jnp.float32)] * 3,
        compiler_params=pltpu.CompilerParams(vmem_limit_bytes=VMEM_LIMIT),
        cost_estimate=pl.CostEstimate(
            flops=200 * rows * radii, bytes_accessed=44 * rows * radii, transcendentals=0
        ),
        name="prepare_points",
    )(picked)


def radial(values, amount, fill):
    extent = values.shape[-1]
    rolled = pltpu.roll(values, (-amount) % extent, values.ndim - 1)
    position = lax.broadcasted_iota(jnp.int32, values.shape, values.ndim - 1) + amount
    return jnp.where((position >= 0) & (position < extent), rolled, fill)


def advance(own, before, after, left, right, ext_ref, visc_ref):
    cells_s, cells_g, _ = own[0].shape
    mid = ROWS

    def along_s(stack, amount):
        return stack[2 + amount : 2 + amount + cells_s]

    def along_g(ref, amount):
        return ref[:, mid + amount : mid + amount + cells_g, :]

    def viscosity(energy, rate):
        return base_viscosity + energy / (rate + wall_rate)

    stacks = [jnp.concatenate([before[f], own[f], after[f]], axis=0) for f in range(6)]
    for f in range(6):
        ext_ref[f, :, mid - 2 : mid, :] = left[f]
        ext_ref[f, :, mid : mid + cells_g, :] = own[f]
        ext_ref[f, :, mid + cells_g : mid + cells_g + 2, :] = right[f]
    middle = viscosity(own[4], own[5])
    visc_stack = viscosity(stacks[4], stacks[5])
    visc_ref[:, mid - 2 : mid, :] = viscosity(left[4], left[5])
    visc_ref[:, mid : mid + cells_g, :] = middle
    visc_ref[:, mid + cells_g : mid + cells_g + 2, :] = viscosity(right[4], right[5])
    faces = [
        (
            0.5 * (middle + along_s(visc_stack, 1)),
            0.5 * (middle + along_s(visc_stack, -1)),
        ),
        (
            0.5 * (middle + along_g(visc_ref, 1)),
            0.5 * (middle + along_g(visc_ref, -1)),
        ),
        (
            0.5 * (middle + radial(middle, 1, base_viscosity)),
            0.5 * (middle + radial(middle, -1, base_viscosity)),
        ),
    ]

    def neighbour(f, direction, amount):
        if direction == 0:
            return along_s(stacks[f], amount)
        if direction == 1:
            return along_g(ext_ref.at[f], amount)
        return radial(own[f], amount, 0.0)

    def terms(f, direction):
        up, down = neighbour(f, direction, 1), neighbour(f, direction, -1)
        far = neighbour(f, direction, 2) - neighbour(f, direction, -2)
        gradient = (8.0 * (up - down) - far) * (1.0 / 12.0)
        above, below = faces[direction]
        return gradient, above * (up - own[f]) - below * (own[f] - down)

    strain = None
    updated = []
    for f in range(3):
        change = -terms(3, f)[0]
        for direction in range(3):
            gradient, spread = terms(f, direction)
            strain = gradient * gradient if strain is None else strain + gradient * gradient
            change = change - own[direction] * gradient + spread
        updated.append(own[f] + time_step * change)
    energy = own[4] / (own[5] + wall_rate) * strain - beta_star * own[4] * own[5]
    rate = alpha_rate * strain - beta_rate * own[5] * own[5]
    for direction in range(3):
        gradient, spread = terms(4, direction)
        energy = energy - own[direction] * gradient + spread
        gradient, spread = terms(5, direction)
        rate = rate - own[direction] * gradient + spread
    return updated, own[4] + time_step * energy, own[5] + time_step * rate


def girth_sums(parts):
    row = lax.broadcasted_iota(jnp.int32, parts[0].shape, 0)

    def swapped(values, distance):
        up = pltpu.roll(values, distance, 0)
        if 2 * distance == ROWS:
            return up
        return jnp.where((row & distance) != 0, up, pltpu.roll(values, ROWS - distance, 0))

    distance = ROWS // 2
    while distance > 0:
        low = (row & distance) == 0
        parts = [
            jnp.where(low, x, y) + swapped(jnp.where(low, y, x), distance)
            for x, y in zip(parts[:distance], parts[distance:])
        ]
        distance //= 2
    return parts[0]


def section_kernel(
    devices,
    count_ref,
    vel_ref,
    p_ref,
    k_ref,
    w_ref,
    stream_a,
    stream_b,
    girth_a,
    girth_b,
    q_ref,
    fr_ref,
    xs_ref,
    xg_ref,
    moves_ref,
    chosen_ref,
    new_vel_hbm,
    new_k_hbm,
    new_w_hbm,
    keep_ref,
    give_ref,
    new_vel_ref,
    new_k_ref,
    new_w_ref,
    ext_ref,
    visc_ref,
    field_ref,
    gather_ref,
    value_ref,
    disk_ref,
    harm_ref,
    stored,
):
    cells_s, cells_g, cells_r = p_ref.shape
    rows = fr_ref.shape[0]
    pad = moves_ref.shape[0] - rows
    passes = network(rows)
    valid = 1 << SHIFT - 1
    stream_odd = lax.axis_index("stream") % 2 == 1
    girth_odd = lax.axis_index("girth") % 2 == 1

    own = [vel_ref[0], vel_ref[1], vel_ref[2], p_ref[...], k_ref[...], w_ref[...]]
    six = range(6)
    updated, energy, rate = advance(
        own,
        [jnp.where(stream_odd, stream_a[f], stream_b[f]) for f in six],
        [jnp.where(stream_odd, stream_b[f], stream_a[f]) for f in six],
        [jnp.where(girth_odd, girth_a[f], girth_b[f]) for f in six],
        [jnp.where(girth_odd, girth_b[f], girth_a[f]) for f in six],
        ext_ref,
        visc_ref,
    )
    new_k_ref[...] = energy
    new_w_ref[...] = rate

    def halved(values):
        high = values.astype(jnp.bfloat16)
        return high, (values - high.astype(jnp.float32)).astype(jnp.bfloat16)

    def rounded(values):
        return values.astype(jnp.bfloat16).astype(jnp.float32)

    halves = cells_r // LANES
    for c in range(3):
        new_vel_ref[c] = updated[c]
        slope = radial(updated[c], 1, 0.0) - updated[c]
        for kind, values in enumerate((updated[c], slope)):
            if c < PRODUCTS:
                high = rounded(values)
                field_ref[c, :, 2 * kind] = high
                field_ref[c, :, 2 * kind + 1] = rounded(values - high)
            else:
                for h in range(halves):
                    lanes = slice(h * LANES, (h + 1) * LANES)
                    gather_ref[c - PRODUCTS, :, kind, h] = values[:, :, lanes]
    results = ((new_vel_ref, new_vel_hbm), (new_k_ref, new_k_hbm), (new_w_ref, new_w_hbm))
    copies = [
        pltpu.make_async_copy(source, target, stored.at[i])
        for i, (source, target) in enumerate(results)
    ]
    for copy in copies:
        copy.start()

    kinds = 4
    table = field_ref[...].reshape(PRODUCTS * cells_s * kinds * cells_g, cells_r)
    table = table.astype(jnp.bfloat16)
    pair = 2 * LANES
    girth_row = lax.broadcasted_iota(jnp.int32, (cells_g, pair), 0).astype(jnp.float32)
    index_type = jnp.bfloat16 if cells_r <= 256 else jnp.float32
    radial_row = lax.broadcasted_iota(jnp.int32, (cells_r, pair), 0).astype(jnp.float32)
    radial_row = radial_row.astype(index_type)
    one, none = jnp.ones((), jnp.bfloat16), jnp.zeros((), jnp.bfloat16)

    def two(values, j):
        return jnp.concatenate([values[j : j + 1], values[j + 1 : j + 2]], axis=1)

    def spread(values, j):
        return jnp.broadcast_to(values[j : j + 1], (cells_g, LANES))

    def pick(c, s, kind, index, half_of):
        out = None
        for h in range(halves):
            got = jnp.take_along_axis(
                gather_ref[c - PRODUCTS, s, kind, h], index, axis=1, mode="promise_in_bounds"
            )
            out = got if out is None else jnp.where(half_of[h], got, out)
        return out

    def eight(at):
        here = pl.ds(at, ROWS)
        q8, fr8, xg8, xs8 = (r[here, :] for r in (q_ref, fr_ref, xg_ref, xs_ref))
        hs8 = [jnp.maximum(1.0 - jnp.abs(xs8 - float(s)), 0.0) for s in range(cells_s)]
        index8 = q8 & (LANES - 1)
        qf8 = q8.astype(jnp.float32)
        sums = [[], [], []]
        for j in range(0, ROWS, 2):
            chosen_q = jnp.broadcast_to(two(qf8, j), (cells_r, pair)).astype(index_type)
            hot = jnp.where(radial_row == chosen_q, one, none)
            got = jnp.dot(table, hot, preferred_element_type=jnp.float32)
            got = got.reshape(PRODUCTS, cells_s, kinds, cells_g, pair)
            fr = two(fr8, j)
            hg = jnp.maximum(1.0 - jnp.abs(two(xg8, j) - girth_row), 0.0)
            hs = [two(hs8[s], j) for s in range(cells_s)]
            for c in range(PRODUCTS):
                total = None
                for s in range(cells_s):
                    value = got[c, s, 0] + got[c, s, 1] + fr * (got[c, s, 2] + got[c, s, 3])
                    value = hs[s] * value
                    total = value if total is None else total + value
                total = hg * total
                sums[c] += [total[:, :LANES], total[:, LANES:]]
            for i in (j, j + 1):
                index, q = spread(index8, i), spread(q8, i)
                half_of = [q >= h * LANES for h in range(halves)]
                own_hg = hg[:, (i - j) * LANES : (i - j + 1) * LANES]
                for c in range(PRODUCTS, 3):
                    total = None
                    for s in range(cells_s):
                        value = pick(c, s, 0, index, half_of)
                        value = value + fr8[i : i + 1] * pick(c, s, 1, index, half_of)
                        value = hs8[s][i : i + 1] * value
                        total = value if total is None else total + value
                    sums[c].append(own_hg * total)
        for c in range(3):
            value_ref[0, c, pl.ds(pad + at, ROWS), :] = girth_sums(sums[c])

    def step(group, carry):
        for part in range(2):
            eight(pl.multiple_of((2 * group + part) * ROWS, ROWS))
        return carry

    lax.fori_loop(0, (count_ref[0] + 2 * ROWS - 1) // (2 * ROWS), step, jnp.int32(0))

    for number, (low, digits) in enumerate(reversed(passes)):
        a, b = number % 2, 1 - number % 2
        mask = digits - 1 << low
        last = number == len(passes) - 1
        for at in range(0, rows, CHUNK):
            here = pl.ds(pad + at, CHUNK)
            there = [pl.ds(pad + at - (k << low), CHUNK) for k in range(1, digits)]
            moved = [(moves_ref[there[k], :] & mask) == (k + 1 << low) for k in range(digits - 1)]
            if last:
                kept = (moves_ref[here, :] & valid) != 0
            for c in range(3):
                value = value_ref[a, c, here, :]
                for k in range(digits - 1):
                    value = jnp.where(moved[k], value_ref[a, c, there[k], :], value)
                if last:
                    disk_ref[c, pl.ds(at, CHUNK), :] = jnp.where(kept, value, 0.0)
                else:
                    value_ref[b, c, here, :] = value

    turned = jnp.concatenate([disk_ref[c].T for c in range(3)], axis=0)
    high, low = halved(turned)
    wave_high, wave_low = halved(chosen_ref[...])
    waves = jnp.dot(high, wave_high, preferred_element_type=jnp.float32)
    waves += jnp.dot(high, wave_low, preferred_element_type=jnp.float32)
    waves += jnp.dot(low, wave_high, preferred_element_type=jnp.float32)
    radii = harm_ref.shape[0]
    for c in range(3):
        harm_ref[:, c * 2 * NH : (c + 1) * 2 * NH] = waves[c * radii : (c + 1) * radii]
    block = radii // devices
    for place in range(devices // 2):
        even = harm_ref[2 * place * block : (2 * place + 1) * block, :]
        odd = harm_ref[(2 * place + 1) * block : (2 * place + 2) * block, :]
        keep_ref[place * block : (place + 1) * block, :] = jnp.where(girth_odd, odd, even)
        give_ref[place * block : (place + 1) * block, :] = jnp.where(girth_odd, even, odd)
    for copy in copies:
        copy.wait()


def section(velocity, pressure, energy, rate, halos, points, devices):
    _, cells_s, cells_g, cells_r = velocity.shape
    *lists, moves, chosen, counts = points
    rows, radii = lists[0].shape
    shape = functools.partial(jax.ShapeDtypeStruct, dtype=jnp.float32)
    scratch = lambda *dims: pltpu.VMEM(dims, jnp.float32)
    vmem = pl.BlockSpec(memory_space=pltpu.VMEM)
    smem = pl.BlockSpec(memory_space=pltpu.SMEM)
    return pl.pallas_call(
        functools.partial(section_kernel, devices),
        out_shape=(
            shape(velocity.shape),
            shape(energy.shape),
            shape(rate.shape),
            shape((radii // 2, 6 * NH)),
            shape((radii // 2, 6 * NH)),
        ),
        in_specs=[smem] + [vmem] * 14,
        out_specs=[pl.BlockSpec(memory_space=pl.ANY)] * 3 + [vmem] * 2,
        scratch_shapes=[
            scratch(*velocity.shape),
            scratch(*energy.shape),
            scratch(*rate.shape),
            scratch(6, cells_s, 3 * ROWS, cells_r),
            scratch(cells_s, 3 * ROWS, cells_r),
            scratch(PRODUCTS, cells_s, 4, cells_g, cells_r),
            scratch(3 - PRODUCTS, cells_s, 2, cells_r // LANES, cells_g, LANES),
            scratch(2, 3, moves.shape[0], radii),
            scratch(3, rows, radii),
            scratch(radii, 6 * NH),
            pltpu.SemaphoreType.DMA((3,)),
        ],
        compiler_params=pltpu.CompilerParams(vmem_limit_bytes=VMEM_LIMIT),
        name="section_and_disk",
    )(counts, velocity, pressure, energy, rate, *halos, *lists, moves, chosen)


def fourier_table(azimuths, modes):
    phase = np.arange(azimuths)[:, None] * np.arange(modes)[None, :] % azimuths
    angles = phase * (2.0 * math.pi / azimuths)
    table = np.concatenate([np.cos(angles), -np.sin(angles)], axis=1) / math.sqrt(azimuths)
    return jnp.asarray(table.astype(np.float32))


def body(velocity, pressure, kinetic_energy, dissipation_rate, corner_ids, fractions, sector_owner):
    _, cells_s, cells_g, cells_r = velocity.shape
    radii, azimuths = corner_ids.shape
    stream_count, girth_count = lax.axis_size("stream"), lax.axis_size("girth")
    devices = stream_count * girth_count

    def swap(values, axis, count, start):
        pairs = []
        for i in range(start, count - 1, 2):
            pairs += [(i, i + 1), (i + 1, i)]
        return lax.ppermute(values, axis, pairs)

    slabs = pack(velocity, pressure, kinetic_energy, dissipation_rate)
    stream_halos = (
        swap(slabs[0], "stream", stream_count, 0),
        swap(slabs[1], "stream", stream_count, 1),
    )
    picked, chosen, *girth_slabs = choose(
        sector_owner[:, 0],
        corner_ids,
        fractions,
        fourier_table(azimuths, NH),
        slabs[2:],
        girth_count,
    )
    girth_halos = (
        swap(girth_slabs[0], "girth", girth_count, 0),
        swap(girth_slabs[1], "girth", girth_count, 1),
    )
    *lists, counts = prepare(picked, (cells_s, cells_g, cells_r))
    halos = stream_halos + girth_halos
    points = (*lists, chosen, counts)
    new_velocity, new_energy, new_rate, keep, give = section(
        velocity, pressure, kinetic_energy, dissipation_rate, halos, points, devices
    )
    total = keep + swap(give, "girth", girth_count, 0)
    shares = lax.all_to_all(
        total.reshape(devices // 2, radii // devices, 6 * NH),
        ("stream", "girth"),
        split_axis=0,
        concat_axis=0,
        tiled=True,
        axis_index_groups=[list(range(parity, devices, 2)) for parity in (0, 1)],
    )
    return new_velocity, new_energy, new_rate, jnp.sum(shares, axis=0)


def solution(mesh):
    return jax.shard_map(
        body,
        mesh=mesh,
        in_specs=(
            P(None, "stream", "girth", None),
            P("stream", "girth", None),
            P("stream", "girth", None),
            P("stream", "girth", None),
            P(),
            P(),
            P(),
        ),
        out_specs=(
            P(None, "stream", "girth", None),
            P("stream", "girth", None),
            P("stream", "girth", None),
            P(("stream", "girth"), None),
        ),
        check_vma=False,
    )
```

```python
import functools
import math

import jax
import jax.numpy as jnp
import numpy as np
from jax import lax
from jax.experimental import pallas as pl
from jax.experimental.pallas import tpu as pltpu
from jax.sharding import PartitionSpec as P

NH = 128

base_viscosity = 0.05
time_step = 0.2
beta_star = 0.09
beta_rate = 0.075
alpha_rate = 0.52
wall_rate = 1.0

LANES = 128
ROWS = 8
SHIFT = 10
CHUNK = 32
PRODUCTS = 3
VMEM_LIMIT = 48 * 1024 * 1024


def in_hbm(values):
    return pltpu.with_memory_space_constraint(values, pltpu.HBM)


def pack_kernel(vel_ref, p_ref, k_ref, w_ref, *slabs):
    cells_s, cells_g, _ = p_ref.shape
    stream_odd = lax.axis_index("stream") % 2 == 1
    girth_odd = lax.axis_index("girth") % 2 == 1
    for f in range(6):
        own = vel_ref.at[f] if f < 3 else (p_ref, k_ref, w_ref)[f - 3]
        first, last = own[0:2], own[cells_s - 2 : cells_s]
        slabs[0][f] = jnp.where(stream_odd, first, last)
        slabs[1][f] = jnp.where(stream_odd, last, first)
        first, last = own[:, 0:2, :], own[:, cells_g - 2 : cells_g, :]
        slabs[2][f] = jnp.where(girth_odd, first, last)
        slabs[3][f] = jnp.where(girth_odd, last, first)


def pack(velocity, pressure, energy, rate):
    _, cells_s, cells_g, cells_r = velocity.shape
    stream = pltpu.VMEM((6, 2, cells_g, cells_r), jnp.float32)
    girth = pltpu.VMEM((6, cells_s, 2, cells_r), jnp.float32)
    vmem = pl.BlockSpec(memory_space=pltpu.VMEM)
    return pl.pallas_call(
        pack_kernel,
        out_shape=(stream, stream, girth, girth),
        in_specs=[vmem] * 4,
        out_specs=[vmem] * 4,
        name="pack_halos",
    )(*(in_hbm(x) for x in (velocity, pressure, energy, rate)))


def network(rows):
    steps = (rows - 1).bit_length()
    return [(low, 1 << min(2, steps - low)) for low in range(0, steps, 2)]


def reach(rows):
    return max((digits - 1) << low for low, digits in network(rows))


def split(values, size):
    if size & (size - 1) == 0:
        return values >> (size.bit_length() - 1), values & (size - 1)
    return values // size, values % size


def prepare_kernel(
    cells_s,
    cells_g,
    cells_r,
    owner_ref,
    ids_hbm,
    frac_hbm,
    table_hbm,
    q_ref,
    fr_ref,
    xs_ref,
    xg_ref,
    moves_ref,
    chosen_ref,
    count_ref,
    ids_ref,
    frac_ref,
    table_ref,
    turned,
    picked,
    keys,
    frs,
    xss,
    xgs,
    order,
    arrived,
):
    copies = [pltpu.make_async_copy(ids_hbm, ids_ref, arrived.at[0])]
    for d in range(3):
        copies.append(pltpu.make_async_copy(frac_hbm.at[d], frac_ref.at[d], arrived.at[1 + d]))
    copies.append(pltpu.make_async_copy(table_hbm, table_ref, arrived.at[4]))
    for copy in copies:
        copy.start()
    stream_first = lax.axis_index("stream") * cells_s
    me = lax.axis_index("girth")
    sectors = owner_ref.shape[0]
    azimuths = ids_ref.shape[1]
    width = azimuths // sectors
    rows = fr_ref.shape[0]
    pad = moves_ref.shape[0] - rows
    passes = network(rows)
    valid = 1 << SHIFT - 1

    def listed(number, count):
        order[jnp.minimum(count, rows // width)] = number
        return count + (owner_ref[number] == me).astype(jnp.int32)

    owned = lax.fori_loop(0, sectors, listed, jnp.int32(0), unroll=8)

    for d in range(4):
        picked[d] = jnp.full(picked.shape[1:], -1.0 if d == 0 else 0.0, jnp.float32)
    chosen_ref[...] = jnp.zeros_like(chosen_ref)
    beyond = pl.ds(rows, pad)
    for slot in range(2):
        keys[slot, beyond, :] = jnp.zeros((pad, LANES), jnp.int32)
    moves_ref[0:pad, :] = jnp.zeros((pad, LANES), jnp.int32)
    for d in range(4):
        copies[d].wait()
        for at in range(0, azimuths, LANES):
            cols = pl.ds(at, LANES)
            plane = ids_ref[:, cols].astype(jnp.float32) if d == 0 else frac_ref[d - 1, :, cols]
            turned[d, cols, :] = plane.T
    copies[4].wait()

    def sector(place, carry):
        source = pl.ds(pl.multiple_of(order[place] * width, width), width)
        target = pl.ds(pl.multiple_of(place * width, width), width)
        chosen_ref[target, :] = table_ref[source, :]
        for d in range(4):
            picked[d, target, :] = turned[d, source, :]
        return carry

    lax.fori_loop(0, owned, sector, jnp.int32(0))

    held = pl.ds(0, rows)
    ids = picked[0].astype(jnp.int32)
    stream_cell, rest = split(jnp.maximum(ids, 0), cells_g * cells_r)
    girth_cell, radial_cell = split(rest, cells_r)
    xs = (stream_cell - stream_first).astype(jnp.float32) + picked[1]
    kept = (ids >= 0) & (xs > -1.0) & (xs < float(cells_s))
    xss[0, held, :] = xs
    xgs[0, held, :] = girth_cell.astype(jnp.float32) + picked[2]
    frs[0, held, :] = picked[3]
    earlier = lax.broadcasted_iota(jnp.int32, (rows, rows), 0) > lax.broadcasted_iota(
        jnp.int32, (rows, rows), 1
    )
    earlier = earlier.astype(jnp.float32).astype(jnp.bfloat16)
    skipped = jnp.where(kept, 0.0, 1.0)
    before = jnp.dot(
        earlier, skipped.astype(jnp.bfloat16), preferred_element_type=jnp.float32
    ).astype(jnp.int32)
    counts = rows - jnp.sum(skipped, axis=0, keepdims=True).astype(jnp.int32)
    count_ref[0] = jnp.max(counts)
    moves_ref[pad : pad + rows, :] = jnp.where(kept, valid, 0)
    keys[0, held, :] = (radial_cell << SHIFT) + jnp.where(kept, before, 0)
    for number, (low, digits) in enumerate(passes):
        a, b = number % 2, 1 - number % 2
        mask = digits - 1 << low
        last = number == len(passes) - 1
        for at in range(0, rows, CHUNK):
            here, target = pl.ds(at, CHUNK), pl.ds(pad + at, CHUNK)
            there = [pl.ds(at + (k << low), CHUNK) for k in range(1, digits)]
            key = keys[a, here, :]
            arriving = [keys[a, t, :] for t in there]
            moved = [(arriving[k] & mask) == (k + 1 << low) for k in range(digits - 1)]
            key = jnp.where((key & mask) != 0, key & -(1 << SHIFT), key)
            came = moves_ref[target, :]
            out = [r[a, here, :] for r in (frs, xss, xgs)]
            for k in range(digits - 1):
                key = jnp.where(moved[k], arriving[k], key)
                came = came | jnp.where(moved[k], k + 1 << low, 0)
                out = [
                    jnp.where(moved[k], r[a, there[k], :], o) for r, o in zip((frs, xss, xgs), out)
                ]
            moves_ref[target, :] = came
            if last:
                q_ref[here, :] = key >> SHIFT
                fr_ref[here, :] = out[0]
                xs_ref[here, :] = out[1]
                xg_ref[here, :] = out[2]
            else:
                keys[b, here, :] = key
                frs[b, here, :] = out[0]
                xss[b, here, :] = out[1]
                xgs[b, here, :] = out[2]


def prepare(owners, corner_ids, fractions, table, cells, girth_count):
    cells_s, cells_g, cells_r = cells
    radii, azimuths = corner_ids.shape
    sectors = owners.shape[0]
    rows = 3 * sectors // girth_count * (azimuths // sectors)
    pad = reach(rows)
    shape = jax.ShapeDtypeStruct
    lists = (rows, radii)
    vmem = pl.BlockSpec(memory_space=pltpu.VMEM)
    smem = pl.BlockSpec(memory_space=pltpu.SMEM)
    hbm = pl.BlockSpec(memory_space=pltpu.HBM)
    return pl.pallas_call(
        functools.partial(prepare_kernel, cells_s, cells_g, cells_r),
        out_shape=(
            shape(lists, jnp.int32),
            shape(lists, jnp.float32),
            shape(lists, jnp.float32),
            shape(lists, jnp.float32),
            shape((pad + rows, radii), jnp.int32),
            shape((rows, 2 * NH), jnp.float32),
            shape((1,), jnp.int32),
        ),
        in_specs=[smem, hbm, hbm, hbm],
        out_specs=[vmem] * 6 + [smem],
        scratch_shapes=[
            pltpu.VMEM(corner_ids.shape, jnp.int32),
            pltpu.VMEM(fractions.shape, jnp.float32),
            pltpu.VMEM(table.shape, jnp.float32),
            pltpu.VMEM((4, azimuths, radii), jnp.float32),
            pltpu.VMEM((4, rows, radii), jnp.float32),
            pltpu.VMEM((2, rows + pad, radii), jnp.int32),
        ]
        + [pltpu.VMEM((2, rows + pad, radii), jnp.float32)] * 3
        + [pltpu.SMEM((rows // (azimuths // sectors) + 1,), jnp.int32)]
        + [pltpu.SemaphoreType.DMA((5,))],
        compiler_params=pltpu.CompilerParams(vmem_limit_bytes=VMEM_LIMIT),
        cost_estimate=pl.CostEstimate(
            flops=20 * radii * azimuths, bytes_accessed=44 * radii * azimuths, transcendentals=0
        ),
        name="prepare_points",
    )(*(in_hbm(x) for x in (owners, corner_ids, fractions, table)))


def radial(values, amount, fill):
    extent = values.shape[-1]
    rolled = pltpu.roll(values, (-amount) % extent, values.ndim - 1)
    position = lax.broadcasted_iota(jnp.int32, values.shape, values.ndim - 1) + amount
    return jnp.where((position >= 0) & (position < extent), rolled, fill)


def advance(own, before, after, left, right, ext_ref, visc_ref):
    cells_s, cells_g, _ = own[0].shape
    mid = ROWS

    def along_s(stack, amount):
        return stack[2 + amount : 2 + amount + cells_s]

    def along_g(ref, amount):
        return ref[:, mid + amount : mid + amount + cells_g, :]

    def viscosity(energy, rate):
        return base_viscosity + energy / (rate + wall_rate)

    stacks = [jnp.concatenate([before[f], own[f], after[f]], axis=0) for f in range(6)]
    for f in range(6):
        ext_ref[f, :, mid - 2 : mid, :] = left[f]
        ext_ref[f, :, mid : mid + cells_g, :] = own[f]
        ext_ref[f, :, mid + cells_g : mid + cells_g + 2, :] = right[f]
    middle = viscosity(own[4], own[5])
    visc_stack = viscosity(stacks[4], stacks[5])
    visc_ref[:, mid - 2 : mid, :] = viscosity(left[4], left[5])
    visc_ref[:, mid : mid + cells_g, :] = middle
    visc_ref[:, mid + cells_g : mid + cells_g + 2, :] = viscosity(right[4], right[5])
    faces = [
        (
            0.5 * (middle + along_s(visc_stack, 1)),
            0.5 * (middle + along_s(visc_stack, -1)),
        ),
        (
            0.5 * (middle + along_g(visc_ref, 1)),
            0.5 * (middle + along_g(visc_ref, -1)),
        ),
        (
            0.5 * (middle + radial(middle, 1, base_viscosity)),
            0.5 * (middle + radial(middle, -1, base_viscosity)),
        ),
    ]

    def neighbour(f, direction, amount):
        if direction == 0:
            return along_s(stacks[f], amount)
        if direction == 1:
            return along_g(ext_ref.at[f], amount)
        return radial(own[f], amount, 0.0)

    def terms(f, direction):
        up, down = neighbour(f, direction, 1), neighbour(f, direction, -1)
        far = neighbour(f, direction, 2) - neighbour(f, direction, -2)
        gradient = (8.0 * (up - down) - far) * (1.0 / 12.0)
        above, below = faces[direction]
        return gradient, above * (up - own[f]) - below * (own[f] - down)

    strain = None
    updated = []
    for f in range(3):
        change = -terms(3, f)[0]
        for direction in range(3):
            gradient, spread = terms(f, direction)
            strain = gradient * gradient if strain is None else strain + gradient * gradient
            change = change - own[direction] * gradient + spread
        updated.append(own[f] + time_step * change)
    energy = own[4] / (own[5] + wall_rate) * strain - beta_star * own[4] * own[5]
    rate = alpha_rate * strain - beta_rate * own[5] * own[5]
    for direction in range(3):
        gradient, spread = terms(4, direction)
        energy = energy - own[direction] * gradient + spread
        gradient, spread = terms(5, direction)
        rate = rate - own[direction] * gradient + spread
    return updated, own[4] + time_step * energy, own[5] + time_step * rate


def girth_sums(parts):
    row = lax.broadcasted_iota(jnp.int32, parts[0].shape, 0)

    def swapped(values, distance):
        up = pltpu.roll(values, distance, 0)
        if 2 * distance == ROWS:
            return up
        return jnp.where((row & distance) != 0, up, pltpu.roll(values, ROWS - distance, 0))

    distance = ROWS // 2
    while distance > 0:
        low = (row & distance) == 0
        parts = [
            jnp.where(low, x, y) + swapped(jnp.where(low, y, x), distance)
            for x, y in zip(parts[:distance], parts[distance:])
        ]
        distance //= 2
    return parts[0]


def section_kernel(
    devices,
    count_ref,
    vel_ref,
    p_ref,
    k_ref,
    w_ref,
    stream_a,
    stream_b,
    girth_a,
    girth_b,
    q_ref,
    fr_ref,
    xs_ref,
    xg_ref,
    moves_ref,
    chosen_ref,
    new_vel_hbm,
    new_k_hbm,
    new_w_hbm,
    keep_ref,
    give_ref,
    new_vel_ref,
    new_k_ref,
    new_w_ref,
    ext_ref,
    visc_ref,
    field_ref,
    gather_ref,
    value_ref,
    disk_ref,
    harm_ref,
    stored,
):
    cells_s, cells_g, cells_r = p_ref.shape
    rows = fr_ref.shape[0]
    pad = moves_ref.shape[0] - rows
    passes = network(rows)
    valid = 1 << SHIFT - 1
    stream_odd = lax.axis_index("stream") % 2 == 1
    girth_odd = lax.axis_index("girth") % 2 == 1

    own = [vel_ref[0], vel_ref[1], vel_ref[2], p_ref[...], k_ref[...], w_ref[...]]
    six = range(6)
    updated, energy, rate = advance(
        own,
        [jnp.where(stream_odd, stream_a[f], stream_b[f]) for f in six],
        [jnp.where(stream_odd, stream_b[f], stream_a[f]) for f in six],
        [jnp.where(girth_odd, girth_a[f], girth_b[f]) for f in six],
        [jnp.where(girth_odd, girth_b[f], girth_a[f]) for f in six],
        ext_ref,
        visc_ref,
    )
    new_k_ref[...] = energy
    new_w_ref[...] = rate

    def halved(values):
        high = values.astype(jnp.bfloat16)
        return high, (values - high.astype(jnp.float32)).astype(jnp.bfloat16)

    def rounded(values):
        return values.astype(jnp.bfloat16).astype(jnp.float32)

    halves = cells_r // LANES
    for c in range(3):
        new_vel_ref[c] = updated[c]
        slope = radial(updated[c], 1, 0.0) - updated[c]
        for kind, values in enumerate((updated[c], slope)):
            if c < PRODUCTS:
                high = rounded(values)
                field_ref[c, :, 2 * kind] = high
                field_ref[c, :, 2 * kind + 1] = rounded(values - high)
            else:
                for h in range(halves):
                    lanes = slice(h * LANES, (h + 1) * LANES)
                    gather_ref[c - PRODUCTS, :, kind, h] = values[:, :, lanes]
    results = ((new_vel_ref, new_vel_hbm), (new_k_ref, new_k_hbm), (new_w_ref, new_w_hbm))
    copies = [
        pltpu.make_async_copy(source, target, stored.at[i])
        for i, (source, target) in enumerate(results)
    ]
    for copy in copies:
        copy.start()

    kinds = 4
    table = field_ref[...].reshape(PRODUCTS * cells_s * kinds * cells_g, cells_r)
    table = table.astype(jnp.bfloat16)
    pair = 2 * LANES
    girth_row = lax.broadcasted_iota(jnp.int32, (cells_g, pair), 0).astype(jnp.float32)
    index_type = jnp.bfloat16 if cells_r <= 256 else jnp.float32
    radial_row = lax.broadcasted_iota(jnp.int32, (cells_r, pair), 0).astype(jnp.float32)
    radial_row = radial_row.astype(index_type)
    one, none = jnp.ones((), jnp.bfloat16), jnp.zeros((), jnp.bfloat16)

    def two(values, j):
        return jnp.concatenate([values[j : j + 1], values[j + 1 : j + 2]], axis=1)

    def spread(values, j):
        return jnp.broadcast_to(values[j : j + 1], (cells_g, LANES))

    def pick(c, s, kind, index, half_of):
        out = None
        for h in range(halves):
            got = jnp.take_along_axis(
                gather_ref[c - PRODUCTS, s, kind, h], index, axis=1, mode="promise_in_bounds"
            )
            out = got if out is None else jnp.where(half_of[h], got, out)
        return out

    def eight(at):
        here = pl.ds(at, ROWS)
        q8, fr8, xg8, xs8 = (r[here, :] for r in (q_ref, fr_ref, xg_ref, xs_ref))
        hs8 = [jnp.maximum(1.0 - jnp.abs(xs8 - float(s)), 0.0) for s in range(cells_s)]
        index8 = q8 & (LANES - 1)
        qf8 = q8.astype(jnp.float32)
        sums = [[], [], []]
        for j in range(0, ROWS, 2):
            chosen_q = jnp.broadcast_to(two(qf8, j), (cells_r, pair)).astype(index_type)
            hot = jnp.where(radial_row == chosen_q, one, none)
            got = jnp.dot(table, hot, preferred_element_type=jnp.float32)
            got = got.reshape(PRODUCTS, cells_s, kinds, cells_g, pair)
            fr = two(fr8, j)
            hg = jnp.maximum(1.0 - jnp.abs(two(xg8, j) - girth_row), 0.0)
            hs = [two(hs8[s], j) for s in range(cells_s)]
            for c in range(PRODUCTS):
                total = None
                for s in range(cells_s):
                    value = got[c, s, 0] + got[c, s, 1] + fr * (got[c, s, 2] + got[c, s, 3])
                    value = hs[s] * value
                    total = value if total is None else total + value
                total = hg * total
                sums[c] += [total[:, :LANES], total[:, LANES:]]
            for i in (j, j + 1):
                index, q = spread(index8, i), spread(q8, i)
                half_of = [q >= h * LANES for h in range(halves)]
                own_hg = hg[:, (i - j) * LANES : (i - j + 1) * LANES]
                for c in range(PRODUCTS, 3):
                    total = None
                    for s in range(cells_s):
                        value = pick(c, s, 0, index, half_of)
                        value = value + fr8[i : i + 1] * pick(c, s, 1, index, half_of)
                        value = hs8[s][i : i + 1] * value
                        total = value if total is None else total + value
                    sums[c].append(own_hg * total)
        for c in range(3):
            value_ref[0, c, pl.ds(pad + at, ROWS), :] = girth_sums(sums[c])

    def step(group, carry):
        for part in range(2):
            eight(pl.multiple_of((2 * group + part) * ROWS, ROWS))
        return carry

    lax.fori_loop(0, (count_ref[0] + 2 * ROWS - 1) // (2 * ROWS), step, jnp.int32(0))

    for number, (low, digits) in enumerate(reversed(passes)):
        a, b = number % 2, 1 - number % 2
        mask = digits - 1 << low
        last = number == len(passes) - 1
        for at in range(0, rows, CHUNK):
            here = pl.ds(pad + at, CHUNK)
            there = [pl.ds(pad + at - (k << low), CHUNK) for k in range(1, digits)]
            moved = [(moves_ref[there[k], :] & mask) == (k + 1 << low) for k in range(digits - 1)]
            if last:
                kept = (moves_ref[here, :] & valid) != 0
            for c in range(3):
                value = value_ref[a, c, here, :]
                for k in range(digits - 1):
                    value = jnp.where(moved[k], value_ref[a, c, there[k], :], value)
                if last:
                    disk_ref[c, pl.ds(at, CHUNK), :] = jnp.where(kept, value, 0.0)
                else:
                    value_ref[b, c, here, :] = value

    turned = jnp.concatenate([disk_ref[c].T for c in range(3)], axis=0)
    high, low = halved(turned)
    wave_high, wave_low = halved(chosen_ref[...])
    waves = jnp.dot(high, wave_high, preferred_element_type=jnp.float32)
    waves += jnp.dot(high, wave_low, preferred_element_type=jnp.float32)
    waves += jnp.dot(low, wave_high, preferred_element_type=jnp.float32)
    radii = harm_ref.shape[0]
    for c in range(3):
        harm_ref[:, c * 2 * NH : (c + 1) * 2 * NH] = waves[c * radii : (c + 1) * radii]
    block = radii // devices
    for place in range(devices // 2):
        even = harm_ref[2 * place * block : (2 * place + 1) * block, :]
        odd = harm_ref[(2 * place + 1) * block : (2 * place + 2) * block, :]
        keep_ref[place * block : (place + 1) * block, :] = jnp.where(girth_odd, odd, even)
        give_ref[place * block : (place + 1) * block, :] = jnp.where(girth_odd, even, odd)
    for copy in copies:
        copy.wait()


def section(velocity, pressure, energy, rate, halos, points, devices):
    _, cells_s, cells_g, cells_r = velocity.shape
    *lists, moves, chosen, counts = points
    rows, radii = lists[0].shape
    shape = functools.partial(jax.ShapeDtypeStruct, dtype=jnp.float32)
    scratch = lambda *dims: pltpu.VMEM(dims, jnp.float32)
    vmem = pl.BlockSpec(memory_space=pltpu.VMEM)
    smem = pl.BlockSpec(memory_space=pltpu.SMEM)
    return pl.pallas_call(
        functools.partial(section_kernel, devices),
        out_shape=(
            shape(velocity.shape),
            shape(energy.shape),
            shape(rate.shape),
            shape((radii // 2, 6 * NH)),
            shape((radii // 2, 6 * NH)),
        ),
        in_specs=[smem] + [vmem] * 14,
        out_specs=[pl.BlockSpec(memory_space=pl.ANY)] * 3 + [vmem] * 2,
        scratch_shapes=[
            scratch(*velocity.shape),
            scratch(*energy.shape),
            scratch(*rate.shape),
            scratch(6, cells_s, 3 * ROWS, cells_r),
            scratch(cells_s, 3 * ROWS, cells_r),
            scratch(PRODUCTS, cells_s, 4, cells_g, cells_r),
            scratch(max(1, 3 - PRODUCTS), cells_s, 2, cells_r // LANES, cells_g, LANES),
            scratch(2, 3, moves.shape[0], radii),
            scratch(3, rows, radii),
            scratch(radii, 6 * NH),
            pltpu.SemaphoreType.DMA((3,)),
        ],
        compiler_params=pltpu.CompilerParams(vmem_limit_bytes=VMEM_LIMIT),
        name="section_and_disk",
    )(counts, velocity, pressure, energy, rate, *halos, *lists, moves, chosen)


def fourier_table(azimuths, modes):
    phase = np.arange(azimuths)[:, None] * np.arange(modes)[None, :] % azimuths
    angles = phase * (2.0 * math.pi / azimuths)
    table = np.concatenate([np.cos(angles), -np.sin(angles)], axis=1) / math.sqrt(azimuths)
    return jnp.asarray(table.astype(np.float32))


def body(velocity, pressure, kinetic_energy, dissipation_rate, corner_ids, fractions, sector_owner):
    _, cells_s, cells_g, cells_r = velocity.shape
    radii, azimuths = corner_ids.shape
    stream_count, girth_count = lax.axis_size("stream"), lax.axis_size("girth")
    devices = stream_count * girth_count

    def swap(values, axis, count, start):
        pairs = []
        for i in range(start, count - 1, 2):
            pairs += [(i, i + 1), (i + 1, i)]
        return lax.ppermute(values, axis, pairs)

    slabs = pack(velocity, pressure, kinetic_energy, dissipation_rate)
    girth_halos = (
        swap(slabs[2], "girth", girth_count, 0),
        swap(slabs[3], "girth", girth_count, 1),
    )
    stream_halos = (
        swap(slabs[0], "stream", stream_count, 0),
        swap(slabs[1], "stream", stream_count, 1),
    )
    halos = stream_halos + girth_halos
    points = prepare(
        sector_owner[:, 0],
        corner_ids,
        fractions,
        fourier_table(azimuths, NH),
        (cells_s, cells_g, cells_r),
        girth_count,
    )
    new_velocity, new_energy, new_rate, keep, give = section(
        velocity, pressure, kinetic_energy, dissipation_rate, halos, points, devices
    )
    total = keep + swap(give, "girth", girth_count, 0)
    shares = lax.all_to_all(
        total.reshape(devices // 2, radii // devices, 6 * NH),
        ("stream", "girth"),
        split_axis=0,
        concat_axis=0,
        tiled=True,
        axis_index_groups=[list(range(parity, devices, 2)) for parity in (0, 1)],
    )
    return new_velocity, new_energy, new_rate, jnp.sum(shares, axis=0)


def solution(mesh):
    return jax.shard_map(
        body,
        mesh=mesh,
        in_specs=(
            P(None, "stream", "girth", None),
            P("stream", "girth", None),
            P("stream", "girth", None),
            P("stream", "girth", None),
            P(),
            P(),
            P(),
        ),
        out_specs=(
            P(None, "stream", "girth", None),
            P("stream", "girth", None),
            P("stream", "girth", None),
            P(("stream", "girth"), None),
        ),
        check_vma=False,
    )
```

```python
import functools
import math

import jax
import jax.numpy as jnp
import numpy as np
from jax import lax
from jax.experimental import pallas as pl
from jax.experimental.pallas import tpu as pltpu
from jax.sharding import PartitionSpec as P

NH = 128

base_viscosity = 0.05
time_step = 0.2
beta_star = 0.09
beta_rate = 0.075
alpha_rate = 0.52
wall_rate = 1.0

LANES = 128
ROWS = 8
SHIFT = 10
CHUNK = 32
PRODUCTS = 6
VMEM_LIMIT = 48 * 1024 * 1024


def in_hbm(values):
    return pltpu.with_memory_space_constraint(values, pltpu.HBM)


def pack_kernel(vel_ref, p_ref, k_ref, w_ref, *slabs):
    cells_s, cells_g, _ = p_ref.shape
    stream_odd = lax.axis_index("stream") % 2 == 1
    girth_odd = lax.axis_index("girth") % 2 == 1
    for f in range(6):
        own = vel_ref.at[f] if f < 3 else (p_ref, k_ref, w_ref)[f - 3]
        first, last = own[0:2], own[cells_s - 2 : cells_s]
        slabs[0][f] = jnp.where(stream_odd, first, last)
        slabs[1][f] = jnp.where(stream_odd, last, first)
        first, last = own[:, 0:2, :], own[:, cells_g - 2 : cells_g, :]
        slabs[2][f] = jnp.where(girth_odd, first, last)
        slabs[3][f] = jnp.where(girth_odd, last, first)


def pack(velocity, pressure, energy, rate):
    _, cells_s, cells_g, cells_r = velocity.shape
    stream = pltpu.VMEM((6, 2, cells_g, cells_r), jnp.float32)
    girth = pltpu.VMEM((6, cells_s, 2, cells_r), jnp.float32)
    vmem = pl.BlockSpec(memory_space=pltpu.VMEM)
    return pl.pallas_call(
        pack_kernel,
        out_shape=(stream, stream, girth, girth),
        in_specs=[vmem] * 4,
        out_specs=[vmem] * 4,
        name="pack_halos",
    )(*(in_hbm(x) for x in (velocity, pressure, energy, rate)))


def network(rows):
    steps = (rows - 1).bit_length()
    return [(low, 1 << min(2, steps - low)) for low in range(0, steps, 2)]


def reach(rows):
    return max((digits - 1) << low for low, digits in network(rows))


def split(values, size):
    if size & (size - 1) == 0:
        return values >> (size.bit_length() - 1), values & (size - 1)
    return values // size, values % size


def prepare_kernel(
    cells_s,
    cells_g,
    cells_r,
    owner_ref,
    ids_hbm,
    frac_hbm,
    table_hbm,
    key_ref,
    fr_ref,
    xs_ref,
    xg_ref,
    moves_ref,
    chosen_ref,
    count_ref,
    ids_ref,
    frac_ref,
    table_ref,
    turned,
    picked,
    order,
    arrived,
):
    copies = [pltpu.make_async_copy(ids_hbm, ids_ref, arrived.at[0])]
    for d in range(3):
        copies.append(pltpu.make_async_copy(frac_hbm.at[d], frac_ref.at[d], arrived.at[1 + d]))
    copies.append(pltpu.make_async_copy(table_hbm, table_ref, arrived.at[4]))
    for copy in copies:
        copy.start()
    stream_first = lax.axis_index("stream") * cells_s
    me = lax.axis_index("girth")
    sectors = owner_ref.shape[0]
    azimuths = ids_ref.shape[1]
    width = azimuths // sectors
    rows = chosen_ref.shape[0]
    pad = moves_ref.shape[0] - rows
    passes = network(rows)
    valid = 1 << SHIFT - 1

    def listed(number, count):
        order[jnp.minimum(count, rows // width)] = number
        return count + (owner_ref[number] == me).astype(jnp.int32)

    owned = lax.fori_loop(0, sectors, listed, jnp.int32(0), unroll=8)

    for d in range(4):
        picked[d] = jnp.full(picked.shape[1:], -1.0 if d == 0 else 0.0, jnp.float32)
    chosen_ref[...] = jnp.zeros_like(chosen_ref)
    key_ref[rows : rows + pad, :] = jnp.zeros((pad, LANES), jnp.int32)
    moves_ref[0:pad, :] = jnp.zeros((pad, LANES), jnp.int32)
    for d in range(4):
        copies[d].wait()
        for at in range(0, azimuths, LANES):
            cols = pl.ds(at, LANES)
            plane = ids_ref[:, cols].astype(jnp.float32) if d == 0 else frac_ref[d - 1, :, cols]
            turned[d, cols, :] = plane.T
    copies[4].wait()

    def sector(place, carry):
        source = pl.ds(pl.multiple_of(order[place] * width, width), width)
        target = pl.ds(pl.multiple_of(place * width, width), width)
        chosen_ref[target, :] = table_ref[source, :]
        for d in range(4):
            picked[d, target, :] = turned[d, source, :]
        return carry

    lax.fori_loop(0, owned, sector, jnp.int32(0))

    held = pl.ds(0, rows)
    ids = picked[0].astype(jnp.int32)
    stream_cell, rest = split(jnp.maximum(ids, 0), cells_g * cells_r)
    girth_cell, radial_cell = split(rest, cells_r)
    xs = (stream_cell - stream_first).astype(jnp.float32) + picked[1]
    kept = (ids >= 0) & (xs > -1.0) & (xs < float(cells_s))
    xs_ref[held, :] = xs
    xg_ref[held, :] = girth_cell.astype(jnp.float32) + picked[2]
    fr_ref[held, :] = picked[3]
    earlier = lax.broadcasted_iota(jnp.int32, (rows, rows), 0) > lax.broadcasted_iota(
        jnp.int32, (rows, rows), 1
    )
    earlier = earlier.astype(jnp.float32).astype(jnp.bfloat16)
    skipped = jnp.where(kept, 0.0, 1.0)
    before = jnp.dot(
        earlier, skipped.astype(jnp.bfloat16), preferred_element_type=jnp.float32
    ).astype(jnp.int32)
    counts = rows - jnp.sum(skipped, axis=0, keepdims=True).astype(jnp.int32)
    count_ref[0] = jnp.max(counts)
    moves_ref[pad : pad + rows, :] = jnp.where(kept, valid, 0)
    key_ref[held, :] = (radial_cell << SHIFT) + jnp.where(kept, before, 0)
    for low, digits in passes:
        mask = digits - 1 << low
        for at in range(0, rows, CHUNK):
            here, target = pl.ds(at, CHUNK), pl.ds(pad + at, CHUNK)
            there = {k: pl.ds(at + (k << low), CHUNK) for k in range(1, digits) if at + (k << low) < rows}
            if not there and (low, digits) == passes[-1]:
                continue
            key = key_ref[here, :]
            arriving = {k: key_ref[t, :] for k, t in there.items()}
            moved = {k: (arriving[k] & mask) == k << low for k in there}
            key = jnp.where((key & mask) != 0, key & -(1 << SHIFT), key)
            for k in there:
                key = jnp.where(moved[k], arriving[k], key)
            key_ref[here, :] = key
            if there:
                came = moves_ref[target, :]
                for k in there:
                    came = came | jnp.where(moved[k], k << low, 0)
                moves_ref[target, :] = came
                for ref in (fr_ref, xs_ref, xg_ref):
                    value = ref[here, :]
                    for k, t in there.items():
                        value = jnp.where(moved[k], ref[t, :], value)
                    ref[here, :] = value


def prepare(owners, corner_ids, fractions, table, cells, girth_count):
    cells_s, cells_g, cells_r = cells
    radii, azimuths = corner_ids.shape
    sectors = owners.shape[0]
    rows = 3 * sectors // girth_count * (azimuths // sectors)
    pad = reach(rows)
    shape = jax.ShapeDtypeStruct
    lists = (rows + pad, radii)
    vmem = pl.BlockSpec(memory_space=pltpu.VMEM)
    smem = pl.BlockSpec(memory_space=pltpu.SMEM)
    hbm = pl.BlockSpec(memory_space=pltpu.HBM)
    return pl.pallas_call(
        functools.partial(prepare_kernel, cells_s, cells_g, cells_r),
        out_shape=(
            shape(lists, jnp.int32),
            shape(lists, jnp.float32),
            shape(lists, jnp.float32),
            shape(lists, jnp.float32),
            shape((pad + rows, radii), jnp.int32),
            shape((rows, 2 * NH), jnp.float32),
            shape((1,), jnp.int32),
        ),
        in_specs=[smem, hbm, hbm, hbm],
        out_specs=[vmem] * 6 + [smem],
        scratch_shapes=[
            pltpu.VMEM(corner_ids.shape, jnp.int32),
            pltpu.VMEM(fractions.shape, jnp.float32),
            pltpu.VMEM(table.shape, jnp.float32),
            pltpu.VMEM((4, azimuths, radii), jnp.float32),
            pltpu.VMEM((4, rows, radii), jnp.float32),
        ]
        + [pltpu.SMEM((rows // (azimuths // sectors) + 1,), jnp.int32)]
        + [pltpu.SemaphoreType.DMA((5,))],
        compiler_params=pltpu.CompilerParams(vmem_limit_bytes=VMEM_LIMIT),
        cost_estimate=pl.CostEstimate(
            flops=20 * radii * azimuths, bytes_accessed=44 * radii * azimuths, transcendentals=0
        ),
        name="prepare_points",
    )(*(in_hbm(x) for x in (owners, corner_ids, fractions, table)))


def radial(values, amount, fill):
    extent = values.shape[-1]
    rolled = pltpu.roll(values, (-amount) % extent, values.ndim - 1)
    position = lax.broadcasted_iota(jnp.int32, values.shape, values.ndim - 1) + amount
    return jnp.where((position >= 0) & (position < extent), rolled, fill)


def advance(own, before, after, left, right, ext_ref, visc_ref):
    cells_s, cells_g, _ = own[0].shape
    mid = ROWS

    def along_s(stack, amount):
        return stack[2 + amount : 2 + amount + cells_s]

    def along_g(ref, amount):
        return ref[:, mid + amount : mid + amount + cells_g, :]

    def viscosity(energy, rate):
        return base_viscosity + energy / (rate + wall_rate)

    stacks = [jnp.concatenate([before[f], own[f], after[f]], axis=0) for f in range(6)]
    for f in range(6):
        ext_ref[f, :, mid - 2 : mid, :] = left[f]
        ext_ref[f, :, mid : mid + cells_g, :] = own[f]
        ext_ref[f, :, mid + cells_g : mid + cells_g + 2, :] = right[f]
    middle = viscosity(own[4], own[5])
    visc_stack = viscosity(stacks[4], stacks[5])
    visc_ref[:, mid - 2 : mid, :] = viscosity(left[4], left[5])
    visc_ref[:, mid : mid + cells_g, :] = middle
    visc_ref[:, mid + cells_g : mid + cells_g + 2, :] = viscosity(right[4], right[5])
    faces = [
        (
            0.5 * (middle + along_s(visc_stack, 1)),
            0.5 * (middle + along_s(visc_stack, -1)),
        ),
        (
            0.5 * (middle + along_g(visc_ref, 1)),
            0.5 * (middle + along_g(visc_ref, -1)),
        ),
        (
            0.5 * (middle + radial(middle, 1, base_viscosity)),
            0.5 * (middle + radial(middle, -1, base_viscosity)),
        ),
    ]

    def neighbour(f, direction, amount):
        if direction == 0:
            return along_s(stacks[f], amount)
        if direction == 1:
            return along_g(ext_ref.at[f], amount)
        return radial(own[f], amount, 0.0)

    def terms(f, direction):
        up, down = neighbour(f, direction, 1), neighbour(f, direction, -1)
        far = neighbour(f, direction, 2) - neighbour(f, direction, -2)
        gradient = (8.0 * (up - down) - far) * (1.0 / 12.0)
        above, below = faces[direction]
        return gradient, above * (up - own[f]) - below * (own[f] - down)

    strain = None
    updated = []
    for f in range(3):
        change = -terms(3, f)[0]
        for direction in range(3):
            gradient, spread = terms(f, direction)
            strain = gradient * gradient if strain is None else strain + gradient * gradient
            change = change - own[direction] * gradient + spread
        updated.append(own[f] + time_step * change)
    energy = own[4] / (own[5] + wall_rate) * strain - beta_star * own[4] * own[5]
    rate = alpha_rate * strain - beta_rate * own[5] * own[5]
    for direction in range(3):
        gradient, spread = terms(4, direction)
        energy = energy - own[direction] * gradient + spread
        gradient, spread = terms(5, direction)
        rate = rate - own[direction] * gradient + spread
    return updated, own[4] + time_step * energy, own[5] + time_step * rate


def girth_sums(parts):
    row = lax.broadcasted_iota(jnp.int32, parts[0].shape, 0)

    def swapped(values, distance):
        up = pltpu.roll(values, distance, 0)
        if 2 * distance == ROWS:
            return up
        return jnp.where((row & distance) != 0, up, pltpu.roll(values, ROWS - distance, 0))

    distance = ROWS // 2
    while distance > 0:
        low = (row & distance) == 0
        parts = [
            jnp.where(low, x, y) + swapped(jnp.where(low, y, x), distance)
            for x, y in zip(parts[:distance], parts[distance:])
        ]
        distance //= 2
    return parts[0]


def section_kernel(
    devices,
    count_ref,
    vel_ref,
    p_ref,
    k_ref,
    w_ref,
    stream_a,
    stream_b,
    girth_a,
    girth_b,
    key_ref,
    fr_ref,
    xs_ref,
    xg_ref,
    moves_ref,
    chosen_ref,
    new_vel_hbm,
    new_k_hbm,
    new_w_hbm,
    keep_ref,
    give_ref,
    new_vel_ref,
    new_k_ref,
    new_w_ref,
    ext_ref,
    visc_ref,
    field_ref,
    gather_ref,
    value_ref,
    disk_ref,
    harm_ref,
    stored,
):
    cells_s, cells_g, cells_r = p_ref.shape
    rows = chosen_ref.shape[0]
    pad = moves_ref.shape[0] - rows
    passes = network(rows)
    valid = 1 << SHIFT - 1
    stream_odd = lax.axis_index("stream") % 2 == 1
    girth_odd = lax.axis_index("girth") % 2 == 1

    own = [vel_ref[0], vel_ref[1], vel_ref[2], p_ref[...], k_ref[...], w_ref[...]]
    six = range(6)
    updated, energy, rate = advance(
        own,
        [jnp.where(stream_odd, stream_a[f], stream_b[f]) for f in six],
        [jnp.where(stream_odd, stream_b[f], stream_a[f]) for f in six],
        [jnp.where(girth_odd, girth_a[f], girth_b[f]) for f in six],
        [jnp.where(girth_odd, girth_b[f], girth_a[f]) for f in six],
        ext_ref,
        visc_ref,
    )
    new_k_ref[...] = energy
    new_w_ref[...] = rate

    def halved(values):
        high = values.astype(jnp.bfloat16)
        return high, (values - high.astype(jnp.float32)).astype(jnp.bfloat16)

    def rounded(values):
        return values.astype(jnp.bfloat16).astype(jnp.float32)

    halves = cells_r // LANES
    for c in range(3):
        new_vel_ref[c] = updated[c]
        slope = radial(updated[c], 1, 0.0) - updated[c]
        for kind, values in enumerate((updated[c], slope)):
            for layer in range(cells_s):
                place = c * cells_s + layer
                if place < PRODUCTS:
                    high = rounded(values[layer])
                    field_ref[place, 2 * kind] = high
                    field_ref[place, 2 * kind + 1] = rounded(values[layer] - high)
                else:
                    for h in range(halves):
                        lanes = slice(h * LANES, (h + 1) * LANES)
                        gather_ref[place - PRODUCTS, kind, h] = values[layer, :, lanes]
    results = ((new_vel_ref, new_vel_hbm), (new_k_ref, new_k_hbm), (new_w_ref, new_w_hbm))
    copies = [
        pltpu.make_async_copy(source, target, stored.at[i])
        for i, (source, target) in enumerate(results)
    ]
    for copy in copies:
        copy.start()

    kinds = 4
    table = field_ref[...].reshape(PRODUCTS * kinds * cells_g, cells_r)
    table = table.astype(jnp.bfloat16)
    pair = 2 * LANES
    girth_row = lax.broadcasted_iota(jnp.int32, (cells_g, pair), 0).astype(jnp.float32)
    index_type = jnp.bfloat16 if cells_r <= 256 else jnp.float32
    radial_row = lax.broadcasted_iota(jnp.int32, (cells_r, pair), 0).astype(jnp.float32)
    radial_row = radial_row.astype(index_type)
    one, none = jnp.ones((), jnp.bfloat16), jnp.zeros((), jnp.bfloat16)

    def two(values, j):
        return jnp.concatenate([values[j : j + 1], values[j + 1 : j + 2]], axis=1)

    def spread(values, j):
        return jnp.broadcast_to(values[j : j + 1], (cells_g, LANES))

    def pick(place, kind, index, half_of):
        out = None
        for h in range(halves):
            got = jnp.take_along_axis(
                gather_ref[place - PRODUCTS, kind, h], index, axis=1, mode="promise_in_bounds"
            )
            out = got if out is None else jnp.where(half_of[h], got, out)
        return out

    def eight(at):
        here = pl.ds(at, ROWS)
        key8, fr8, xg8, xs8 = (r[here, :] for r in (key_ref, fr_ref, xg_ref, xs_ref))
        q8 = key8 >> SHIFT
        hs8 = [jnp.maximum(1.0 - jnp.abs(xs8 - float(s)), 0.0) for s in range(cells_s)]
        index8 = q8 & (LANES - 1)
        qf8 = q8.astype(jnp.float32)
        sums = [[], [], []]
        for j in range(0, ROWS, 2):
            chosen_q = jnp.broadcast_to(two(qf8, j), (cells_r, pair)).astype(index_type)
            hot = jnp.where(radial_row == chosen_q, one, none)
            got = jnp.dot(table, hot, preferred_element_type=jnp.float32)
            got = got.reshape(PRODUCTS, kinds, cells_g, pair)
            fr = two(fr8, j)
            hg = jnp.maximum(1.0 - jnp.abs(two(xg8, j) - girth_row), 0.0)
            hs = [two(hs8[s], j) for s in range(cells_s)]
            gathered = []
            for i in (j, j + 1):
                index, q = spread(index8, i), spread(q8, i)
                half_of = [q >= h * LANES for h in range(halves)]
                parts = {}
                for place in range(PRODUCTS, 3 * cells_s):
                    c, s = divmod(place, cells_s)
                    value = pick(place, 0, index, half_of)
                    value = value + fr8[i : i + 1] * pick(place, 1, index, half_of)
                    value = hs8[s][i : i + 1] * value
                    parts[c] = value if c not in parts else parts[c] + value
                gathered.append(parts)
            for c in range(3):
                total = None
                for s in range(cells_s):
                    place = c * cells_s + s
                    if place < PRODUCTS:
                        value = got[place, 0] + got[place, 1] + fr * (got[place, 2] + got[place, 3])
                        value = hs[s] * value
                        total = value if total is None else total + value
                for i in range(2):
                    lanes = slice(i * LANES, (i + 1) * LANES)
                    both = [] if total is None else [total[:, lanes]]
                    if c in gathered[i]:
                        both.append(gathered[i][c])
                    sums[c].append(hg[:, lanes] * sum(both[1:], both[0]))
        for c in range(3):
            value_ref[c, pl.ds(pad + at, ROWS), :] = girth_sums(sums[c])

    def step(group, carry):
        for part in range(2):
            eight(pl.multiple_of((2 * group + part) * ROWS, ROWS))
        return carry

    lax.fori_loop(0, (count_ref[0] + 2 * ROWS - 1) // (2 * ROWS), step, jnp.int32(0))

    for low, digits in reversed(passes):
        mask = digits - 1 << low
        last = (low, digits) == passes[0]
        for at in range(rows - CHUNK, -1, -CHUNK):
            here = pl.ds(pad + at, CHUNK)
            there = {
                k: pl.ds(pad + at - (k << low), CHUNK)
                for k in range(1, digits)
                if at + CHUNK > k << low
            }
            if not there and not last:
                continue
            moved = {k: (moves_ref[t, :] & mask) == k << low for k, t in there.items()}
            if last:
                kept = (moves_ref[here, :] & valid) != 0
            for c in range(3):
                value = value_ref[c, here, :]
                for k, t in there.items():
                    value = jnp.where(moved[k], value_ref[c, t, :], value)
                if last:
                    disk_ref[c, pl.ds(at, CHUNK), :] = jnp.where(kept, value, 0.0)
                else:
                    value_ref[c, here, :] = value

    turned = jnp.concatenate([disk_ref[c].T for c in range(3)], axis=0)
    high, low = halved(turned)
    wave_high, wave_low = halved(chosen_ref[...])
    waves = jnp.dot(high, wave_high, preferred_element_type=jnp.float32)
    waves += jnp.dot(high, wave_low, preferred_element_type=jnp.float32)
    waves += jnp.dot(low, wave_high, preferred_element_type=jnp.float32)
    radii = harm_ref.shape[0]
    for c in range(3):
        harm_ref[:, c * 2 * NH : (c + 1) * 2 * NH] = waves[c * radii : (c + 1) * radii]
    block = radii // devices
    for place in range(devices // 2):
        even = harm_ref[2 * place * block : (2 * place + 1) * block, :]
        odd = harm_ref[(2 * place + 1) * block : (2 * place + 2) * block, :]
        keep_ref[place * block : (place + 1) * block, :] = jnp.where(girth_odd, odd, even)
        give_ref[place * block : (place + 1) * block, :] = jnp.where(girth_odd, even, odd)
    for copy in copies:
        copy.wait()


def section(velocity, pressure, energy, rate, halos, points, devices):
    _, cells_s, cells_g, cells_r = velocity.shape
    *lists, moves, chosen, counts = points
    rows, radii = chosen.shape[0], lists[0].shape[1]
    shape = functools.partial(jax.ShapeDtypeStruct, dtype=jnp.float32)
    scratch = lambda *dims: pltpu.VMEM(dims, jnp.float32)
    vmem = pl.BlockSpec(memory_space=pltpu.VMEM)
    smem = pl.BlockSpec(memory_space=pltpu.SMEM)
    return pl.pallas_call(
        functools.partial(section_kernel, devices),
        out_shape=(
            shape(velocity.shape),
            shape(energy.shape),
            shape(rate.shape),
            shape((radii // 2, 6 * NH)),
            shape((radii // 2, 6 * NH)),
        ),
        in_specs=[smem] + [vmem] * 14,
        out_specs=[pl.BlockSpec(memory_space=pl.ANY)] * 3 + [vmem] * 2,
        scratch_shapes=[
            scratch(*velocity.shape),
            scratch(*energy.shape),
            scratch(*rate.shape),
            scratch(6, cells_s, 3 * ROWS, cells_r),
            scratch(cells_s, 3 * ROWS, cells_r),
            scratch(PRODUCTS, 4, cells_g, cells_r),
            scratch(3 * cells_s - PRODUCTS, 2, cells_r // LANES, cells_g, LANES),
            scratch(3, moves.shape[0], radii),
            scratch(3, rows, radii),
            scratch(radii, 6 * NH),
            pltpu.SemaphoreType.DMA((3,)),
        ],
        compiler_params=pltpu.CompilerParams(vmem_limit_bytes=VMEM_LIMIT),
        name="section_and_disk",
    )(counts, velocity, pressure, energy, rate, *halos, *lists, moves, chosen)


def fourier_table(azimuths, modes):
    phase = np.arange(azimuths)[:, None] * np.arange(modes)[None, :] % azimuths
    angles = phase * (2.0 * math.pi / azimuths)
    table = np.concatenate([np.cos(angles), -np.sin(angles)], axis=1) / math.sqrt(azimuths)
    return jnp.asarray(table.astype(np.float32))


def body(velocity, pressure, kinetic_energy, dissipation_rate, corner_ids, fractions, sector_owner):
    _, cells_s, cells_g, cells_r = velocity.shape
    radii, azimuths = corner_ids.shape
    stream_count, girth_count = lax.axis_size("stream"), lax.axis_size("girth")
    devices = stream_count * girth_count

    def swap(values, axis, count, start):
        pairs = []
        for i in range(start, count - 1, 2):
            pairs += [(i, i + 1), (i + 1, i)]
        return lax.ppermute(values, axis, pairs)

    slabs = pack(velocity, pressure, kinetic_energy, dissipation_rate)
    girth_halos = (
        swap(slabs[2], "girth", girth_count, 0),
        swap(slabs[3], "girth", girth_count, 1),
    )
    stream_halos = (
        swap(slabs[0], "stream", stream_count, 0),
        swap(slabs[1], "stream", stream_count, 1),
    )
    halos = stream_halos + girth_halos
    points = prepare(
        sector_owner[:, 0],
        corner_ids,
        fractions,
        fourier_table(azimuths, NH),
        (cells_s, cells_g, cells_r),
        girth_count,
    )
    new_velocity, new_energy, new_rate, keep, give = section(
        velocity, pressure, kinetic_energy, dissipation_rate, halos, points, devices
    )
    total = keep + swap(give, "girth", girth_count, 0)
    shares = lax.all_to_all(
        total.reshape(devices // 2, radii // devices, 6 * NH),
        ("stream", "girth"),
        split_axis=0,
        concat_axis=0,
        tiled=True,
        axis_index_groups=[list(range(parity, devices, 2)) for parity in (0, 1)],
    )
    return new_velocity, new_energy, new_rate, jnp.sum(shares, axis=0)


def solution(mesh):
    return jax.shard_map(
        body,
        mesh=mesh,
        in_specs=(
            P(None, "stream", "girth", None),
            P("stream", "girth", None),
            P("stream", "girth", None),
            P("stream", "girth", None),
            P(),
            P(),
            P(),
        ),
        out_specs=(
            P(None, "stream", "girth", None),
            P("stream", "girth", None),
            P("stream", "girth", None),
            P(("stream", "girth"), None),
        ),
        check_vma=False,
    )
```

```python
import functools
import math

import jax
import jax.numpy as jnp
import numpy as np
from jax import lax
from jax.experimental import pallas as pl
from jax.experimental.pallas import tpu as pltpu
from jax.sharding import PartitionSpec as P

NH = 128

base_viscosity = 0.05
time_step = 0.2
beta_star = 0.09
beta_rate = 0.075
alpha_rate = 0.52
wall_rate = 1.0

LANES = 128
ROWS = 8
SHIFT = 10
CHUNK = 32
PRODUCTS = 2
VMEM_LIMIT = 48 * 1024 * 1024


def in_hbm(values):
    return pltpu.with_memory_space_constraint(values, pltpu.HBM)


def pack_kernel(vel_ref, p_ref, k_ref, w_ref, *slabs):
    cells_s, cells_g, _ = p_ref.shape
    stream_odd = lax.axis_index("stream") % 2 == 1
    girth_odd = lax.axis_index("girth") % 2 == 1
    for f in range(6):
        own = vel_ref.at[f] if f < 3 else (p_ref, k_ref, w_ref)[f - 3]
        first, last = own[0:2], own[cells_s - 2 : cells_s]
        slabs[0][f] = jnp.where(stream_odd, first, last)
        slabs[1][f] = jnp.where(stream_odd, last, first)
        first, last = own[:, 0:2, :], own[:, cells_g - 2 : cells_g, :]
        slabs[2][f] = jnp.where(girth_odd, first, last)
        slabs[3][f] = jnp.where(girth_odd, last, first)


def pack(velocity, pressure, energy, rate):
    _, cells_s, cells_g, cells_r = velocity.shape
    stream = pltpu.VMEM((6, 2, cells_g, cells_r), jnp.float32)
    girth = pltpu.VMEM((6, cells_s, 2, cells_r), jnp.float32)
    vmem = pl.BlockSpec(memory_space=pltpu.VMEM)
    return pl.pallas_call(
        pack_kernel,
        out_shape=(stream, stream, girth, girth),
        in_specs=[vmem] * 4,
        out_specs=[vmem] * 4,
        name="pack_halos",
    )(*(in_hbm(x) for x in (velocity, pressure, energy, rate)))


def network(rows):
    steps = (rows - 1).bit_length()
    return [(low, 1 << min(2, steps - low)) for low in range(0, steps, 2)]


def reach(rows):
    return max((digits - 1) << low for low, digits in network(rows))


def split(values, size):
    if size & (size - 1) == 0:
        return values >> (size.bit_length() - 1), values & (size - 1)
    return values // size, values % size


def prepare_kernel(
    cells_s,
    cells_g,
    cells_r,
    owner_ref,
    ids_hbm,
    frac_hbm,
    table_hbm,
    q_ref,
    fr_ref,
    xs_ref,
    xg_ref,
    moves_ref,
    chosen_ref,
    count_ref,
    ids_ref,
    frac_ref,
    table_ref,
    turned,
    picked,
    keys,
    frs,
    xss,
    xgs,
    order,
    arrived,
):
    copies = [pltpu.make_async_copy(ids_hbm, ids_ref, arrived.at[0])]
    for d in range(3):
        copies.append(pltpu.make_async_copy(frac_hbm.at[d], frac_ref.at[d], arrived.at[1 + d]))
    copies.append(pltpu.make_async_copy(table_hbm, table_ref, arrived.at[4]))
    for copy in copies:
        copy.start()
    stream_first = lax.axis_index("stream") * cells_s
    me = lax.axis_index("girth")
    sectors = owner_ref.shape[0]
    azimuths = ids_ref.shape[1]
    width = azimuths // sectors
    rows = fr_ref.shape[0]
    pad = moves_ref.shape[0] - rows
    passes = network(rows)
    valid = 1 << SHIFT - 1

    def listed(number, count):
        order[jnp.minimum(count, rows // width)] = number
        return count + (owner_ref[number] == me).astype(jnp.int32)

    owned = lax.fori_loop(0, sectors, listed, jnp.int32(0), unroll=8)

    for d in range(4):
        picked[d] = jnp.full(picked.shape[1:], -1.0 if d == 0 else 0.0, jnp.float32)
    chosen_ref[...] = jnp.zeros_like(chosen_ref)
    beyond = pl.ds(rows, pad)
    for slot in range(2):
        keys[slot, beyond, :] = jnp.zeros((pad, LANES), jnp.int32)
    moves_ref[0:pad, :] = jnp.zeros((pad, LANES), jnp.int32)
    for d in range(4):
        copies[d].wait()
        for at in range(0, azimuths, LANES):
            cols = pl.ds(at, LANES)
            plane = ids_ref[:, cols].astype(jnp.float32) if d == 0 else frac_ref[d - 1, :, cols]
            turned[d, cols, :] = plane.T
    copies[4].wait()

    def sector(place, carry):
        source = pl.ds(pl.multiple_of(order[place] * width, width), width)
        target = pl.ds(pl.multiple_of(place * width, width), width)
        chosen_ref[target, :] = table_ref[source, :]
        for d in range(4):
            picked[d, target, :] = turned[d, source, :]
        return carry

    lax.fori_loop(0, owned, sector, jnp.int32(0))

    held = pl.ds(0, rows)
    ids = picked[0].astype(jnp.int32)
    stream_cell, rest = split(jnp.maximum(ids, 0), cells_g * cells_r)
    girth_cell, radial_cell = split(rest, cells_r)
    xs = (stream_cell - stream_first).astype(jnp.float32) + picked[1]
    kept = (ids >= 0) & (xs > -1.0) & (xs < float(cells_s))
    xss[0, held, :] = xs
    xgs[0, held, :] = girth_cell.astype(jnp.float32) + picked[2]
    frs[0, held, :] = picked[3]
    earlier = lax.broadcasted_iota(jnp.int32, (rows, rows), 0) > lax.broadcasted_iota(
        jnp.int32, (rows, rows), 1
    )
    earlier = earlier.astype(jnp.float32).astype(jnp.bfloat16)
    skipped = jnp.where(kept, 0.0, 1.0)
    before = jnp.dot(
        earlier, skipped.astype(jnp.bfloat16), preferred_element_type=jnp.float32
    ).astype(jnp.int32)
    counts = rows - jnp.sum(skipped, axis=0, keepdims=True).astype(jnp.int32)
    count_ref[0] = jnp.max(counts)
    moves_ref[pad : pad + rows, :] = jnp.where(kept, valid, 0)
    keys[0, held, :] = (radial_cell << SHIFT) + jnp.where(kept, before, 0)
    for number, (low, digits) in enumerate(passes):
        a, b = number % 2, 1 - number % 2
        mask = digits - 1 << low
        last = number == len(passes) - 1
        for at in range(0, rows, CHUNK):
            here, target = pl.ds(at, CHUNK), pl.ds(pad + at, CHUNK)
            there = [pl.ds(at + (k << low), CHUNK) for k in range(1, digits)]
            key = keys[a, here, :]
            arriving = [keys[a, t, :] for t in there]
            moved = [(arriving[k] & mask) == (k + 1 << low) for k in range(digits - 1)]
            key = jnp.where((key & mask) != 0, key & -(1 << SHIFT), key)
            came = moves_ref[target, :]
            out = [r[a, here, :] for r in (frs, xss, xgs)]
            for k in range(digits - 1):
                key = jnp.where(moved[k], arriving[k], key)
                came = came | jnp.where(moved[k], k + 1 << low, 0)
                out = [
                    jnp.where(moved[k], r[a, there[k], :], o) for r, o in zip((frs, xss, xgs), out)
                ]
            moves_ref[target, :] = came
            if last:
                q_ref[here, :] = key >> SHIFT
                fr_ref[here, :] = out[0]
                xs_ref[here, :] = out[1]
                xg_ref[here, :] = out[2]
            else:
                keys[b, here, :] = key
                frs[b, here, :] = out[0]
                xss[b, here, :] = out[1]
                xgs[b, here, :] = out[2]


def prepare(owners, corner_ids, fractions, table, cells, girth_count):
    cells_s, cells_g, cells_r = cells
    radii, azimuths = corner_ids.shape
    sectors = owners.shape[0]
    rows = 3 * sectors // girth_count * (azimuths // sectors)
    pad = reach(rows)
    shape = jax.ShapeDtypeStruct
    lists = (rows, radii)
    vmem = pl.BlockSpec(memory_space=pltpu.VMEM)
    smem = pl.BlockSpec(memory_space=pltpu.SMEM)
    hbm = pl.BlockSpec(memory_space=pltpu.HBM)
    return pl.pallas_call(
        functools.partial(prepare_kernel, cells_s, cells_g, cells_r),
        out_shape=(
            shape(lists, jnp.int32),
            shape(lists, jnp.float32),
            shape(lists, jnp.float32),
            shape(lists, jnp.float32),
            shape((pad + rows, radii), jnp.int32),
            shape((rows, 2 * NH), jnp.float32),
            shape((1,), jnp.int32),
        ),
        in_specs=[smem, hbm, hbm, hbm],
        out_specs=[vmem] * 6 + [smem],
        scratch_shapes=[
            pltpu.VMEM(corner_ids.shape, jnp.int32),
            pltpu.VMEM(fractions.shape, jnp.float32),
            pltpu.VMEM(table.shape, jnp.float32),
            pltpu.VMEM((4, azimuths, radii), jnp.float32),
            pltpu.VMEM((4, rows, radii), jnp.float32),
            pltpu.VMEM((2, rows + pad, radii), jnp.int32),
        ]
        + [pltpu.VMEM((2, rows + pad, radii), jnp.float32)] * 3
        + [pltpu.SMEM((rows // (azimuths // sectors) + 1,), jnp.int32)]
        + [pltpu.SemaphoreType.DMA((5,))],
        compiler_params=pltpu.CompilerParams(vmem_limit_bytes=VMEM_LIMIT),
        cost_estimate=pl.CostEstimate(
            flops=20 * radii * azimuths, bytes_accessed=44 * radii * azimuths, transcendentals=0
        ),
        name="prepare_points",
    )(*(in_hbm(x) for x in (owners, corner_ids, fractions, table)))


def radial(values, amount, fill):
    extent = values.shape[-1]
    rolled = pltpu.roll(values, (-amount) % extent, values.ndim - 1)
    position = lax.broadcasted_iota(jnp.int32, values.shape, values.ndim - 1) + amount
    return jnp.where((position >= 0) & (position < extent), rolled, fill)


def advance(own, before, after, left, right, ext_ref, visc_ref):
    cells_s, cells_g, _ = own[0].shape
    mid = ROWS

    def along_s(stack, amount):
        return stack[2 + amount : 2 + amount + cells_s]

    def along_g(ref, amount):
        return ref[:, mid + amount : mid + amount + cells_g, :]

    def viscosity(energy, rate):
        return base_viscosity + energy / (rate + wall_rate)

    stacks = [jnp.concatenate([before[f], own[f], after[f]], axis=0) for f in range(6)]
    for f in range(6):
        ext_ref[f, :, mid - 2 : mid, :] = left[f]
        ext_ref[f, :, mid : mid + cells_g, :] = own[f]
        ext_ref[f, :, mid + cells_g : mid + cells_g + 2, :] = right[f]
    middle = viscosity(own[4], own[5])
    visc_stack = viscosity(stacks[4], stacks[5])
    visc_ref[:, mid - 2 : mid, :] = viscosity(left[4], left[5])
    visc_ref[:, mid : mid + cells_g, :] = middle
    visc_ref[:, mid + cells_g : mid + cells_g + 2, :] = viscosity(right[4], right[5])
    faces = [
        (
            0.5 * (middle + along_s(visc_stack, 1)),
            0.5 * (middle + along_s(visc_stack, -1)),
        ),
        (
            0.5 * (middle + along_g(visc_ref, 1)),
            0.5 * (middle + along_g(visc_ref, -1)),
        ),
        (
            0.5 * (middle + radial(middle, 1, base_viscosity)),
            0.5 * (middle + radial(middle, -1, base_viscosity)),
        ),
    ]

    def neighbour(f, direction, amount):
        if direction == 0:
            return along_s(stacks[f], amount)
        if direction == 1:
            return along_g(ext_ref.at[f], amount)
        return radial(own[f], amount, 0.0)

    def terms(f, direction):
        up, down = neighbour(f, direction, 1), neighbour(f, direction, -1)
        far = neighbour(f, direction, 2) - neighbour(f, direction, -2)
        gradient = (8.0 * (up - down) - far) * (1.0 / 12.0)
        above, below = faces[direction]
        return gradient, above * (up - own[f]) - below * (own[f] - down)

    strain = None
    updated = []
    for f in range(3):
        change = -terms(3, f)[0]
        for direction in range(3):
            gradient, spread = terms(f, direction)
            strain = gradient * gradient if strain is None else strain + gradient * gradient
            change = change - own[direction] * gradient + spread
        updated.append(own[f] + time_step * change)
    energy = own[4] / (own[5] + wall_rate) * strain - beta_star * own[4] * own[5]
    rate = alpha_rate * strain - beta_rate * own[5] * own[5]
    for direction in range(3):
        gradient, spread = terms(4, direction)
        energy = energy - own[direction] * gradient + spread
        gradient, spread = terms(5, direction)
        rate = rate - own[direction] * gradient + spread
    return updated, own[4] + time_step * energy, own[5] + time_step * rate


def girth_sums(parts):
    row = lax.broadcasted_iota(jnp.int32, parts[0].shape, 0)

    def swapped(values, distance):
        up = pltpu.roll(values, distance, 0)
        if 2 * distance == ROWS:
            return up
        return jnp.where((row & distance) != 0, up, pltpu.roll(values, ROWS - distance, 0))

    distance = ROWS // 2
    while distance > 0:
        low = (row & distance) == 0
        parts = [
            jnp.where(low, x, y) + swapped(jnp.where(low, y, x), distance)
            for x, y in zip(parts[:distance], parts[distance:])
        ]
        distance //= 2
    return parts[0]


def section_kernel(
    devices,
    count_ref,
    vel_ref,
    p_ref,
    k_ref,
    w_ref,
    stream_a,
    stream_b,
    girth_a,
    girth_b,
    q_ref,
    fr_ref,
    xs_ref,
    xg_ref,
    moves_ref,
    chosen_ref,
    new_vel_hbm,
    new_k_hbm,
    new_w_hbm,
    keep_ref,
    give_ref,
    new_vel_ref,
    new_k_ref,
    new_w_ref,
    ext_ref,
    visc_ref,
    field_ref,
    gather_ref,
    weight_ref,
    value_ref,
    disk_ref,
    harm_ref,
    stored,
):
    cells_s, cells_g, cells_r = p_ref.shape
    rows = fr_ref.shape[0]
    pad = moves_ref.shape[0] - rows
    passes = network(rows)
    valid = 1 << SHIFT - 1
    stream_odd = lax.axis_index("stream") % 2 == 1
    girth_odd = lax.axis_index("girth") % 2 == 1

    own = [vel_ref[0], vel_ref[1], vel_ref[2], p_ref[...], k_ref[...], w_ref[...]]
    six = range(6)
    updated, energy, rate = advance(
        own,
        [jnp.where(stream_odd, stream_a[f], stream_b[f]) for f in six],
        [jnp.where(stream_odd, stream_b[f], stream_a[f]) for f in six],
        [jnp.where(girth_odd, girth_a[f], girth_b[f]) for f in six],
        [jnp.where(girth_odd, girth_b[f], girth_a[f]) for f in six],
        ext_ref,
        visc_ref,
    )
    new_k_ref[...] = energy
    new_w_ref[...] = rate

    def halved(values):
        high = values.astype(jnp.bfloat16)
        return high, (values - high.astype(jnp.float32)).astype(jnp.bfloat16)

    def rounded(values):
        return values.astype(jnp.bfloat16).astype(jnp.float32)

    halves = cells_r // LANES
    for c in range(3):
        new_vel_ref[c] = updated[c]
        slope = radial(updated[c], 1, 0.0) - updated[c]
        for kind, values in enumerate((updated[c], slope)):
            if c < PRODUCTS:
                high = rounded(values)
                field_ref[c, :, 2 * kind] = high
                field_ref[c, :, 2 * kind + 1] = rounded(values - high)
            else:
                for h in range(halves):
                    lanes = slice(h * LANES, (h + 1) * LANES)
                    gather_ref[c - PRODUCTS, :, kind, h] = values[:, :, lanes]
    results = ((new_vel_ref, new_vel_hbm), (new_k_ref, new_k_hbm), (new_w_ref, new_w_hbm))
    copies = [
        pltpu.make_async_copy(source, target, stored.at[i])
        for i, (source, target) in enumerate(results)
    ]
    for copy in copies:
        copy.start()

    kinds = 4
    table = field_ref[...].reshape(PRODUCTS * cells_s * kinds * cells_g, cells_r)
    table = table.astype(jnp.bfloat16)
    pair = 2 * LANES
    girth_row = lax.broadcasted_iota(jnp.int32, (cells_g, LANES), 0).astype(jnp.float32)
    index_type = jnp.bfloat16 if cells_r <= 256 else jnp.float32
    radial_row = lax.broadcasted_iota(jnp.int32, (cells_r, pair), 0).astype(jnp.float32)
    radial_row = radial_row.astype(index_type)
    one, none = jnp.ones((), jnp.bfloat16), jnp.zeros((), jnp.bfloat16)

    def row(ref, at):
        return jnp.broadcast_to(ref[pl.ds(at, 1), :], (cells_g, LANES))

    def wide(parts):
        return jnp.concatenate(parts, axis=1)

    def pick(c, s, kind, index, half_of):
        out = None
        for h in range(halves):
            got = jnp.take_along_axis(
                gather_ref[c - PRODUCTS, s, kind, h], index, axis=1, mode="promise_in_bounds"
            )
            out = got if out is None else jnp.where(half_of[h], got, out)
        return out

    def eight(at, part):
        xs8 = xs_ref[pl.ds(at, ROWS), :]
        for s in range(cells_s):
            weight_ref[part, s] = jnp.maximum(1.0 - jnp.abs(xs8 - float(s)), 0.0)
        sums = [[], [], []]
        for j in range(0, ROWS, 2):
            both = (j, j + 1)
            q = [row(q_ref, at + i) for i in both]
            fr = [row(fr_ref, at + i) for i in both]
            hs = [[row(weight_ref.at[part, s], i) for i in both] for s in range(cells_s)]
            hg = [jnp.maximum(1.0 - jnp.abs(row(xg_ref, at + i) - girth_row), 0.0) for i in both]
            spread = wide(q).astype(jnp.float32)
            spread = jnp.concatenate([spread] * (cells_r // cells_g), axis=0).astype(index_type)
            hot = jnp.where(radial_row == spread, one, none)
            got = jnp.dot(table, hot, preferred_element_type=jnp.float32)
            got = got.reshape(PRODUCTS, cells_s, kinds, cells_g, pair)
            for i in range(2):
                lanes = slice(i * LANES, (i + 1) * LANES)
                index = q[i] & (LANES - 1)
                half_of = [q[i] >= h * LANES for h in range(halves)]
                for c in range(3):
                    total = None
                    for s in range(cells_s):
                        if c < PRODUCTS:
                            high, low, slope_high, slope_low = (got[c, s, k, :, lanes] for k in range(kinds))
                            value = high + low + fr[i] * (slope_high + slope_low)
                        else:
                            value = pick(c, s, 0, index, half_of)
                            value = value + fr[i] * pick(c, s, 1, index, half_of)
                        value = hs[s][i] * value
                        total = value if total is None else total + value
                    sums[c].append(hg[i] * total)
        for c in range(3):
            value_ref[0, c, pl.ds(pad + at, ROWS), :] = girth_sums(sums[c])

    def step(group, carry):
        for part in range(2):
            eight(pl.multiple_of((2 * group + part) * ROWS, ROWS), part)
        return carry

    lax.fori_loop(0, (count_ref[0] + 2 * ROWS - 1) // (2 * ROWS), step, jnp.int32(0))

    for number, (low, digits) in enumerate(reversed(passes)):
        a, b = number % 2, 1 - number % 2
        mask = digits - 1 << low
        last = number == len(passes) - 1
        for at in range(0, rows, CHUNK):
            here = pl.ds(pad + at, CHUNK)
            there = [pl.ds(pad + at - (k << low), CHUNK) for k in range(1, digits)]
            moved = [(moves_ref[there[k], :] & mask) == (k + 1 << low) for k in range(digits - 1)]
            if last:
                kept = (moves_ref[here, :] & valid) != 0
            for c in range(3):
                value = value_ref[a, c, here, :]
                for k in range(digits - 1):
                    value = jnp.where(moved[k], value_ref[a, c, there[k], :], value)
                if last:
                    disk_ref[c, pl.ds(at, CHUNK), :] = jnp.where(kept, value, 0.0)
                else:
                    value_ref[b, c, here, :] = value

    turned = jnp.concatenate([disk_ref[c].T for c in range(3)], axis=0)
    high, low = halved(turned)
    wave_high, wave_low = halved(chosen_ref[...])
    waves = jnp.dot(high, wave_high, preferred_element_type=jnp.float32)
    waves += jnp.dot(high, wave_low, preferred_element_type=jnp.float32)
    waves += jnp.dot(low, wave_high, preferred_element_type=jnp.float32)
    radii = harm_ref.shape[0]
    for c in range(3):
        harm_ref[:, c * 2 * NH : (c + 1) * 2 * NH] = waves[c * radii : (c + 1) * radii]
    block = radii // devices
    for place in range(devices // 2):
        even = harm_ref[2 * place * block : (2 * place + 1) * block, :]
        odd = harm_ref[(2 * place + 1) * block : (2 * place + 2) * block, :]
        keep_ref[place * block : (place + 1) * block, :] = jnp.where(girth_odd, odd, even)
        give_ref[place * block : (place + 1) * block, :] = jnp.where(girth_odd, even, odd)
    for copy in copies:
        copy.wait()


def section(velocity, pressure, energy, rate, halos, points, devices):
    _, cells_s, cells_g, cells_r = velocity.shape
    *lists, moves, chosen, counts = points
    rows, radii = lists[0].shape
    shape = functools.partial(jax.ShapeDtypeStruct, dtype=jnp.float32)
    scratch = lambda *dims: pltpu.VMEM(dims, jnp.float32)
    vmem = pl.BlockSpec(memory_space=pltpu.VMEM)
    smem = pl.BlockSpec(memory_space=pltpu.SMEM)
    return pl.pallas_call(
        functools.partial(section_kernel, devices),
        out_shape=(
            shape(velocity.shape),
            shape(energy.shape),
            shape(rate.shape),
            shape((radii // 2, 6 * NH)),
            shape((radii // 2, 6 * NH)),
        ),
        in_specs=[smem] + [vmem] * 14,
        out_specs=[pl.BlockSpec(memory_space=pl.ANY)] * 3 + [vmem] * 2,
        scratch_shapes=[
            scratch(*velocity.shape),
            scratch(*energy.shape),
            scratch(*rate.shape),
            scratch(6, cells_s, 3 * ROWS, cells_r),
            scratch(cells_s, 3 * ROWS, cells_r),
            scratch(PRODUCTS, cells_s, 4, cells_g, cells_r),
            scratch(3 - PRODUCTS, cells_s, 2, cells_r // LANES, cells_g, LANES),
            scratch(2, cells_s, ROWS, radii),
            scratch(2, 3, moves.shape[0], radii),
            scratch(3, rows, radii),
            scratch(radii, 6 * NH),
            pltpu.SemaphoreType.DMA((3,)),
        ],
        compiler_params=pltpu.CompilerParams(vmem_limit_bytes=VMEM_LIMIT),
        name="section_and_disk",
    )(counts, velocity, pressure, energy, rate, *halos, *lists, moves, chosen)


def fourier_table(azimuths, modes):
    phase = np.arange(azimuths)[:, None] * np.arange(modes)[None, :] % azimuths
    angles = phase * (2.0 * math.pi / azimuths)
    table = np.concatenate([np.cos(angles), -np.sin(angles)], axis=1) / math.sqrt(azimuths)
    return jnp.asarray(table.astype(np.float32))


def body(velocity, pressure, kinetic_energy, dissipation_rate, corner_ids, fractions, sector_owner):
    _, cells_s, cells_g, cells_r = velocity.shape
    radii, azimuths = corner_ids.shape
    stream_count, girth_count = lax.axis_size("stream"), lax.axis_size("girth")
    devices = stream_count * girth_count

    def swap(values, axis, count, start):
        pairs = []
        for i in range(start, count - 1, 2):
            pairs += [(i, i + 1), (i + 1, i)]
        return lax.ppermute(values, axis, pairs)

    slabs = pack(velocity, pressure, kinetic_energy, dissipation_rate)
    girth_halos = (
        swap(slabs[2], "girth", girth_count, 0),
        swap(slabs[3], "girth", girth_count, 1),
    )
    stream_halos = (
        swap(slabs[0], "stream", stream_count, 0),
        swap(slabs[1], "stream", stream_count, 1),
    )
    halos = stream_halos + girth_halos
    points = prepare(
        sector_owner[:, 0],
        corner_ids,
        fractions,
        fourier_table(azimuths, NH),
        (cells_s, cells_g, cells_r),
        girth_count,
    )
    new_velocity, new_energy, new_rate, keep, give = section(
        velocity, pressure, kinetic_energy, dissipation_rate, halos, points, devices
    )
    total = keep + swap(give, "girth", girth_count, 0)
    shares = lax.all_to_all(
        total.reshape(devices // 2, radii // devices, 6 * NH),
        ("stream", "girth"),
        split_axis=0,
        concat_axis=0,
        tiled=True,
        axis_index_groups=[list(range(parity, devices, 2)) for parity in (0, 1)],
    )
    return new_velocity, new_energy, new_rate, jnp.sum(shares, axis=0)


def solution(mesh):
    return jax.shard_map(
        body,
        mesh=mesh,
        in_specs=(
            P(None, "stream", "girth", None),
            P("stream", "girth", None),
            P("stream", "girth", None),
            P("stream", "girth", None),
            P(),
            P(),
            P(),
        ),
        out_specs=(
            P(None, "stream", "girth", None),
            P("stream", "girth", None),
            P("stream", "girth", None),
            P(("stream", "girth"), None),
        ),
        check_vma=False,
    )
```

```python
import functools
import math

import jax
import jax.numpy as jnp
import numpy as np
from jax import lax
from jax.experimental import pallas as pl
from jax.experimental.pallas import tpu as pltpu
from jax.sharding import PartitionSpec as P

NH = 128

base_viscosity = 0.05
time_step = 0.2
beta_star = 0.09
beta_rate = 0.075
alpha_rate = 0.52
wall_rate = 1.0

LANES = 128
ROWS = 8
SHIFT = 10
CHUNK = 32
PRODUCTS = 2
VMEM_LIMIT = 48 * 1024 * 1024


def in_hbm(values):
    return pltpu.with_memory_space_constraint(values, pltpu.HBM)


def pack_kernel(vel_hbm, p_hbm, k_hbm, w_hbm, ids_hbm, frac_hbm, *rest):
    *slabs, ids_ref, frac_ref, fields, arrived = rest
    moves = [(vel_hbm, fields.at[0:3]), (p_hbm, fields.at[3]), (k_hbm, fields.at[4])]
    moves += [(w_hbm, fields.at[5]), (ids_hbm, ids_ref), (frac_hbm, frac_ref)]
    copies = [
        pltpu.make_async_copy(source, target, arrived.at[i])
        for i, (source, target) in enumerate(moves)
    ]
    for copy in copies:
        copy.start()
    _, cells_s, cells_g, _ = fields.shape
    stream_odd = lax.axis_index("stream") % 2 == 1
    girth_odd = lax.axis_index("girth") % 2 == 1
    for copy in copies[:4]:
        copy.wait()
    for f in range(6):
        first, last = fields[f, 0:2], fields[f, cells_s - 2 : cells_s]
        slabs[0][f] = jnp.where(stream_odd, first, last)
        slabs[1][f] = jnp.where(stream_odd, last, first)
        first, last = fields[f, :, 0:2, :], fields[f, :, cells_g - 2 : cells_g, :]
        slabs[2][f] = jnp.where(girth_odd, first, last)
        slabs[3][f] = jnp.where(girth_odd, last, first)
    for copy in copies[4:]:
        copy.wait()


def pack(velocity, pressure, energy, rate, corner_ids, fractions):
    _, cells_s, cells_g, cells_r = velocity.shape
    stream = pltpu.VMEM((6, 2, cells_g, cells_r), jnp.float32)
    girth = pltpu.VMEM((6, cells_s, 2, cells_r), jnp.float32)
    points = [pltpu.VMEM(x.shape, x.dtype) for x in (corner_ids, fractions)]
    inputs = (velocity, pressure, energy, rate, corner_ids, fractions)
    return pl.pallas_call(
        pack_kernel,
        out_shape=[stream, stream, girth, girth] + points,
        in_specs=[pl.BlockSpec(memory_space=pltpu.HBM)] * 6,
        out_specs=[pl.BlockSpec(memory_space=pltpu.VMEM)] * 6,
        scratch_shapes=[
            pltpu.VMEM((6, cells_s, cells_g, cells_r), jnp.float32),
            pltpu.SemaphoreType.DMA((6,)),
        ],
        compiler_params=pltpu.CompilerParams(vmem_limit_bytes=VMEM_LIMIT),
        name="pack_halos",
    )(*(in_hbm(x) for x in inputs))


def network(rows):
    steps = (rows - 1).bit_length()
    return [(low, 1 << min(2, steps - low)) for low in range(0, steps, 2)]


def reach(rows):
    return max((digits - 1) << low for low, digits in network(rows))


def split(values, size):
    if size & (size - 1) == 0:
        return values >> (size.bit_length() - 1), values & (size - 1)
    return values // size, values % size


def prepare_kernel(
    cells_s,
    cells_g,
    cells_r,
    owner_ref,
    ids_ref,
    frac_ref,
    table_hbm,
    q_ref,
    fr_ref,
    xs_ref,
    xg_ref,
    moves_ref,
    chosen_ref,
    count_ref,
    turned,
    picked,
    keys,
    frs,
    xss,
    xgs,
    order,
    arrived,
):
    stream_first = lax.axis_index("stream") * cells_s
    me = lax.axis_index("girth")
    sectors = owner_ref.shape[0]
    azimuths = ids_ref.shape[1]
    width = azimuths // sectors
    rows = fr_ref.shape[0]
    pad = moves_ref.shape[0] - rows
    passes = network(rows)
    valid = 1 << SHIFT - 1

    for place in range(rows // width):
        order[place] = 0

    def listed(number, count):
        order[jnp.minimum(count, rows // width)] = number
        return count + (owner_ref[number] == me).astype(jnp.int32)

    owned = lax.fori_loop(0, sectors, listed, jnp.int32(0), unroll=8)
    for place in range(rows // width):
        source = pl.ds(pl.multiple_of(order[place] * width, width), width)
        pltpu.make_async_copy(
            table_hbm.at[source, :], chosen_ref.at[pl.ds(place * width, width), :], arrived.at[0]
        ).start()

    for d in range(4):
        picked[d] = jnp.full(picked.shape[1:], -1.0 if d == 0 else 0.0, jnp.float32)
    beyond = pl.ds(rows, pad)
    for slot in range(2):
        keys[slot, beyond, :] = jnp.zeros((pad, LANES), jnp.int32)
    moves_ref[0:pad, :] = jnp.zeros((pad, LANES), jnp.int32)
    for d in range(4):
        for at in range(0, azimuths, LANES):
            cols = pl.ds(at, LANES)
            plane = ids_ref[:, cols].astype(jnp.float32) if d == 0 else frac_ref[d - 1, :, cols]
            turned[d, cols, :] = plane.T

    def sector(place, carry):
        source = pl.ds(pl.multiple_of(order[place] * width, width), width)
        target = pl.ds(pl.multiple_of(place * width, width), width)
        for d in range(4):
            picked[d, target, :] = turned[d, source, :]
        return carry

    lax.fori_loop(0, owned, sector, jnp.int32(0))

    held = pl.ds(0, rows)
    ids = picked[0].astype(jnp.int32)
    stream_cell, rest = split(jnp.maximum(ids, 0), cells_g * cells_r)
    girth_cell, radial_cell = split(rest, cells_r)
    xs = (stream_cell - stream_first).astype(jnp.float32) + picked[1]
    kept = (ids >= 0) & (xs > -1.0) & (xs < float(cells_s))
    xss[0, held, :] = xs
    xgs[0, held, :] = girth_cell.astype(jnp.float32) + picked[2]
    frs[0, held, :] = picked[3]
    earlier = lax.broadcasted_iota(jnp.int32, (rows, rows), 0) > lax.broadcasted_iota(
        jnp.int32, (rows, rows), 1
    )
    earlier = earlier.astype(jnp.float32).astype(jnp.bfloat16)
    skipped = jnp.where(kept, 0.0, 1.0)
    before = jnp.dot(
        earlier, skipped.astype(jnp.bfloat16), preferred_element_type=jnp.float32
    ).astype(jnp.int32)
    counts = rows - jnp.sum(skipped, axis=0, keepdims=True).astype(jnp.int32)
    count_ref[0] = jnp.max(counts)
    moves_ref[pad : pad + rows, :] = jnp.where(kept, valid, 0)
    keys[0, held, :] = (radial_cell << SHIFT) + jnp.where(kept, before, 0)
    for number, (low, digits) in enumerate(passes):
        a, b = number % 2, 1 - number % 2
        mask = digits - 1 << low
        last = number == len(passes) - 1
        for at in range(0, rows, CHUNK):
            here, target = pl.ds(at, CHUNK), pl.ds(pad + at, CHUNK)
            there = [pl.ds(at + (k << low), CHUNK) for k in range(1, digits)]
            key = keys[a, here, :]
            arriving = [keys[a, t, :] for t in there]
            moved = [(arriving[k] & mask) == (k + 1 << low) for k in range(digits - 1)]
            key = jnp.where((key & mask) != 0, key & -(1 << SHIFT), key)
            came = moves_ref[target, :]
            out = [r[a, here, :] for r in (frs, xss, xgs)]
            for k in range(digits - 1):
                key = jnp.where(moved[k], arriving[k], key)
                came = came | jnp.where(moved[k], k + 1 << low, 0)
                out = [
                    jnp.where(moved[k], r[a, there[k], :], o) for r, o in zip((frs, xss, xgs), out)
                ]
            moves_ref[target, :] = came
            if last:
                q_ref[here, :] = key >> SHIFT
                fr_ref[here, :] = out[0]
                xs_ref[here, :] = out[1]
                xg_ref[here, :] = out[2]
            else:
                keys[b, here, :] = key
                frs[b, here, :] = out[0]
                xss[b, here, :] = out[1]
                xgs[b, here, :] = out[2]
    pltpu.make_async_copy(table_hbm.at[pl.ds(0, rows), :], chosen_ref, arrived.at[0]).wait()


def prepare(owners, corner_ids, fractions, table, cells, girth_count):
    cells_s, cells_g, cells_r = cells
    radii, azimuths = corner_ids.shape
    sectors = owners.shape[0]
    rows = 3 * sectors // girth_count * (azimuths // sectors)
    pad = reach(rows)
    shape = jax.ShapeDtypeStruct
    lists = (rows, radii)
    vmem = pl.BlockSpec(memory_space=pltpu.VMEM)
    smem = pl.BlockSpec(memory_space=pltpu.SMEM)
    hbm = pl.BlockSpec(memory_space=pltpu.HBM)
    return pl.pallas_call(
        functools.partial(prepare_kernel, cells_s, cells_g, cells_r),
        out_shape=(
            shape(lists, jnp.int32),
            shape(lists, jnp.float32),
            shape(lists, jnp.float32),
            shape(lists, jnp.float32),
            shape((pad + rows, radii), jnp.int32),
            shape((rows, 2 * NH), jnp.float32),
            shape((1,), jnp.int32),
        ),
        in_specs=[smem, vmem, vmem, hbm],
        out_specs=[vmem] * 6 + [smem],
        scratch_shapes=[
            pltpu.VMEM((4, azimuths, radii), jnp.float32),
            pltpu.VMEM((4, rows, radii), jnp.float32),
            pltpu.VMEM((2, rows + pad, radii), jnp.int32),
        ]
        + [pltpu.VMEM((2, rows + pad, radii), jnp.float32)] * 3
        + [pltpu.SMEM((rows // (azimuths // sectors) + 1,), jnp.int32)]
        + [pltpu.SemaphoreType.DMA((1,))],
        compiler_params=pltpu.CompilerParams(vmem_limit_bytes=VMEM_LIMIT),
        cost_estimate=pl.CostEstimate(
            flops=20 * radii * azimuths, bytes_accessed=44 * radii * azimuths, transcendentals=0
        ),
        name="prepare_points",
    )(in_hbm(owners), corner_ids, fractions, in_hbm(table))


def radial(values, amount, fill):
    extent = values.shape[-1]
    rolled = pltpu.roll(values, (-amount) % extent, values.ndim - 1)
    position = lax.broadcasted_iota(jnp.int32, values.shape, values.ndim - 1) + amount
    return jnp.where((position >= 0) & (position < extent), rolled, fill)


def advance(own, before, after, left, right, ext_ref, visc_ref):
    cells_s, cells_g, _ = own[0].shape
    mid = ROWS

    def along_s(stack, amount):
        return stack[2 + amount : 2 + amount + cells_s]

    def along_g(ref, amount):
        return ref[:, mid + amount : mid + amount + cells_g, :]

    def viscosity(energy, rate):
        return base_viscosity + energy / (rate + wall_rate)

    stacks = [jnp.concatenate([before[f], own[f], after[f]], axis=0) for f in range(6)]
    for f in range(6):
        ext_ref[f, :, mid - 2 : mid, :] = left[f]
        ext_ref[f, :, mid : mid + cells_g, :] = own[f]
        ext_ref[f, :, mid + cells_g : mid + cells_g + 2, :] = right[f]
    middle = viscosity(own[4], own[5])
    visc_stack = viscosity(stacks[4], stacks[5])
    visc_ref[:, mid - 2 : mid, :] = viscosity(left[4], left[5])
    visc_ref[:, mid : mid + cells_g, :] = middle
    visc_ref[:, mid + cells_g : mid + cells_g + 2, :] = viscosity(right[4], right[5])
    faces = [
        (
            0.5 * (middle + along_s(visc_stack, 1)),
            0.5 * (middle + along_s(visc_stack, -1)),
        ),
        (
            0.5 * (middle + along_g(visc_ref, 1)),
            0.5 * (middle + along_g(visc_ref, -1)),
        ),
        (
            0.5 * (middle + radial(middle, 1, base_viscosity)),
            0.5 * (middle + radial(middle, -1, base_viscosity)),
        ),
    ]

    def neighbour(f, direction, amount):
        if direction == 0:
            return along_s(stacks[f], amount)
        if direction == 1:
            return along_g(ext_ref.at[f], amount)
        return radial(own[f], amount, 0.0)

    def terms(f, direction):
        up, down = neighbour(f, direction, 1), neighbour(f, direction, -1)
        far = neighbour(f, direction, 2) - neighbour(f, direction, -2)
        gradient = (8.0 * (up - down) - far) * (1.0 / 12.0)
        above, below = faces[direction]
        return gradient, above * (up - own[f]) - below * (own[f] - down)

    strain = None
    updated = []
    for f in range(3):
        change = -terms(3, f)[0]
        for direction in range(3):
            gradient, spread = terms(f, direction)
            strain = gradient * gradient if strain is None else strain + gradient * gradient
            change = change - own[direction] * gradient + spread
        updated.append(own[f] + time_step * change)
    energy = own[4] / (own[5] + wall_rate) * strain - beta_star * own[4] * own[5]
    rate = alpha_rate * strain - beta_rate * own[5] * own[5]
    for direction in range(3):
        gradient, spread = terms(4, direction)
        energy = energy - own[direction] * gradient + spread
        gradient, spread = terms(5, direction)
        rate = rate - own[direction] * gradient + spread
    return updated, own[4] + time_step * energy, own[5] + time_step * rate


def girth_sums(parts):
    row = lax.broadcasted_iota(jnp.int32, parts[0].shape, 0)

    def swapped(values, distance):
        up = pltpu.roll(values, distance, 0)
        if 2 * distance == ROWS:
            return up
        return jnp.where((row & distance) != 0, up, pltpu.roll(values, ROWS - distance, 0))

    distance = ROWS // 2
    while distance > 0:
        low = (row & distance) == 0
        parts = [
            jnp.where(low, x, y) + swapped(jnp.where(low, y, x), distance)
            for x, y in zip(parts[:distance], parts[distance:])
        ]
        distance //= 2
    return parts[0]


def section_kernel(
    devices,
    count_ref,
    vel_ref,
    p_ref,
    k_ref,
    w_ref,
    stream_a,
    stream_b,
    girth_a,
    girth_b,
    q_ref,
    fr_ref,
    xs_ref,
    xg_ref,
    moves_ref,
    chosen_ref,
    new_vel_hbm,
    new_k_hbm,
    new_w_hbm,
    keep_ref,
    give_ref,
    new_vel_ref,
    new_k_ref,
    new_w_ref,
    ext_ref,
    visc_ref,
    field_ref,
    gather_ref,
    value_ref,
    disk_ref,
    harm_ref,
    stored,
):
    cells_s, cells_g, cells_r = p_ref.shape
    rows = fr_ref.shape[0]
    pad = moves_ref.shape[0] - rows
    passes = network(rows)
    valid = 1 << SHIFT - 1
    stream_odd = lax.axis_index("stream") % 2 == 1
    girth_odd = lax.axis_index("girth") % 2 == 1

    own = [vel_ref[0], vel_ref[1], vel_ref[2], p_ref[...], k_ref[...], w_ref[...]]
    six = range(6)
    updated, energy, rate = advance(
        own,
        [jnp.where(stream_odd, stream_a[f], stream_b[f]) for f in six],
        [jnp.where(stream_odd, stream_b[f], stream_a[f]) for f in six],
        [jnp.where(girth_odd, girth_a[f], girth_b[f]) for f in six],
        [jnp.where(girth_odd, girth_b[f], girth_a[f]) for f in six],
        ext_ref,
        visc_ref,
    )
    new_k_ref[...] = energy
    new_w_ref[...] = rate

    def halved(values):
        high = values.astype(jnp.bfloat16)
        return high, (values - high.astype(jnp.float32)).astype(jnp.bfloat16)

    def rounded(values):
        return values.astype(jnp.bfloat16).astype(jnp.float32)

    halves = cells_r // LANES
    for c in range(3):
        new_vel_ref[c] = updated[c]
        slope = radial(updated[c], 1, 0.0) - updated[c]
        for kind, values in enumerate((updated[c], slope)):
            if c < PRODUCTS:
                high = rounded(values)
                field_ref[c, :, 2 * kind] = high
                field_ref[c, :, 2 * kind + 1] = rounded(values - high)
            else:
                for h in range(halves):
                    lanes = slice(h * LANES, (h + 1) * LANES)
                    gather_ref[c - PRODUCTS, :, kind, h] = values[:, :, lanes]
    results = ((new_vel_ref, new_vel_hbm), (new_k_ref, new_k_hbm), (new_w_ref, new_w_hbm))
    copies = [
        pltpu.make_async_copy(source, target, stored.at[i])
        for i, (source, target) in enumerate(results)
    ]
    for copy in copies:
        copy.start()

    kinds = 4
    table = field_ref[...].reshape(PRODUCTS * cells_s * kinds * cells_g, cells_r)
    table = table.astype(jnp.bfloat16)
    pair = 2 * LANES
    girth_row = lax.broadcasted_iota(jnp.int32, (cells_g, pair), 0).astype(jnp.float32)
    index_type = jnp.bfloat16 if cells_r <= 256 else jnp.float32
    radial_row = lax.broadcasted_iota(jnp.int32, (cells_r, pair), 0).astype(jnp.float32)
    radial_row = radial_row.astype(index_type)
    one, none = jnp.ones((), jnp.bfloat16), jnp.zeros((), jnp.bfloat16)

    def two(values, j):
        return jnp.concatenate([values[j : j + 1], values[j + 1 : j + 2]], axis=1)

    def spread(values, j):
        return jnp.broadcast_to(values[j : j + 1], (cells_g, LANES))

    def pick(c, s, kind, index, half_of):
        out = None
        for h in range(halves):
            got = jnp.take_along_axis(
                gather_ref[c - PRODUCTS, s, kind, h], index, axis=1, mode="promise_in_bounds"
            )
            out = got if out is None else jnp.where(half_of[h], got, out)
        return out

    def eight(at):
        here = pl.ds(at, ROWS)
        q8, fr8, xg8, xs8 = (r[here, :] for r in (q_ref, fr_ref, xg_ref, xs_ref))
        hs8 = [jnp.maximum(1.0 - jnp.abs(xs8 - float(s)), 0.0) for s in range(cells_s)]
        index8 = q8 & (LANES - 1)
        qf8 = q8.astype(jnp.float32)
        sums = [[], [], []]
        for j in range(0, ROWS, 2):
            chosen_q = jnp.broadcast_to(two(qf8, j), (cells_r, pair)).astype(index_type)
            hot = jnp.where(radial_row == chosen_q, one, none)
            got = jnp.dot(table, hot, preferred_element_type=jnp.float32)
            got = got.reshape(PRODUCTS, cells_s, kinds, cells_g, pair)
            fr = two(fr8, j)
            hg = jnp.maximum(1.0 - jnp.abs(two(xg8, j) - girth_row), 0.0)
            hs = [two(hs8[s], j) for s in range(cells_s)]
            for c in range(PRODUCTS):
                total = None
                for s in range(cells_s):
                    value = got[c, s, 0] + got[c, s, 1] + fr * (got[c, s, 2] + got[c, s, 3])
                    value = hs[s] * value
                    total = value if total is None else total + value
                total = hg * total
                sums[c] += [total[:, :LANES], total[:, LANES:]]
            for i in (j, j + 1):
                index, q = spread(index8, i), spread(q8, i)
                half_of = [q >= h * LANES for h in range(halves)]
                own_hg = hg[:, (i - j) * LANES : (i - j + 1) * LANES]
                for c in range(PRODUCTS, 3):
                    total = None
                    for s in range(cells_s):
                        value = pick(c, s, 0, index, half_of)
                        value = value + fr8[i : i + 1] * pick(c, s, 1, index, half_of)
                        value = hs8[s][i : i + 1] * value
                        total = value if total is None else total + value
                    sums[c].append(own_hg * total)
        for c in range(3):
            value_ref[0, c, pl.ds(pad + at, ROWS), :] = girth_sums(sums[c])

    def step(group, carry):
        for part in range(2):
            eight(pl.multiple_of((2 * group + part) * ROWS, ROWS))
        return carry

    lax.fori_loop(0, (count_ref[0] + 2 * ROWS - 1) // (2 * ROWS), step, jnp.int32(0))

    for number, (low, digits) in enumerate(reversed(passes)):
        a, b = number % 2, 1 - number % 2
        mask = digits - 1 << low
        last = number == len(passes) - 1
        for at in range(0, rows, CHUNK):
            here = pl.ds(pad + at, CHUNK)
            there = [pl.ds(pad + at - (k << low), CHUNK) for k in range(1, digits)]
            moved = [(moves_ref[there[k], :] & mask) == (k + 1 << low) for k in range(digits - 1)]
            if last:
                kept = (moves_ref[here, :] & valid) != 0
            for c in range(3):
                value = value_ref[a, c, here, :]
                for k in range(digits - 1):
                    value = jnp.where(moved[k], value_ref[a, c, there[k], :], value)
                if last:
                    disk_ref[c, pl.ds(at, CHUNK), :] = jnp.where(kept, value, 0.0)
                else:
                    value_ref[b, c, here, :] = value

    turned = jnp.concatenate([disk_ref[c].T for c in range(3)], axis=0)
    high, low = halved(turned)
    wave_high, wave_low = halved(chosen_ref[...])
    waves = jnp.dot(high, wave_high, preferred_element_type=jnp.float32)
    waves += jnp.dot(high, wave_low, preferred_element_type=jnp.float32)
    waves += jnp.dot(low, wave_high, preferred_element_type=jnp.float32)
    radii = harm_ref.shape[0]
    for c in range(3):
        harm_ref[:, c * 2 * NH : (c + 1) * 2 * NH] = waves[c * radii : (c + 1) * radii]
    block = radii // devices
    for place in range(devices // 2):
        even = harm_ref[2 * place * block : (2 * place + 1) * block, :]
        odd = harm_ref[(2 * place + 1) * block : (2 * place + 2) * block, :]
        keep_ref[place * block : (place + 1) * block, :] = jnp.where(girth_odd, odd, even)
        give_ref[place * block : (place + 1) * block, :] = jnp.where(girth_odd, even, odd)
    for copy in copies:
        copy.wait()


def section(velocity, pressure, energy, rate, halos, points, devices):
    _, cells_s, cells_g, cells_r = velocity.shape
    *lists, moves, chosen, counts = points
    rows, radii = lists[0].shape
    shape = functools.partial(jax.ShapeDtypeStruct, dtype=jnp.float32)
    scratch = lambda *dims: pltpu.VMEM(dims, jnp.float32)
    vmem = pl.BlockSpec(memory_space=pltpu.VMEM)
    smem = pl.BlockSpec(memory_space=pltpu.SMEM)
    return pl.pallas_call(
        functools.partial(section_kernel, devices),
        out_shape=(
            shape(velocity.shape),
            shape(energy.shape),
            shape(rate.shape),
            shape((radii // 2, 6 * NH)),
            shape((radii // 2, 6 * NH)),
        ),
        in_specs=[smem] + [vmem] * 14,
        out_specs=[pl.BlockSpec(memory_space=pl.ANY)] * 3 + [vmem] * 2,
        scratch_shapes=[
            scratch(*velocity.shape),
            scratch(*energy.shape),
            scratch(*rate.shape),
            scratch(6, cells_s, 3 * ROWS, cells_r),
            scratch(cells_s, 3 * ROWS, cells_r),
            scratch(PRODUCTS, cells_s, 4, cells_g, cells_r),
            scratch(3 - PRODUCTS, cells_s, 2, cells_r // LANES, cells_g, LANES),
            scratch(2, 3, moves.shape[0], radii),
            scratch(3, rows, radii),
            scratch(radii, 6 * NH),
            pltpu.SemaphoreType.DMA((3,)),
        ],
        compiler_params=pltpu.CompilerParams(vmem_limit_bytes=VMEM_LIMIT),
        name="section_and_disk",
    )(counts, velocity, pressure, energy, rate, *halos, *lists, moves, chosen)


def fourier_table(azimuths, modes):
    phase = np.arange(azimuths)[:, None] * np.arange(modes)[None, :] % azimuths
    angles = phase * (2.0 * math.pi / azimuths)
    table = np.concatenate([np.cos(angles), -np.sin(angles)], axis=1) / math.sqrt(azimuths)
    return jnp.asarray(table.astype(np.float32))


def body(velocity, pressure, kinetic_energy, dissipation_rate, corner_ids, fractions, sector_owner):
    _, cells_s, cells_g, cells_r = velocity.shape
    radii, azimuths = corner_ids.shape
    stream_count, girth_count = lax.axis_size("stream"), lax.axis_size("girth")
    devices = stream_count * girth_count

    def swap(values, axis, count, start):
        pairs = []
        for i in range(start, count - 1, 2):
            pairs += [(i, i + 1), (i + 1, i)]
        return lax.ppermute(values, axis, pairs)

    *slabs, ids, fracs = pack(
        velocity, pressure, kinetic_energy, dissipation_rate, corner_ids, fractions
    )
    girth_halos = (
        swap(slabs[2], "girth", girth_count, 0),
        swap(slabs[3], "girth", girth_count, 1),
    )
    stream_halos = (
        swap(slabs[0], "stream", stream_count, 0),
        swap(slabs[1], "stream", stream_count, 1),
    )
    halos = stream_halos + girth_halos
    points = prepare(
        sector_owner[:, 0],
        ids,
        fracs,
        fourier_table(azimuths, NH),
        (cells_s, cells_g, cells_r),
        girth_count,
    )
    new_velocity, new_energy, new_rate, keep, give = section(
        velocity, pressure, kinetic_energy, dissipation_rate, halos, points, devices
    )
    total = keep + swap(give, "girth", girth_count, 0)
    shares = lax.all_to_all(
        total.reshape(devices // 2, radii // devices, 6 * NH),
        ("stream", "girth"),
        split_axis=0,
        concat_axis=0,
        tiled=True,
        axis_index_groups=[list(range(parity, devices, 2)) for parity in (0, 1)],
    )
    return new_velocity, new_energy, new_rate, jnp.sum(shares, axis=0)


def solution(mesh):
    return jax.shard_map(
        body,
        mesh=mesh,
        in_specs=(
            P(None, "stream", "girth", None),
            P("stream", "girth", None),
            P("stream", "girth", None),
            P("stream", "girth", None),
            P(),
            P(),
            P(),
        ),
        out_specs=(
            P(None, "stream", "girth", None),
            P("stream", "girth", None),
            P("stream", "girth", None),
            P(("stream", "girth"), None),
        ),
        check_vma=False,
    )
```

```python
import functools
import math

import jax
import jax.numpy as jnp
import numpy as np
from jax import lax
from jax.experimental import pallas as pl
from jax.experimental.pallas import tpu as pltpu
from jax.sharding import PartitionSpec as P

NH = 128

base_viscosity = 0.05
time_step = 0.2
beta_star = 0.09
beta_rate = 0.075
alpha_rate = 0.52
wall_rate = 1.0

LANES = 128
ROWS = 8
SHIFT = 10
CHUNK = 32
PRODUCTS = 2
VMEM_LIMIT = 48 * 1024 * 1024


def in_hbm(values):
    return pltpu.with_memory_space_constraint(values, pltpu.HBM)


def pack_kernel(vel_hbm, p_hbm, k_hbm, w_hbm, ids_hbm, frac_hbm, *rest):
    *slabs, ids_ref, first_ref, fields, arrived = rest
    moves = [(vel_hbm, fields.at[0:3]), (p_hbm, fields.at[3]), (k_hbm, fields.at[4])]
    moves += [(w_hbm, fields.at[5]), (ids_hbm, ids_ref), (frac_hbm.at[0], first_ref)]
    copies = [
        pltpu.make_async_copy(source, target, arrived.at[i])
        for i, (source, target) in enumerate(moves)
    ]
    for copy in copies:
        copy.start()
    _, cells_s, cells_g, _ = fields.shape
    stream_odd = lax.axis_index("stream") % 2 == 1
    girth_odd = lax.axis_index("girth") % 2 == 1
    for copy in copies[:4]:
        copy.wait()
    for f in range(6):
        first, last = fields[f, 0:2], fields[f, cells_s - 2 : cells_s]
        slabs[0][f] = jnp.where(stream_odd, first, last)
        slabs[1][f] = jnp.where(stream_odd, last, first)
        first, last = fields[f, :, 0:2, :], fields[f, :, cells_g - 2 : cells_g, :]
        slabs[2][f] = jnp.where(girth_odd, first, last)
        slabs[3][f] = jnp.where(girth_odd, last, first)
    for copy in copies[4:]:
        copy.wait()


def pack(velocity, pressure, energy, rate, corner_ids, fractions):
    _, cells_s, cells_g, cells_r = velocity.shape
    stream = pltpu.VMEM((6, 2, cells_g, cells_r), jnp.float32)
    girth = pltpu.VMEM((6, cells_s, 2, cells_r), jnp.float32)
    points = [pltpu.VMEM(corner_ids.shape, x.dtype) for x in (corner_ids, fractions)]
    inputs = (velocity, pressure, energy, rate, corner_ids, fractions)
    return pl.pallas_call(
        pack_kernel,
        out_shape=[stream, stream, girth, girth] + points,
        in_specs=[pl.BlockSpec(memory_space=pltpu.HBM)] * 6,
        out_specs=[pl.BlockSpec(memory_space=pltpu.VMEM)] * 6,
        scratch_shapes=[
            pltpu.VMEM((6, cells_s, cells_g, cells_r), jnp.float32),
            pltpu.SemaphoreType.DMA((6,)),
        ],
        compiler_params=pltpu.CompilerParams(vmem_limit_bytes=VMEM_LIMIT),
        name="pack_halos",
    )(*(in_hbm(x) for x in inputs))


def network(rows):
    steps = (rows - 1).bit_length()
    return [(low, 1 << min(2, steps - low)) for low in range(0, steps, 2)]


def reach(rows):
    return max((digits - 1) << low for low, digits in network(rows))


def split(values, size):
    if size & (size - 1) == 0:
        return values >> (size.bit_length() - 1), values & (size - 1)
    return values // size, values % size


def prepare_kernel(
    cells_s,
    cells_g,
    cells_r,
    owner_ref,
    ids_ref,
    first_ref,
    frac_hbm,
    table_hbm,
    q_ref,
    fr_ref,
    xs_ref,
    xg_ref,
    moves_ref,
    chosen_ref,
    count_ref,
    frac_ref,
    table_ref,
    turned,
    picked,
    keys,
    frs,
    xss,
    xgs,
    order,
    arrived,
):
    copies = [
        pltpu.make_async_copy(frac_hbm.at[1], frac_ref.at[0], arrived.at[0]),
        pltpu.make_async_copy(frac_hbm.at[2], frac_ref.at[1], arrived.at[1]),
        pltpu.make_async_copy(table_hbm, table_ref, arrived.at[2]),
    ]
    for copy in copies:
        copy.start()
    stream_first = lax.axis_index("stream") * cells_s
    me = lax.axis_index("girth")
    sectors = owner_ref.shape[0]
    azimuths = ids_ref.shape[1]
    width = azimuths // sectors
    rows = fr_ref.shape[0]
    pad = moves_ref.shape[0] - rows
    passes = network(rows)
    valid = 1 << SHIFT - 1

    def listed(number, count):
        order[jnp.minimum(count, rows // width)] = number
        return count + (owner_ref[number] == me).astype(jnp.int32)

    owned = lax.fori_loop(0, sectors, listed, jnp.int32(0), unroll=8)
    for d in range(4):
        picked[d] = jnp.full(picked.shape[1:], -1.0 if d == 0 else 0.0, jnp.float32)
    chosen_ref[...] = jnp.zeros_like(chosen_ref)
    beyond = pl.ds(rows, pad)
    for slot in range(2):
        keys[slot, beyond, :] = jnp.zeros((pad, LANES), jnp.int32)
    moves_ref[0:pad, :] = jnp.zeros((pad, LANES), jnp.int32)
    planes = (ids_ref, first_ref, frac_ref.at[0], frac_ref.at[1])
    for d in range(4):
        if d >= 2:
            copies[d - 2].wait()
        for at in range(0, azimuths, LANES):
            cols = pl.ds(at, LANES)
            turned[d, cols, :] = planes[d][:, cols].astype(jnp.float32).T
    copies[2].wait()

    def sector(place, carry):
        source = pl.ds(pl.multiple_of(order[place] * width, width), width)
        target = pl.ds(pl.multiple_of(place * width, width), width)
        chosen_ref[target, :] = table_ref[source, :]
        for d in range(4):
            picked[d, target, :] = turned[d, source, :]
        return carry

    lax.fori_loop(0, owned, sector, jnp.int32(0))

    held = pl.ds(0, rows)
    ids = picked[0].astype(jnp.int32)
    stream_cell, rest = split(jnp.maximum(ids, 0), cells_g * cells_r)
    girth_cell, radial_cell = split(rest, cells_r)
    xs = (stream_cell - stream_first).astype(jnp.float32) + picked[1]
    kept = (ids >= 0) & (xs > -1.0) & (xs < float(cells_s))
    xss[0, held, :] = xs
    xgs[0, held, :] = girth_cell.astype(jnp.float32) + picked[2]
    frs[0, held, :] = picked[3]
    earlier = lax.broadcasted_iota(jnp.int32, (rows, rows), 0) > lax.broadcasted_iota(
        jnp.int32, (rows, rows), 1
    )
    earlier = earlier.astype(jnp.float32).astype(jnp.bfloat16)
    skipped = jnp.where(kept, 0.0, 1.0)
    before = jnp.dot(
        earlier, skipped.astype(jnp.bfloat16), preferred_element_type=jnp.float32
    ).astype(jnp.int32)
    counts = rows - jnp.sum(skipped, axis=0, keepdims=True).astype(jnp.int32)
    count_ref[0] = jnp.max(counts)
    moves_ref[pad : pad + rows, :] = jnp.where(kept, valid, 0)
    keys[0, held, :] = (radial_cell << SHIFT) + jnp.where(kept, before, 0)
    for number, (low, digits) in enumerate(passes):
        a, b = number % 2, 1 - number % 2
        mask = digits - 1 << low
        last = number == len(passes) - 1
        for at in range(0, rows, CHUNK):
            here, target = pl.ds(at, CHUNK), pl.ds(pad + at, CHUNK)
            there = [pl.ds(at + (k << low), CHUNK) for k in range(1, digits)]
            key = keys[a, here, :]
            arriving = [keys[a, t, :] for t in there]
            moved = [(arriving[k] & mask) == (k + 1 << low) for k in range(digits - 1)]
            key = jnp.where((key & mask) != 0, key & -(1 << SHIFT), key)
            came = moves_ref[target, :]
            out = [r[a, here, :] for r in (frs, xss, xgs)]
            for k in range(digits - 1):
                key = jnp.where(moved[k], arriving[k], key)
                came = came | jnp.where(moved[k], k + 1 << low, 0)
                out = [
                    jnp.where(moved[k], r[a, there[k], :], o) for r, o in zip((frs, xss, xgs), out)
                ]
            moves_ref[target, :] = came
            if last:
                q_ref[here, :] = key >> SHIFT
                fr_ref[here, :] = out[0]
                xs_ref[here, :] = out[1]
                xg_ref[here, :] = out[2]
            else:
                keys[b, here, :] = key
                frs[b, here, :] = out[0]
                xss[b, here, :] = out[1]
                xgs[b, here, :] = out[2]


def prepare(owners, corner_ids, first, fractions, table, cells, girth_count):
    cells_s, cells_g, cells_r = cells
    radii, azimuths = corner_ids.shape
    sectors = owners.shape[0]
    rows = 3 * sectors // girth_count * (azimuths // sectors)
    pad = reach(rows)
    shape = jax.ShapeDtypeStruct
    lists = (rows, radii)
    vmem = pl.BlockSpec(memory_space=pltpu.VMEM)
    smem = pl.BlockSpec(memory_space=pltpu.SMEM)
    hbm = pl.BlockSpec(memory_space=pltpu.HBM)
    return pl.pallas_call(
        functools.partial(prepare_kernel, cells_s, cells_g, cells_r),
        out_shape=(
            shape(lists, jnp.int32),
            shape(lists, jnp.float32),
            shape(lists, jnp.float32),
            shape(lists, jnp.float32),
            shape((pad + rows, radii), jnp.int32),
            shape((rows, 2 * NH), jnp.float32),
            shape((1,), jnp.int32),
        ),
        in_specs=[smem, vmem, vmem, hbm, hbm],
        out_specs=[vmem] * 6 + [smem],
        scratch_shapes=[
            pltpu.VMEM((2, radii, azimuths), jnp.float32),
            pltpu.VMEM(table.shape, jnp.float32),
            pltpu.VMEM((4, azimuths, radii), jnp.float32),
            pltpu.VMEM((4, rows, radii), jnp.float32),
            pltpu.VMEM((2, rows + pad, radii), jnp.int32),
        ]
        + [pltpu.VMEM((2, rows + pad, radii), jnp.float32)] * 3
        + [pltpu.SMEM((rows // (azimuths // sectors) + 1,), jnp.int32)]
        + [pltpu.SemaphoreType.DMA((3,))],
        compiler_params=pltpu.CompilerParams(vmem_limit_bytes=VMEM_LIMIT),
        cost_estimate=pl.CostEstimate(
            flops=20 * radii * azimuths, bytes_accessed=44 * radii * azimuths, transcendentals=0
        ),
        name="prepare_points",
    )(in_hbm(owners), corner_ids, first, in_hbm(fractions), in_hbm(table))


def radial(values, amount, fill):
    extent = values.shape[-1]
    rolled = pltpu.roll(values, (-amount) % extent, values.ndim - 1)
    position = lax.broadcasted_iota(jnp.int32, values.shape, values.ndim - 1) + amount
    return jnp.where((position >= 0) & (position < extent), rolled, fill)


def advance(own, before, after, left, right, ext_ref, visc_ref):
    cells_s, cells_g, _ = own[0].shape
    mid = ROWS

    def along_s(stack, amount):
        return stack[2 + amount : 2 + amount + cells_s]

    def along_g(ref, amount):
        return ref[:, mid + amount : mid + amount + cells_g, :]

    def viscosity(energy, rate):
        return base_viscosity + energy / (rate + wall_rate)

    stacks = [jnp.concatenate([before[f], own[f], after[f]], axis=0) for f in range(6)]
    for f in range(6):
        ext_ref[f, :, mid - 2 : mid, :] = left[f]
        ext_ref[f, :, mid : mid + cells_g, :] = own[f]
        ext_ref[f, :, mid + cells_g : mid + cells_g + 2, :] = right[f]
    middle = viscosity(own[4], own[5])
    visc_stack = viscosity(stacks[4], stacks[5])
    visc_ref[:, mid - 2 : mid, :] = viscosity(left[4], left[5])
    visc_ref[:, mid : mid + cells_g, :] = middle
    visc_ref[:, mid + cells_g : mid + cells_g + 2, :] = viscosity(right[4], right[5])
    faces = [
        (
            0.5 * (middle + along_s(visc_stack, 1)),
            0.5 * (middle + along_s(visc_stack, -1)),
        ),
        (
            0.5 * (middle + along_g(visc_ref, 1)),
            0.5 * (middle + along_g(visc_ref, -1)),
        ),
        (
            0.5 * (middle + radial(middle, 1, base_viscosity)),
            0.5 * (middle + radial(middle, -1, base_viscosity)),
        ),
    ]

    def neighbour(f, direction, amount):
        if direction == 0:
            return along_s(stacks[f], amount)
        if direction == 1:
            return along_g(ext_ref.at[f], amount)
        return radial(own[f], amount, 0.0)

    def terms(f, direction):
        up, down = neighbour(f, direction, 1), neighbour(f, direction, -1)
        far = neighbour(f, direction, 2) - neighbour(f, direction, -2)
        gradient = (8.0 * (up - down) - far) * (1.0 / 12.0)
        above, below = faces[direction]
        return gradient, above * (up - own[f]) - below * (own[f] - down)

    strain = None
    updated = []
    for f in range(3):
        change = -terms(3, f)[0]
        for direction in range(3):
            gradient, spread = terms(f, direction)
            strain = gradient * gradient if strain is None else strain + gradient * gradient
            change = change - own[direction] * gradient + spread
        updated.append(own[f] + time_step * change)
    energy = own[4] / (own[5] + wall_rate) * strain - beta_star * own[4] * own[5]
    rate = alpha_rate * strain - beta_rate * own[5] * own[5]
    for direction in range(3):
        gradient, spread = terms(4, direction)
        energy = energy - own[direction] * gradient + spread
        gradient, spread = terms(5, direction)
        rate = rate - own[direction] * gradient + spread
    return updated, own[4] + time_step * energy, own[5] + time_step * rate


def girth_sums(parts):
    row = lax.broadcasted_iota(jnp.int32, parts[0].shape, 0)

    def swapped(values, distance):
        up = pltpu.roll(values, distance, 0)
        if 2 * distance == ROWS:
            return up
        return jnp.where((row & distance) != 0, up, pltpu.roll(values, ROWS - distance, 0))

    distance = ROWS // 2
    while distance > 0:
        low = (row & distance) == 0
        parts = [
            jnp.where(low, x, y) + swapped(jnp.where(low, y, x), distance)
            for x, y in zip(parts[:distance], parts[distance:])
        ]
        distance //= 2
    return parts[0]


def section_kernel(
    devices,
    count_ref,
    vel_ref,
    p_ref,
    k_ref,
    w_ref,
    stream_a,
    stream_b,
    girth_a,
    girth_b,
    q_ref,
    fr_ref,
    xs_ref,
    xg_ref,
    moves_ref,
    chosen_ref,
    new_vel_hbm,
    new_k_hbm,
    new_w_hbm,
    keep_ref,
    give_ref,
    new_vel_ref,
    new_k_ref,
    new_w_ref,
    ext_ref,
    visc_ref,
    field_ref,
    gather_ref,
    value_ref,
    disk_ref,
    harm_ref,
    stored,
):
    cells_s, cells_g, cells_r = p_ref.shape
    rows = fr_ref.shape[0]
    pad = moves_ref.shape[0] - rows
    passes = network(rows)
    valid = 1 << SHIFT - 1
    stream_odd = lax.axis_index("stream") % 2 == 1
    girth_odd = lax.axis_index("girth") % 2 == 1

    own = [vel_ref[0], vel_ref[1], vel_ref[2], p_ref[...], k_ref[...], w_ref[...]]
    six = range(6)
    updated, energy, rate = advance(
        own,
        [jnp.where(stream_odd, stream_a[f], stream_b[f]) for f in six],
        [jnp.where(stream_odd, stream_b[f], stream_a[f]) for f in six],
        [jnp.where(girth_odd, girth_a[f], girth_b[f]) for f in six],
        [jnp.where(girth_odd, girth_b[f], girth_a[f]) for f in six],
        ext_ref,
        visc_ref,
    )
    new_k_ref[...] = energy
    new_w_ref[...] = rate

    def halved(values):
        high = values.astype(jnp.bfloat16)
        return high, (values - high.astype(jnp.float32)).astype(jnp.bfloat16)

    def rounded(values):
        return values.astype(jnp.bfloat16).astype(jnp.float32)

    halves = cells_r // LANES
    for c in range(3):
        new_vel_ref[c] = updated[c]
        slope = radial(updated[c], 1, 0.0) - updated[c]
        for kind, values in enumerate((updated[c], slope)):
            if c < PRODUCTS:
                high = rounded(values)
                field_ref[c, :, 2 * kind] = high
                field_ref[c, :, 2 * kind + 1] = rounded(values - high)
            else:
                for h in range(halves):
                    lanes = slice(h * LANES, (h + 1) * LANES)
                    gather_ref[c - PRODUCTS, :, kind, h] = values[:, :, lanes]
    results = ((new_vel_ref, new_vel_hbm), (new_k_ref, new_k_hbm), (new_w_ref, new_w_hbm))
    copies = [
        pltpu.make_async_copy(source, target, stored.at[i])
        for i, (source, target) in enumerate(results)
    ]
    for copy in copies:
        copy.start()

    kinds = 4
    table = field_ref[...].reshape(PRODUCTS * cells_s * kinds * cells_g, cells_r)
    table = table.astype(jnp.bfloat16)
    pair = 2 * LANES
    girth_row = lax.broadcasted_iota(jnp.int32, (cells_g, pair), 0).astype(jnp.float32)
    index_type = jnp.bfloat16 if cells_r <= 256 else jnp.float32
    radial_row = lax.broadcasted_iota(jnp.int32, (cells_r, pair), 0).astype(jnp.float32)
    radial_row = radial_row.astype(index_type)
    one, none = jnp.ones((), jnp.bfloat16), jnp.zeros((), jnp.bfloat16)

    def two(values, j):
        return jnp.concatenate([values[j : j + 1], values[j + 1 : j + 2]], axis=1)

    def spread(values, j):
        return jnp.broadcast_to(values[j : j + 1], (cells_g, LANES))

    def pick(c, s, kind, index, half_of):
        out = None
        for h in range(halves):
            got = jnp.take_along_axis(
                gather_ref[c - PRODUCTS, s, kind, h], index, axis=1, mode="promise_in_bounds"
            )
            out = got if out is None else jnp.where(half_of[h], got, out)
        return out

    def eight(at):
        here = pl.ds(at, ROWS)
        q8, fr8, xg8, xs8 = (r[here, :] for r in (q_ref, fr_ref, xg_ref, xs_ref))
        hs8 = [jnp.maximum(1.0 - jnp.abs(xs8 - float(s)), 0.0) for s in range(cells_s)]
        index8 = q8 & (LANES - 1)
        qf8 = q8.astype(jnp.float32)
        sums = [[], [], []]
        for j in range(0, ROWS, 2):
            chosen_q = jnp.broadcast_to(two(qf8, j), (cells_r, pair)).astype(index_type)
            hot = jnp.where(radial_row == chosen_q, one, none)
            got = jnp.dot(table, hot, preferred_element_type=jnp.float32)
            got = got.reshape(PRODUCTS, cells_s, kinds, cells_g, pair)
            fr = two(fr8, j)
            hg = jnp.maximum(1.0 - jnp.abs(two(xg8, j) - girth_row), 0.0)
            hs = [two(hs8[s], j) for s in range(cells_s)]
            for c in range(PRODUCTS):
                total = None
                for s in range(cells_s):
                    value = got[c, s, 0] + got[c, s, 1] + fr * (got[c, s, 2] + got[c, s, 3])
                    value = hs[s] * value
                    total = value if total is None else total + value
                total = hg * total
                sums[c] += [total[:, :LANES], total[:, LANES:]]
            for i in (j, j + 1):
                index, q = spread(index8, i), spread(q8, i)
                half_of = [q >= h * LANES for h in range(halves)]
                own_hg = hg[:, (i - j) * LANES : (i - j + 1) * LANES]
                for c in range(PRODUCTS, 3):
                    total = None
                    for s in range(cells_s):
                        value = pick(c, s, 0, index, half_of)
                        value = value + fr8[i : i + 1] * pick(c, s, 1, index, half_of)
                        value = hs8[s][i : i + 1] * value
                        total = value if total is None else total + value
                    sums[c].append(own_hg * total)
        for c in range(3):
            value_ref[0, c, pl.ds(pad + at, ROWS), :] = girth_sums(sums[c])

    def step(group, carry):
        for part in range(2):
            eight(pl.multiple_of((2 * group + part) * ROWS, ROWS))
        return carry

    lax.fori_loop(0, (count_ref[0] + 2 * ROWS - 1) // (2 * ROWS), step, jnp.int32(0))

    for number, (low, digits) in enumerate(reversed(passes)):
        a, b = number % 2, 1 - number % 2
        mask = digits - 1 << low
        last = number == len(passes) - 1
        for at in range(0, rows, CHUNK):
            here = pl.ds(pad + at, CHUNK)
            there = [pl.ds(pad + at - (k << low), CHUNK) for k in range(1, digits)]
            moved = [(moves_ref[there[k], :] & mask) == (k + 1 << low) for k in range(digits - 1)]
            if last:
                kept = (moves_ref[here, :] & valid) != 0
            for c in range(3):
                value = value_ref[a, c, here, :]
                for k in range(digits - 1):
                    value = jnp.where(moved[k], value_ref[a, c, there[k], :], value)
                if last:
                    disk_ref[c, pl.ds(at, CHUNK), :] = jnp.where(kept, value, 0.0)
                else:
                    value_ref[b, c, here, :] = value

    turned = jnp.concatenate([disk_ref[c].T for c in range(3)], axis=0)
    high, low = halved(turned)
    wave_high, wave_low = halved(chosen_ref[...])
    waves = jnp.dot(high, wave_high, preferred_element_type=jnp.float32)
    waves += jnp.dot(high, wave_low, preferred_element_type=jnp.float32)
    waves += jnp.dot(low, wave_high, preferred_element_type=jnp.float32)
    radii = harm_ref.shape[0]
    for c in range(3):
        harm_ref[:, c * 2 * NH : (c + 1) * 2 * NH] = waves[c * radii : (c + 1) * radii]
    block = radii // devices
    for place in range(devices // 2):
        even = harm_ref[2 * place * block : (2 * place + 1) * block, :]
        odd = harm_ref[(2 * place + 1) * block : (2 * place + 2) * block, :]
        keep_ref[place * block : (place + 1) * block, :] = jnp.where(girth_odd, odd, even)
        give_ref[place * block : (place + 1) * block, :] = jnp.where(girth_odd, even, odd)
    for copy in copies:
        copy.wait()


def section(velocity, pressure, energy, rate, halos, points, devices):
    _, cells_s, cells_g, cells_r = velocity.shape
    *lists, moves, chosen, counts = points
    rows, radii = lists[0].shape
    shape = functools.partial(jax.ShapeDtypeStruct, dtype=jnp.float32)
    scratch = lambda *dims: pltpu.VMEM(dims, jnp.float32)
    vmem = pl.BlockSpec(memory_space=pltpu.VMEM)
    smem = pl.BlockSpec(memory_space=pltpu.SMEM)
    return pl.pallas_call(
        functools.partial(section_kernel, devices),
        out_shape=(
            shape(velocity.shape),
            shape(energy.shape),
            shape(rate.shape),
            shape((radii // 2, 6 * NH)),
            shape((radii // 2, 6 * NH)),
        ),
        in_specs=[smem] + [vmem] * 14,
        out_specs=[pl.BlockSpec(memory_space=pl.ANY)] * 3 + [vmem] * 2,
        scratch_shapes=[
            scratch(*velocity.shape),
            scratch(*energy.shape),
            scratch(*rate.shape),
            scratch(6, cells_s, 3 * ROWS, cells_r),
            scratch(cells_s, 3 * ROWS, cells_r),
            scratch(PRODUCTS, cells_s, 4, cells_g, cells_r),
            scratch(3 - PRODUCTS, cells_s, 2, cells_r // LANES, cells_g, LANES),
            scratch(2, 3, moves.shape[0], radii),
            scratch(3, rows, radii),
            scratch(radii, 6 * NH),
            pltpu.SemaphoreType.DMA((3,)),
        ],
        compiler_params=pltpu.CompilerParams(vmem_limit_bytes=VMEM_LIMIT),
        name="section_and_disk",
    )(counts, velocity, pressure, energy, rate, *halos, *lists, moves, chosen)


def fourier_table(azimuths, modes):
    phase = np.arange(azimuths)[:, None] * np.arange(modes)[None, :] % azimuths
    angles = phase * (2.0 * math.pi / azimuths)
    table = np.concatenate([np.cos(angles), -np.sin(angles)], axis=1) / math.sqrt(azimuths)
    return jnp.asarray(table.astype(np.float32))


def body(velocity, pressure, kinetic_energy, dissipation_rate, corner_ids, fractions, sector_owner):
    _, cells_s, cells_g, cells_r = velocity.shape
    radii, azimuths = corner_ids.shape
    stream_count, girth_count = lax.axis_size("stream"), lax.axis_size("girth")
    devices = stream_count * girth_count

    def swap(values, axis, count, start):
        pairs = []
        for i in range(start, count - 1, 2):
            pairs += [(i, i + 1), (i + 1, i)]
        return lax.ppermute(values, axis, pairs)

    *slabs, ids, first = pack(
        velocity, pressure, kinetic_energy, dissipation_rate, corner_ids, fractions
    )
    girth_halos = (
        swap(slabs[2], "girth", girth_count, 0),
        swap(slabs[3], "girth", girth_count, 1),
    )
    stream_halos = (
        swap(slabs[0], "stream", stream_count, 0),
        swap(slabs[1], "stream", stream_count, 1),
    )
    halos = stream_halos + girth_halos
    points = prepare(
        sector_owner[:, 0],
        ids,
        first,
        fractions,
        fourier_table(azimuths, NH),
        (cells_s, cells_g, cells_r),
        girth_count,
    )
    new_velocity, new_energy, new_rate, keep, give = section(
        velocity, pressure, kinetic_energy, dissipation_rate, halos, points, devices
    )
    total = keep + swap(give, "girth", girth_count, 0)
    shares = lax.all_to_all(
        total.reshape(devices // 2, radii // devices, 6 * NH),
        ("stream", "girth"),
        split_axis=0,
        concat_axis=0,
        tiled=True,
        axis_index_groups=[list(range(parity, devices, 2)) for parity in (0, 1)],
    )
    return new_velocity, new_energy, new_rate, jnp.sum(shares, axis=0)


def solution(mesh):
    return jax.shard_map(
        body,
        mesh=mesh,
        in_specs=(
            P(None, "stream", "girth", None),
            P("stream", "girth", None),
            P("stream", "girth", None),
            P("stream", "girth", None),
            P(),
            P(),
            P(),
        ),
        out_specs=(
            P(None, "stream", "girth", None),
            P("stream", "girth", None),
            P("stream", "girth", None),
            P(("stream", "girth"), None),
        ),
        check_vma=False,
    )
```

```python
import functools
import math

import jax
import jax.numpy as jnp
import numpy as np
from jax import lax
from jax.experimental import pallas as pl
from jax.experimental.pallas import tpu as pltpu
from jax.sharding import PartitionSpec as P

NH = 128

base_viscosity = 0.05
time_step = 0.2
beta_star = 0.09
beta_rate = 0.075
alpha_rate = 0.52
wall_rate = 1.0

LANES = 128
ROWS = 8
SHIFT = 10
CHUNK = 32
PRODUCTS = 2
VMEM_LIMIT = 48 * 1024 * 1024


def in_hbm(values):
    return pltpu.with_memory_space_constraint(values, pltpu.HBM)


def pack_kernel(vel_hbm, p_hbm, k_hbm, w_hbm, ids_hbm, frac_hbm, *rest):
    *slabs, ids_ref, first_ref, fields, arrived = rest
    moves = [(vel_hbm, fields.at[0:3]), (p_hbm, fields.at[3]), (k_hbm, fields.at[4])]
    moves += [(w_hbm, fields.at[5]), (ids_hbm, ids_ref), (frac_hbm.at[0], first_ref)]
    copies = [
        pltpu.make_async_copy(source, target, arrived.at[i])
        for i, (source, target) in enumerate(moves)
    ]
    for copy in copies:
        copy.start()
    _, cells_s, cells_g, _ = fields.shape
    stream_odd = lax.axis_index("stream") % 2 == 1
    girth_odd = lax.axis_index("girth") % 2 == 1
    for copy in copies[:4]:
        copy.wait()
    for f in range(6):
        first, last = fields[f, 0:2], fields[f, cells_s - 2 : cells_s]
        slabs[0][f] = jnp.where(stream_odd, first, last)
        slabs[1][f] = jnp.where(stream_odd, last, first)
        first, last = fields[f, :, 0:2, :], fields[f, :, cells_g - 2 : cells_g, :]
        slabs[2][f] = jnp.where(girth_odd, first, last)
        slabs[3][f] = jnp.where(girth_odd, last, first)
    for copy in copies[4:]:
        copy.wait()


def pack(velocity, pressure, energy, rate, corner_ids, fractions):
    _, cells_s, cells_g, cells_r = velocity.shape
    stream = pltpu.VMEM((6, 2, cells_g, cells_r), jnp.float32)
    girth = pltpu.VMEM((6, cells_s, 2, cells_r), jnp.float32)
    points = [pltpu.VMEM(corner_ids.shape, x.dtype) for x in (corner_ids, fractions)]
    inputs = (velocity, pressure, energy, rate, corner_ids, fractions)
    return pl.pallas_call(
        pack_kernel,
        out_shape=[stream, stream, girth, girth] + points,
        in_specs=[pl.BlockSpec(memory_space=pltpu.HBM)] * 6,
        out_specs=[pl.BlockSpec(memory_space=pltpu.VMEM)] * 6,
        scratch_shapes=[
            pltpu.VMEM((6, cells_s, cells_g, cells_r), jnp.float32),
            pltpu.SemaphoreType.DMA((6,)),
        ],
        compiler_params=pltpu.CompilerParams(vmem_limit_bytes=VMEM_LIMIT),
        name="pack_halos",
    )(*(in_hbm(x) for x in inputs))


def network(rows):
    steps = (rows - 1).bit_length()
    return [(low, 1 << min(2, steps - low)) for low in range(0, steps, 2)]


def reach(rows):
    return max((digits - 1) << low for low, digits in network(rows))


def split(values, size):
    if size & (size - 1) == 0:
        return values >> (size.bit_length() - 1), values & (size - 1)
    return values // size, values % size


def prepare_kernel(
    cells_s,
    cells_g,
    cells_r,
    owner_ref,
    ids_ref,
    first_ref,
    frac_hbm,
    table_hbm,
    q_ref,
    fr_ref,
    xs_ref,
    xg_ref,
    moves_ref,
    chosen_ref,
    count_ref,
    frac_ref,
    table_ref,
    turned,
    picked,
    keys,
    frs,
    xss,
    xgs,
    order,
    arrived,
):
    copies = [
        pltpu.make_async_copy(frac_hbm.at[1], frac_ref.at[0], arrived.at[0]),
        pltpu.make_async_copy(frac_hbm.at[2], frac_ref.at[1], arrived.at[1]),
        pltpu.make_async_copy(table_hbm, table_ref, arrived.at[2]),
    ]
    for copy in copies:
        copy.start()
    stream_first = lax.axis_index("stream") * cells_s
    me = lax.axis_index("girth")
    sectors = owner_ref.shape[0]
    azimuths = ids_ref.shape[1]
    width = azimuths // sectors
    rows = fr_ref.shape[0]
    pad = moves_ref.shape[0] - rows
    passes = network(rows)
    valid = 1 << SHIFT - 1

    def listed(number, count):
        order[jnp.minimum(count, rows // width)] = number
        return count + (owner_ref[number] == me).astype(jnp.int32)

    owned = lax.fori_loop(0, sectors, listed, jnp.int32(0), unroll=8)
    for d in range(4):
        picked[d] = jnp.full(picked.shape[1:], -1.0 if d == 0 else 0.0, jnp.float32)
    chosen_ref[...] = jnp.zeros_like(chosen_ref)
    beyond = pl.ds(rows, pad)
    for slot in range(2):
        keys[slot, beyond, :] = jnp.zeros((pad, LANES), jnp.int32)
    moves_ref[0:pad, :] = jnp.zeros((pad, LANES), jnp.int32)
    planes = (ids_ref, first_ref, frac_ref.at[0], frac_ref.at[1])
    for d in range(4):
        if d >= 2:
            copies[d - 2].wait()
        for at in range(0, azimuths, LANES):
            cols = pl.ds(at, LANES)
            turned[d, cols, :] = planes[d][:, cols].astype(jnp.float32).T
    copies[2].wait()

    def sector(place, carry):
        source = pl.ds(pl.multiple_of(order[place] * width, width), width)
        target = pl.ds(pl.multiple_of(place * width, width), width)
        chosen_ref[target, :] = table_ref[source, :]
        for d in range(4):
            picked[d, target, :] = turned[d, source, :]
        return carry

    lax.fori_loop(0, owned, sector, jnp.int32(0))

    held = pl.ds(0, rows)
    ids = picked[0].astype(jnp.int32)
    stream_cell, rest = split(jnp.maximum(ids, 0), cells_g * cells_r)
    girth_cell, radial_cell = split(rest, cells_r)
    xs = (stream_cell - stream_first).astype(jnp.float32) + picked[1]
    kept = (ids >= 0) & (xs > -1.0) & (xs < float(cells_s))
    xss[0, held, :] = xs
    xgs[0, held, :] = girth_cell.astype(jnp.float32) + picked[2]
    frs[0, held, :] = picked[3]
    earlier = lax.broadcasted_iota(jnp.int32, (rows, rows), 0) > lax.broadcasted_iota(
        jnp.int32, (rows, rows), 1
    )
    earlier = earlier.astype(jnp.float32).astype(jnp.bfloat16)
    skipped = jnp.where(kept, 0.0, 1.0)
    before = jnp.dot(
        earlier, skipped.astype(jnp.bfloat16), preferred_element_type=jnp.float32
    ).astype(jnp.int32)
    counts = rows - jnp.sum(skipped, axis=0, keepdims=True).astype(jnp.int32)
    count_ref[0] = jnp.max(counts)
    moves_ref[pad : pad + rows, :] = jnp.where(kept, valid, 0)
    keys[0, held, :] = (radial_cell << SHIFT) + jnp.where(kept, before, 0)
    for number, (low, digits) in enumerate(passes):
        a, b = number % 2, 1 - number % 2
        mask = digits - 1 << low
        last = number == len(passes) - 1
        for at in range(0, rows, CHUNK):
            here, target = pl.ds(at, CHUNK), pl.ds(pad + at, CHUNK)
            there = [pl.ds(at + (k << low), CHUNK) for k in range(1, digits)]
            key = keys[a, here, :]
            arriving = [keys[a, t, :] for t in there]
            moved = [(arriving[k] & mask) == (k + 1 << low) for k in range(digits - 1)]
            key = jnp.where((key & mask) != 0, key & -(1 << SHIFT), key)
            came = moves_ref[target, :]
            out = [r[a, here, :] for r in (frs, xss, xgs)]
            for k in range(digits - 1):
                key = jnp.where(moved[k], arriving[k], key)
                came = came | jnp.where(moved[k], k + 1 << low, 0)
                out = [
                    jnp.where(moved[k], r[a, there[k], :], o) for r, o in zip((frs, xss, xgs), out)
                ]
            moves_ref[target, :] = came
            if last:
                q_ref[here, :] = key >> SHIFT
                fr_ref[here, :] = out[0]
                xs_ref[here, :] = out[1]
                xg_ref[here, :] = out[2]
            else:
                keys[b, here, :] = key
                frs[b, here, :] = out[0]
                xss[b, here, :] = out[1]
                xgs[b, here, :] = out[2]


def prepare(owners, corner_ids, first, fractions, table, cells, girth_count):
    cells_s, cells_g, cells_r = cells
    radii, azimuths = corner_ids.shape
    sectors = owners.shape[0]
    rows = 3 * sectors // girth_count * (azimuths // sectors)
    pad = reach(rows)
    shape = jax.ShapeDtypeStruct
    lists = (rows, radii)
    vmem = pl.BlockSpec(memory_space=pltpu.VMEM)
    smem = pl.BlockSpec(memory_space=pltpu.SMEM)
    hbm = pl.BlockSpec(memory_space=pltpu.HBM)
    return pl.pallas_call(
        functools.partial(prepare_kernel, cells_s, cells_g, cells_r),
        out_shape=(
            shape(lists, jnp.int32),
            shape(lists, jnp.float32),
            shape(lists, jnp.float32),
            shape(lists, jnp.float32),
            shape((pad + rows, radii), jnp.int32),
            shape((rows, 2 * NH), jnp.float32),
            shape((1,), jnp.int32),
        ),
        in_specs=[smem, vmem, vmem, hbm, hbm],
        out_specs=[vmem] * 6 + [smem],
        scratch_shapes=[
            pltpu.VMEM((2, radii, azimuths), jnp.float32),
            pltpu.VMEM(table.shape, jnp.float32),
            pltpu.VMEM((4, azimuths, radii), jnp.float32),
            pltpu.VMEM((4, rows, radii), jnp.float32),
            pltpu.VMEM((2, rows + pad, radii), jnp.int32),
        ]
        + [pltpu.VMEM((2, rows + pad, radii), jnp.float32)] * 3
        + [pltpu.SMEM((rows // (azimuths // sectors) + 1,), jnp.int32)]
        + [pltpu.SemaphoreType.DMA((3,))],
        compiler_params=pltpu.CompilerParams(vmem_limit_bytes=VMEM_LIMIT),
        cost_estimate=pl.CostEstimate(
            flops=20 * radii * azimuths, bytes_accessed=44 * radii * azimuths, transcendentals=0
        ),
        name="prepare_points",
    )(in_hbm(owners), corner_ids, first, in_hbm(fractions), in_hbm(table))


def radial(values, amount, fill):
    extent = values.shape[-1]
    rolled = pltpu.roll(values, (-amount) % extent, values.ndim - 1)
    position = lax.broadcasted_iota(jnp.int32, values.shape, values.ndim - 1) + amount
    return jnp.where((position >= 0) & (position < extent), rolled, fill)


def advance(own, before, after, left, right, ext_ref, visc_ref):
    cells_s, cells_g, _ = own[0].shape
    mid = ROWS

    def along_s(stack, amount):
        return stack[2 + amount : 2 + amount + cells_s]

    def along_g(ref, amount):
        return ref[:, mid + amount : mid + amount + cells_g, :]

    def viscosity(energy, rate):
        return base_viscosity + energy / (rate + wall_rate)

    stacks = [jnp.concatenate([before[f], own[f], after[f]], axis=0) for f in range(6)]
    for f in range(6):
        ext_ref[f, :, mid - 2 : mid, :] = left[f]
        ext_ref[f, :, mid : mid + cells_g, :] = own[f]
        ext_ref[f, :, mid + cells_g : mid + cells_g + 2, :] = right[f]
    middle = viscosity(own[4], own[5])
    visc_stack = viscosity(stacks[4], stacks[5])
    visc_ref[:, mid - 2 : mid, :] = viscosity(left[4], left[5])
    visc_ref[:, mid : mid + cells_g, :] = middle
    visc_ref[:, mid + cells_g : mid + cells_g + 2, :] = viscosity(right[4], right[5])
    faces = [
        (
            0.5 * (middle + along_s(visc_stack, 1)),
            0.5 * (middle + along_s(visc_stack, -1)),
        ),
        (
            0.5 * (middle + along_g(visc_ref, 1)),
            0.5 * (middle + along_g(visc_ref, -1)),
        ),
        (
            0.5 * (middle + radial(middle, 1, base_viscosity)),
            0.5 * (middle + radial(middle, -1, base_viscosity)),
        ),
    ]

    def neighbour(f, direction, amount):
        if direction == 0:
            return along_s(stacks[f], amount)
        if direction == 1:
            return along_g(ext_ref.at[f], amount)
        return radial(own[f], amount, 0.0)

    def terms(f, direction):
        up, down = neighbour(f, direction, 1), neighbour(f, direction, -1)
        far = neighbour(f, direction, 2) - neighbour(f, direction, -2)
        gradient = (8.0 * (up - down) - far) * (1.0 / 12.0)
        above, below = faces[direction]
        return gradient, above * (up - own[f]) - below * (own[f] - down)

    strain = None
    updated = []
    for f in range(3):
        change = -terms(3, f)[0]
        for direction in range(3):
            gradient, spread = terms(f, direction)
            strain = gradient * gradient if strain is None else strain + gradient * gradient
            change = change - own[direction] * gradient + spread
        updated.append(own[f] + time_step * change)
    energy = own[4] / (own[5] + wall_rate) * strain - beta_star * own[4] * own[5]
    rate = alpha_rate * strain - beta_rate * own[5] * own[5]
    for direction in range(3):
        gradient, spread = terms(4, direction)
        energy = energy - own[direction] * gradient + spread
        gradient, spread = terms(5, direction)
        rate = rate - own[direction] * gradient + spread
    return updated, own[4] + time_step * energy, own[5] + time_step * rate


def girth_sums(parts):
    row = lax.broadcasted_iota(jnp.int32, parts[0].shape, 0)

    def swapped(values, distance):
        up = pltpu.roll(values, distance, 0)
        if 2 * distance == ROWS:
            return up
        return jnp.where((row & distance) != 0, up, pltpu.roll(values, ROWS - distance, 0))

    distance = ROWS // 2
    while distance > 0:
        low = (row & distance) == 0
        parts = [
            jnp.where(low, x, y) + swapped(jnp.where(low, y, x), distance)
            for x, y in zip(parts[:distance], parts[distance:])
        ]
        distance //= 2
    return parts[0]


def section_kernel(
    devices,
    girth_count,
    count_ref,
    vel_ref,
    p_ref,
    k_ref,
    w_ref,
    stream_a,
    stream_b,
    girth_a,
    girth_b,
    q_ref,
    fr_ref,
    xs_ref,
    xg_ref,
    moves_ref,
    chosen_ref,
    new_vel_hbm,
    new_k_hbm,
    new_w_hbm,
    keep_ref,
    give_ref,
    new_vel_ref,
    new_k_ref,
    new_w_ref,
    ext_ref,
    visc_ref,
    field_ref,
    gather_ref,
    value_ref,
    disk_ref,
    harm_ref,
    stored,
):
    cells_s, cells_g, cells_r = p_ref.shape
    rows = fr_ref.shape[0]
    pad = moves_ref.shape[0] - rows
    passes = network(rows)
    valid = 1 << SHIFT - 1
    stream_odd = lax.axis_index("stream") % 2 == 1
    girth_odd = lax.axis_index("girth") % 2 == 1

    own = [vel_ref[0], vel_ref[1], vel_ref[2], p_ref[...], k_ref[...], w_ref[...]]
    six = range(6)
    updated, energy, rate = advance(
        own,
        [jnp.where(stream_odd, stream_a[f], stream_b[f]) for f in six],
        [jnp.where(stream_odd, stream_b[f], stream_a[f]) for f in six],
        [jnp.where(girth_odd, girth_a[f], girth_b[f]) for f in six],
        [jnp.where(girth_odd, girth_b[f], girth_a[f]) for f in six],
        ext_ref,
        visc_ref,
    )
    new_k_ref[...] = energy
    new_w_ref[...] = rate

    def halved(values):
        high = values.astype(jnp.bfloat16)
        return high, (values - high.astype(jnp.float32)).astype(jnp.bfloat16)

    def rounded(values):
        return values.astype(jnp.bfloat16).astype(jnp.float32)

    halves = cells_r // LANES
    for c in range(3):
        new_vel_ref[c] = updated[c]
        slope = radial(updated[c], 1, 0.0) - updated[c]
        for kind, values in enumerate((updated[c], slope)):
            if c < PRODUCTS:
                high = rounded(values)
                field_ref[c, :, 2 * kind] = high
                field_ref[c, :, 2 * kind + 1] = rounded(values - high)
            else:
                for h in range(halves):
                    lanes = slice(h * LANES, (h + 1) * LANES)
                    gather_ref[c - PRODUCTS, :, kind, h] = values[:, :, lanes]
    results = ((new_vel_ref, new_vel_hbm), (new_k_ref, new_k_hbm), (new_w_ref, new_w_hbm))
    copies = [
        pltpu.make_async_copy(source, target, stored.at[i])
        for i, (source, target) in enumerate(results)
    ]
    for copy in copies:
        copy.start()

    kinds = 4
    table = field_ref[...].reshape(PRODUCTS * cells_s * kinds * cells_g, cells_r)
    table = table.astype(jnp.bfloat16)
    pair = 2 * LANES
    girth_row = lax.broadcasted_iota(jnp.int32, (cells_g, pair), 0).astype(jnp.float32)
    index_type = jnp.bfloat16 if cells_r <= 256 else jnp.float32
    radial_row = lax.broadcasted_iota(jnp.int32, (cells_r, pair), 0).astype(jnp.float32)
    radial_row = radial_row.astype(index_type)
    one, none = jnp.ones((), jnp.bfloat16), jnp.zeros((), jnp.bfloat16)

    def two(values, j):
        return jnp.concatenate([values[j : j + 1], values[j + 1 : j + 2]], axis=1)

    def spread(values, j):
        return jnp.broadcast_to(values[j : j + 1], (cells_g, LANES))

    def pick(c, s, kind, index, half_of):
        out = None
        for h in range(halves):
            got = jnp.take_along_axis(
                gather_ref[c - PRODUCTS, s, kind, h], index, axis=1, mode="promise_in_bounds"
            )
            out = got if out is None else jnp.where(half_of[h], got, out)
        return out

    def eight(at):
        here = pl.ds(at, ROWS)
        q8, fr8, xg8, xs8 = (r[here, :] for r in (q_ref, fr_ref, xg_ref, xs_ref))
        hs8 = [jnp.maximum(1.0 - jnp.abs(xs8 - float(s)), 0.0) for s in range(cells_s)]
        index8 = q8 & (LANES - 1)
        qf8 = q8.astype(jnp.float32)
        sums = [[], [], []]
        for j in range(0, ROWS, 2):
            chosen_q = jnp.broadcast_to(two(qf8, j), (cells_r, pair)).astype(index_type)
            hot = jnp.where(radial_row == chosen_q, one, none)
            got = jnp.dot(table, hot, preferred_element_type=jnp.float32)
            got = got.reshape(PRODUCTS, cells_s, kinds, cells_g, pair)
            fr = two(fr8, j)
            hg = jnp.maximum(1.0 - jnp.abs(two(xg8, j) - girth_row), 0.0)
            hs = [two(hs8[s], j) for s in range(cells_s)]
            for c in range(PRODUCTS):
                total = None
                for s in range(cells_s):
                    value = got[c, s, 0] + got[c, s, 1] + fr * (got[c, s, 2] + got[c, s, 3])
                    value = hs[s] * value
                    total = value if total is None else total + value
                total = hg * total
                sums[c] += [total[:, :LANES], total[:, LANES:]]
            for i in (j, j + 1):
                index, q = spread(index8, i), spread(q8, i)
                half_of = [q >= h * LANES for h in range(halves)]
                own_hg = hg[:, (i - j) * LANES : (i - j + 1) * LANES]
                for c in range(PRODUCTS, 3):
                    total = None
                    for s in range(cells_s):
                        value = pick(c, s, 0, index, half_of)
                        value = value + fr8[i : i + 1] * pick(c, s, 1, index, half_of)
                        value = hs8[s][i : i + 1] * value
                        total = value if total is None else total + value
                    sums[c].append(own_hg * total)
        for c in range(3):
            value_ref[0, c, pl.ds(pad + at, ROWS), :] = girth_sums(sums[c])

    def step(group, carry):
        for part in range(2):
            eight(pl.multiple_of((2 * group + part) * ROWS, ROWS))
        return carry

    lax.fori_loop(0, (count_ref[0] + 2 * ROWS - 1) // (2 * ROWS), step, jnp.int32(0))

    for number, (low, digits) in enumerate(reversed(passes)):
        a, b = number % 2, 1 - number % 2
        mask = digits - 1 << low
        last = number == len(passes) - 1
        for at in range(0, rows, CHUNK):
            here = pl.ds(pad + at, CHUNK)
            there = [pl.ds(pad + at - (k << low), CHUNK) for k in range(1, digits)]
            moved = [(moves_ref[there[k], :] & mask) == (k + 1 << low) for k in range(digits - 1)]
            if last:
                kept = (moves_ref[here, :] & valid) != 0
            for c in range(3):
                value = value_ref[a, c, here, :]
                for k in range(digits - 1):
                    value = jnp.where(moved[k], value_ref[a, c, there[k], :], value)
                if last:
                    disk_ref[c, pl.ds(at, CHUNK), :] = jnp.where(kept, value, 0.0)
                else:
                    value_ref[b, c, here, :] = value

    turned = jnp.concatenate([disk_ref[c].T for c in range(3)], axis=0)
    high, low = halved(turned)
    wave_high, wave_low = halved(chosen_ref[...])
    waves = jnp.dot(high, wave_high, preferred_element_type=jnp.float32)
    waves += jnp.dot(high, wave_low, preferred_element_type=jnp.float32)
    waves += jnp.dot(low, wave_high, preferred_element_type=jnp.float32)
    radii = harm_ref.shape[0]
    for c in range(3):
        harm_ref[:, c * 2 * NH : (c + 1) * 2 * NH] = waves[c * radii : (c + 1) * radii]
    block = radii // devices
    for place in range(devices // 2):
        second, rest = divmod(place, devices // 4)
        stream, high = divmod(rest, girth_count // 4)
        at = (stream * girth_count + 4 * high + 2 * second) * block
        even, odd = harm_ref[at : at + block, :], harm_ref[at + block : at + 2 * block, :]
        target = slice(place * block, (place + 1) * block)
        keep_ref[target, :] = jnp.where(girth_odd, odd, even)
        give_ref[target, :] = jnp.where(girth_odd, even, odd)
    for copy in copies:
        copy.wait()


def section(velocity, pressure, energy, rate, halos, points, devices, girth_count):
    _, cells_s, cells_g, cells_r = velocity.shape
    *lists, moves, chosen, counts = points
    rows, radii = lists[0].shape
    shape = functools.partial(jax.ShapeDtypeStruct, dtype=jnp.float32)
    scratch = lambda *dims: pltpu.VMEM(dims, jnp.float32)
    vmem = pl.BlockSpec(memory_space=pltpu.VMEM)
    smem = pl.BlockSpec(memory_space=pltpu.SMEM)
    return pl.pallas_call(
        functools.partial(section_kernel, devices, girth_count),
        out_shape=(
            shape(velocity.shape),
            shape(energy.shape),
            shape(rate.shape),
            shape((radii // 2, 6 * NH)),
            shape((radii // 2, 6 * NH)),
        ),
        in_specs=[smem] + [vmem] * 14,
        out_specs=[pl.BlockSpec(memory_space=pl.ANY)] * 3 + [vmem] * 2,
        scratch_shapes=[
            scratch(*velocity.shape),
            scratch(*energy.shape),
            scratch(*rate.shape),
            scratch(6, cells_s, 3 * ROWS, cells_r),
            scratch(cells_s, 3 * ROWS, cells_r),
            scratch(PRODUCTS, cells_s, 4, cells_g, cells_r),
            scratch(3 - PRODUCTS, cells_s, 2, cells_r // LANES, cells_g, LANES),
            scratch(2, 3, moves.shape[0], radii),
            scratch(3, rows, radii),
            scratch(radii, 6 * NH),
            pltpu.SemaphoreType.DMA((3,)),
        ],
        compiler_params=pltpu.CompilerParams(vmem_limit_bytes=VMEM_LIMIT),
        name="section_and_disk",
    )(counts, velocity, pressure, energy, rate, *halos, *lists, moves, chosen)


def fourier_table(azimuths, modes):
    phase = np.arange(azimuths)[:, None] * np.arange(modes)[None, :] % azimuths
    angles = phase * (2.0 * math.pi / azimuths)
    table = np.concatenate([np.cos(angles), -np.sin(angles)], axis=1) / math.sqrt(azimuths)
    return jnp.asarray(table.astype(np.float32))


def body(velocity, pressure, kinetic_energy, dissipation_rate, corner_ids, fractions, sector_owner):
    _, cells_s, cells_g, cells_r = velocity.shape
    radii, azimuths = corner_ids.shape
    stream_count, girth_count = lax.axis_size("stream"), lax.axis_size("girth")
    devices = stream_count * girth_count

    def swap(values, axis, count, start):
        pairs = []
        for i in range(start, count - 1, 2):
            pairs += [(i, i + 1), (i + 1, i)]
        return lax.ppermute(values, axis, pairs)

    *slabs, ids, first = pack(
        velocity, pressure, kinetic_energy, dissipation_rate, corner_ids, fractions
    )
    girth_halos = (
        swap(slabs[2], "girth", girth_count, 0),
        swap(slabs[3], "girth", girth_count, 1),
    )
    stream_halos = (
        swap(slabs[0], "stream", stream_count, 0),
        swap(slabs[1], "stream", stream_count, 1),
    )
    halos = stream_halos + girth_halos
    points = prepare(
        sector_owner[:, 0],
        ids,
        first,
        fractions,
        fourier_table(azimuths, NH),
        (cells_s, cells_g, cells_r),
        girth_count,
    )
    new_velocity, new_energy, new_rate, keep, give = section(
        velocity, pressure, kinetic_energy, dissipation_rate, halos, points, devices, girth_count
    )
    total = keep + swap(give, "girth", girth_count, 0)
    half = radii // 4
    second = lax.axis_index("girth") // 2 % 2
    give = lax.dynamic_slice_in_dim(total, (1 - second) * half, half, axis=0)
    keep = lax.dynamic_slice_in_dim(total, second * half, half, axis=0)
    total = keep + lax.ppermute(give, "girth", [(i, i ^ 2) for i in range(girth_count)])
    shares = lax.all_to_all(
        total.reshape(devices // 4, radii // devices, 6 * NH),
        ("stream", "girth"),
        split_axis=0,
        concat_axis=0,
        tiled=True,
        axis_index_groups=[list(range(part, devices, 4)) for part in range(4)],
    )
    return new_velocity, new_energy, new_rate, jnp.sum(shares, axis=0)


def solution(mesh):
    return jax.shard_map(
        body,
        mesh=mesh,
        in_specs=(
            P(None, "stream", "girth", None),
            P("stream", "girth", None),
            P("stream", "girth", None),
            P("stream", "girth", None),
            P(),
            P(),
            P(),
        ),
        out_specs=(
            P(None, "stream", "girth", None),
            P("stream", "girth", None),
            P("stream", "girth", None),
            P(("stream", "girth"), None),
        ),
        check_vma=False,
    )
```

```python
import functools
import math

import jax
import jax.numpy as jnp
import numpy as np
from jax import lax
from jax.experimental import pallas as pl
from jax.experimental.pallas import tpu as pltpu
from jax.sharding import PartitionSpec as P

NH = 128

base_viscosity = 0.05
time_step = 0.2
beta_star = 0.09
beta_rate = 0.075
alpha_rate = 0.52
wall_rate = 1.0

LANES = 128
ROWS = 8
SHIFT = 10
CHUNK = 32
PRODUCTS = 2
VMEM_LIMIT = 48 * 1024 * 1024


def in_hbm(values):
    return pltpu.with_memory_space_constraint(values, pltpu.HBM)


def pack_kernel(vel_hbm, p_hbm, k_hbm, w_hbm, ids_hbm, frac_hbm, *rest):
    *slabs, ids_ref, first_ref, fields, arrived = rest
    moves = [(vel_hbm, fields.at[0:3]), (p_hbm, fields.at[3]), (k_hbm, fields.at[4])]
    moves += [(w_hbm, fields.at[5]), (ids_hbm, ids_ref), (frac_hbm.at[0], first_ref)]
    copies = [
        pltpu.make_async_copy(source, target, arrived.at[i])
        for i, (source, target) in enumerate(moves)
    ]
    for copy in copies:
        copy.start()
    _, cells_s, cells_g, _ = fields.shape
    stream_odd = lax.axis_index("stream") % 2 == 1
    girth_odd = lax.axis_index("girth") % 2 == 1
    for copy in copies[:4]:
        copy.wait()
    for f in range(6):
        first, last = fields[f, 0:2], fields[f, cells_s - 2 : cells_s]
        slabs[0][f] = jnp.where(stream_odd, first, last)
        slabs[1][f] = jnp.where(stream_odd, last, first)
        first, last = fields[f, :, 0:2, :], fields[f, :, cells_g - 2 : cells_g, :]
        slabs[2][f] = jnp.where(girth_odd, first, last)
        slabs[3][f] = jnp.where(girth_odd, last, first)
    for copy in copies[4:]:
        copy.wait()


def pack(velocity, pressure, energy, rate, corner_ids, fractions):
    _, cells_s, cells_g, cells_r = velocity.shape
    stream = pltpu.VMEM((6, 2, cells_g, cells_r), jnp.float32)
    girth = pltpu.VMEM((6, cells_s, 2, cells_r), jnp.float32)
    points = [pltpu.VMEM(corner_ids.shape, x.dtype) for x in (corner_ids, fractions)]
    inputs = (velocity, pressure, energy, rate, corner_ids, fractions)
    return pl.pallas_call(
        pack_kernel,
        out_shape=[stream, stream, girth, girth] + points,
        in_specs=[pl.BlockSpec(memory_space=pltpu.HBM)] * 6,
        out_specs=[pl.BlockSpec(memory_space=pltpu.VMEM)] * 6,
        scratch_shapes=[
            pltpu.VMEM((6, cells_s, cells_g, cells_r), jnp.float32),
            pltpu.SemaphoreType.DMA((6,)),
        ],
        compiler_params=pltpu.CompilerParams(vmem_limit_bytes=VMEM_LIMIT),
        name="pack_halos",
    )(*(in_hbm(x) for x in inputs))


def network(rows):
    steps = (rows - 1).bit_length()
    return [(low, 1 << min(2, steps - low)) for low in range(0, steps, 2)]


def reach(rows):
    return max((digits - 1) << low for low, digits in network(rows))


def split(values, size):
    if size & (size - 1) == 0:
        return values >> (size.bit_length() - 1), values & (size - 1)
    return values // size, values % size


def prepare_kernel(
    cells_s,
    cells_g,
    cells_r,
    owner_ref,
    ids_ref,
    first_ref,
    frac_hbm,
    table_hbm,
    q_ref,
    fr_ref,
    xs_ref,
    xg_ref,
    moves_ref,
    chosen_ref,
    count_ref,
    frac_ref,
    table_ref,
    turned,
    picked,
    keys,
    frs,
    xss,
    xgs,
    order,
    arrived,
):
    copies = [
        pltpu.make_async_copy(frac_hbm.at[1], frac_ref.at[0], arrived.at[0]),
        pltpu.make_async_copy(frac_hbm.at[2], frac_ref.at[1], arrived.at[1]),
        pltpu.make_async_copy(table_hbm, table_ref, arrived.at[2]),
    ]
    for copy in copies:
        copy.start()
    stream_first = lax.axis_index("stream") * cells_s
    me = lax.axis_index("girth")
    sectors = owner_ref.shape[0]
    azimuths = ids_ref.shape[1]
    width = azimuths // sectors
    rows = fr_ref.shape[0]
    pad = moves_ref.shape[0] - rows
    passes = network(rows)
    valid = 1 << SHIFT - 1

    places = rows // width
    for place in range(places):
        order[place] = 0

    def listed(number, count):
        order[jnp.minimum(count, places)] = number
        return count + (owner_ref[number] == me).astype(jnp.int32)

    owned = lax.fori_loop(0, sectors, listed, jnp.int32(0), unroll=8)
    beyond = pl.ds(rows, pad)
    for slot in range(2):
        keys[slot, beyond, :] = jnp.zeros((pad, LANES), jnp.int32)
    moves_ref[0:pad, :] = jnp.zeros((pad, LANES), jnp.int32)
    planes = (ids_ref, first_ref, frac_ref.at[0], frac_ref.at[1])
    for d in range(4):
        if d >= 2:
            copies[d - 2].wait()
        for at in range(0, azimuths, LANES):
            cols = pl.ds(at, LANES)
            turned[d, cols, :] = planes[d][:, cols].astype(jnp.float32).T
    copies[2].wait()

    for place in range(places):
        source = pl.ds(pl.multiple_of(order[place] * width, width), width)
        target = pl.ds(place * width, width)
        chosen_ref[target, :] = table_ref[source, :]
        picked[0, target, :] = jnp.where(place < owned, turned[0, source, :], -1.0)
        for d in range(1, 4):
            picked[d, target, :] = turned[d, source, :]

    held = pl.ds(0, rows)
    ids = picked[0].astype(jnp.int32)
    stream_cell, rest = split(jnp.maximum(ids, 0), cells_g * cells_r)
    girth_cell, radial_cell = split(rest, cells_r)
    xs = (stream_cell - stream_first).astype(jnp.float32) + picked[1]
    kept = (ids >= 0) & (xs > -1.0) & (xs < float(cells_s))
    xss[0, held, :] = xs
    xgs[0, held, :] = girth_cell.astype(jnp.float32) + picked[2]
    frs[0, held, :] = picked[3]
    earlier = lax.broadcasted_iota(jnp.int32, (rows, rows), 0) > lax.broadcasted_iota(
        jnp.int32, (rows, rows), 1
    )
    earlier = earlier.astype(jnp.float32).astype(jnp.bfloat16)
    skipped = jnp.where(kept, 0.0, 1.0)
    before = jnp.dot(
        earlier, skipped.astype(jnp.bfloat16), preferred_element_type=jnp.float32
    ).astype(jnp.int32)
    counts = rows - jnp.sum(skipped, axis=0, keepdims=True).astype(jnp.int32)
    count_ref[0] = jnp.max(counts)
    moves_ref[pad : pad + rows, :] = jnp.where(kept, valid, 0)
    keys[0, held, :] = (radial_cell << SHIFT) + jnp.where(kept, before, 0)
    for number, (low, digits) in enumerate(passes):
        a, b = number % 2, 1 - number % 2
        mask = digits - 1 << low
        last = number == len(passes) - 1
        for at in range(0, rows, CHUNK):
            here, target = pl.ds(at, CHUNK), pl.ds(pad + at, CHUNK)
            there = [pl.ds(at + (k << low), CHUNK) for k in range(1, digits)]
            key = keys[a, here, :]
            arriving = [keys[a, t, :] for t in there]
            moved = [(arriving[k] & mask) == (k + 1 << low) for k in range(digits - 1)]
            key = jnp.where((key & mask) != 0, key & -(1 << SHIFT), key)
            came = moves_ref[target, :]
            out = [r[a, here, :] for r in (frs, xss, xgs)]
            for k in range(digits - 1):
                key = jnp.where(moved[k], arriving[k], key)
                came = came | jnp.where(moved[k], k + 1 << low, 0)
                out = [
                    jnp.where(moved[k], r[a, there[k], :], o) for r, o in zip((frs, xss, xgs), out)
                ]
            moves_ref[target, :] = came
            if last:
                q_ref[here, :] = key >> SHIFT
                fr_ref[here, :] = out[0]
                xs_ref[here, :] = out[1]
                xg_ref[here, :] = out[2]
            else:
                keys[b, here, :] = key
                frs[b, here, :] = out[0]
                xss[b, here, :] = out[1]
                xgs[b, here, :] = out[2]


def prepare(owners, corner_ids, first, fractions, table, cells, girth_count):
    cells_s, cells_g, cells_r = cells
    radii, azimuths = corner_ids.shape
    sectors = owners.shape[0]
    rows = 3 * sectors // girth_count * (azimuths // sectors)
    pad = reach(rows)
    shape = jax.ShapeDtypeStruct
    lists = (rows, radii)
    vmem = pl.BlockSpec(memory_space=pltpu.VMEM)
    smem = pl.BlockSpec(memory_space=pltpu.SMEM)
    hbm = pl.BlockSpec(memory_space=pltpu.HBM)
    return pl.pallas_call(
        functools.partial(prepare_kernel, cells_s, cells_g, cells_r),
        out_shape=(
            shape(lists, jnp.int32),
            shape(lists, jnp.float32),
            shape(lists, jnp.float32),
            shape(lists, jnp.float32),
            shape((pad + rows, radii), jnp.int32),
            shape((rows, 2 * NH), jnp.float32),
            shape((1,), jnp.int32),
        ),
        in_specs=[smem, vmem, vmem, hbm, hbm],
        out_specs=[vmem] * 6 + [smem],
        scratch_shapes=[
            pltpu.VMEM((2, radii, azimuths), jnp.float32),
            pltpu.VMEM(table.shape, jnp.float32),
            pltpu.VMEM((4, azimuths, radii), jnp.float32),
            pltpu.VMEM((4, rows, radii), jnp.float32),
            pltpu.VMEM((2, rows + pad, radii), jnp.int32),
        ]
        + [pltpu.VMEM((2, rows + pad, radii), jnp.float32)] * 3
        + [pltpu.SMEM((rows // (azimuths // sectors) + 1,), jnp.int32)]
        + [pltpu.SemaphoreType.DMA((3,))],
        compiler_params=pltpu.CompilerParams(vmem_limit_bytes=VMEM_LIMIT),
        cost_estimate=pl.CostEstimate(
            flops=20 * radii * azimuths, bytes_accessed=44 * radii * azimuths, transcendentals=0
        ),
        name="prepare_points",
    )(in_hbm(owners), corner_ids, first, in_hbm(fractions), in_hbm(table))


def radial(values, amount, fill):
    extent = values.shape[-1]
    rolled = pltpu.roll(values, (-amount) % extent, values.ndim - 1)
    position = lax.broadcasted_iota(jnp.int32, values.shape, values.ndim - 1) + amount
    return jnp.where((position >= 0) & (position < extent), rolled, fill)


def advance(own, before, after, left, right, ext_ref, visc_ref):
    cells_s, cells_g, _ = own[0].shape
    mid = ROWS

    def along_s(stack, amount):
        return stack[2 + amount : 2 + amount + cells_s]

    def along_g(ref, amount):
        return ref[:, mid + amount : mid + amount + cells_g, :]

    def viscosity(energy, rate):
        return base_viscosity + energy / (rate + wall_rate)

    stacks = [jnp.concatenate([before[f], own[f], after[f]], axis=0) for f in range(6)]
    for f in range(6):
        ext_ref[f, :, mid - 2 : mid, :] = left[f]
        ext_ref[f, :, mid : mid + cells_g, :] = own[f]
        ext_ref[f, :, mid + cells_g : mid + cells_g + 2, :] = right[f]
    middle = viscosity(own[4], own[5])
    visc_stack = viscosity(stacks[4], stacks[5])
    visc_ref[:, mid - 2 : mid, :] = viscosity(left[4], left[5])
    visc_ref[:, mid : mid + cells_g, :] = middle
    visc_ref[:, mid + cells_g : mid + cells_g + 2, :] = viscosity(right[4], right[5])
    faces = [
        (
            0.5 * (middle + along_s(visc_stack, 1)),
            0.5 * (middle + along_s(visc_stack, -1)),
        ),
        (
            0.5 * (middle + along_g(visc_ref, 1)),
            0.5 * (middle + along_g(visc_ref, -1)),
        ),
        (
            0.5 * (middle + radial(middle, 1, base_viscosity)),
            0.5 * (middle + radial(middle, -1, base_viscosity)),
        ),
    ]

    def neighbour(f, direction, amount):
        if direction == 0:
            return along_s(stacks[f], amount)
        if direction == 1:
            return along_g(ext_ref.at[f], amount)
        return radial(own[f], amount, 0.0)

    def terms(f, direction):
        up, down = neighbour(f, direction, 1), neighbour(f, direction, -1)
        far = neighbour(f, direction, 2) - neighbour(f, direction, -2)
        gradient = (8.0 * (up - down) - far) * (1.0 / 12.0)
        above, below = faces[direction]
        return gradient, above * (up - own[f]) - below * (own[f] - down)

    strain = None
    updated = []
    for f in range(3):
        change = -terms(3, f)[0]
        for direction in range(3):
            gradient, spread = terms(f, direction)
            strain = gradient * gradient if strain is None else strain + gradient * gradient
            change = change - own[direction] * gradient + spread
        updated.append(own[f] + time_step * change)
    energy = own[4] / (own[5] + wall_rate) * strain - beta_star * own[4] * own[5]
    rate = alpha_rate * strain - beta_rate * own[5] * own[5]
    for direction in range(3):
        gradient, spread = terms(4, direction)
        energy = energy - own[direction] * gradient + spread
        gradient, spread = terms(5, direction)
        rate = rate - own[direction] * gradient + spread
    return updated, own[4] + time_step * energy, own[5] + time_step * rate


def girth_sums(parts):
    row = lax.broadcasted_iota(jnp.int32, parts[0].shape, 0)

    def swapped(values, distance):
        up = pltpu.roll(values, distance, 0)
        if 2 * distance == ROWS:
            return up
        return jnp.where((row & distance) != 0, up, pltpu.roll(values, ROWS - distance, 0))

    distance = ROWS // 2
    while distance > 0:
        low = (row & distance) == 0
        parts = [
            jnp.where(low, x, y) + swapped(jnp.where(low, y, x), distance)
            for x, y in zip(parts[:distance], parts[distance:])
        ]
        distance //= 2
    return parts[0]


def section_kernel(
    devices,
    count_ref,
    vel_ref,
    p_ref,
    k_ref,
    w_ref,
    stream_a,
    stream_b,
    girth_a,
    girth_b,
    q_ref,
    fr_ref,
    xs_ref,
    xg_ref,
    moves_ref,
    chosen_ref,
    new_vel_hbm,
    new_k_hbm,
    new_w_hbm,
    keep_ref,
    give_ref,
    new_vel_ref,
    new_k_ref,
    new_w_ref,
    ext_ref,
    visc_ref,
    field_ref,
    gather_ref,
    value_ref,
    disk_ref,
    harm_ref,
    stored,
):
    cells_s, cells_g, cells_r = p_ref.shape
    rows = fr_ref.shape[0]
    pad = moves_ref.shape[0] - rows
    passes = network(rows)
    valid = 1 << SHIFT - 1
    stream_odd = lax.axis_index("stream") % 2 == 1
    girth_odd = lax.axis_index("girth") % 2 == 1

    own = [vel_ref[0], vel_ref[1], vel_ref[2], p_ref[...], k_ref[...], w_ref[...]]
    six = range(6)
    updated, energy, rate = advance(
        own,
        [jnp.where(stream_odd, stream_a[f], stream_b[f]) for f in six],
        [jnp.where(stream_odd, stream_b[f], stream_a[f]) for f in six],
        [jnp.where(girth_odd, girth_a[f], girth_b[f]) for f in six],
        [jnp.where(girth_odd, girth_b[f], girth_a[f]) for f in six],
        ext_ref,
        visc_ref,
    )
    new_k_ref[...] = energy
    new_w_ref[...] = rate

    def halved(values):
        high = values.astype(jnp.bfloat16)
        return high, (values - high.astype(jnp.float32)).astype(jnp.bfloat16)

    def rounded(values):
        return values.astype(jnp.bfloat16).astype(jnp.float32)

    halves = cells_r // LANES
    for c in range(3):
        new_vel_ref[c] = updated[c]
        slope = radial(updated[c], 1, 0.0) - updated[c]
        for kind, values in enumerate((updated[c], slope)):
            if c < PRODUCTS:
                high = rounded(values)
                field_ref[c, :, 2 * kind] = high
                field_ref[c, :, 2 * kind + 1] = rounded(values - high)
            else:
                for h in range(halves):
                    lanes = slice(h * LANES, (h + 1) * LANES)
                    gather_ref[c - PRODUCTS, :, kind, h] = values[:, :, lanes]
    results = ((new_vel_ref, new_vel_hbm), (new_k_ref, new_k_hbm), (new_w_ref, new_w_hbm))
    copies = [
        pltpu.make_async_copy(source, target, stored.at[i])
        for i, (source, target) in enumerate(results)
    ]
    for copy in copies:
        copy.start()

    kinds = 4
    table = field_ref[...].reshape(PRODUCTS * cells_s * kinds * cells_g, cells_r)
    table = table.astype(jnp.bfloat16)
    pair = 2 * LANES
    girth_row = lax.broadcasted_iota(jnp.int32, (cells_g, pair), 0).astype(jnp.float32)
    index_type = jnp.bfloat16 if cells_r <= 256 else jnp.float32
    radial_row = lax.broadcasted_iota(jnp.int32, (cells_r, pair), 0).astype(jnp.float32)
    radial_row = radial_row.astype(index_type)
    one, none = jnp.ones((), jnp.bfloat16), jnp.zeros((), jnp.bfloat16)

    def two(values, j):
        return jnp.concatenate([values[j : j + 1], values[j + 1 : j + 2]], axis=1)

    def spread(values, j):
        return jnp.broadcast_to(values[j : j + 1], (cells_g, LANES))

    def pick(c, s, kind, index, half_of):
        out = None
        for h in range(halves):
            got = jnp.take_along_axis(
                gather_ref[c - PRODUCTS, s, kind, h], index, axis=1, mode="promise_in_bounds"
            )
            out = got if out is None else jnp.where(half_of[h], got, out)
        return out

    def eight(at):
        here = pl.ds(at, ROWS)
        q8, fr8, xg8, xs8 = (r[here, :] for r in (q_ref, fr_ref, xg_ref, xs_ref))
        hs8 = [jnp.maximum(1.0 - jnp.abs(xs8 - float(s)), 0.0) for s in range(cells_s)]
        index8 = q8 & (LANES - 1)
        qf8 = q8.astype(jnp.float32)
        sums = [[], [], []]
        for j in range(0, ROWS, 2):
            chosen_q = jnp.broadcast_to(two(qf8, j), (cells_r, pair)).astype(index_type)
            hot = jnp.where(radial_row == chosen_q, one, none)
            got = jnp.dot(table, hot, preferred_element_type=jnp.float32)
            got = got.reshape(PRODUCTS, cells_s, kinds, cells_g, pair)
            fr = two(fr8, j)
            hg = jnp.maximum(1.0 - jnp.abs(two(xg8, j) - girth_row), 0.0)
            hs = [two(hs8[s], j) for s in range(cells_s)]
            for c in range(PRODUCTS):
                total = None
                for s in range(cells_s):
                    value = got[c, s, 0] + got[c, s, 1] + fr * (got[c, s, 2] + got[c, s, 3])
                    value = hs[s] * value
                    total = value if total is None else total + value
                total = hg * total
                sums[c] += [total[:, :LANES], total[:, LANES:]]
            for i in (j, j + 1):
                index, q = spread(index8, i), spread(q8, i)
                half_of = [q >= h * LANES for h in range(halves)]
                own_hg = hg[:, (i - j) * LANES : (i - j + 1) * LANES]
                for c in range(PRODUCTS, 3):
                    total = None
                    for s in range(cells_s):
                        value = pick(c, s, 0, index, half_of)
                        value = value + fr8[i : i + 1] * pick(c, s, 1, index, half_of)
                        value = hs8[s][i : i + 1] * value
                        total = value if total is None else total + value
                    sums[c].append(own_hg * total)
        for c in range(3):
            value_ref[0, c, pl.ds(pad + at, ROWS), :] = girth_sums(sums[c])

    def step(group, carry):
        for part in range(2):
            eight(pl.multiple_of((2 * group + part) * ROWS, ROWS))
        return carry

    lax.fori_loop(0, (count_ref[0] + 2 * ROWS - 1) // (2 * ROWS), step, jnp.int32(0))

    for number, (low, digits) in enumerate(reversed(passes)):
        a, b = number % 2, 1 - number % 2
        mask = digits - 1 << low
        last = number == len(passes) - 1
        for at in range(0, rows, CHUNK):
            here = pl.ds(pad + at, CHUNK)
            there = [pl.ds(pad + at - (k << low), CHUNK) for k in range(1, digits)]
            moved = [(moves_ref[there[k], :] & mask) == (k + 1 << low) for k in range(digits - 1)]
            if last:
                kept = (moves_ref[here, :] & valid) != 0
            for c in range(3):
                value = value_ref[a, c, here, :]
                for k in range(digits - 1):
                    value = jnp.where(moved[k], value_ref[a, c, there[k], :], value)
                if last:
                    disk_ref[c, pl.ds(at, CHUNK), :] = jnp.where(kept, value, 0.0)
                else:
                    value_ref[b, c, here, :] = value

    turned = jnp.concatenate([disk_ref[c].T for c in range(3)], axis=0)
    high, low = halved(turned)
    wave_high, wave_low = halved(chosen_ref[...])
    waves = jnp.dot(high, wave_high, preferred_element_type=jnp.float32)
    waves += jnp.dot(high, wave_low, preferred_element_type=jnp.float32)
    waves += jnp.dot(low, wave_high, preferred_element_type=jnp.float32)
    radii = harm_ref.shape[0]
    for c in range(3):
        harm_ref[:, c * 2 * NH : (c + 1) * 2 * NH] = waves[c * radii : (c + 1) * radii]
    block = radii // devices
    for place in range(devices // 2):
        even = harm_ref[2 * place * block : (2 * place + 1) * block, :]
        odd = harm_ref[(2 * place + 1) * block : (2 * place + 2) * block, :]
        keep_ref[place * block : (place + 1) * block, :] = jnp.where(girth_odd, odd, even)
        give_ref[place * block : (place + 1) * block, :] = jnp.where(girth_odd, even, odd)
    for copy in copies:
        copy.wait()


def section(velocity, pressure, energy, rate, halos, points, devices):
    _, cells_s, cells_g, cells_r = velocity.shape
    *lists, moves, chosen, counts = points
    rows, radii = lists[0].shape
    shape = functools.partial(jax.ShapeDtypeStruct, dtype=jnp.float32)
    scratch = lambda *dims: pltpu.VMEM(dims, jnp.float32)
    vmem = pl.BlockSpec(memory_space=pltpu.VMEM)
    smem = pl.BlockSpec(memory_space=pltpu.SMEM)
    return pl.pallas_call(
        functools.partial(section_kernel, devices),
        out_shape=(
            shape(velocity.shape),
            shape(energy.shape),
            shape(rate.shape),
            shape((radii // 2, 6 * NH)),
            shape((radii // 2, 6 * NH)),
        ),
        in_specs=[smem] + [vmem] * 14,
        out_specs=[pl.BlockSpec(memory_space=pl.ANY)] * 3 + [vmem] * 2,
        scratch_shapes=[
            scratch(*velocity.shape),
            scratch(*energy.shape),
            scratch(*rate.shape),
            scratch(6, cells_s, 3 * ROWS, cells_r),
            scratch(cells_s, 3 * ROWS, cells_r),
            scratch(PRODUCTS, cells_s, 4, cells_g, cells_r),
            scratch(3 - PRODUCTS, cells_s, 2, cells_r // LANES, cells_g, LANES),
            scratch(2, 3, moves.shape[0], radii),
            scratch(3, rows, radii),
            scratch(radii, 6 * NH),
            pltpu.SemaphoreType.DMA((3,)),
        ],
        compiler_params=pltpu.CompilerParams(vmem_limit_bytes=VMEM_LIMIT),
        name="section_and_disk",
    )(counts, velocity, pressure, energy, rate, *halos, *lists, moves, chosen)


def fourier_table(azimuths, modes):
    phase = np.arange(azimuths)[:, None] * np.arange(modes)[None, :] % azimuths
    angles = phase * (2.0 * math.pi / azimuths)
    table = np.concatenate([np.cos(angles), -np.sin(angles)], axis=1) / math.sqrt(azimuths)
    return jnp.asarray(table.astype(np.float32))


def body(velocity, pressure, kinetic_energy, dissipation_rate, corner_ids, fractions, sector_owner):
    _, cells_s, cells_g, cells_r = velocity.shape
    radii, azimuths = corner_ids.shape
    stream_count, girth_count = lax.axis_size("stream"), lax.axis_size("girth")
    devices = stream_count * girth_count

    def swap(values, axis, count, start):
        pairs = []
        for i in range(start, count - 1, 2):
            pairs += [(i, i + 1), (i + 1, i)]
        return lax.ppermute(values, axis, pairs)

    *slabs, ids, first = pack(
        velocity, pressure, kinetic_energy, dissipation_rate, corner_ids, fractions
    )
    girth_halos = (
        swap(slabs[2], "girth", girth_count, 0),
        swap(slabs[3], "girth", girth_count, 1),
    )
    stream_halos = (
        swap(slabs[0], "stream", stream_count, 0),
        swap(slabs[1], "stream", stream_count, 1),
    )
    halos = stream_halos + girth_halos
    points = prepare(
        sector_owner[:, 0],
        ids,
        first,
        fractions,
        fourier_table(azimuths, NH),
        (cells_s, cells_g, cells_r),
        girth_count,
    )
    new_velocity, new_energy, new_rate, keep, give = section(
        velocity, pressure, kinetic_energy, dissipation_rate, halos, points, devices
    )
    total = keep + swap(give, "girth", girth_count, 0)
    shares = lax.all_to_all(
        total.reshape(devices // 2, radii // devices, 6 * NH),
        ("stream", "girth"),
        split_axis=0,
        concat_axis=0,
        tiled=True,
        axis_index_groups=[list(range(parity, devices, 2)) for parity in (0, 1)],
    )
    return new_velocity, new_energy, new_rate, jnp.sum(shares, axis=0)


def solution(mesh):
    return jax.shard_map(
        body,
        mesh=mesh,
        in_specs=(
            P(None, "stream", "girth", None),
            P("stream", "girth", None),
            P("stream", "girth", None),
            P("stream", "girth", None),
            P(),
            P(),
            P(),
        ),
        out_specs=(
            P(None, "stream", "girth", None),
            P("stream", "girth", None),
            P("stream", "girth", None),
            P(("stream", "girth"), None),
        ),
        check_vma=False,
    )
```
